128 devices in a mesh: lon: 8 (over y, z_hi), lat: 16 (over z_lo, x, core).
Axes of the slice: x: 4, y: 4, z: 4 (z_hi: 2, z_lo: 2; z = z_hi * 2 + z_lo), core: 2. Of those that a mesh axis runs over, the one named last changes fastest.
Arguments:
- tokens: bfloat16 [2, 96, 96, 192], P(None, 'lat', 'lon'), may hold values from -6 to 6
- cotangent: bfloat16 [2, 96, 96, 192], P(None, 'lat', 'lon'), may hold values from -6 to 6
- ln1_gain: float32 [192], replicated, may hold values from 0.1 to 1.9
- w_qkv: bfloat16 [192, 576], replicated, may hold values from -0.4375 to 0.4375
- b_qkv: float32 [576], replicated, may hold values from -3 to 3
- bias_table: float32 [1, 16, 6, 3312], P(None, 'lat'), may hold values from -5 to 250
- w_proj: bfloat16 [192, 192], replicated, may hold values from -0.4375 to 0.4375
- ln2_gain: float32 [192], replicated, may hold values from 0.1 to 1.9
- w_fc1: bfloat16 [192, 768], replicated, may hold values from -0.4375 to 0.4375
- b_fc1: float32 [768], replicated, may hold values from -3 to 3
- w_fc2: bfloat16 [768, 192], replicated, may hold values from -0.21875 to 0.21875
Outputs:
- block_out: bfloat16 [2, 96, 96, 192], P(None, 'lat', 'lon')
- d_tokens: bfloat16 [2, 96, 96, 192], P(None, 'lat', 'lon')
- d_ln1_gain: float32 [192], replicated
- d_w_qkv: float32 [192, 576], replicated
- d_b_qkv: float32 [576], replicated
- d_bias_table: float32 [1, 16, 6, 3312], P(None, 'lat')
- d_w_proj: float32 [192, 192], replicated
- d_ln2_gain: float32 [192], replicated
- d_w_fc1: float32 [192, 768], replicated
- d_b_fc1: float32 [768], replicated
- d_w_fc2: float32 [768, 192], replicated
The draws below stay inside these ranges and needn't reach their ends.
All inputs are finite; a program needn't handle non-finite values.
Results may differ from the reference program's by a relative error of at most 0.015.
Values may be sent and summed in bfloat16 or wider, within the bound.
A program may use at most 128 MiB of HBM per device.

```python
import jax
import jax.numpy as jnp
from jax import lax

C = 192
HEADS = 6
HID = 768
LEV = 2
WIN_Z = 2
WIN_H = 6
WIN_W = 12
NREL = 3312
NLAT = 96
NLON = 96


def draw_bias_table(key, part):
    key = jax.random.fold_in(key, 7)
    level_types = LEV // WIN_Z
    row_types = NLAT // WIN_H
    noise_key = jax.random.fold_in(key, 0)
    return jnp.clip(jax.random.normal(noise_key, (level_types, row_types, HEADS, NREL), jnp.float32), -5.0, 5.0)


def block_scale(stream_key, shape, shards, low, top_value):
    level = 1.0
    for dim, blocks in shards:
        steps = jax.random.uniform(jax.random.fold_in(jax.random.fold_in(stream_key, 6), dim), (blocks,), jnp.float32, low / len(shards), top_value / len(shards))
        level = level * jnp.repeat(jnp.exp(steps), shape[dim] // blocks).reshape((-1,) + (1,) * (len(shape) - 1 - dim))
    return level


def noise(stream_key, dims, scale, bound, cuts=(), held_as=jnp.bfloat16):
    values = scale * jax.random.normal(stream_key, dims, jnp.float32)
    if cuts:
        values = values * block_scale(stream_key, dims, cuts, -0.22, 0.18)
    return jnp.clip(values, -bound, bound).astype(held_as)


def setup_inputs(seed: int = 0) -> dict:
    keys = jax.random.split(jax.random.key(seed), 12)
    return {
        "tokens": noise(keys[0], (LEV, NLAT, NLON, C), 1.0, 6.0, ((1, 16), (2, 8))),
        "cotangent": noise(keys[1], (LEV, NLAT, NLON, C), 1.0, 6.0, ((1, 16), (2, 8))),
        "ln1_gain": jnp.clip(1.0 + 0.18 * jax.random.normal(keys[2], (C,), jnp.float32), 0.1, 1.9),
        "w_qkv": noise(keys[3], (C, 3 * C), C ** -0.5, 0.4375),
        "b_qkv": noise(keys[4], (3 * C,), 0.5, 3.0, (), jnp.float32),
        "bias_table": draw_bias_table(jax.random.fold_in(keys[11], 71), 0),
        "w_proj": noise(keys[6], (C, C), C ** -0.5, 0.4375),
        "ln2_gain": jnp.clip(1.0 + 0.18 * jax.random.normal(keys[7], (C,), jnp.float32), 0.1, 1.9),
        "w_fc1": noise(keys[8], (C, HID), C ** -0.5, 0.4375),
        "b_fc1": noise(keys[9], (HID,), 0.5, 3.0, (), jnp.float32),
        "w_fc2": noise(keys[10], (HID, C), HID ** -0.5, 0.21875),
    }


EPSILON = 1e-05

def rel_index():
    positions = jnp.arange(WIN_Z * WIN_H * WIN_W, dtype=jnp.int32)
    level_at = positions // (WIN_H * WIN_W)
    row_at = positions // WIN_W % WIN_H
    col_at = positions % WIN_W
    index = ((level_at[:, None] * WIN_Z + level_at[None, :]) * WIN_H + row_at[:, None]) * WIN_H + row_at[None, :]
    index = index * (2 * WIN_W - 1) + col_at[:, None] - col_at[None, :] + WIN_W - 1
    return index.reshape(-1).astype(jnp.int32)

def normalize(values, gain_vec):
    average = lax.optimization_barrier(jnp.mean(values, -1, keepdims=True))
    centered = values - average
    inv_std = lax.rsqrt(lax.optimization_barrier(jnp.mean(centered * centered, -1, keepdims=True)) + EPSILON)
    normal_hat = centered * inv_std
    return (normal_hat * gain_vec, normal_hat, inv_std)

def norm_back(normal_hat, inv_std, gain_vec, gradient):
    scaled = gradient * gain_vec
    result = inv_std * (scaled - lax.optimization_barrier(jnp.mean(scaled, -1, keepdims=True)) - normal_hat * lax.optimization_barrier(jnp.mean(scaled * normal_hat, -1, keepdims=True)))
    gain_grad = lax.optimization_barrier(jnp.sum((gradient * normal_hat).reshape(-1, normal_hat.shape[-1]), 0))
    return (result, gain_grad)

def gelu_parts(pre_act):
    cdf_part = 0.5 * (1.0 + lax.erf(pre_act * 0.7071067811865476))
    density = jnp.exp(-0.5 * pre_act * pre_act) * 0.3989422804014327
    return (pre_act * cdf_part, cdf_part + pre_act * density)

def to_windows(frame_field):
    levels, lat_rows, lon_cols, channels = frame_field.shape
    pieces = frame_field.reshape(levels // WIN_Z, WIN_Z, lat_rows // WIN_H, WIN_H, lon_cols // WIN_W, WIN_W, channels)
    return pieces.transpose(0, 2, 4, 1, 3, 5, 6).reshape(levels // WIN_Z, lat_rows // WIN_H, lon_cols // WIN_W, WIN_Z * WIN_H * WIN_W, channels)

def from_windows(blocks):
    level_wins, row_wins, col_wins, win_tokens, channels = blocks.shape
    pieces = blocks.reshape(level_wins, row_wins, col_wins, WIN_Z, WIN_H, WIN_W, channels)
    return pieces.transpose(0, 3, 1, 4, 2, 5, 6).reshape(level_wins * WIN_Z, row_wins * WIN_H, col_wins * WIN_W, channels)

def as_float(array):
    return array.astype(jnp.float32)

def mix_scores(blocks, bias_rows, key_valid, w_qkv, b_qkv):
    level_wins, row_wins, col_wins, win_tokens, channels = blocks.shape
    head_size = channels // HEADS
    projected = (jnp.dot(blocks.reshape(-1, channels), w_qkv, preferred_element_type=jnp.float32) + b_qkv).astype(jnp.bfloat16)
    projected = projected.reshape(level_wins, row_wins, col_wins, win_tokens, 3, HEADS, head_size)
    queries = projected[:, :, :, :, 0]
    key_rows = projected[:, :, :, :, 1]
    values = projected[:, :, :, :, 2]
    factor = head_size ** (-0.5)
    bias_full = jnp.take(bias_rows, rel_index(), axis=-1).reshape(level_wins, row_wins, HEADS, win_tokens, win_tokens)
    scores = jnp.einsum('zrwqhd,zrwkhd->zrwhqk', as_float(queries), as_float(key_rows)) * factor + bias_full[:, :, None]
    scores = jnp.where(key_valid[None, :, None, None, None, :], scores, -1e+30)
    maxima = lax.optimization_barrier(jnp.max(scores, -1, keepdims=True))
    expsum = jnp.exp(scores - maxima)
    probabilities = expsum / lax.optimization_barrier(jnp.sum(expsum, -1, keepdims=True))
    probs_low = probabilities.astype(jnp.bfloat16)
    mixed = jnp.einsum('zrwhqk,zrwkhd->zrwqhd', as_float(probs_low), as_float(values)).astype(jnp.bfloat16)
    return (queries, key_rows, values, probabilities, probs_low, mixed)

def attend(blocks, bias_rows, key_valid, w_qkv, b_qkv, w_proj):
    channels = blocks.shape[-1]
    mixed = mix_scores(blocks, bias_rows, key_valid, w_qkv, b_qkv)[5]
    result = jnp.dot(mixed.reshape(-1, channels), w_proj, preferred_element_type=jnp.float32)
    return result.astype(jnp.bfloat16).reshape(blocks.shape)

def attend_back(blocks, grad_blocks, bias_rows, key_valid, w_qkv, b_qkv, w_proj):
    level_wins, row_wins, col_wins, win_tokens, channels = blocks.shape
    head_size = channels // HEADS
    factor = head_size ** (-0.5)
    queries, key_rows, values, probabilities, probs_low, mixed = mix_scores(blocks, bias_rows, key_valid, w_qkv, b_qkv)
    flat_grad = grad_blocks.reshape(-1, channels)
    flat_mixed = mixed.reshape(-1, channels)
    grad_proj = jnp.dot(flat_mixed.T, flat_grad, preferred_element_type=jnp.float32)
    grad_mixed = jnp.dot(flat_grad, w_proj.T, preferred_element_type=jnp.float32).astype(jnp.bfloat16)
    grad_mixed = grad_mixed.reshape(level_wins, row_wins, col_wins, win_tokens, HEADS, head_size)
    grad_probs = jnp.einsum('zrwqhd,zrwkhd->zrwhqk', as_float(grad_mixed), as_float(values))
    grad_values = jnp.einsum('zrwhqk,zrwqhd->zrwkhd', as_float(probs_low), as_float(grad_mixed))
    grad_scores = probabilities * (grad_probs - lax.optimization_barrier(jnp.sum(probabilities * grad_probs, -1, keepdims=True)))
    summed = lax.optimization_barrier(jnp.sum(grad_scores, 2)).reshape(level_wins * row_wins * HEADS, win_tokens * win_tokens)
    grad_table = jax.ops.segment_sum(summed.T, rel_index(), NREL).T.reshape(level_wins, row_wins, HEADS, NREL)
    scaled_grad = (grad_scores * factor).astype(jnp.bfloat16)
    grad_queries = jnp.einsum('zrwhqk,zrwkhd->zrwqhd', as_float(scaled_grad), as_float(key_rows))
    grad_keys = jnp.einsum('zrwhqk,zrwqhd->zrwkhd', as_float(scaled_grad), as_float(queries))
    grad_qkv = jnp.stack([grad_queries, grad_keys, grad_values], 4).astype(jnp.bfloat16).reshape(-1, 3 * channels)
    flat_blocks = blocks.reshape(-1, channels)
    grad_wqkv = jnp.dot(flat_blocks.T, grad_qkv, preferred_element_type=jnp.float32)
    grad_bqkv = lax.optimization_barrier(jnp.sum(grad_qkv.astype(jnp.float32), 0))
    grad_input = jnp.dot(grad_qkv, w_qkv.T, preferred_element_type=jnp.float32).astype(jnp.bfloat16).reshape(blocks.shape)
    return (grad_input, grad_wqkv, grad_bqkv, grad_proj, grad_table)

def feed_forward(inner, grad_out, ln2_gain, w_fc1, b_fc1, w_fc2):
    channels = inner.shape[-1]
    flat_inner = inner.reshape(-1, channels)
    normed, normal_hat, inv_std = normalize(flat_inner, ln2_gain)
    second = normed.astype(jnp.bfloat16)
    pre_act = jnp.dot(second, w_fc1, preferred_element_type=jnp.float32) + b_fc1
    activated, slope = gelu_parts(pre_act)
    act_low = activated.astype(jnp.bfloat16)
    result = (flat_inner + jnp.dot(act_low, w_fc2, preferred_element_type=jnp.float32)).astype(jnp.bfloat16)
    flat_grad = grad_out.reshape(-1, channels)
    grad_fc2 = jnp.dot(act_low.T, flat_grad, preferred_element_type=jnp.float32)
    grad_act = jnp.dot(flat_grad, w_fc2.T, preferred_element_type=jnp.float32)
    grad_pre = (grad_act * slope).astype(jnp.bfloat16)
    grad_fc1 = jnp.dot(second.T, grad_pre, preferred_element_type=jnp.float32)
    grad_bfc1 = lax.optimization_barrier(jnp.sum(grad_pre.astype(jnp.float32), 0))
    grad_second = jnp.dot(grad_pre, w_fc1.T, preferred_element_type=jnp.float32)
    grad_norm, grad_gain = norm_back(normal_hat, inv_std, ln2_gain, grad_second)
    grad_inner = flat_grad.astype(jnp.float32) + grad_norm
    return (result.reshape(inner.shape), grad_inner.reshape(inner.shape), grad_gain, grad_fc1, grad_bfc1, grad_fc2)

def reference(tokens, cotangent, ln1_gain, w_qkv, b_qkv, bias_table, w_proj, ln2_gain, w_fc1, b_fc1, w_fc2):
    levels, lat_rows, lon_cols, channels = tokens.shape
    half_h = WIN_H // 2
    half_w = WIN_W // 2
    lat_windows = lat_rows // WIN_H
    win_tokens = WIN_Z * WIN_H * WIN_W
    normed, hat_first, inv_first = normalize(tokens.astype(jnp.float32), ln1_gain)
    first = normed.astype(jnp.bfloat16)

    def framed(field):
        rolled = jnp.roll(field, half_w, axis=2)
        return jnp.pad(rolled, ((0, 0), (half_h, half_h), (0, 0), (0, 0)))

    def unframed(field):
        return jnp.roll(field[:, half_h:half_h + lat_rows], -half_w, axis=2)
    first_frame = framed(first)
    row_ids = jnp.arange(lat_windows + 1, dtype=jnp.int32)
    token_row = jnp.arange(win_tokens, dtype=jnp.int32) // WIN_W % WIN_H

    def row_inputs(window_row):
        block_rows = lax.dynamic_slice_in_dim(first_frame, window_row * WIN_H, WIN_H, 1)
        slot = jnp.minimum(window_row, lat_windows - 1).astype(jnp.int32)
        bias_rows = lax.dynamic_slice_in_dim(bias_table, slot, 1, 1)
        global_row = window_row * WIN_H - half_h + token_row
        key_valid = ((global_row >= 0) & (global_row < lat_rows))[None, :]
        return (to_windows(block_rows), bias_rows, key_valid)

    def forward_row(window_row):
        blocks, bias_rows, key_valid = row_inputs(window_row)
        return attend(blocks, bias_rows, key_valid, w_qkv, b_qkv, w_proj)
    attended_rows = lax.map(forward_row, row_ids)[:, :, 0].transpose(1, 0, 2, 3, 4)
    attended = unframed(from_windows(attended_rows))
    inner = tokens.astype(jnp.float32) + attended.astype(jnp.float32)
    block_out, grad_inner, d_ln2_gain, d_w_fc1, d_b_fc1, d_w_fc2 = feed_forward(inner, cotangent, ln2_gain, w_fc1, b_fc1, w_fc2)
    grad_frame = framed(grad_inner.astype(jnp.bfloat16))

    def backward_row(window_row):
        blocks, bias_rows, key_valid = row_inputs(window_row)
        grad_rows = to_windows(lax.dynamic_slice_in_dim(grad_frame, window_row * WIN_H, WIN_H, 1))
        return attend_back(blocks, grad_rows, bias_rows, key_valid, w_qkv, b_qkv, w_proj)
    grad_rows, grad_wqkv, grad_bqkv, grad_proj, grad_table = lax.map(backward_row, row_ids)
    grad_first = unframed(from_windows(grad_rows[:, :, 0].transpose(1, 0, 2, 3, 4)))
    grad_part, d_ln1_gain = norm_back(hat_first, inv_first, ln1_gain, grad_first.astype(jnp.float32))
    d_tokens = (grad_inner + grad_part).astype(jnp.bfloat16)
    table_rows = grad_table[:, :, 0]
    table_sum = table_rows[:lat_windows].at[lat_windows - 1].add(table_rows[lat_windows])
    d_bias_table = table_sum.transpose(1, 0, 2, 3)
    return (block_out, d_tokens, d_ln1_gain, lax.optimization_barrier(jnp.sum(grad_wqkv, 0)), lax.optimization_barrier(jnp.sum(grad_bqkv, 0)), d_bias_table, lax.optimization_barrier(jnp.sum(grad_proj, 0)), d_ln2_gain, d_w_fc1, d_b_fc1, d_w_fc2)
```

```python
import jax
import jax.numpy as jnp
import numpy as np
from jax import lax
from jax.experimental import pallas as pl
from jax.experimental.pallas import tpu as pltpu
from jax.sharding import PartitionSpec as P

HEADS = 6
WIN_Z = 2
WIN_H = 6
WIN_W = 12
SPAN = 2 * WIN_W - 1
GROUPS = WIN_Z * WIN_H
T = GROUPS * WIN_W
C = 192
HID = 768
HEAD = C // HEADS
NREL = GROUPS * GROUPS * SPAN
SLOT = 48
FC = 43
ATT = 14
UNITS = FC + ATT
CHIPS = 64
STEP = 7
STEP_INV = 55
BANDS = 16
STRIPS = 8
PARTS = 6
EPSILON = 1e-05
VMEM_LIMIT = 56 * 1024 * 1024
FACTOR = HEAD ** (-0.5)
F32 = jnp.float32
BF16 = jnp.bfloat16
MESH = pl.DeviceIdType.MESH


def window_order():
    grid = np.zeros((T, 4 * SLOT), np.float32)
    for w in range(WIN_W):
        for z in range(WIN_Z):
            for h in range(WIN_H):
                slot = (h // 3) * 2 + w // 6
                grid[w * GROUPS + z * WIN_H + h, slot * SLOT + (h % 3) * 12 + (w % 6) * 2 + z] = 1
    return grid


def table_order():
    grid = np.zeros((512, 384), np.float32)
    for z in range(WIN_Z):
        for h in range(WIN_H):
            for i in range(SPAN):
                grid[z * 256 + h * SPAN + i, (SPAN - 1 - i) * GROUPS + z * WIN_H + h] = 1
    return grid


def cross_pairs():
    g = np.arange(96)[:, None] // 8 % WIN_H
    q = np.arange(384)[None, :] % GROUPS % WIN_H
    return np.where((g < 3) != (q < 3), -1e30, 0.0).astype(np.float32)


def dot(a, b):
    return jnp.dot(a, b, preferred_element_type=F32)


def dot_nt(a, b):
    return lax.dot_general(a, b, (((1,), (1,)), ((), ())), preferred_element_type=F32)


def dot_tn(a, b):
    return lax.dot_general(a, b, (((0,), (0,)), ((), ())), preferred_element_type=F32)


def normalize(values, gain):
    average = jnp.mean(values, -1, keepdims=True)
    centered = values - average
    inv = lax.rsqrt(jnp.mean(centered * centered, -1, keepdims=True) + EPSILON)
    hat = centered * inv
    return hat * gain, hat, inv


def norm_back(hat, inv, gain, grad):
    scaled = grad * gain
    return inv * (
        scaled
        - jnp.mean(scaled, -1, keepdims=True)
        - hat * jnp.mean(scaled * hat, -1, keepdims=True)
    )


def slot_rows(h, w):
    at = ((h // 3) * 2 + w // 6) * SLOT + (h % 3) * 12 + (w % 6) * 2
    return slice(at, at + 2)


def block_kernel(
    tok_any, cot_any, g1_any, wqkv_any, bqkv_any, table_any, wproj_any, g2_any, wfc1_any,
    bfc1_any, wfc2_any, order_any, back_any, perm_any, unperm_any, cross_any,
    gath_ref, ret_ref, dtab_ref,
    tok_ref, cot_ref, g1_ref, wqkv_ref, bqkv_ref, table_ref, wproj_ref, g2_ref, wfc1_ref,
    bfc1_ref, wfc2_ref, order_ref, back_ref, perm_ref, unperm_ref, cross_ref,
    stage, send, arrive, out_stage,
    tabw, tab15, tin, ymat, bias, prob, plow, dsc, dmat, vec,
    bsend, brecv, bfin, bbs, bbr,
    parts, core_in, rs_in,
    in_sem,
    ex_send, ex_recv, rt_send, rt_recv, one_send, one_recv, c_send, c_recv,
    s_send, s_recv, a_send, a_recv, d_send, d_recv, b_send, b_recv,
):
    places = (
        (table_any, table_ref), (tok_any, tok_ref), (perm_any, perm_ref), (cot_any, cot_ref),
        (cross_any, cross_ref), (order_any, order_ref), (g1_any, g1_ref), (wqkv_any, wqkv_ref),
        (bqkv_any, bqkv_ref), (wproj_any, wproj_ref), (g2_any, g2_ref), (wfc1_any, wfc1_ref),
        (bfc1_any, bfc1_ref), (wfc2_any, wfc2_ref), (back_any, back_ref),
        (unperm_any, unperm_ref),
    )
    loads = [pltpu.make_async_copy(src, dst, in_sem.at[n]) for n, (src, dst) in enumerate(places)]
    for load in loads:
        load.start()
    lon = lax.axis_index("lon")
    lat = lax.axis_index("lat")
    core = lax.rem(lat, 2)
    other = 1 - core
    pair_row = lat // 2
    chip = lon * 8 + pair_row
    me = lax.rem(chip * STEP_INV, CHIPS)
    east = lax.rem(lon + 1, STRIPS)
    west = lax.rem(lon + STRIPS - 1, STRIPS)
    south = lax.rem(lat + 1, BANDS)
    north = lax.rem(lat + BANDS - 1, BANDS)
    sibling = (lon, lat - core + other)

    def to_chips(act):
        def strip_step(at, carry):
            for row in range(8):
                @pl.when((at != lon) | (row != pair_row))
                def _():
                    act((at, row * 2 + core))

            return carry

        lax.fori_loop(0, STRIPS, strip_step, 0)

    barrier = pltpu.get_barrier_semaphore()

    def greet(target):
        pl.semaphore_signal(barrier, inc=1, device_id=target, device_id_type=MESH)

    for target in (
        (east, lat), (west, lat), (lon, south), (lon, north), (east, south), (west, north), sibling,
    ):
        greet(target)
    to_chips(greet)

    tabw[...] = jnp.zeros_like(tabw)
    loads[0].wait()
    for head in range(HEADS):
        tabw[head : head + 1, 0:NREL] = table_ref[0, head]

    stage[...] = jnp.zeros_like(stage)
    for a, src in enumerate((tok_ref, cot_ref)):
        loads[(1, 3)[a]].wait()
        for h in range(WIN_H):
            for w in range(WIN_W):
                stage[slot_rows(h, w), :] = src[h, w].astype(F32)
        send[a] = stage[...].astype(BF16).reshape(4, SLOT, C)
        arrive[a, 3] = send[a, 0]

    pl.semaphore_wait(barrier, 7 + CHIPS - 1)

    ahead = ((east, lat), (lon, south), (east, south))
    behind = ((west, lat), (lon, north), (west, north))

    def exchange(a, i):
        return pltpu.make_async_remote_copy(
            src_ref=send.at[a, i + 1],
            dst_ref=arrive.at[a, 2 - i],
            send_sem=ex_send.at[a, i],
            recv_sem=ex_recv.at[a, i],
            device_id=ahead[i],
            device_id_type=MESH,
        )

    def table_copy():
        return pltpu.make_async_remote_copy(
            src_ref=tabw,
            dst_ref=tab15,
            send_sem=one_send.at[0],
            recv_sem=one_recv.at[0],
            device_id=(lon, south),
            device_id_type=MESH,
        )

    @pl.when(lat == BANDS - 1)
    def _():
        table_copy().start()

    for a in range(2):
        for i in range(3):
            exchange(a, i).start()

    tin[...] = jnp.zeros_like(tin)

    def spread(src, zp, zq, hp, width):
        j = (zp * WIN_Z + zq) * WIN_H + hp
        first = j * WIN_H * SPAN
        base = first // 128 * 128
        wide = src[:, base : base + 384]
        moved = pltpu.roll(wide, (384 - (first - base)) % 384, axis=1)
        g = zp * WIN_H + hp
        tin[g * 8 : g * 8 + 8, zq * 256 : zq * 256 + width] = moved[:, :width]

    for zp in range(WIN_Z):
        for zq in range(WIN_Z):
            for hp in range(WIN_H):
                spread(tabw, zp, zq, hp, WIN_H * SPAN)

    @pl.when(lat == 0)
    def _():
        table_copy().wait_recv()
        for zp in range(WIN_Z):
            for zq in range(WIN_Z):
                for hp in range(3):
                    spread(tab15, zp, zq, hp, 3 * SPAN)

    whole = tin[...]
    high = whole.astype(BF16)
    rest = whole - high.astype(F32)
    middle = rest.astype(BF16)
    low = (rest - middle.astype(F32)).astype(BF16)
    loads[2].wait()
    perm = perm_ref[...]
    spread_rows = dot(high, perm) + dot(middle, perm) + dot(low, perm)
    for n in range(3):
        ymat[n, 0:96, :] = spread_rows[:, 128 * n : 128 * (n + 1)]
        ymat[n, 96:128, :] = jnp.zeros((32, 128), F32)
    loads[4].wait()

    @pl.when(lat == 0)
    def _():
        for n in range(3):
            ymat[n, 0:96, :] = ymat[n, 0:96, :] + cross_ref[:, 128 * n : 128 * (n + 1)]

    for head in range(HEADS):
        rows = jnp.concatenate(
            [ymat[n, pl.ds(head, 16, stride=8), :] for n in range(3)], -1
        )
        for w in range(WIN_W):
            moved = pltpu.roll(rows, (384 - (WIN_W - 1 - w) * GROUPS) % 384, axis=1)
            bias[head, w * GROUPS : (w + 1) * GROUPS, :] = moved[:GROUPS, :T]

    for n in range(5, 16):
        loads[n].wait()
    lane = lax.broadcasted_iota(jnp.int32, (T, C), 1)
    masks = [(lane >= HEAD * i) & (lane < HEAD * (i + 1)) for i in range(HEADS)]
    order = order_ref[...]
    back = back_ref[...]
    gain1 = g1_ref[...].reshape(1, C)
    gain2 = g2_ref[...].reshape(1, C)

    def arrived(a):
        for i in range(3):
            exchange(a, i).wait_recv()
        return dot(order, arrive[a].reshape(4 * SLOT, C))

    tokens = arrived(0)
    normed, hat1, inv1 = normalize(tokens, gain1)
    first = normed.astype(BF16)
    qkv = (dot(first, wqkv_ref[...]) + bqkv_ref[...].reshape(1, 3 * C)).astype(BF16)
    queries = qkv[:, 0:C]
    keys = qkv[:, C : 2 * C]
    values = qkv[:, 2 * C : 3 * C]
    queries_t = queries.T
    mixed = jnp.zeros((T, C), F32)
    for head in range(HEADS):
        q = jnp.where(masks[head], queries, jnp.zeros_like(queries))
        scores = dot_nt(q, keys) * FACTOR + bias[head]
        top = jnp.max(scores, -1, keepdims=True)
        raised = jnp.exp(scores - top)
        probs = raised * (1.0 / jnp.sum(raised, -1, keepdims=True))
        prob[head] = probs
        probs_low = probs.astype(BF16)
        plow[head] = probs_low
        mixed = jnp.where(masks[head], dot(probs_low, values), mixed)
    mixed = mixed.astype(BF16)
    inner = tokens + dot(mixed, wproj_ref[...]).astype(BF16).astype(F32)

    cot = arrived(1)
    cot_low = cot.astype(BF16)
    normed, hat2, inv2 = normalize(inner, gain2)
    second = normed.astype(BF16)
    second_t = second.T
    cot_t = cot_low.T
    total = inner
    grad_second = jnp.zeros((T, C), F32)
    bfc1 = bfc1_ref[...].reshape(1, HID)
    vec[...] = jnp.zeros_like(vec)
    for n in range(3):
        cols = slice(256 * n, 256 * (n + 1))
        pre = dot(second, wfc1_ref[:, cols]) + bfc1[:, cols]
        cdf = 0.5 * (1.0 + lax.erf(pre * 0.7071067811865476))
        density = jnp.exp(-0.5 * pre * pre) * 0.3989422804014327
        act = (pre * cdf).astype(BF16)
        total = total + dot_nt(act, wfc2_ref[:, cols])
        grad_pre = (dot(cot_low, wfc2_ref[:, cols]) * (cdf + pre * density)).astype(BF16)
        grad_second = grad_second + dot_nt(grad_pre, wfc1_ref[:, cols])
        parts[0, 12 * n : 12 * (n + 1)] = dot(second_t, grad_pre).astype(BF16).reshape(12, 16, 256)
        parts[1, 12 * n : 12 * (n + 1)] = dot(cot_t, act).astype(BF16).reshape(12, 16, 256)
        vec[n : n + 1, :] = jnp.sum(grad_pre.astype(F32), 0, keepdims=True)

    def pair(seg, at, count):
        return pltpu.make_async_remote_copy(
            src_ref=parts.at[other, pl.ds(at, count)],
            dst_ref=core_in.at[pl.ds(at, count)],
            send_sem=c_send.at[seg],
            recv_sem=c_recv.at[seg],
            device_id=sibling,
            device_id_type=MESH,
        )

    def give_back(a, i):
        return pltpu.make_async_remote_copy(
            src_ref=out_stage.at[a, 2 - i],
            dst_ref=ret_ref.at[a, i + 1],
            send_sem=rt_send.at[a, i],
            recv_sem=rt_recv.at[a, i],
            device_id=behind[i],
            device_id_type=MESH,
        )

    def hand_out(a, field):
        out_stage[a] = dot(back, field).astype(BF16).reshape(4, SLOT, C)
        for i in range(3):
            give_back(a, i).start()
        ret_ref[a, 0] = out_stage[a, 3]

    grad_inner = cot + norm_back(hat2, inv2, gain2, grad_second)
    grad_att = grad_inner.astype(BF16)
    proj_grad = dot_tn(mixed, grad_att).astype(BF16)
    proj_grad = jnp.concatenate([proj_grad, jnp.zeros((C, 64), BF16)], -1).reshape(12, 16, 256)
    parts[0, 36:42] = proj_grad[:6]
    parts[1, 36:42] = proj_grad[6:]
    vec[3:4, 0:C] = jnp.sum(grad_second * hat2, 0, keepdims=True)
    parts[0, 42] = vec[...].astype(BF16)
    parts[1, 42] = jnp.zeros((16, 256), BF16)
    pair(0, 0, FC).start()
    hand_out(0, total.astype(BF16))

    def share(seg, start, count):
        pair(seg, start, count).wait_recv()
        rows = pl.ds(start, count)
        parts[core, rows] = (
            parts[core, rows].astype(F32) + core_in[rows].astype(F32)
        ).astype(BF16)
        for unit in range(start, start + count):
            owner = unit * STEP % CHIPS

            @pl.when(chip != owner)
            def _():
                pltpu.make_async_remote_copy(
                    src_ref=parts.at[core, unit],
                    dst_ref=rs_in.at[chip],
                    send_sem=s_send.at[seg],
                    recv_sem=s_recv.at[seg],
                    device_id=(owner // 8, owner % 8 * 2 + core),
                    device_id_type=MESH,
                ).start()

    def owns(start, count):
        return (me >= start) & (me < start + count)

    def wait_bytes(ref, sem):
        pltpu.make_async_copy(ref, ref, sem).wait()

    others = rs_in.at[pl.ds(0, CHIPS - 1)]

    def settle(seg, start, count):
        @pl.when(owns(start, count))
        def _():
            rs_in[chip] = parts[core, me]
            wait_bytes(others, s_recv.at[seg])
            summed = jnp.sum(rs_in[...].astype(F32), 0)
            gath_ref[core, me] = summed.astype(BF16)

            def push(target):
                pltpu.make_async_remote_copy(
                    src_ref=gath_ref.at[core, me],
                    dst_ref=gath_ref.at[core, me],
                    send_sem=a_send.at[seg],
                    recv_sem=a_recv.at[seg],
                    device_id=target,
                    device_id_type=MESH,
                ).start()

            to_chips(push)

    def swap(seg, start, count):
        return pltpu.make_async_remote_copy(
            src_ref=gath_ref.at[core, pl.ds(start, count)],
            dst_ref=gath_ref.at[core, pl.ds(start, count)],
            send_sem=d_send.at[seg],
            recv_sem=d_recv.at[seg],
            device_id=sibling,
            device_id_type=MESH,
        )

    def wait_units(ref, sem, start, count):
        mine = owns(start, count)

        @pl.when(mine)
        def _():
            wait_bytes(ref.at[0, pl.ds(start, count - 1)], sem)

        @pl.when(jnp.logical_not(mine))
        def _():
            wait_bytes(ref.at[0, pl.ds(start, count)], sem)

    grad_mixed = dot_nt(grad_att, wproj_ref[...]).astype(BF16)
    grad_mixed_t = grad_mixed.T
    dsc[...] = jnp.zeros_like(dsc)
    grad_q = jnp.zeros((T, C), F32)
    grad_k_t = []
    grad_v_t = []
    for head in range(HEADS):
        rows = slice(HEAD * head, HEAD * (head + 1))
        gm = jnp.where(masks[head], grad_mixed, jnp.zeros_like(grad_mixed))
        probs = prob[head]
        grad_probs = dot_nt(gm, values)
        inside = jnp.sum(probs * grad_probs, -1, keepdims=True)
        grad_scores = probs * (grad_probs - inside)
        dsc[head, 0:T, 0:T] = grad_scores
        scaled = (grad_scores * FACTOR).astype(BF16)
        grad_q = jnp.where(masks[head], dot(scaled, keys), grad_q)
        grad_k_t.append(dot(queries_t[rows], scaled))
        grad_v_t.append(dot(grad_mixed_t[rows], plow[head]))
        if head == 2:
            share(0, 0, FC)
    grad_k = jnp.concatenate(grad_k_t, 0).T
    grad_v = jnp.concatenate(grad_v_t, 0).T

    grad_qkv = jnp.concatenate([grad_q, grad_k, grad_v], -1).astype(BF16)
    wide = dot_tn(first, grad_qkv).astype(BF16)
    edge = [wide[48 * n : 48 * (n + 1), 512:576] for n in range(4)]
    parts[0, FC : FC + 12] = wide[:, 0:256].reshape(12, 16, 256)
    parts[1, FC : FC + 12] = wide[:, 256:512].reshape(12, 16, 256)
    edge = jnp.concatenate(edge, -1).reshape(3, 16, 256)
    parts[0, FC + 12] = edge[0]
    parts[1, FC + 12 : FC + 14] = edge[1:]
    grad_first = dot_nt(grad_qkv, wqkv_ref[...]).astype(BF16).astype(F32)
    sums = jnp.sum(grad_qkv.astype(F32), 0, keepdims=True)
    for n in range(3):
        vec[n : n + 1, 0:C] = sums[:, C * n : C * (n + 1)]
    vec[3:4, 0:C] = jnp.sum(grad_first * hat1, 0, keepdims=True)
    parts[0, FC + 13] = vec[...].astype(BF16)
    pair(1, FC, ATT).start()
    settle(0, 0, FC)
    d_tokens = grad_inner + norm_back(hat1, inv1, gain1, grad_first)
    hand_out(1, d_tokens.astype(BF16))
    share(1, FC, ATT)

    dmat[...] = jnp.zeros_like(dmat)
    for head in range(HEADS):
        acc = jnp.zeros((16, 384), F32)
        for w in range(WIN_W):
            acc = acc + pltpu.roll(
                dsc[head, w * GROUPS : w * GROUPS + 16, :], (WIN_W - 1 - w) * GROUPS, axis=1
            )
        for n in range(3):
            dmat[n, pl.ds(head, 16, stride=8), :] = acc[:, 128 * n : 128 * (n + 1)]

    def table_grad():
        return jnp.concatenate([dmat[n, 0:96, :] for n in range(3)], -1)

    def keep_table(field):
        for n in range(3):
            dmat[n, 0:96, :] = field[:, 128 * n : 128 * (n + 1)]

    def edge_copy():
        return pltpu.make_async_remote_copy(
            src_ref=bbs,
            dst_ref=bbr,
            send_sem=one_send.at[1],
            recv_sem=one_recv.at[1],
            device_id=(lon, north),
            device_id_type=MESH,
        )

    @pl.when(lat == 0)
    def _():
        row = lax.broadcasted_iota(jnp.int32, (96, 384), 0)
        upper = (row < 24) | ((row >= 48) & (row < 72))
        full = table_grad()
        bbs[...] = jnp.where(upper, full, 0.0).astype(BF16)
        edge_copy().start()
        keep_table(jnp.where(upper, 0.0, full))

    @pl.when(lat == BANDS - 1)
    def _():
        edge_copy().wait_recv()
        keep_table(table_grad() + bbr[...].astype(F32))

    bsend[...] = table_grad().astype(BF16).reshape(PARTS, 16, 384)

    def strip(d):
        return lax.rem(lon + d, STRIPS)

    for owner in range(PARTS):
        @pl.when(lon != owner)
        def _():
            pltpu.make_async_remote_copy(
                src_ref=bsend.at[owner],
                dst_ref=brecv.at[lon],
                send_sem=b_send.at[0],
                recv_sem=b_recv.at[0],
                device_id=(owner, lat),
                device_id_type=MESH,
            ).start()

    settle(1, FC, ATT)
    seven = brecv.at[pl.ds(0, STRIPS - 1)]

    @pl.when(lon < PARTS)
    def _():
        brecv[lon] = bsend[lon]
        wait_bytes(seven, b_recv.at[0])
        bfin[lon] = jnp.sum(brecv[...].astype(F32), 0).astype(BF16)
        for d in range(1, STRIPS):
            pltpu.make_async_remote_copy(
                src_ref=bfin.at[lon],
                dst_ref=bfin.at[lon],
                send_sem=b_send.at[1],
                recv_sem=b_recv.at[1],
                device_id=(strip(d), lat),
                device_id_type=MESH,
            ).start()

    wait_units(gath_ref, a_recv.at[0], 0, FC)
    swap(0, 0, FC).start()

    @pl.when(lon < PARTS)
    def _():
        wait_bytes(bfin.at[pl.ds(0, PARTS - 1)], b_recv.at[1])

    @pl.when(lon >= PARTS)
    def _():
        wait_bytes(bfin, b_recv.at[1])

    tin[...] = dot(bfin[...].reshape(96, 384), unperm_ref[...])
    dtab_ref[...] = jnp.zeros_like(dtab_ref)
    for zp in range(WIN_Z):
        for zq in range(WIN_Z):
            for hp in range(WIN_H):
                j = (zp * WIN_Z + zq) * WIN_H + hp
                first_lane = j * WIN_H * SPAN
                base = first_lane // 128 * 128
                g = zp * WIN_H + hp
                piece = tin[g * 8 : g * 8 + 8, zq * 256 : zq * 256 + 256]
                piece = jnp.concatenate([piece, jnp.zeros((8, 128), F32)], -1)
                moved = pltpu.roll(piece, first_lane - base, axis=1)
                dtab_ref[:, base : base + 384] = dtab_ref[:, base : base + 384] + moved

    wait_units(gath_ref, a_recv.at[1], FC, ATT)
    swap(1, FC, ATT).start()

    for a in range(2):
        for i in range(3):
            exchange(a, i).wait_send()
            give_back(a, i).wait()

    @pl.when(lat == BANDS - 1)
    def _():
        table_copy().wait_send()

    @pl.when(lat == 0)
    def _():
        edge_copy().wait_send()

    for seg, start, count in ((0, 0, FC), (1, FC, ATT)):
        pair(seg, start, count).wait_send()
        wait_units(parts, s_send.at[seg], start, count)

        @pl.when(owns(start, count))
        def _():
            wait_bytes(others, a_send.at[seg])

        swap(seg, start, count).wait()

    @pl.when(lon < PARTS)
    def _():
        wait_bytes(bsend.at[pl.ds(0, PARTS - 1)], b_send.at[0])
        wait_bytes(seven, b_send.at[1])

    @pl.when(lon >= PARTS)
    def _():
        wait_bytes(bsend, b_send.at[0])


def output_kernel(
    gath_ref, ret_ref, dtab_ref,
    out_ref, dtok_ref, dln1_ref, dwqkv_ref, dbqkv_ref, dbias_ref, dwproj_ref, dln2_ref,
    dwfc1_ref, dbfc1_ref, dwfc2_ref,
    stage,
):
    for a, dst in enumerate((out_ref, dtok_ref)):
        stage[...] = ret_ref[a].reshape(4 * SLOT, C).astype(F32)
        for h in range(WIN_H):
            for w in range(WIN_W):
                dst[h, w] = stage[slot_rows(h, w), :].astype(BF16)
    for n in range(3):
        cols = slice(256 * n, 256 * (n + 1))
        rows = slice(12 * n, 12 * (n + 1))
        dwfc1_ref[:, cols] = gath_ref[0, rows].reshape(C, 256).astype(F32)
        dwfc2_ref[:, cols] = gath_ref[1, rows].reshape(C, 256).astype(F32)
    for k in range(2):
        dwproj_ref[96 * k : 96 * (k + 1), :] = (
            gath_ref[k, 36:42].reshape(96, 256)[:, 0:C].astype(F32)
        )
        dwqkv_ref[:, 256 * k : 256 * (k + 1)] = (
            gath_ref[k, FC : FC + 12].reshape(C, 256).astype(F32)
        )
    for n, edge in enumerate((gath_ref[0, FC + 12], gath_ref[1, FC + 12], gath_ref[1, FC + 13])):
        edge = edge.astype(F32)
        for k in range(4):
            at = 48 * k + 16 * n
            dwqkv_ref[at : at + 16, 512:576] = edge[:, 64 * k : 64 * (k + 1)]
    vec = gath_ref[0, 42].astype(F32)
    dbfc1_ref[...] = jnp.concatenate([vec[n : n + 1] for n in range(3)], -1).reshape(HID)
    dln2_ref[...] = vec[3:4, :C].reshape(C)
    vec = gath_ref[0, FC + 13].astype(F32)
    dbqkv_ref[...] = jnp.concatenate([vec[n : n + 1, :C] for n in range(3)], -1).reshape(3 * C)
    dln1_ref[...] = vec[3:4, :C].reshape(C)
    for head in range(HEADS):
        dbias_ref[0, head] = dtab_ref[head : head + 1, 0:NREL]


def per_device(
    tokens, cotangent, ln1_gain, w_qkv, b_qkv, bias_table, w_proj, ln2_gain, w_fc1, b_fc1, w_fc2
):
    vmem = pl.BlockSpec(memory_space=pltpu.VMEM)
    order = window_order()
    perm = table_order()
    dma = pltpu.SemaphoreType.DMA
    args = (
        tokens.transpose(1, 2, 0, 3), cotangent.transpose(1, 2, 0, 3), ln1_gain, w_qkv, b_qkv,
        bias_table.transpose(0, 2, 1, 3), w_proj, ln2_gain, w_fc1, b_fc1, w_fc2.T,
        jnp.asarray(order, BF16), jnp.asarray(order.T, BF16),
        jnp.asarray(perm, BF16), jnp.asarray(perm.T, BF16),
        jnp.asarray(cross_pairs()),
    )
    gathered, returned, table = pl.pallas_call(
        block_kernel,
        out_shape=(
            jax.ShapeDtypeStruct((2, UNITS, 16, 256), BF16),
            jax.ShapeDtypeStruct((2, 4, SLOT, C), BF16),
            jax.ShapeDtypeStruct((8, 3456), F32),
        ),
        in_specs=[pl.BlockSpec(memory_space=pl.ANY)] * len(args),
        out_specs=(vmem,) * 3,
        scratch_shapes=[pltpu.VMEM(a.shape, a.dtype) for a in args]
        + [
            pltpu.VMEM((4 * SLOT, C), F32),
            pltpu.VMEM((2, 4, SLOT, C), BF16),
            pltpu.VMEM((2, 4, SLOT, C), BF16),
            pltpu.VMEM((2, 4, SLOT, C), BF16),
            pltpu.VMEM((8, 3456), F32),
            pltpu.VMEM((8, 3456), F32),
            pltpu.VMEM((96, 512), F32),
            pltpu.VMEM((3, 128, 128), F32),
            pltpu.VMEM((HEADS, T, T), F32),
            pltpu.VMEM((HEADS, T, T), F32),
            pltpu.VMEM((HEADS, T, T), BF16),
            pltpu.VMEM((HEADS, 160, 384), F32),
            pltpu.VMEM((3, 128, 128), F32),
            pltpu.VMEM((16, 256), F32),
            pltpu.VMEM((PARTS, 16, 384), BF16),
            pltpu.VMEM((STRIPS, 16, 384), BF16),
            pltpu.VMEM((PARTS, 16, 384), BF16),
            pltpu.VMEM((96, 384), BF16),
            pltpu.VMEM((96, 384), BF16),
            pltpu.VMEM((2, UNITS, 16, 256), BF16),
            pltpu.VMEM((UNITS, 16, 256), BF16),
            pltpu.VMEM((CHIPS, 16, 256), BF16),
            dma((len(args),)),
            dma((2, 3)), dma((2, 3)), dma((2, 3)), dma((2, 3)),
            dma((2,)), dma((2,)), dma((2,)), dma((2,)),
            dma((2,)), dma((2,)), dma((2,)), dma((2,)),
            dma((2,)), dma((2,)), dma((2,)), dma((2,)),
        ],
        compiler_params=pltpu.CompilerParams(
            collective_id=0, has_side_effects=True, vmem_limit_bytes=VMEM_LIMIT
        ),
    )(*args)
    shape = jax.ShapeDtypeStruct
    grid_shape = (WIN_H, WIN_W, WIN_Z, C)
    outs = pl.pallas_call(
        output_kernel,
        out_shape=(
            shape(grid_shape, BF16), shape(grid_shape, BF16),
            shape((C,), F32), shape((C, 3 * C), F32), shape((3 * C,), F32),
            shape((1, HEADS, 1, NREL), F32), shape((C, C), F32), shape((C,), F32),
            shape((C, HID), F32), shape((HID,), F32), shape((C, HID), F32),
        ),
        in_specs=[vmem] * 3,
        out_specs=(vmem,) * 11,
        scratch_shapes=[pltpu.VMEM((4 * SLOT, C), F32)],
        compiler_params=pltpu.CompilerParams(vmem_limit_bytes=VMEM_LIMIT),
    )(gathered, returned, table)
    out, d_tok, d_ln1, d_wqkv, d_bqkv, d_bias, d_wproj, d_ln2, d_wfc1, d_bfc1, d_wfc2 = outs
    return (
        out.transpose(2, 0, 1, 3), d_tok.transpose(2, 0, 1, 3), d_ln1, d_wqkv, d_bqkv,
        d_bias.transpose(0, 2, 1, 3), d_wproj, d_ln2, d_wfc1, d_bfc1, d_wfc2.T,
    )


def solution(mesh):
    grid = P(None, "lat", "lon", None)
    rows = P(None, "lat", None, None)
    return jax.shard_map(
        per_device,
        mesh=mesh,
        in_specs=(grid, grid, P(), P(), P(), rows, P(), P(), P(), P(), P()),
        out_specs=(grid, grid, P(), P(), P(), rows, P(), P(), P(), P(), P()),
        check_vma=False,
    )
```

```python
import jax
import jax.numpy as jnp
import numpy as np
from jax import lax
from jax.experimental import pallas as pl
from jax.experimental.pallas import tpu as pltpu
from jax.sharding import PartitionSpec as P

HEADS = 6
WIN_Z = 2
WIN_H = 6
WIN_W = 12
SPAN = 2 * WIN_W - 1
GROUPS = WIN_Z * WIN_H
T = GROUPS * WIN_W
C = 192
HID = 768
HEAD = C // HEADS
NREL = GROUPS * GROUPS * SPAN
SLOT = 48
FC = 43
ATT = 28
COUNTS = (FC, ATT)
FIRST = (0, 36)
CHIPS = 64
BANDS = 16
STRIPS = 8
PARTS = 6
EPSILON = 1e-05
VMEM_LIMIT = 56 * 1024 * 1024
FACTOR = HEAD ** (-0.5)
F32 = jnp.float32
BF16 = jnp.bfloat16
MESH = pl.DeviceIdType.MESH


def window_order():
    grid = np.zeros((T, 4 * SLOT), np.float32)
    for w in range(WIN_W):
        for z in range(WIN_Z):
            for h in range(WIN_H):
                slot = (h // 3) * 2 + w // 6
                grid[w * GROUPS + z * WIN_H + h, slot * SLOT + (h % 3) * 12 + (w % 6) * 2 + z] = 1
    return grid


def table_order():
    grid = np.zeros((512, 384), np.float32)
    for z in range(WIN_Z):
        for h in range(WIN_H):
            for i in range(SPAN):
                grid[z * 256 + h * SPAN + i, (SPAN - 1 - i) * GROUPS + z * WIN_H + h] = 1
    return grid


def cross_pairs():
    g = np.arange(96)[:, None] // 8 % WIN_H
    q = np.arange(384)[None, :] % GROUPS % WIN_H
    return np.where((g < 3) != (q < 3), -1e30, 0.0).astype(np.float32)


def dot(a, b):
    return jnp.dot(a, b, preferred_element_type=F32)


def dot_nt(a, b):
    return lax.dot_general(a, b, (((1,), (1,)), ((), ())), preferred_element_type=F32)


def dot_tn(a, b):
    return lax.dot_general(a, b, (((0,), (0,)), ((), ())), preferred_element_type=F32)


def normalize(values, gain):
    average = jnp.mean(values, -1, keepdims=True)
    centered = values - average
    inv = lax.rsqrt(jnp.mean(centered * centered, -1, keepdims=True) + EPSILON)
    hat = centered * inv
    return hat * gain, hat, inv


def norm_back(hat, inv, gain, grad):
    scaled = grad * gain
    return inv * (
        scaled
        - jnp.mean(scaled, -1, keepdims=True)
        - hat * jnp.mean(scaled * hat, -1, keepdims=True)
    )


def slot_rows(h, w):
    at = ((h // 3) * 2 + w // 6) * SLOT + (h % 3) * 12 + (w % 6) * 2
    return slice(at, at + 2)


def block_kernel(
    tok_any, cot_any, g1_any, wqkv_any, bqkv_any, table_any, wproj_any, g2_any, wfc1_any,
    bfc1_any, wfc2_any, order_any, back_any, perm_any, unperm_any, cross_any,
    gath_fc, gath_att, ret_ref, dtab_ref,
    tok_ref, cot_ref, g1_ref, wqkv_ref, bqkv_ref, table_ref, wproj_ref, g2_ref, wfc1_ref,
    bfc1_ref, wfc2_ref, order_ref, back_ref, perm_ref, unperm_ref, cross_ref,
    stage, send, arrive, out_stage,
    tabw, tab15, tin, ymat, bias, prob, plow, dsc, dmat, vec,
    bsend, brecv, bfin, bbs, bbr,
    parts_fc, parts_att, core_fc, core_att, rs_fc, rs_att,
    in_sem,
    ex_send, ex_recv, rt_send, rt_recv, one_send, one_recv, c_send, c_recv,
    s_send, s_recv, a_send, a_recv, d_send, d_recv, b_send, b_recv,
):
    places = (
        (table_any, table_ref), (tok_any, tok_ref), (perm_any, perm_ref), (cot_any, cot_ref),
        (cross_any, cross_ref), (order_any, order_ref), (g1_any, g1_ref), (wqkv_any, wqkv_ref),
        (bqkv_any, bqkv_ref), (wproj_any, wproj_ref), (g2_any, g2_ref), (wfc1_any, wfc1_ref),
        (bfc1_any, bfc1_ref), (wfc2_any, wfc2_ref), (back_any, back_ref),
        (unperm_any, unperm_ref),
    )
    loads = [pltpu.make_async_copy(src, dst, in_sem.at[n]) for n, (src, dst) in enumerate(places)]
    for load in loads:
        load.start()
    lon = lax.axis_index("lon")
    lat = lax.axis_index("lat")
    core = lax.rem(lat, 2)
    other = 1 - core
    pair_row = lat // 2
    chip = lon * 8 + pair_row
    gath = (gath_fc, gath_att)
    parts = (parts_fc, parts_att)
    core_in = (core_fc, core_att)
    rs_in = (rs_fc, rs_att)
    east = lax.rem(lon + 1, STRIPS)
    west = lax.rem(lon + STRIPS - 1, STRIPS)
    south = lax.rem(lat + 1, BANDS)
    north = lax.rem(lat + BANDS - 1, BANDS)
    sibling = (lon, lat - core + other)

    pair_rows = [lax.rem(pair_row + d, 8) for d in range(8)]

    def to_chips(act):
        def strip_step(step, carry):
            at = lax.rem(lon + step, STRIPS)
            for n, row in enumerate(pair_rows):
                if n:
                    act((at, row * 2 + core), at * 8 + row)
                else:
                    @pl.when(step > 0)
                    def _():
                        act((at, row * 2 + core), at * 8 + row)

            return carry

        lax.fori_loop(0, STRIPS, strip_step, 0)

    def unit_of(seg, at):
        return lax.rem(at + 2 * CHIPS - FIRST[seg] - 32 * core, CHIPS)

    mine = [unit_of(seg, chip) for seg in range(2)]

    barrier = pltpu.get_barrier_semaphore()

    def greet(target, at=None):
        pl.semaphore_signal(barrier, inc=1, device_id=target, device_id_type=MESH)

    for target in (
        (east, lat), (west, lat), (lon, south), (lon, north), (east, south), (west, north), sibling,
    ):
        greet(target)
    to_chips(greet)

    tabw[...] = jnp.zeros_like(tabw)
    loads[0].wait()
    for head in range(HEADS):
        tabw[head : head + 1, 0:NREL] = table_ref[0, head]

    stage[...] = jnp.zeros_like(stage)
    for a, src in enumerate((tok_ref, cot_ref)):
        loads[(1, 3)[a]].wait()
        for h in range(WIN_H):
            for w in range(WIN_W):
                stage[slot_rows(h, w), :] = src[h, w].astype(F32)
        send[a] = stage[...].astype(BF16).reshape(4, SLOT, C)
        arrive[a, 3] = send[a, 0]

    pl.semaphore_wait(barrier, 7 + CHIPS - 1)

    ahead = ((east, lat), (lon, south), (east, south))
    behind = ((west, lat), (lon, north), (west, north))

    def exchange(a, i):
        return pltpu.make_async_remote_copy(
            src_ref=send.at[a, i + 1],
            dst_ref=arrive.at[a, 2 - i],
            send_sem=ex_send.at[a, i],
            recv_sem=ex_recv.at[a, i],
            device_id=ahead[i],
            device_id_type=MESH,
        )

    def table_copy():
        return pltpu.make_async_remote_copy(
            src_ref=tabw,
            dst_ref=tab15,
            send_sem=one_send.at[0],
            recv_sem=one_recv.at[0],
            device_id=(lon, south),
            device_id_type=MESH,
        )

    @pl.when(lat == BANDS - 1)
    def _():
        table_copy().start()

    for a in range(2):
        for i in range(3):
            exchange(a, i).start()

    tin[...] = jnp.zeros_like(tin)

    def spread(src, zp, zq, hp, width):
        j = (zp * WIN_Z + zq) * WIN_H + hp
        first = j * WIN_H * SPAN
        base = first // 128 * 128
        wide = src[:, base : base + 384]
        moved = pltpu.roll(wide, (384 - (first - base)) % 384, axis=1)
        g = zp * WIN_H + hp
        tin[g * 8 : g * 8 + 8, zq * 256 : zq * 256 + width] = moved[:, :width]

    for zp in range(WIN_Z):
        for zq in range(WIN_Z):
            for hp in range(WIN_H):
                spread(tabw, zp, zq, hp, WIN_H * SPAN)

    @pl.when(lat == 0)
    def _():
        table_copy().wait_recv()
        for zp in range(WIN_Z):
            for zq in range(WIN_Z):
                for hp in range(3):
                    spread(tab15, zp, zq, hp, 3 * SPAN)

    whole = tin[...]
    high = whole.astype(BF16)
    rest = whole - high.astype(F32)
    middle = rest.astype(BF16)
    low = (rest - middle.astype(F32)).astype(BF16)
    loads[2].wait()
    perm = perm_ref[...]
    spread_rows = dot(high, perm) + dot(middle, perm) + dot(low, perm)
    for n in range(3):
        ymat[n, 0:96, :] = spread_rows[:, 128 * n : 128 * (n + 1)]
        ymat[n, 96:128, :] = jnp.zeros((32, 128), F32)
    loads[4].wait()

    @pl.when(lat == 0)
    def _():
        for n in range(3):
            ymat[n, 0:96, :] = ymat[n, 0:96, :] + cross_ref[:, 128 * n : 128 * (n + 1)]

    for head in range(HEADS):
        rows = jnp.concatenate(
            [ymat[n, pl.ds(head, 16, stride=8), :] for n in range(3)], -1
        )
        for w in range(WIN_W):
            moved = pltpu.roll(rows, (384 - (WIN_W - 1 - w) * GROUPS) % 384, axis=1)
            bias[head, w * GROUPS : (w + 1) * GROUPS, :] = moved[:GROUPS, :T]

    for n in range(5, 16):
        loads[n].wait()
    lane = lax.broadcasted_iota(jnp.int32, (T, C), 1)
    masks = [(lane >= HEAD * i) & (lane < HEAD * (i + 1)) for i in range(HEADS)]
    order = order_ref[...]
    back = back_ref[...]
    gain1 = g1_ref[...].reshape(1, C)
    gain2 = g2_ref[...].reshape(1, C)

    def arrived(a):
        for i in range(3):
            exchange(a, i).wait_recv()
        return dot(order, arrive[a].reshape(4 * SLOT, C))

    tokens = arrived(0)
    normed, hat1, inv1 = normalize(tokens, gain1)
    first = normed.astype(BF16)
    qkv = (dot(first, wqkv_ref[...]) + bqkv_ref[...].reshape(1, 3 * C)).astype(BF16)
    queries = qkv[:, 0:C]
    keys = qkv[:, C : 2 * C]
    values = qkv[:, 2 * C : 3 * C]
    queries_t = queries.T
    mixed = jnp.zeros((T, C), F32)
    for head in range(HEADS):
        q = jnp.where(masks[head], queries, jnp.zeros_like(queries))
        scores = dot_nt(q, keys) * FACTOR + bias[head]
        top = jnp.max(scores, -1, keepdims=True)
        raised = jnp.exp(scores - top)
        probs = raised * (1.0 / jnp.sum(raised, -1, keepdims=True))
        prob[head] = probs
        probs_low = probs.astype(BF16)
        plow[head] = probs_low
        mixed = jnp.where(masks[head], dot(probs_low, values), mixed)
    mixed = mixed.astype(BF16)
    inner = tokens + dot(mixed, wproj_ref[...]).astype(BF16).astype(F32)

    cot = arrived(1)
    cot_low = cot.astype(BF16)
    normed, hat2, inv2 = normalize(inner, gain2)
    second = normed.astype(BF16)
    second_t = second.T
    cot_t = cot_low.T
    total = inner
    grad_second = jnp.zeros((T, C), F32)
    bfc1 = bfc1_ref[...].reshape(1, HID)
    vec[...] = jnp.zeros_like(vec)
    for n in range(3):
        cols = slice(256 * n, 256 * (n + 1))
        pre = dot(second, wfc1_ref[:, cols]) + bfc1[:, cols]
        cdf = 0.5 * (1.0 + lax.erf(pre * 0.7071067811865476))
        density = jnp.exp(-0.5 * pre * pre) * 0.3989422804014327
        act = (pre * cdf).astype(BF16)
        total = total + dot_nt(act, wfc2_ref[:, cols])
        grad_pre = (dot(cot_low, wfc2_ref[:, cols]) * (cdf + pre * density)).astype(BF16)
        grad_second = grad_second + dot_nt(grad_pre, wfc1_ref[:, cols])
        parts_fc[0, 12 * n : 12 * (n + 1)] = dot(second_t, grad_pre).astype(BF16).reshape(12, 16, 256)
        parts_fc[1, 12 * n : 12 * (n + 1)] = dot(cot_t, act).astype(BF16).reshape(12, 16, 256)
        vec[n : n + 1, :] = jnp.sum(grad_pre.astype(F32), 0, keepdims=True)

    def pair(seg):
        return pltpu.make_async_remote_copy(
            src_ref=parts[seg].at[other],
            dst_ref=core_in[seg],
            send_sem=c_send.at[seg],
            recv_sem=c_recv.at[seg],
            device_id=sibling,
            device_id_type=MESH,
        )

    def give_back(a, i):
        return pltpu.make_async_remote_copy(
            src_ref=out_stage.at[a, 2 - i],
            dst_ref=ret_ref.at[a, i + 1],
            send_sem=rt_send.at[a, i],
            recv_sem=rt_recv.at[a, i],
            device_id=behind[i],
            device_id_type=MESH,
        )

    def hand_out(a, field):
        out_stage[a] = dot(back, field).astype(BF16).reshape(4, SLOT, C)
        for i in range(3):
            give_back(a, i).start()
        ret_ref[a, 0] = out_stage[a, 3]

    grad_inner = cot + norm_back(hat2, inv2, gain2, grad_second)
    grad_att = grad_inner.astype(BF16)
    proj_grad = dot_tn(mixed, grad_att).astype(BF16)
    proj_grad = jnp.concatenate([proj_grad, jnp.zeros((C, 64), BF16)], -1).reshape(12, 16, 256)
    parts_fc[0, 36:42] = proj_grad[:6]
    parts_fc[1, 36:42] = proj_grad[6:]
    vec[3:4, 0:C] = jnp.sum(grad_second * hat2, 0, keepdims=True)
    parts_fc[0, 42] = vec[...].astype(BF16)
    parts_fc[1, 42] = jnp.zeros((16, 256), BF16)
    pair(0).start()
    hand_out(0, total.astype(BF16))

    def share(seg):
        pair(seg).wait_recv()
        parts[seg][core] = (
            parts[seg][core].astype(F32) + core_in[seg][...].astype(F32)
        ).astype(BF16)

        def push(target, at):
            unit = unit_of(seg, at)

            @pl.when(unit < COUNTS[seg])
            def _():
                pltpu.make_async_remote_copy(
                    src_ref=parts[seg].at[core, unit],
                    dst_ref=rs_in[seg].at[chip],
                    send_sem=s_send.at[seg],
                    recv_sem=s_recv.at[seg],
                    device_id=target,
                    device_id_type=MESH,
                ).start()

        to_chips(push)

    def wait_bytes(ref, sem):
        pltpu.make_async_copy(ref, ref, sem).wait()

    others = [ref.at[pl.ds(0, CHIPS - 1)] for ref in rs_in]

    def settle(seg):
        at = mine[seg]

        @pl.when(at < COUNTS[seg])
        def _():
            rs_in[seg][chip] = parts[seg][core, at]
            wait_bytes(others[seg], s_recv.at[seg])
            gath[seg][core, at] = jnp.sum(rs_in[seg][...].astype(F32), 0).astype(BF16)

            def push(target, _):
                pltpu.make_async_remote_copy(
                    src_ref=gath[seg].at[core, at],
                    dst_ref=gath[seg].at[core, at],
                    send_sem=a_send.at[seg],
                    recv_sem=a_recv.at[seg],
                    device_id=target,
                    device_id_type=MESH,
                ).start()

            to_chips(push)

    def swap(seg):
        return pltpu.make_async_remote_copy(
            src_ref=gath[seg].at[core],
            dst_ref=gath[seg].at[core],
            send_sem=d_send.at[seg],
            recv_sem=d_recv.at[seg],
            device_id=sibling,
            device_id_type=MESH,
        )

    def wait_units(seg, sem):
        @pl.when(mine[seg] < COUNTS[seg])
        def _():
            wait_bytes(parts[seg].at[0, pl.ds(0, COUNTS[seg] - 1)], sem)

        @pl.when(mine[seg] >= COUNTS[seg])
        def _():
            wait_bytes(parts[seg].at[0], sem)

    grad_mixed = dot_nt(grad_att, wproj_ref[...]).astype(BF16)
    grad_mixed_t = grad_mixed.T
    dsc[...] = jnp.zeros_like(dsc)
    grad_q = jnp.zeros((T, C), F32)
    grad_k_t = []
    grad_v_t = []
    for head in range(HEADS):
        rows = slice(HEAD * head, HEAD * (head + 1))
        gm = jnp.where(masks[head], grad_mixed, jnp.zeros_like(grad_mixed))
        probs = prob[head]
        grad_probs = dot_nt(gm, values)
        inside = jnp.sum(probs * grad_probs, -1, keepdims=True)
        grad_scores = probs * (grad_probs - inside)
        dsc[head, 0:T, 0:T] = grad_scores
        scaled = (grad_scores * FACTOR).astype(BF16)
        grad_q = jnp.where(masks[head], dot(scaled, keys), grad_q)
        grad_k_t.append(dot(queries_t[rows], scaled))
        grad_v_t.append(dot(grad_mixed_t[rows], plow[head]))
        if head == 1:
            share(0)
    grad_k = jnp.concatenate(grad_k_t, 0).T
    grad_v = jnp.concatenate(grad_v_t, 0).T

    grad_qkv = jnp.concatenate([grad_q, grad_k, grad_v], -1).astype(BF16)
    wide = dot_tn(first, grad_qkv).astype(BF16)
    for n in range(4):
        parts_att[n // 2, n % 2 * 12 : n % 2 * 12 + 12] = (
            wide[:, 128 * n : 128 * (n + 1)].reshape(12, 16, 128)
        )
    edge = jnp.concatenate([wide[:96, 512:576], wide[96:, 512:576]], -1).reshape(6, 16, 128)
    parts_att[0, 24:27] = edge[:3]
    parts_att[1, 24:27] = edge[3:]
    grad_first = dot_nt(grad_qkv, wqkv_ref[...]).astype(BF16).astype(F32)
    vec[...] = jnp.zeros_like(vec)
    sums = jnp.sum(grad_qkv.astype(F32), 0, keepdims=True)
    sums = [sums[:, C * n : C * (n + 1)] for n in range(3)]
    sums.append(jnp.sum(grad_first * hat1, 0, keepdims=True))
    for n in range(4):
        vec[2 * n : 2 * n + 1, 0:128] = sums[n][:, 0:128]
        vec[2 * n + 1 : 2 * n + 2, 0:64] = sums[n][:, 128:C]
    parts_att[0, 27] = vec[:, 0:128].astype(BF16)
    parts_att[1, 27] = jnp.zeros((16, 128), BF16)
    pair(1).start()
    settle(0)
    d_tokens = grad_inner + norm_back(hat1, inv1, gain1, grad_first)
    hand_out(1, d_tokens.astype(BF16))
    share(1)

    dmat[...] = jnp.zeros_like(dmat)
    for head in range(HEADS):
        acc = jnp.zeros((16, 384), F32)
        for w in range(WIN_W):
            acc = acc + pltpu.roll(
                dsc[head, w * GROUPS : w * GROUPS + 16, :], (WIN_W - 1 - w) * GROUPS, axis=1
            )
        for n in range(3):
            dmat[n, pl.ds(head, 16, stride=8), :] = acc[:, 128 * n : 128 * (n + 1)]

    def table_grad():
        return jnp.concatenate([dmat[n, 0:96, :] for n in range(3)], -1)

    def keep_table(field):
        for n in range(3):
            dmat[n, 0:96, :] = field[:, 128 * n : 128 * (n + 1)]

    def edge_copy():
        return pltpu.make_async_remote_copy(
            src_ref=bbs,
            dst_ref=bbr,
            send_sem=one_send.at[1],
            recv_sem=one_recv.at[1],
            device_id=(lon, north),
            device_id_type=MESH,
        )

    @pl.when(lat == 0)
    def _():
        row = lax.broadcasted_iota(jnp.int32, (96, 384), 0)
        upper = (row < 24) | ((row >= 48) & (row < 72))
        full = table_grad()
        bbs[...] = jnp.where(upper, full, 0.0).astype(BF16)
        edge_copy().start()
        keep_table(jnp.where(upper, 0.0, full))

    @pl.when(lat == BANDS - 1)
    def _():
        edge_copy().wait_recv()
        keep_table(table_grad() + bbr[...].astype(F32))

    bsend[...] = table_grad().astype(BF16).reshape(PARTS, 16, 384)

    def strip(d):
        return lax.rem(lon + d, STRIPS)

    for owner in range(PARTS):
        @pl.when(lon != owner)
        def _():
            pltpu.make_async_remote_copy(
                src_ref=bsend.at[owner],
                dst_ref=brecv.at[lon],
                send_sem=b_send.at[0],
                recv_sem=b_recv.at[0],
                device_id=(owner, lat),
                device_id_type=MESH,
            ).start()

    settle(1)
    seven = brecv.at[pl.ds(0, STRIPS - 1)]

    @pl.when(lon < PARTS)
    def _():
        brecv[lon] = bsend[lon]
        wait_bytes(seven, b_recv.at[0])
        bfin[lon] = jnp.sum(brecv[...].astype(F32), 0).astype(BF16)
        for d in range(1, STRIPS):
            pltpu.make_async_remote_copy(
                src_ref=bfin.at[lon],
                dst_ref=bfin.at[lon],
                send_sem=b_send.at[1],
                recv_sem=b_recv.at[1],
                device_id=(strip(d), lat),
                device_id_type=MESH,
            ).start()

    wait_units(0, a_recv.at[0])
    swap(0).start()

    @pl.when(lon < PARTS)
    def _():
        wait_bytes(bfin.at[pl.ds(0, PARTS - 1)], b_recv.at[1])

    @pl.when(lon >= PARTS)
    def _():
        wait_bytes(bfin, b_recv.at[1])

    tin[...] = dot(bfin[...].reshape(96, 384), unperm_ref[...])
    dtab_ref[...] = jnp.zeros_like(dtab_ref)
    for zp in range(WIN_Z):
        for zq in range(WIN_Z):
            for hp in range(WIN_H):
                j = (zp * WIN_Z + zq) * WIN_H + hp
                first_lane = j * WIN_H * SPAN
                base = first_lane // 128 * 128
                g = zp * WIN_H + hp
                piece = tin[g * 8 : g * 8 + 8, zq * 256 : zq * 256 + 256]
                piece = jnp.concatenate([piece, jnp.zeros((8, 128), F32)], -1)
                moved = pltpu.roll(piece, first_lane - base, axis=1)
                dtab_ref[:, base : base + 384] = dtab_ref[:, base : base + 384] + moved

    wait_units(1, a_recv.at[1])
    swap(1).start()

    for a in range(2):
        for i in range(3):
            exchange(a, i).wait_send()
            give_back(a, i).wait()

    @pl.when(lat == BANDS - 1)
    def _():
        table_copy().wait_send()

    @pl.when(lat == 0)
    def _():
        edge_copy().wait_send()

    for seg in range(2):
        pair(seg).wait_send()
        wait_units(seg, s_send.at[seg])

        @pl.when(mine[seg] < COUNTS[seg])
        def _():
            wait_bytes(others[seg], a_send.at[seg])

        swap(seg).wait()

    @pl.when(lon < PARTS)
    def _():
        wait_bytes(bsend.at[pl.ds(0, PARTS - 1)], b_send.at[0])
        wait_bytes(seven, b_send.at[1])

    @pl.when(lon >= PARTS)
    def _():
        wait_bytes(bsend, b_send.at[0])


def output_kernel(
    gath_ref, gath_att, ret_ref, dtab_ref,
    out_ref, dtok_ref, dln1_ref, dwqkv_ref, dbqkv_ref, dbias_ref, dwproj_ref, dln2_ref,
    dwfc1_ref, dbfc1_ref, dwfc2_ref,
    stage,
):
    for a, dst in enumerate((out_ref, dtok_ref)):
        stage[...] = ret_ref[a].reshape(4 * SLOT, C).astype(F32)
        for h in range(WIN_H):
            for w in range(WIN_W):
                dst[h, w] = stage[slot_rows(h, w), :].astype(BF16)
    for n in range(3):
        cols = slice(256 * n, 256 * (n + 1))
        rows = slice(12 * n, 12 * (n + 1))
        dwfc1_ref[:, cols] = gath_ref[0, rows].reshape(C, 256).astype(F32)
        dwfc2_ref[:, cols] = gath_ref[1, rows].reshape(C, 256).astype(F32)
    for k in range(2):
        dwproj_ref[96 * k : 96 * (k + 1), :] = (
            gath_ref[k, 36:42].reshape(96, 256)[:, 0:C].astype(F32)
        )
        for n in range(2):
            cols = slice(256 * k + 128 * n, 256 * k + 128 * (n + 1))
            dwqkv_ref[:, cols] = gath_att[k, 12 * n : 12 * (n + 1)].reshape(C, 128).astype(F32)
        edge = gath_att[k, 24:27].reshape(48, 128).astype(F32)
        for n in range(2):
            at = 96 * n + 48 * k
            dwqkv_ref[at : at + 48, 512:576] = edge[:, 64 * n : 64 * (n + 1)]
    vec = gath_ref[0, 42].astype(F32)
    dbfc1_ref[...] = jnp.concatenate([vec[n : n + 1] for n in range(3)], -1).reshape(HID)
    dln2_ref[...] = vec[3:4, :C].reshape(C)
    vec = gath_att[0, 27].astype(F32)
    sums = [
        jnp.concatenate([vec[2 * n : 2 * n + 1], vec[2 * n + 1 : 2 * n + 2, :64]], -1)
        for n in range(4)
    ]
    dbqkv_ref[...] = jnp.concatenate(sums[:3], -1).reshape(3 * C)
    dln1_ref[...] = sums[3].reshape(C)
    for head in range(HEADS):
        dbias_ref[0, head] = dtab_ref[head : head + 1, 0:NREL]


def per_device(
    tokens, cotangent, ln1_gain, w_qkv, b_qkv, bias_table, w_proj, ln2_gain, w_fc1, b_fc1, w_fc2
):
    vmem = pl.BlockSpec(memory_space=pltpu.VMEM)
    order = window_order()
    perm = table_order()
    dma = pltpu.SemaphoreType.DMA
    args = (
        tokens.transpose(1, 2, 0, 3), cotangent.transpose(1, 2, 0, 3), ln1_gain, w_qkv, b_qkv,
        bias_table.transpose(0, 2, 1, 3), w_proj, ln2_gain, w_fc1, b_fc1, w_fc2.T,
        jnp.asarray(order, BF16), jnp.asarray(order.T, BF16),
        jnp.asarray(perm, BF16), jnp.asarray(perm.T, BF16),
        jnp.asarray(cross_pairs()),
    )
    results = pl.pallas_call(
        block_kernel,
        out_shape=(
            jax.ShapeDtypeStruct((2, FC, 16, 256), BF16),
            jax.ShapeDtypeStruct((2, ATT, 16, 128), BF16),
            jax.ShapeDtypeStruct((2, 4, SLOT, C), BF16),
            jax.ShapeDtypeStruct((8, 3456), F32),
        ),
        in_specs=[pl.BlockSpec(memory_space=pl.ANY)] * len(args),
        out_specs=(vmem,) * 4,
        scratch_shapes=[pltpu.VMEM(a.shape, a.dtype) for a in args]
        + [
            pltpu.VMEM((4 * SLOT, C), F32),
            pltpu.VMEM((2, 4, SLOT, C), BF16),
            pltpu.VMEM((2, 4, SLOT, C), BF16),
            pltpu.VMEM((2, 4, SLOT, C), BF16),
            pltpu.VMEM((8, 3456), F32),
            pltpu.VMEM((8, 3456), F32),
            pltpu.VMEM((96, 512), F32),
            pltpu.VMEM((3, 128, 128), F32),
            pltpu.VMEM((HEADS, T, T), F32),
            pltpu.VMEM((HEADS, T, T), F32),
            pltpu.VMEM((HEADS, T, T), BF16),
            pltpu.VMEM((HEADS, 160, 384), F32),
            pltpu.VMEM((3, 128, 128), F32),
            pltpu.VMEM((16, 256), F32),
            pltpu.VMEM((PARTS, 16, 384), BF16),
            pltpu.VMEM((STRIPS, 16, 384), BF16),
            pltpu.VMEM((PARTS, 16, 384), BF16),
            pltpu.VMEM((96, 384), BF16),
            pltpu.VMEM((96, 384), BF16),
            pltpu.VMEM((2, FC, 16, 256), BF16),
            pltpu.VMEM((2, ATT, 16, 128), BF16),
            pltpu.VMEM((FC, 16, 256), BF16),
            pltpu.VMEM((ATT, 16, 128), BF16),
            pltpu.VMEM((CHIPS, 16, 256), BF16),
            pltpu.VMEM((CHIPS, 16, 128), BF16),
            dma((len(args),)),
            dma((2, 3)), dma((2, 3)), dma((2, 3)), dma((2, 3)),
            dma((2,)), dma((2,)), dma((2,)), dma((2,)),
            dma((2,)), dma((2,)), dma((2,)), dma((2,)),
            dma((2,)), dma((2,)), dma((2,)), dma((2,)),
        ],
        compiler_params=pltpu.CompilerParams(
            collective_id=0, has_side_effects=True, vmem_limit_bytes=VMEM_LIMIT
        ),
    )(*args)
    shape = jax.ShapeDtypeStruct
    grid_shape = (WIN_H, WIN_W, WIN_Z, C)
    outs = pl.pallas_call(
        output_kernel,
        out_shape=(
            shape(grid_shape, BF16), shape(grid_shape, BF16),
            shape((C,), F32), shape((C, 3 * C), F32), shape((3 * C,), F32),
            shape((1, HEADS, 1, NREL), F32), shape((C, C), F32), shape((C,), F32),
            shape((C, HID), F32), shape((HID,), F32), shape((C, HID), F32),
        ),
        in_specs=[vmem] * 4,
        out_specs=(vmem,) * 11,
        scratch_shapes=[pltpu.VMEM((4 * SLOT, C), F32)],
        compiler_params=pltpu.CompilerParams(vmem_limit_bytes=VMEM_LIMIT),
    )(*results)
    out, d_tok, d_ln1, d_wqkv, d_bqkv, d_bias, d_wproj, d_ln2, d_wfc1, d_bfc1, d_wfc2 = outs
    return (
        out.transpose(2, 0, 1, 3), d_tok.transpose(2, 0, 1, 3), d_ln1, d_wqkv, d_bqkv,
        d_bias.transpose(0, 2, 1, 3), d_wproj, d_ln2, d_wfc1, d_bfc1, d_wfc2.T,
    )


def solution(mesh):
    grid = P(None, "lat", "lon", None)
    rows = P(None, "lat", None, None)
    return jax.shard_map(
        per_device,
        mesh=mesh,
        in_specs=(grid, grid, P(), P(), P(), rows, P(), P(), P(), P(), P()),
        out_specs=(grid, grid, P(), P(), P(), rows, P(), P(), P(), P(), P()),
        check_vma=False,
    )
```

```python
import jax
import jax.numpy as jnp
import numpy as np
from jax import lax
from jax.experimental import pallas as pl
from jax.experimental.pallas import tpu as pltpu
from jax.sharding import PartitionSpec as P

HEADS = 6
WIN_Z = 2
WIN_H = 6
WIN_W = 12
SPAN = 2 * WIN_W - 1
GROUPS = WIN_Z * WIN_H
T = GROUPS * WIN_W
C = 192
HID = 768
HEAD = C // HEADS
NREL = GROUPS * GROUPS * SPAN
SLOT = 48
FC = 44
ATT = 28
WIDE = 2
COUNTS = (FC // WIDE, ATT)
FIRST = (0, FC // WIDE)
CHIPS = 64
BANDS = 16
STRIPS = 8
PARTS = 6
EPSILON = 1e-05
VMEM_LIMIT = 56 * 1024 * 1024
FACTOR = HEAD ** (-0.5)
F32 = jnp.float32
BF16 = jnp.bfloat16
MESH = pl.DeviceIdType.MESH


def window_order():
    grid = np.zeros((T, 4 * SLOT), np.float32)
    for w in range(WIN_W):
        for z in range(WIN_Z):
            for h in range(WIN_H):
                slot = (h // 3) * 2 + w // 6
                grid[w * GROUPS + z * WIN_H + h, slot * SLOT + (h % 3) * 12 + (w % 6) * 2 + z] = 1
    return grid


def table_order():
    grid = np.zeros((512, 384), np.float32)
    for z in range(WIN_Z):
        for h in range(WIN_H):
            for i in range(SPAN):
                grid[z * 256 + h * SPAN + i, (SPAN - 1 - i) * GROUPS + z * WIN_H + h] = 1
    return grid


def cross_pairs():
    g = np.arange(96)[:, None] // 8 % WIN_H
    q = np.arange(384)[None, :] % GROUPS % WIN_H
    return np.where((g < 3) != (q < 3), -1e30, 0.0).astype(np.float32)


def dot(a, b):
    return jnp.dot(a, b, preferred_element_type=F32)


def dot_nt(a, b):
    return lax.dot_general(a, b, (((1,), (1,)), ((), ())), preferred_element_type=F32)


def dot_tn(a, b):
    return lax.dot_general(a, b, (((0,), (0,)), ((), ())), preferred_element_type=F32)


def normalize(values, gain):
    average = jnp.mean(values, -1, keepdims=True)
    centered = values - average
    inv = lax.rsqrt(jnp.mean(centered * centered, -1, keepdims=True) + EPSILON)
    hat = centered * inv
    return hat * gain, hat, inv


def norm_back(hat, inv, gain, grad):
    scaled = grad * gain
    return inv * (
        scaled
        - jnp.mean(scaled, -1, keepdims=True)
        - hat * jnp.mean(scaled * hat, -1, keepdims=True)
    )


def slot_rows(h, w):
    at = ((h // 3) * 2 + w // 6) * SLOT + (h % 3) * 12 + (w % 6) * 2
    return slice(at, at + 2)


def block_kernel(
    tok_any, cot_any, g1_any, wqkv_any, bqkv_any, table_any, wproj_any, g2_any, wfc1_any,
    bfc1_any, wfc2_any, order_any, back_any, perm_any, unperm_any, cross_any,
    gath_fc, gath_att, ret_ref, dtab_ref,
    tok_ref, cot_ref, g1_ref, wqkv_ref, bqkv_ref, table_ref, wproj_ref, g2_ref, wfc1_ref,
    bfc1_ref, wfc2_ref, order_ref, back_ref, perm_ref, unperm_ref, cross_ref,
    stage, send, arrive, out_stage,
    tabw, tab15, tin, ymat, bias, prob, plow, dsc, dmat, vec,
    bsend, brecv, bfin, bbs, bbr,
    parts_fc, parts_att, core_fc, core_att, rs_fc, rs_att,
    in_sem,
    ex_send, ex_recv, rt_send, rt_recv, one_send, one_recv, c_send, c_recv,
    s_send, s_recv, a_send, a_recv, d_send, d_recv, b_send, b_recv,
):
    places = (
        (table_any, table_ref), (tok_any, tok_ref), (perm_any, perm_ref), (cot_any, cot_ref),
        (cross_any, cross_ref), (order_any, order_ref), (g1_any, g1_ref), (wqkv_any, wqkv_ref),
        (bqkv_any, bqkv_ref), (wproj_any, wproj_ref), (g2_any, g2_ref), (wfc1_any, wfc1_ref),
        (bfc1_any, bfc1_ref), (wfc2_any, wfc2_ref), (back_any, back_ref),
        (unperm_any, unperm_ref),
    )
    loads = [pltpu.make_async_copy(src, dst, in_sem.at[n]) for n, (src, dst) in enumerate(places)]
    for load in loads:
        load.start()
    lon = lax.axis_index("lon")
    lat = lax.axis_index("lat")
    core = lax.rem(lat, 2)
    other = 1 - core
    pair_row = lat // 2
    chip = lon * 8 + pair_row
    gath = (gath_fc, gath_att)
    parts = (parts_fc, parts_att)
    core_in = (core_fc, core_att)
    rs_in = (rs_fc, rs_att)
    east = lax.rem(lon + 1, STRIPS)
    west = lax.rem(lon + STRIPS - 1, STRIPS)
    south = lax.rem(lat + 1, BANDS)
    north = lax.rem(lat + BANDS - 1, BANDS)
    sibling = (lon, lat - core + other)

    pair_rows = [lax.rem(pair_row + d, 8) for d in range(8)]

    def to_chips(act):
        def strip_step(step, carry):
            at = lax.rem(lon + step, STRIPS)
            for n, row in enumerate(pair_rows):
                if n:
                    act((at, row * 2 + core), at * 8 + row)
                else:
                    @pl.when(step > 0)
                    def _():
                        act((at, row * 2 + core), at * 8 + row)

            return carry

        lax.fori_loop(0, STRIPS, strip_step, 0)

    def unit_of(seg, at):
        return lax.rem(at + 2 * CHIPS - FIRST[seg] - 32 * core, CHIPS)

    mine = [unit_of(seg, chip) for seg in range(2)]

    def tiles(seg, unit):
        return pl.ds(unit * WIDE, WIDE) if seg == 0 else unit

    barrier = pltpu.get_barrier_semaphore()

    def greet(target, at=None):
        pl.semaphore_signal(barrier, inc=1, device_id=target, device_id_type=MESH)

    for target in (
        (east, lat), (west, lat), (lon, south), (lon, north), (east, south), (west, north), sibling,
    ):
        greet(target)
    to_chips(greet)

    stage[...] = jnp.zeros_like(stage)

    def quadrants(a, src):
        loads[(1, 3)[a]].wait()
        for h in range(WIN_H):
            for w in range(WIN_W):
                stage[slot_rows(h, w), :] = src[h, w].astype(F32)
        send[a] = stage[...].astype(BF16).reshape(4, SLOT, C)
        arrive[a, 3] = send[a, 0]

    quadrants(0, tok_ref)
    pl.semaphore_wait(barrier, 7 + CHIPS - 1)

    ahead = ((east, lat), (lon, south), (east, south))
    behind = ((west, lat), (lon, north), (west, north))

    def exchange(a, i):
        return pltpu.make_async_remote_copy(
            src_ref=send.at[a, i + 1],
            dst_ref=arrive.at[a, 2 - i],
            send_sem=ex_send.at[a, i],
            recv_sem=ex_recv.at[a, i],
            device_id=ahead[i],
            device_id_type=MESH,
        )

    def table_copy():
        return pltpu.make_async_remote_copy(
            src_ref=tabw,
            dst_ref=tab15,
            send_sem=one_send.at[0],
            recv_sem=one_recv.at[0],
            device_id=(lon, south),
            device_id_type=MESH,
        )

    for i in range(3):
        exchange(0, i).start()

    tabw[...] = jnp.zeros_like(tabw)
    loads[0].wait()
    for head in range(HEADS):
        tabw[head : head + 1, 0:NREL] = table_ref[0, head]

    @pl.when(lat == BANDS - 1)
    def _():
        table_copy().start()

    quadrants(1, cot_ref)
    for i in range(3):
        exchange(1, i).start()

    tin[...] = jnp.zeros_like(tin)

    def spread(src, zp, zq, hp, width):
        j = (zp * WIN_Z + zq) * WIN_H + hp
        first = j * WIN_H * SPAN
        base = first // 128 * 128
        wide = src[:, base : base + 384]
        moved = pltpu.roll(wide, (384 - (first - base)) % 384, axis=1)
        g = zp * WIN_H + hp
        tin[g * 8 : g * 8 + 8, zq * 256 : zq * 256 + width] = moved[:, :width]

    for zp in range(WIN_Z):
        for zq in range(WIN_Z):
            for hp in range(WIN_H):
                spread(tabw, zp, zq, hp, WIN_H * SPAN)

    @pl.when(lat == 0)
    def _():
        table_copy().wait_recv()
        for zp in range(WIN_Z):
            for zq in range(WIN_Z):
                for hp in range(3):
                    spread(tab15, zp, zq, hp, 3 * SPAN)

    whole = tin[...]
    high = whole.astype(BF16)
    rest = whole - high.astype(F32)
    middle = rest.astype(BF16)
    low = (rest - middle.astype(F32)).astype(BF16)
    loads[2].wait()
    perm = perm_ref[...]
    spread_rows = dot(high, perm) + dot(middle, perm) + dot(low, perm)
    for n in range(3):
        ymat[n, 0:96, :] = spread_rows[:, 128 * n : 128 * (n + 1)]
        ymat[n, 96:128, :] = jnp.zeros((32, 128), F32)
    loads[4].wait()

    @pl.when(lat == 0)
    def _():
        for n in range(3):
            ymat[n, 0:96, :] = ymat[n, 0:96, :] + cross_ref[:, 128 * n : 128 * (n + 1)]

    for head in range(HEADS):
        rows = jnp.concatenate(
            [ymat[n, pl.ds(head, 16, stride=8), :] for n in range(3)], -1
        )
        for w in range(WIN_W):
            moved = pltpu.roll(rows, (384 - (WIN_W - 1 - w) * GROUPS) % 384, axis=1)
            bias[head, w * GROUPS : (w + 1) * GROUPS, :] = moved[:GROUPS, :T]

    for n in range(5, 16):
        loads[n].wait()
    lane = lax.broadcasted_iota(jnp.int32, (T, C), 1)
    masks = [(lane >= HEAD * i) & (lane < HEAD * (i + 1)) for i in range(HEADS)]
    ones = [jnp.where(mask[0:16], 1.0, 0.0).astype(BF16)[0:1] for mask in masks]
    order = order_ref[...]
    back = back_ref[...]
    gain1 = g1_ref[...].reshape(1, C)
    gain2 = g2_ref[...].reshape(1, C)

    def arrived(a):
        for i in range(3):
            exchange(a, i).wait_recv()
        return dot(order, arrive[a].reshape(4 * SLOT, C))

    tokens = arrived(0)
    normed, hat1, inv1 = normalize(tokens, gain1)
    first = normed.astype(BF16)
    qkv = (dot(first, wqkv_ref[...]) + bqkv_ref[...].reshape(1, 3 * C)).astype(BF16)
    queries = qkv[:, 0:C]
    keys = qkv[:, C : 2 * C]
    values = qkv[:, 2 * C : 3 * C]
    queries_t = queries.T
    mixed = jnp.zeros((T, C), F32)
    for head in range(HEADS):
        q = queries * ones[head]
        scores = dot_nt(q, keys) * FACTOR + bias[head]
        top = jnp.max(scores, -1, keepdims=True)
        raised = jnp.exp(scores - top)
        probs = raised * (1.0 / jnp.sum(raised, -1, keepdims=True))
        prob[head] = probs
        probs_low = probs.astype(BF16)
        plow[head] = probs_low
        mixed = jnp.where(masks[head], dot(probs_low, values), mixed)
    mixed = mixed.astype(BF16)
    inner = tokens + dot(mixed, wproj_ref[...]).astype(BF16).astype(F32)

    cot = arrived(1)
    cot_low = cot.astype(BF16)
    normed, hat2, inv2 = normalize(inner, gain2)
    second = normed.astype(BF16)
    second_t = second.T
    cot_t = cot_low.T
    total = inner
    grad_second = jnp.zeros((T, C), F32)
    bfc1 = bfc1_ref[...].reshape(1, HID)
    vec[...] = jnp.zeros_like(vec)
    for n in range(3):
        cols = slice(256 * n, 256 * (n + 1))
        pre = dot(second, wfc1_ref[:, cols]) + bfc1[:, cols]
        cdf = 0.5 * (1.0 + lax.erf(pre * 0.7071067811865476))
        density = jnp.exp(-0.5 * pre * pre) * 0.3989422804014327
        act = (pre * cdf).astype(BF16)
        total = total + dot_nt(act, wfc2_ref[:, cols])
        grad_pre = (dot(cot_low, wfc2_ref[:, cols]) * (cdf + pre * density)).astype(BF16)
        grad_second = grad_second + dot_nt(grad_pre, wfc1_ref[:, cols])
        parts_fc[0, 12 * n : 12 * (n + 1)] = dot(second_t, grad_pre).astype(BF16).reshape(12, 16, 256)
        parts_fc[1, 12 * n : 12 * (n + 1)] = dot(cot_t, act).astype(BF16).reshape(12, 16, 256)
        vec[n : n + 1, :] = jnp.sum(grad_pre.astype(F32), 0, keepdims=True)

    def pair(seg):
        return pltpu.make_async_remote_copy(
            src_ref=parts[seg].at[other],
            dst_ref=core_in[seg],
            send_sem=c_send.at[seg],
            recv_sem=c_recv.at[seg],
            device_id=sibling,
            device_id_type=MESH,
        )

    def give_back(a, i):
        return pltpu.make_async_remote_copy(
            src_ref=out_stage.at[a, 2 - i],
            dst_ref=ret_ref.at[a, i + 1],
            send_sem=rt_send.at[a, i],
            recv_sem=rt_recv.at[a, i],
            device_id=behind[i],
            device_id_type=MESH,
        )

    def hand_out(a, field):
        out_stage[a] = dot(back, field).astype(BF16).reshape(4, SLOT, C)
        for i in range(3):
            give_back(a, i).start()
        ret_ref[a, 0] = out_stage[a, 3]

    grad_inner = cot + norm_back(hat2, inv2, gain2, grad_second)
    grad_att = grad_inner.astype(BF16)
    proj_grad = dot_tn(mixed, grad_att).astype(BF16)
    proj_grad = jnp.concatenate([proj_grad, jnp.zeros((C, 64), BF16)], -1).reshape(12, 16, 256)
    parts_fc[0, 36:42] = proj_grad[:6]
    parts_fc[1, 36:42] = proj_grad[6:]
    vec[3:4, 0:C] = jnp.sum(grad_second * hat2, 0, keepdims=True)
    parts_fc[0, 42] = vec[...].astype(BF16)
    parts_fc[1, 42] = jnp.zeros((16, 256), BF16)
    parts_fc[:, 43] = jnp.zeros((2, 16, 256), BF16)
    pair(0).start()
    hand_out(0, total.astype(BF16))

    def share(seg):
        pair(seg).wait_recv()
        parts[seg][core] = (
            parts[seg][core].astype(F32) + core_in[seg][...].astype(F32)
        ).astype(BF16)

        def push(target, at):
            unit = unit_of(seg, at)

            @pl.when(unit < COUNTS[seg])
            def _():
                pltpu.make_async_remote_copy(
                    src_ref=parts[seg].at[core, tiles(seg, unit)],
                    dst_ref=rs_in[seg].at[chip],
                    send_sem=s_send.at[seg],
                    recv_sem=s_recv.at[seg],
                    device_id=target,
                    device_id_type=MESH,
                ).start()

        to_chips(push)

    def wait_bytes(ref, sem):
        pltpu.make_async_copy(ref, ref, sem).wait()

    others = [ref.at[pl.ds(0, CHIPS - 1)] for ref in rs_in]

    def settle(seg):
        at = mine[seg]

        @pl.when(at < COUNTS[seg])
        def _():
            rs_in[seg][chip] = parts[seg][core, tiles(seg, at)]
            wait_bytes(others[seg], s_recv.at[seg])
            gath[seg][core, tiles(seg, at)] = jnp.sum(rs_in[seg][...].astype(F32), 0).astype(BF16)

            def push(target, _):
                pltpu.make_async_remote_copy(
                    src_ref=gath[seg].at[core, tiles(seg, at)],
                    dst_ref=gath[seg].at[core, tiles(seg, at)],
                    send_sem=a_send.at[seg],
                    recv_sem=a_recv.at[seg],
                    device_id=target,
                    device_id_type=MESH,
                ).start()

            to_chips(push)

    def swap(seg):
        return pltpu.make_async_remote_copy(
            src_ref=gath[seg].at[core],
            dst_ref=gath[seg].at[core],
            send_sem=d_send.at[seg],
            recv_sem=d_recv.at[seg],
            device_id=sibling,
            device_id_type=MESH,
        )

    def wait_units(seg, sem):
        @pl.when(mine[seg] < COUNTS[seg])
        def _():
            wait_bytes(parts[seg].at[0, pl.ds(0, (COUNTS[seg] - 1) * (WIDE, 1)[seg])], sem)

        @pl.when(mine[seg] >= COUNTS[seg])
        def _():
            wait_bytes(parts[seg].at[0], sem)

    grad_mixed = dot_nt(grad_att, wproj_ref[...]).astype(BF16)
    grad_mixed_t = grad_mixed.T
    dsc[...] = jnp.zeros_like(dsc)
    grad_q = jnp.zeros((T, C), F32)
    grad_k_t = []
    grad_v_t = []
    for head in range(HEADS):
        rows = slice(HEAD * head, HEAD * (head + 1))
        gm = grad_mixed * ones[head]
        probs = prob[head]
        grad_probs = dot_nt(gm, values)
        inside = jnp.sum(probs * grad_probs, -1, keepdims=True)
        grad_scores = probs * (grad_probs - inside)
        dsc[head, 0:T, 0:T] = grad_scores
        scaled = (grad_scores * FACTOR).astype(BF16)
        grad_q = jnp.where(masks[head], dot(scaled, keys), grad_q)
        grad_k_t.append(dot(queries_t[rows], scaled))
        grad_v_t.append(dot(grad_mixed_t[rows], plow[head]))
        if head == 1:
            share(0)
    grad_k = jnp.concatenate(grad_k_t, 0).T
    grad_v = jnp.concatenate(grad_v_t, 0).T

    grad_qkv = jnp.concatenate([grad_q, grad_k, grad_v], -1).astype(BF16)
    wide = dot_tn(first, grad_qkv).astype(BF16)
    for n in range(4):
        parts_att[n // 2, n % 2 * 12 : n % 2 * 12 + 12] = (
            wide[:, 128 * n : 128 * (n + 1)].reshape(12, 16, 128)
        )
    edge = jnp.concatenate([wide[:96, 512:576], wide[96:, 512:576]], -1).reshape(6, 16, 128)
    parts_att[0, 24:27] = edge[:3]
    parts_att[1, 24:27] = edge[3:]
    grad_first = dot_nt(grad_qkv, wqkv_ref[...]).astype(BF16).astype(F32)
    vec[...] = jnp.zeros_like(vec)
    sums = jnp.sum(grad_qkv.astype(F32), 0, keepdims=True)
    sums = [sums[:, C * n : C * (n + 1)] for n in range(3)]
    sums.append(jnp.sum(grad_first * hat1, 0, keepdims=True))
    for n in range(4):
        vec[2 * n : 2 * n + 1, 0:128] = sums[n][:, 0:128]
        vec[2 * n + 1 : 2 * n + 2, 0:64] = sums[n][:, 128:C]
    parts_att[0, 27] = vec[:, 0:128].astype(BF16)
    parts_att[1, 27] = jnp.zeros((16, 128), BF16)
    pair(1).start()
    d_tokens = grad_inner + norm_back(hat1, inv1, gain1, grad_first)
    hand_out(1, d_tokens.astype(BF16))
    share(1)
    settle(0)

    dmat[...] = jnp.zeros_like(dmat)
    for head in range(HEADS):
        acc = jnp.zeros((16, 384), F32)
        for w in range(WIN_W):
            acc = acc + pltpu.roll(
                dsc[head, w * GROUPS : w * GROUPS + 16, :], (WIN_W - 1 - w) * GROUPS, axis=1
            )
        for n in range(3):
            dmat[n, pl.ds(head, 16, stride=8), :] = acc[:, 128 * n : 128 * (n + 1)]

    def table_grad():
        return jnp.concatenate([dmat[n, 0:96, :] for n in range(3)], -1)

    def keep_table(field):
        for n in range(3):
            dmat[n, 0:96, :] = field[:, 128 * n : 128 * (n + 1)]

    def edge_copy():
        return pltpu.make_async_remote_copy(
            src_ref=bbs,
            dst_ref=bbr,
            send_sem=one_send.at[1],
            recv_sem=one_recv.at[1],
            device_id=(lon, north),
            device_id_type=MESH,
        )

    @pl.when(lat == 0)
    def _():
        row = lax.broadcasted_iota(jnp.int32, (96, 384), 0)
        upper = (row < 24) | ((row >= 48) & (row < 72))
        full = table_grad()
        bbs[...] = jnp.where(upper, full, 0.0).astype(BF16)
        edge_copy().start()
        keep_table(jnp.where(upper, 0.0, full))

    @pl.when(lat == BANDS - 1)
    def _():
        edge_copy().wait_recv()
        keep_table(table_grad() + bbr[...].astype(F32))

    bsend[...] = table_grad().astype(BF16).reshape(PARTS, 16, 384)

    def strip(d):
        return lax.rem(lon + d, STRIPS)

    for owner in range(PARTS):
        @pl.when(lon != owner)
        def _():
            pltpu.make_async_remote_copy(
                src_ref=bsend.at[owner],
                dst_ref=brecv.at[lon],
                send_sem=b_send.at[0],
                recv_sem=b_recv.at[0],
                device_id=(owner, lat),
                device_id_type=MESH,
            ).start()

    settle(1)
    seven = brecv.at[pl.ds(0, STRIPS - 1)]

    @pl.when(lon < PARTS)
    def _():
        brecv[lon] = bsend[lon]
        wait_bytes(seven, b_recv.at[0])
        bfin[lon] = jnp.sum(brecv[...].astype(F32), 0).astype(BF16)
        for d in range(1, STRIPS):
            pltpu.make_async_remote_copy(
                src_ref=bfin.at[lon],
                dst_ref=bfin.at[lon],
                send_sem=b_send.at[1],
                recv_sem=b_recv.at[1],
                device_id=(strip(d), lat),
                device_id_type=MESH,
            ).start()

    wait_units(0, a_recv.at[0])
    swap(0).start()

    @pl.when(lon < PARTS)
    def _():
        wait_bytes(bfin.at[pl.ds(0, PARTS - 1)], b_recv.at[1])

    @pl.when(lon >= PARTS)
    def _():
        wait_bytes(bfin, b_recv.at[1])

    tin[...] = dot(bfin[...].reshape(96, 384), unperm_ref[...])
    dtab_ref[...] = jnp.zeros_like(dtab_ref)
    for zp in range(WIN_Z):
        for zq in range(WIN_Z):
            for hp in range(WIN_H):
                j = (zp * WIN_Z + zq) * WIN_H + hp
                first_lane = j * WIN_H * SPAN
                base = first_lane // 128 * 128
                g = zp * WIN_H + hp
                piece = tin[g * 8 : g * 8 + 8, zq * 256 : zq * 256 + 256]
                piece = jnp.concatenate([piece, jnp.zeros((8, 128), F32)], -1)
                moved = pltpu.roll(piece, first_lane - base, axis=1)
                dtab_ref[:, base : base + 384] = dtab_ref[:, base : base + 384] + moved

    wait_units(1, a_recv.at[1])
    swap(1).start()

    for a in range(2):
        for i in range(3):
            exchange(a, i).wait_send()
            give_back(a, i).wait()

    @pl.when(lat == BANDS - 1)
    def _():
        table_copy().wait_send()

    @pl.when(lat == 0)
    def _():
        edge_copy().wait_send()

    for seg in range(2):
        pair(seg).wait_send()
        wait_units(seg, s_send.at[seg])

        @pl.when(mine[seg] < COUNTS[seg])
        def _():
            wait_bytes(others[seg], a_send.at[seg])

        swap(seg).wait()

    @pl.when(lon < PARTS)
    def _():
        wait_bytes(bsend.at[pl.ds(0, PARTS - 1)], b_send.at[0])
        wait_bytes(seven, b_send.at[1])

    @pl.when(lon >= PARTS)
    def _():
        wait_bytes(bsend, b_send.at[0])


def output_kernel(
    gath_ref, gath_att, ret_ref, dtab_ref,
    out_ref, dtok_ref, dln1_ref, dwqkv_ref, dbqkv_ref, dbias_ref, dwproj_ref, dln2_ref,
    dwfc1_ref, dbfc1_ref, dwfc2_ref,
    stage,
):
    for a, dst in enumerate((out_ref, dtok_ref)):
        stage[...] = ret_ref[a].reshape(4 * SLOT, C).astype(F32)
        for h in range(WIN_H):
            for w in range(WIN_W):
                dst[h, w] = stage[slot_rows(h, w), :].astype(BF16)
    for n in range(3):
        cols = slice(256 * n, 256 * (n + 1))
        rows = slice(12 * n, 12 * (n + 1))
        dwfc1_ref[:, cols] = gath_ref[0, rows].reshape(C, 256).astype(F32)
        dwfc2_ref[:, cols] = gath_ref[1, rows].reshape(C, 256).astype(F32)
    for k in range(2):
        dwproj_ref[96 * k : 96 * (k + 1), :] = (
            gath_ref[k, 36:42].reshape(96, 256)[:, 0:C].astype(F32)
        )
        for n in range(2):
            cols = slice(256 * k + 128 * n, 256 * k + 128 * (n + 1))
            dwqkv_ref[:, cols] = gath_att[k, 12 * n : 12 * (n + 1)].reshape(C, 128).astype(F32)
        edge = gath_att[k, 24:27].reshape(48, 128).astype(F32)
        for n in range(2):
            at = 96 * n + 48 * k
            dwqkv_ref[at : at + 48, 512:576] = edge[:, 64 * n : 64 * (n + 1)]
    vec = gath_ref[0, 42].astype(F32)
    dbfc1_ref[...] = jnp.concatenate([vec[n : n + 1] for n in range(3)], -1).reshape(HID)
    dln2_ref[...] = vec[3:4, :C].reshape(C)
    vec = gath_att[0, 27].astype(F32)
    sums = [
        jnp.concatenate([vec[2 * n : 2 * n + 1], vec[2 * n + 1 : 2 * n + 2, :64]], -1)
        for n in range(4)
    ]
    dbqkv_ref[...] = jnp.concatenate(sums[:3], -1).reshape(3 * C)
    dln1_ref[...] = sums[3].reshape(C)
    for head in range(HEADS):
        dbias_ref[0, head] = dtab_ref[head : head + 1, 0:NREL]


def per_device(
    tokens, cotangent, ln1_gain, w_qkv, b_qkv, bias_table, w_proj, ln2_gain, w_fc1, b_fc1, w_fc2
):
    vmem = pl.BlockSpec(memory_space=pltpu.VMEM)
    order = window_order()
    perm = table_order()
    dma = pltpu.SemaphoreType.DMA
    args = (
        tokens.transpose(1, 2, 0, 3), cotangent.transpose(1, 2, 0, 3), ln1_gain, w_qkv, b_qkv,
        bias_table.transpose(0, 2, 1, 3), w_proj, ln2_gain, w_fc1, b_fc1, w_fc2.T,
        jnp.asarray(order, BF16), jnp.asarray(order.T, BF16),
        jnp.asarray(perm, BF16), jnp.asarray(perm.T, BF16),
        jnp.asarray(cross_pairs()),
    )
    results = pl.pallas_call(
        block_kernel,
        out_shape=(
            jax.ShapeDtypeStruct((2, FC, 16, 256), BF16),
            jax.ShapeDtypeStruct((2, ATT, 16, 128), BF16),
            jax.ShapeDtypeStruct((2, 4, SLOT, C), BF16),
            jax.ShapeDtypeStruct((8, 3456), F32),
        ),
        in_specs=[pl.BlockSpec(memory_space=pl.ANY)] * len(args),
        out_specs=(vmem,) * 4,
        scratch_shapes=[pltpu.VMEM(a.shape, a.dtype) for a in args]
        + [
            pltpu.VMEM((4 * SLOT, C), F32),
            pltpu.VMEM((2, 4, SLOT, C), BF16),
            pltpu.VMEM((2, 4, SLOT, C), BF16),
            pltpu.VMEM((2, 4, SLOT, C), BF16),
            pltpu.VMEM((8, 3456), F32),
            pltpu.VMEM((8, 3456), F32),
            pltpu.VMEM((96, 512), F32),
            pltpu.VMEM((3, 128, 128), F32),
            pltpu.VMEM((HEADS, T, T), F32),
            pltpu.VMEM((HEADS, T, T), F32),
            pltpu.VMEM((HEADS, T, T), BF16),
            pltpu.VMEM((HEADS, 160, 384), F32),
            pltpu.VMEM((3, 128, 128), F32),
            pltpu.VMEM((16, 256), F32),
            pltpu.VMEM((PARTS, 16, 384), BF16),
            pltpu.VMEM((STRIPS, 16, 384), BF16),
            pltpu.VMEM((PARTS, 16, 384), BF16),
            pltpu.VMEM((96, 384), BF16),
            pltpu.VMEM((96, 384), BF16),
            pltpu.VMEM((2, FC, 16, 256), BF16),
            pltpu.VMEM((2, ATT, 16, 128), BF16),
            pltpu.VMEM((FC, 16, 256), BF16),
            pltpu.VMEM((ATT, 16, 128), BF16),
            pltpu.VMEM((CHIPS, WIDE, 16, 256), BF16),
            pltpu.VMEM((CHIPS, 16, 128), BF16),
            dma((len(args),)),
            dma((2, 3)), dma((2, 3)), dma((2, 3)), dma((2, 3)),
            dma((2,)), dma((2,)), dma((2,)), dma((2,)),
            dma((2,)), dma((2,)), dma((2,)), dma((2,)),
            dma((2,)), dma((2,)), dma((2,)), dma((2,)),
        ],
        compiler_params=pltpu.CompilerParams(
            collective_id=0, has_side_effects=True, vmem_limit_bytes=VMEM_LIMIT
        ),
    )(*args)
    shape = jax.ShapeDtypeStruct
    grid_shape = (WIN_H, WIN_W, WIN_Z, C)
    outs = pl.pallas_call(
        output_kernel,
        out_shape=(
            shape(grid_shape, BF16), shape(grid_shape, BF16),
            shape((C,), F32), shape((C, 3 * C), F32), shape((3 * C,), F32),
            shape((1, HEADS, 1, NREL), F32), shape((C, C), F32), shape((C,), F32),
            shape((C, HID), F32), shape((HID,), F32), shape((C, HID), F32),
        ),
        in_specs=[vmem] * 4,
        out_specs=(vmem,) * 11,
        scratch_shapes=[pltpu.VMEM((4 * SLOT, C), F32)],
        compiler_params=pltpu.CompilerParams(vmem_limit_bytes=VMEM_LIMIT),
    )(*results)
    out, d_tok, d_ln1, d_wqkv, d_bqkv, d_bias, d_wproj, d_ln2, d_wfc1, d_bfc1, d_wfc2 = outs
    return (
        out.transpose(2, 0, 1, 3), d_tok.transpose(2, 0, 1, 3), d_ln1, d_wqkv, d_bqkv,
        d_bias.transpose(0, 2, 1, 3), d_wproj, d_ln2, d_wfc1, d_bfc1, d_wfc2.T,
    )


def solution(mesh):
    grid = P(None, "lat", "lon", None)
    rows = P(None, "lat", None, None)
    return jax.shard_map(
        per_device,
        mesh=mesh,
        in_specs=(grid, grid, P(), P(), P(), rows, P(), P(), P(), P(), P()),
        out_specs=(grid, grid, P(), P(), P(), rows, P(), P(), P(), P(), P()),
        check_vma=False,
    )
```

```python
import jax
import jax.numpy as jnp
import numpy as np
from jax import lax
from jax.experimental import pallas as pl
from jax.experimental.pallas import tpu as pltpu
from jax.sharding import PartitionSpec as P

HEADS = 6
WIN_Z = 2
WIN_H = 6
WIN_W = 12
SPAN = 2 * WIN_W - 1
GROUPS = WIN_Z * WIN_H
T = GROUPS * WIN_W
C = 192
HID = 768
HEAD = C // HEADS
NREL = GROUPS * GROUPS * SPAN
SLOT = 48
FC = 43
ATT = 14
UNITS = FC + ATT
CHIPS = 64
BANDS = 16
STRIPS = 8
PARTS = 6
EPSILON = 1e-05
VMEM_LIMIT = 48 * 1024 * 1024
FACTOR = HEAD ** (-0.5)
F32 = jnp.float32
BF16 = jnp.bfloat16
MESH = pl.DeviceIdType.MESH


def window_order():
    grid = np.zeros((T, 4 * SLOT), np.float32)
    for w in range(WIN_W):
        for z in range(WIN_Z):
            for h in range(WIN_H):
                slot = (h // 3) * 2 + w // 6
                grid[w * GROUPS + z * WIN_H + h, slot * SLOT + (h % 3) * 12 + (w % 6) * 2 + z] = 1
    return grid


def table_order():
    grid = np.zeros((512, 384), np.float32)
    for z in range(WIN_Z):
        for h in range(WIN_H):
            for i in range(SPAN):
                grid[z * 256 + h * SPAN + i, (SPAN - 1 - i) * GROUPS + z * WIN_H + h] = 1
    return grid


def cross_pairs():
    g = np.arange(96)[:, None] // 8 % WIN_H
    q = np.arange(384)[None, :] % GROUPS % WIN_H
    return np.where((g < 3) != (q < 3), -1e30, 0.0).astype(np.float32)


def dot(a, b):
    return jnp.dot(a, b, preferred_element_type=F32)


def dot_nt(a, b):
    return lax.dot_general(a, b, (((1,), (1,)), ((), ())), preferred_element_type=F32)


def dot_tn(a, b):
    return lax.dot_general(a, b, (((0,), (0,)), ((), ())), preferred_element_type=F32)


def normalize(values, gain):
    average = jnp.mean(values, -1, keepdims=True)
    centered = values - average
    inv = lax.rsqrt(jnp.mean(centered * centered, -1, keepdims=True) + EPSILON)
    hat = centered * inv
    return hat * gain, hat, inv


def norm_back(hat, inv, gain, grad):
    scaled = grad * gain
    return inv * (
        scaled
        - jnp.mean(scaled, -1, keepdims=True)
        - hat * jnp.mean(scaled * hat, -1, keepdims=True)
    )


def slot_rows(h, w):
    at = ((h // 3) * 2 + w // 6) * SLOT + (h % 3) * 12 + (w % 6) * 2
    return slice(at, at + 2)


def block_kernel(
    tok_any, cot_any, g1_any, wqkv_any, bqkv_any, table_any, wproj_any, g2_any, wfc1_any,
    bfc1_any, wfc2_any, order_any, back_any, perm_any, cross_any,
    parts, ret_ref, bsend, bbs,
    tok_ref, cot_ref, g1_ref, wqkv_ref, bqkv_ref, table_ref, wproj_ref, g2_ref, wfc1_ref,
    bfc1_ref, wfc2_ref, order_ref, back_ref, perm_ref, cross_ref,
    stage, send, arrive, out_stage,
    tabw, tab15, tin, ymat, bias, prob, plow, dsc, dmat, vec,
    in_sem,
    ex_send, ex_recv, rt_send, rt_recv, one_send, one_recv,
):
    places = (
        (table_any, table_ref), (tok_any, tok_ref), (perm_any, perm_ref), (cot_any, cot_ref),
        (cross_any, cross_ref), (order_any, order_ref), (g1_any, g1_ref), (wqkv_any, wqkv_ref),
        (bqkv_any, bqkv_ref), (wproj_any, wproj_ref), (g2_any, g2_ref), (wfc1_any, wfc1_ref),
        (bfc1_any, bfc1_ref), (wfc2_any, wfc2_ref), (back_any, back_ref),
    )
    loads = [pltpu.make_async_copy(src, dst, in_sem.at[n]) for n, (src, dst) in enumerate(places)]
    for load in loads:
        load.start()
    lon = lax.axis_index("lon")
    lat = lax.axis_index("lat")
    east = lax.rem(lon + 1, STRIPS)
    west = lax.rem(lon + STRIPS - 1, STRIPS)
    south = lax.rem(lat + 1, BANDS)
    north = lax.rem(lat + BANDS - 1, BANDS)
    ahead = ((east, lat), (lon, south), (east, south))
    behind = ((west, lat), (lon, north), (west, north))
    barrier = pltpu.get_barrier_semaphore()
    for target in ahead + behind:
        pl.semaphore_signal(barrier, inc=1, device_id=target, device_id_type=MESH)

    stage[...] = jnp.zeros_like(stage)

    def quadrants(a, src):
        loads[(1, 3)[a]].wait()
        for h in range(WIN_H):
            for w in range(WIN_W):
                stage[slot_rows(h, w), :] = src[h, w].astype(F32)
        send[a] = stage[...].astype(BF16).reshape(4, SLOT, C)
        arrive[a, 3] = send[a, 0]

    quadrants(0, tok_ref)
    pl.semaphore_wait(barrier, 6)

    def exchange(a, i):
        return pltpu.make_async_remote_copy(
            src_ref=send.at[a, i + 1],
            dst_ref=arrive.at[a, 2 - i],
            send_sem=ex_send.at[a, i],
            recv_sem=ex_recv.at[a, i],
            device_id=ahead[i],
            device_id_type=MESH,
        )

    def table_copy():
        return pltpu.make_async_remote_copy(
            src_ref=tabw,
            dst_ref=tab15,
            send_sem=one_send,
            recv_sem=one_recv,
            device_id=(lon, south),
            device_id_type=MESH,
        )

    for i in range(3):
        exchange(0, i).start()

    tabw[...] = jnp.zeros_like(tabw)
    loads[0].wait()
    for head in range(HEADS):
        tabw[head : head + 1, 0:NREL] = table_ref[0, head]

    @pl.when(lat == BANDS - 1)
    def _():
        table_copy().start()

    quadrants(1, cot_ref)
    for i in range(3):
        exchange(1, i).start()

    tin[...] = jnp.zeros_like(tin)

    def spread(src, zp, zq, hp, width):
        j = (zp * WIN_Z + zq) * WIN_H + hp
        first = j * WIN_H * SPAN
        base = first // 128 * 128
        wide = src[:, base : base + 384]
        moved = pltpu.roll(wide, (384 - (first - base)) % 384, axis=1)
        g = zp * WIN_H + hp
        tin[g * 8 : g * 8 + 8, zq * 256 : zq * 256 + width] = moved[:, :width]

    for zp in range(WIN_Z):
        for zq in range(WIN_Z):
            for hp in range(WIN_H):
                spread(tabw, zp, zq, hp, WIN_H * SPAN)

    @pl.when(lat == 0)
    def _():
        table_copy().wait_recv()
        for zp in range(WIN_Z):
            for zq in range(WIN_Z):
                for hp in range(3):
                    spread(tab15, zp, zq, hp, 3 * SPAN)

    whole = tin[...]
    high = whole.astype(BF16)
    rest = whole - high.astype(F32)
    middle = rest.astype(BF16)
    low = (rest - middle.astype(F32)).astype(BF16)
    loads[2].wait()
    perm = perm_ref[...]
    spread_rows = dot(high, perm) + dot(middle, perm) + dot(low, perm)
    for n in range(3):
        ymat[n, 0:96, :] = spread_rows[:, 128 * n : 128 * (n + 1)]
        ymat[n, 96:128, :] = jnp.zeros((32, 128), F32)
    loads[4].wait()

    @pl.when(lat == 0)
    def _():
        for n in range(3):
            ymat[n, 0:96, :] = ymat[n, 0:96, :] + cross_ref[:, 128 * n : 128 * (n + 1)]

    for head in range(HEADS):
        rows = jnp.concatenate(
            [ymat[n, pl.ds(head, 16, stride=8), :] for n in range(3)], -1
        )
        for w in range(WIN_W):
            moved = pltpu.roll(rows, (384 - (WIN_W - 1 - w) * GROUPS) % 384, axis=1)
            bias[head, w * GROUPS : (w + 1) * GROUPS, :] = moved[:GROUPS, :T]

    for n in range(5, 15):
        loads[n].wait()
    lane = lax.broadcasted_iota(jnp.int32, (T, C), 1)
    masks = [(lane >= HEAD * i) & (lane < HEAD * (i + 1)) for i in range(HEADS)]
    ones = [jnp.where(mask[0:16], 1.0, 0.0).astype(BF16)[0:1] for mask in masks]
    order = order_ref[...]
    back = back_ref[...]
    gain1 = g1_ref[...].reshape(1, C)
    gain2 = g2_ref[...].reshape(1, C)

    def arrived(a):
        for i in range(3):
            exchange(a, i).wait_recv()
        return dot(order, arrive[a].reshape(4 * SLOT, C))

    tokens = arrived(0)
    normed, hat1, inv1 = normalize(tokens, gain1)
    first = normed.astype(BF16)
    qkv = (dot(first, wqkv_ref[...]) + bqkv_ref[...].reshape(1, 3 * C)).astype(BF16)
    queries = qkv[:, 0:C]
    keys = qkv[:, C : 2 * C]
    values = qkv[:, 2 * C : 3 * C]
    queries_t = queries.T
    mixed = jnp.zeros((T, C), F32)
    for head in range(HEADS):
        q = queries * ones[head]
        scores = dot_nt(q, keys) * FACTOR + bias[head]
        top = jnp.max(scores, -1, keepdims=True)
        raised = jnp.exp(scores - top)
        probs = raised * (1.0 / jnp.sum(raised, -1, keepdims=True))
        prob[head] = probs
        probs_low = probs.astype(BF16)
        plow[head] = probs_low
        mixed = jnp.where(masks[head], dot(probs_low, values), mixed)
    mixed = mixed.astype(BF16)
    inner = tokens + dot(mixed, wproj_ref[...]).astype(BF16).astype(F32)

    cot = arrived(1)
    cot_low = cot.astype(BF16)
    normed, hat2, inv2 = normalize(inner, gain2)
    second = normed.astype(BF16)
    second_t = second.T
    cot_t = cot_low.T
    total = inner
    grad_second = jnp.zeros((T, C), F32)
    bfc1 = bfc1_ref[...].reshape(1, HID)
    vec[...] = jnp.zeros_like(vec)
    for n in range(3):
        cols = slice(256 * n, 256 * (n + 1))
        pre = dot(second, wfc1_ref[:, cols]) + bfc1[:, cols]
        cdf = 0.5 * (1.0 + lax.erf(pre * 0.7071067811865476))
        density = jnp.exp(-0.5 * pre * pre) * 0.3989422804014327
        act = (pre * cdf).astype(BF16)
        total = total + dot_nt(act, wfc2_ref[:, cols])
        grad_pre = (dot(cot_low, wfc2_ref[:, cols]) * (cdf + pre * density)).astype(BF16)
        grad_second = grad_second + dot_nt(grad_pre, wfc1_ref[:, cols])
        parts[0, 12 * n : 12 * (n + 1)] = dot(second_t, grad_pre).astype(BF16).reshape(12, 16, 256)
        parts[1, 12 * n : 12 * (n + 1)] = dot(cot_t, act).astype(BF16).reshape(12, 16, 256)
        vec[n : n + 1, :] = jnp.sum(grad_pre.astype(F32), 0, keepdims=True)

    def give_back(a, i):
        return pltpu.make_async_remote_copy(
            src_ref=out_stage.at[a, 2 - i],
            dst_ref=ret_ref.at[a, i + 1],
            send_sem=rt_send.at[a, i],
            recv_sem=rt_recv.at[a, i],
            device_id=behind[i],
            device_id_type=MESH,
        )

    def hand_out(a, field):
        out_stage[a] = dot(back, field).astype(BF16).reshape(4, SLOT, C)
        for i in range(3):
            give_back(a, i).start()
        ret_ref[a, 0] = out_stage[a, 3]

    grad_inner = cot + norm_back(hat2, inv2, gain2, grad_second)
    grad_att = grad_inner.astype(BF16)
    proj_grad = dot_tn(mixed, grad_att).astype(BF16)
    proj_grad = jnp.concatenate([proj_grad, jnp.zeros((C, 64), BF16)], -1).reshape(12, 16, 256)
    parts[0, 36:42] = proj_grad[:6]
    parts[1, 36:42] = proj_grad[6:]
    vec[3:4, 0:C] = jnp.sum(grad_second * hat2, 0, keepdims=True)
    parts[0, 42] = vec[...].astype(BF16)
    parts[1, 42] = jnp.zeros((16, 256), BF16)
    hand_out(0, total.astype(BF16))

    grad_mixed = dot_nt(grad_att, wproj_ref[...]).astype(BF16)
    grad_mixed_t = grad_mixed.T
    dsc[...] = jnp.zeros_like(dsc)
    grad_q = jnp.zeros((T, C), F32)
    grad_k_t = []
    grad_v_t = []
    for head in range(HEADS):
        rows = slice(HEAD * head, HEAD * (head + 1))
        gm = grad_mixed * ones[head]
        probs = prob[head]
        grad_probs = dot_nt(gm, values)
        inside = jnp.sum(probs * grad_probs, -1, keepdims=True)
        grad_scores = probs * (grad_probs - inside)
        dsc[head, 0:T, 0:T] = grad_scores
        scaled = (grad_scores * FACTOR).astype(BF16)
        grad_q = jnp.where(masks[head], dot(scaled, keys), grad_q)
        grad_k_t.append(dot(queries_t[rows], scaled))
        grad_v_t.append(dot(grad_mixed_t[rows], plow[head]))
    grad_k = jnp.concatenate(grad_k_t, 0).T
    grad_v = jnp.concatenate(grad_v_t, 0).T

    grad_qkv = jnp.concatenate([grad_q, grad_k, grad_v], -1).astype(BF16)
    wide = dot_tn(first, grad_qkv).astype(BF16)
    edge = [wide[48 * n : 48 * (n + 1), 512:576] for n in range(4)]
    parts[0, FC : FC + 12] = wide[:, 0:256].reshape(12, 16, 256)
    parts[1, FC : FC + 12] = wide[:, 256:512].reshape(12, 16, 256)
    edge = jnp.concatenate(edge, -1).reshape(3, 16, 256)
    parts[0, FC + 12] = edge[0]
    parts[1, FC + 12 : FC + 14] = edge[1:]
    grad_first = dot_nt(grad_qkv, wqkv_ref[...]).astype(BF16).astype(F32)
    vec[...] = jnp.zeros_like(vec)
    sums = jnp.sum(grad_qkv.astype(F32), 0, keepdims=True)
    for n in range(3):
        vec[n : n + 1, 0:C] = sums[:, C * n : C * (n + 1)]
    vec[3:4, 0:C] = jnp.sum(grad_first * hat1, 0, keepdims=True)
    parts[0, FC + 13] = vec[...].astype(BF16)
    d_tokens = grad_inner + norm_back(hat1, inv1, gain1, grad_first)
    hand_out(1, d_tokens.astype(BF16))

    dmat[...] = jnp.zeros_like(dmat)
    for head in range(HEADS):
        acc = jnp.zeros((16, 384), F32)
        for w in range(WIN_W):
            acc = acc + pltpu.roll(
                dsc[head, w * GROUPS : w * GROUPS + 16, :], (WIN_W - 1 - w) * GROUPS, axis=1
            )
        for n in range(3):
            dmat[n, pl.ds(head, 16, stride=8), :] = acc[:, 128 * n : 128 * (n + 1)]

    def table_grad():
        return jnp.concatenate([dmat[n, 0:96, :] for n in range(3)], -1)

    def keep_table(field):
        for n in range(3):
            dmat[n, 0:96, :] = field[:, 128 * n : 128 * (n + 1)]

    @pl.when(lat == 0)
    def _():
        row = lax.broadcasted_iota(jnp.int32, (96, 384), 0)
        upper = (row < 24) | ((row >= 48) & (row < 72))
        full = table_grad()
        bbs[...] = jnp.where(upper, full, 0.0).astype(BF16)
        keep_table(jnp.where(upper, 0.0, full))

    bsend[...] = table_grad().reshape(PARTS, 16, 384)

    for a in range(2):
        for i in range(3):
            exchange(a, i).wait_send()
            give_back(a, i).wait()

    @pl.when(lat == BANDS - 1)
    def _():
        table_copy().wait_send()


def reduce_kernel(
    parts_ref, btab_ref, bbs, unperm_ref,
    gath, dtab_ref,
    parts, core_in, rs_in, tin, bsend, brecv, bfin, bbr,
    edge_send, edge_recv, c_send, c_recv, s_send, s_recv, a_send, a_recv, d_send, d_recv,
    b_send, b_recv,
):
    lon = lax.axis_index("lon")
    lat = lax.axis_index("lat")
    core = lax.rem(lat, 2)
    other = 1 - core
    pair_row = lat // 2
    chip = lon * 8 + pair_row
    south = lax.rem(lat + 1, BANDS)
    north = lax.rem(lat + BANDS - 1, BANDS)
    sibling = (lon, lat - core + other)
    pair_rows = [lax.rem(pair_row + d, 8) for d in range(8)]

    def to_chips(act):
        def strip_step(step, carry):
            at = lax.rem(lon + step, STRIPS)
            for n, row in enumerate(pair_rows):
                if n:
                    act((at, row * 2 + core), at * 8 + row)
                else:
                    @pl.when(step > 0)
                    def _():
                        act((at, row * 2 + core), at * 8 + row)

            return carry

        lax.fori_loop(0, STRIPS, strip_step, 0)

    def unit_of(at):
        return lax.rem(at + CHIPS - 32 * core, CHIPS)

    mine = unit_of(chip)
    owner = mine < UNITS

    barrier = pltpu.get_barrier_semaphore()

    def greet(target, at=None):
        pl.semaphore_signal(barrier, inc=1, device_id=target, device_id_type=MESH)

    for target in (sibling, (lon, south), (lon, north)):
        greet(target)
    to_chips(greet)
    parts[...] = parts_ref[core]
    pl.semaphore_wait(barrier, CHIPS + 2)

    def remote(src, dst, send, recv, target):
        return pltpu.make_async_remote_copy(
            src_ref=src, dst_ref=dst, send_sem=send, recv_sem=recv,
            device_id=target, device_id_type=MESH,
        )

    def wait_bytes(ref, sem):
        pltpu.make_async_copy(ref, ref, sem).wait()

    pair = remote(parts_ref.at[other], core_in, c_send, c_recv, sibling)
    pair.start()

    edge = remote(bbs, bbr, edge_send, edge_recv, (lon, north))

    @pl.when(lat == 0)
    def _():
        edge.start()

    @pl.when(lat == BANDS - 1)
    def _():
        edge.wait_recv()
        bsend[...] = (
            btab_ref[...] + bbr[...].astype(F32).reshape(PARTS, 16, 384)
        ).astype(BF16)

    @pl.when(lat != BANDS - 1)
    def _():
        bsend[...] = btab_ref[...].astype(BF16)

    def strip(d):
        return lax.rem(lon + d, STRIPS)

    for d in range(1, STRIPS):
        @pl.when(strip(d) < PARTS)
        def _():
            remote(
                bsend.at[strip(d)], brecv.at[lon], b_send.at[0], b_recv.at[0], (strip(d), lat)
            ).start()

    pair.wait_recv()
    parts[...] = (parts[...].astype(F32) + core_in[...].astype(F32)).astype(BF16)

    def scatter(target, at):
        unit = unit_of(at)

        @pl.when(unit < UNITS)
        def _():
            remote(parts.at[unit], rs_in.at[chip], s_send, s_recv, target).start()

    to_chips(scatter)
    seven = brecv.at[pl.ds(0, STRIPS - 1)]

    @pl.when(lon < PARTS)
    def _():
        brecv[lon] = bsend[lon]
        wait_bytes(seven, b_recv.at[0])
        bfin[lon] = jnp.sum(brecv[...].astype(F32), 0).astype(BF16)
        for d in range(1, STRIPS):
            remote(
                bfin.at[lon], bfin.at[lon], b_send.at[1], b_recv.at[1], (strip(d), lat)
            ).start()

    others = rs_in.at[pl.ds(0, CHIPS - 1)]

    @pl.when(owner)
    def _():
        rs_in[chip] = parts[mine]
        wait_bytes(others, s_recv)
        gath[core, mine] = jnp.sum(rs_in[...].astype(F32), 0).astype(BF16)

        def push(target, at):
            unit = gath.at[core, mine]
            remote(unit, unit, a_send, a_recv, target).start()

        to_chips(push)

    @pl.when(lon < PARTS)
    def _():
        wait_bytes(bfin.at[pl.ds(0, PARTS - 1)], b_recv.at[1])

    @pl.when(lon >= PARTS)
    def _():
        wait_bytes(bfin, b_recv.at[1])

    tin[...] = dot(bfin[...].reshape(96, 384), unperm_ref[...])
    dtab_ref[...] = jnp.zeros_like(dtab_ref)
    for zp in range(WIN_Z):
        for zq in range(WIN_Z):
            for hp in range(WIN_H):
                j = (zp * WIN_Z + zq) * WIN_H + hp
                first_lane = j * WIN_H * SPAN
                base = first_lane // 128 * 128
                g = zp * WIN_H + hp
                piece = tin[g * 8 : g * 8 + 8, zq * 256 : zq * 256 + 256]
                piece = jnp.concatenate([piece, jnp.zeros((8, 128), F32)], -1)
                moved = pltpu.roll(piece, first_lane - base, axis=1)
                dtab_ref[:, base : base + 384] = dtab_ref[:, base : base + 384] + moved

    def wait_units(sem):
        @pl.when(owner)
        def _():
            wait_bytes(parts.at[pl.ds(0, UNITS - 1)], sem)

        @pl.when(jnp.logical_not(owner))
        def _():
            wait_bytes(parts, sem)

    wait_units(a_recv)
    swap = remote(gath.at[core], gath.at[core], d_send, d_recv, sibling)
    swap.start()

    pair.wait_send()
    wait_units(s_send)

    @pl.when(owner)
    def _():
        wait_bytes(others, a_send)

    @pl.when(lat == 0)
    def _():
        edge.wait_send()

    @pl.when(lon < PARTS)
    def _():
        wait_bytes(bsend.at[pl.ds(0, PARTS - 1)], b_send.at[0])
        wait_bytes(seven, b_send.at[1])

    @pl.when(lon >= PARTS)
    def _():
        wait_bytes(bsend, b_send.at[0])

    swap.wait()


def output_kernel(
    gath_ref, ret_ref, dtab_ref,
    out_ref, dtok_ref, dln1_ref, dwqkv_ref, dbqkv_ref, dbias_ref, dwproj_ref, dln2_ref,
    dwfc1_ref, dbfc1_ref, dwfc2_ref,
    stage,
):
    for a, dst in enumerate((out_ref, dtok_ref)):
        stage[...] = ret_ref[a].reshape(4 * SLOT, C).astype(F32)
        for h in range(WIN_H):
            for w in range(WIN_W):
                dst[h, w] = stage[slot_rows(h, w), :].astype(BF16)
    for n in range(3):
        cols = slice(256 * n, 256 * (n + 1))
        rows = slice(12 * n, 12 * (n + 1))
        dwfc1_ref[:, cols] = gath_ref[0, rows].reshape(C, 256).astype(F32)
        dwfc2_ref[:, cols] = gath_ref[1, rows].reshape(C, 256).astype(F32)
    for k in range(2):
        dwproj_ref[96 * k : 96 * (k + 1), :] = (
            gath_ref[k, 36:42].reshape(96, 256)[:, 0:C].astype(F32)
        )
        dwqkv_ref[:, 256 * k : 256 * (k + 1)] = (
            gath_ref[k, FC : FC + 12].reshape(C, 256).astype(F32)
        )
    for n, edge in enumerate((gath_ref[0, FC + 12], gath_ref[1, FC + 12], gath_ref[1, FC + 13])):
        edge = edge.astype(F32)
        for k in range(4):
            at = 48 * k + 16 * n
            dwqkv_ref[at : at + 16, 512:576] = edge[:, 64 * k : 64 * (k + 1)]
    vec = gath_ref[0, 42].astype(F32)
    dbfc1_ref[...] = jnp.concatenate([vec[n : n + 1] for n in range(3)], -1).reshape(HID)
    dln2_ref[...] = vec[3:4, :C].reshape(C)
    vec = gath_ref[0, FC + 13].astype(F32)
    dbqkv_ref[...] = jnp.concatenate([vec[n : n + 1, :C] for n in range(3)], -1).reshape(3 * C)
    dln1_ref[...] = vec[3:4, :C].reshape(C)
    for head in range(HEADS):
        dbias_ref[0, head] = dtab_ref[head : head + 1, 0:NREL]


def per_device(
    tokens, cotangent, ln1_gain, w_qkv, b_qkv, bias_table, w_proj, ln2_gain, w_fc1, b_fc1, w_fc2
):
    vmem = pl.BlockSpec(memory_space=pltpu.VMEM)
    order = window_order()
    perm = table_order()
    dma = pltpu.SemaphoreType.DMA
    args = (
        tokens.transpose(1, 2, 0, 3), cotangent.transpose(1, 2, 0, 3), ln1_gain, w_qkv, b_qkv,
        bias_table.transpose(0, 2, 1, 3), w_proj, ln2_gain, w_fc1, b_fc1, w_fc2.T,
        jnp.asarray(order, BF16), jnp.asarray(order.T, BF16),
        jnp.asarray(perm, BF16),
        jnp.asarray(cross_pairs()),
    )
    shape = jax.ShapeDtypeStruct
    parts, returned, table_grad, edge_grad = pl.pallas_call(
        block_kernel,
        out_shape=(
            shape((2, UNITS, 16, 256), BF16),
            shape((2, 4, SLOT, C), BF16),
            shape((PARTS, 16, 384), F32),
            shape((96, 384), BF16),
        ),
        in_specs=[pl.BlockSpec(memory_space=pl.ANY)] * len(args),
        out_specs=(vmem,) * 4,
        scratch_shapes=[pltpu.VMEM(a.shape, a.dtype) for a in args]
        + [
            pltpu.VMEM((4 * SLOT, C), F32),
            pltpu.VMEM((2, 4, SLOT, C), BF16),
            pltpu.VMEM((2, 4, SLOT, C), BF16),
            pltpu.VMEM((2, 4, SLOT, C), BF16),
            pltpu.VMEM((8, 3456), F32),
            pltpu.VMEM((8, 3456), F32),
            pltpu.VMEM((96, 512), F32),
            pltpu.VMEM((3, 128, 128), F32),
            pltpu.VMEM((HEADS, T, T), F32),
            pltpu.VMEM((HEADS, T, T), F32),
            pltpu.VMEM((HEADS, T, T), BF16),
            pltpu.VMEM((HEADS, 160, 384), F32),
            pltpu.VMEM((3, 128, 128), F32),
            pltpu.VMEM((16, 256), F32),
            dma((len(args),)),
            dma((2, 3)), dma((2, 3)), dma((2, 3)), dma((2, 3)), dma, dma,
        ],
        compiler_params=pltpu.CompilerParams(
            collective_id=0, has_side_effects=True, vmem_limit_bytes=VMEM_LIMIT
        ),
    )(*args)
    gathered, table = pl.pallas_call(
        reduce_kernel,
        out_shape=(shape((2, UNITS, 16, 256), BF16), shape((8, 3456), F32)),
        in_specs=[vmem] * 4,
        out_specs=(vmem,) * 2,
        scratch_shapes=[
            pltpu.VMEM((UNITS, 16, 256), BF16),
            pltpu.VMEM((UNITS, 16, 256), BF16),
            pltpu.VMEM((CHIPS, 16, 256), BF16),
            pltpu.VMEM((96, 512), F32),
            pltpu.VMEM((PARTS, 16, 384), BF16),
            pltpu.VMEM((STRIPS, 16, 384), BF16),
            pltpu.VMEM((PARTS, 16, 384), BF16),
            pltpu.VMEM((96, 384), BF16),
        ]
        + [dma] * 10
        + [dma((2,)), dma((2,))],
        compiler_params=pltpu.CompilerParams(
            collective_id=1, has_side_effects=True, vmem_limit_bytes=VMEM_LIMIT
        ),
    )(parts, table_grad, edge_grad, jnp.asarray(perm.T, BF16))
    grid_shape = (WIN_H, WIN_W, WIN_Z, C)
    outs = pl.pallas_call(
        output_kernel,
        out_shape=(
            shape(grid_shape, BF16), shape(grid_shape, BF16),
            shape((C,), F32), shape((C, 3 * C), F32), shape((3 * C,), F32),
            shape((1, HEADS, 1, NREL), F32), shape((C, C), F32), shape((C,), F32),
            shape((C, HID), F32), shape((HID,), F32), shape((C, HID), F32),
        ),
        in_specs=[vmem] * 3,
        out_specs=(vmem,) * 11,
        scratch_shapes=[pltpu.VMEM((4 * SLOT, C), F32)],
        compiler_params=pltpu.CompilerParams(vmem_limit_bytes=VMEM_LIMIT),
    )(gathered, returned, table)
    out, d_tok, d_ln1, d_wqkv, d_bqkv, d_bias, d_wproj, d_ln2, d_wfc1, d_bfc1, d_wfc2 = outs
    return (
        out.transpose(2, 0, 1, 3), d_tok.transpose(2, 0, 1, 3), d_ln1, d_wqkv, d_bqkv,
        d_bias.transpose(0, 2, 1, 3), d_wproj, d_ln2, d_wfc1, d_bfc1, d_wfc2.T,
    )


def solution(mesh):
    grid = P(None, "lat", "lon", None)
    rows = P(None, "lat", None, None)
    return jax.shard_map(
        per_device,
        mesh=mesh,
        in_specs=(grid, grid, P(), P(), P(), rows, P(), P(), P(), P(), P()),
        out_specs=(grid, grid, P(), P(), P(), rows, P(), P(), P(), P(), P()),
        check_vma=False,
    )
```

```python
import jax
import jax.numpy as jnp
import numpy as np
from jax import lax
from jax.experimental import pallas as pl
from jax.experimental.pallas import tpu as pltpu
from jax.sharding import PartitionSpec as P

HEADS = 6
WIN_Z = 2
WIN_H = 6
WIN_W = 12
SPAN = 2 * WIN_W - 1
GROUPS = WIN_Z * WIN_H
T = GROUPS * WIN_W
C = 192
HID = 768
HEAD = C // HEADS
NREL = GROUPS * GROUPS * SPAN
SLOT = 48
FC = 48
ATT = 32
ROWS = 8
BANDS = 16
STRIPS = 8
PARTS = 6
EPSILON = 1e-05
VMEM_LIMIT = 56 * 1024 * 1024
FACTOR = HEAD ** (-0.5)
F32 = jnp.float32
BF16 = jnp.bfloat16
MESH = pl.DeviceIdType.MESH


def window_order():
    grid = np.zeros((T, 4 * SLOT), np.float32)
    for w in range(WIN_W):
        for z in range(WIN_Z):
            for h in range(WIN_H):
                slot = (h // 3) * 2 + w // 6
                grid[w * GROUPS + z * WIN_H + h, slot * SLOT + (h % 3) * 12 + (w % 6) * 2 + z] = 1
    return grid


def table_order():
    grid = np.zeros((512, 384), np.float32)
    for z in range(WIN_Z):
        for h in range(WIN_H):
            for i in range(SPAN):
                grid[z * 256 + h * SPAN + i, (SPAN - 1 - i) * GROUPS + z * WIN_H + h] = 1
    return grid


def cross_pairs():
    g = np.arange(96)[:, None] // 8 % WIN_H
    q = np.arange(384)[None, :] % GROUPS % WIN_H
    return np.where((g < 3) != (q < 3), -1e30, 0.0).astype(np.float32)


def dot(a, b):
    return jnp.dot(a, b, preferred_element_type=F32)


def dot_nt(a, b):
    return lax.dot_general(a, b, (((1,), (1,)), ((), ())), preferred_element_type=F32)


def dot_tn(a, b):
    return lax.dot_general(a, b, (((0,), (0,)), ((), ())), preferred_element_type=F32)


def normalize(values, gain):
    average = jnp.mean(values, -1, keepdims=True)
    centered = values - average
    inv = lax.rsqrt(jnp.mean(centered * centered, -1, keepdims=True) + EPSILON)
    hat = centered * inv
    return hat * gain, hat, inv


def norm_back(hat, inv, gain, grad):
    scaled = grad * gain
    return inv * (
        scaled
        - jnp.mean(scaled, -1, keepdims=True)
        - hat * jnp.mean(scaled * hat, -1, keepdims=True)
    )


def slot_rows(h, w):
    at = ((h // 3) * 2 + w // 6) * SLOT + (h % 3) * 12 + (w % 6) * 2
    return slice(at, at + 2)


def block_kernel(
    tok_any, cot_any, g1_any, wqkv_any, bqkv_any, table_any, wproj_any, g2_any, wfc1_any,
    bfc1_any, wfc2_any, order_any, back_any, perm_any, unperm_any, cross_any,
    gath_fc, gath_att, ret_ref, dtab_ref,
    tok_ref, cot_ref, g1_ref, wqkv_ref, bqkv_ref, table_ref, wproj_ref, g2_ref, wfc1_ref,
    bfc1_ref, wfc2_ref, order_ref, back_ref, perm_ref, unperm_ref, cross_ref,
    stage, send, arrive, out_stage,
    tabw, tab15, tin, ymat, bias, prob, plow, dsc, dmat, vec,
    bsend, brecv, bfin, bbs, bbr,
    parts_fc, parts_att, core_fc, core_att, fold1, sum1, fold2, sum2, fold3, fold_att, sum_att,
    mid_att,
    in_sem,
    ex_send, ex_recv, rt_send, rt_recv, one_send, one_recv, f_send, f_recv,
    a_send, a_recv, b_send, b_recv,
):
    places = (
        (table_any, table_ref), (tok_any, tok_ref), (perm_any, perm_ref), (cot_any, cot_ref),
        (cross_any, cross_ref), (order_any, order_ref), (g1_any, g1_ref), (wqkv_any, wqkv_ref),
        (bqkv_any, bqkv_ref), (wproj_any, wproj_ref), (g2_any, g2_ref), (wfc1_any, wfc1_ref),
        (bfc1_any, bfc1_ref), (wfc2_any, wfc2_ref), (back_any, back_ref),
        (unperm_any, unperm_ref),
    )
    loads = [pltpu.make_async_copy(src, dst, in_sem.at[n]) for n, (src, dst) in enumerate(places)]
    for load in loads:
        load.start()
    lon = lax.axis_index("lon")
    lat = lax.axis_index("lat")
    core = lax.rem(lat, 2)
    other = 1 - core
    pair_row = lat // 2
    east = lax.rem(lon + 1, STRIPS)
    west = lax.rem(lon + STRIPS - 1, STRIPS)
    south = lax.rem(lat + 1, BANDS)
    north = lax.rem(lat + BANDS - 1, BANDS)
    sibling = (lon, lat - core + other)

    spot = (lax.rem(pair_row, 4), lon // 2, lax.rem(lon, 2) * 2 + lat // 8)

    def on_axis(axis, at):
        if axis == 0:
            return (lon, lat // 8 * 8 + at * 2 + core)
        if axis == 1:
            return (at * 2 + lax.rem(lon, 2), lat)
        return (spot[1] * 2 + at // 2, lax.rem(at, 2) * 8 + spot[0] * 2 + core)

    def strip(d):
        return lax.rem(lon + d, STRIPS)

    def row_of(d):
        return lax.rem(pair_row + d, ROWS)

    barrier = pltpu.get_barrier_semaphore()

    def greet(target):
        pl.semaphore_signal(barrier, inc=1, device_id=target, device_id_type=MESH)

    for target in ((lon, south), (lon, north), (east, south), (west, north), sibling):
        greet(target)
    greet(on_axis(2, 3 - spot[2]))
    for d in range(1, 8):
        greet((strip(d), lat))
        greet((lon, row_of(d) * 2 + core))

    stage[...] = jnp.zeros_like(stage)

    def quadrants(a, src):
        loads[(1, 3)[a]].wait()
        for h in range(WIN_H):
            for w in range(WIN_W):
                stage[slot_rows(h, w), :] = src[h, w].astype(F32)
        send[a] = stage[...].astype(BF16).reshape(4, SLOT, C)
        arrive[a, 3] = send[a, 0]

    quadrants(0, tok_ref)
    pl.semaphore_wait(barrier, 20)

    ahead = ((east, lat), (lon, south), (east, south))
    behind = ((west, lat), (lon, north), (west, north))

    def exchange(a, i):
        return pltpu.make_async_remote_copy(
            src_ref=send.at[a, i + 1],
            dst_ref=arrive.at[a, 2 - i],
            send_sem=ex_send.at[a, i],
            recv_sem=ex_recv.at[a, i],
            device_id=ahead[i],
            device_id_type=MESH,
        )

    def table_copy():
        return pltpu.make_async_remote_copy(
            src_ref=tabw,
            dst_ref=tab15,
            send_sem=one_send.at[0],
            recv_sem=one_recv.at[0],
            device_id=(lon, south),
            device_id_type=MESH,
        )

    for i in range(3):
        exchange(0, i).start()

    tabw[...] = jnp.zeros_like(tabw)
    loads[0].wait()
    for head in range(HEADS):
        tabw[head : head + 1, 0:NREL] = table_ref[0, head]

    @pl.when(lat == BANDS - 1)
    def _():
        table_copy().start()

    quadrants(1, cot_ref)
    for i in range(3):
        exchange(1, i).start()

    tin[...] = jnp.zeros_like(tin)

    def spread(src, zp, zq, hp, width):
        j = (zp * WIN_Z + zq) * WIN_H + hp
        first = j * WIN_H * SPAN
        base = first // 128 * 128
        wide = src[:, base : base + 384]
        moved = pltpu.roll(wide, (384 - (first - base)) % 384, axis=1)
        g = zp * WIN_H + hp
        tin[g * 8 : g * 8 + 8, zq * 256 : zq * 256 + width] = moved[:, :width]

    for zp in range(WIN_Z):
        for zq in range(WIN_Z):
            for hp in range(WIN_H):
                spread(tabw, zp, zq, hp, WIN_H * SPAN)

    @pl.when(lat == 0)
    def _():
        table_copy().wait_recv()
        for zp in range(WIN_Z):
            for zq in range(WIN_Z):
                for hp in range(3):
                    spread(tab15, zp, zq, hp, 3 * SPAN)

    whole = tin[...]
    high = whole.astype(BF16)
    rest = whole - high.astype(F32)
    middle = rest.astype(BF16)
    low = (rest - middle.astype(F32)).astype(BF16)
    loads[2].wait()
    perm = perm_ref[...]
    spread_rows = dot(high, perm) + dot(middle, perm) + dot(low, perm)
    for n in range(3):
        ymat[n, 0:96, :] = spread_rows[:, 128 * n : 128 * (n + 1)]
        ymat[n, 96:128, :] = jnp.zeros((32, 128), F32)
    loads[4].wait()

    @pl.when(lat == 0)
    def _():
        for n in range(3):
            ymat[n, 0:96, :] = ymat[n, 0:96, :] + cross_ref[:, 128 * n : 128 * (n + 1)]

    for head in range(HEADS):
        rows = jnp.concatenate(
            [ymat[n, pl.ds(head, 16, stride=8), :] for n in range(3)], -1
        )
        for w in range(WIN_W):
            moved = pltpu.roll(rows, (384 - (WIN_W - 1 - w) * GROUPS) % 384, axis=1)
            bias[head, w * GROUPS : (w + 1) * GROUPS, :] = moved[:GROUPS, :T]

    for n in range(5, 16):
        loads[n].wait()
    lane = lax.broadcasted_iota(jnp.int32, (T, C), 1)
    masks = [(lane >= HEAD * i) & (lane < HEAD * (i + 1)) for i in range(HEADS)]
    ones = [jnp.where(mask[0:16], 1.0, 0.0).astype(BF16)[0:1] for mask in masks]
    order = order_ref[...]
    back = back_ref[...]
    gain1 = g1_ref[...].reshape(1, C)
    gain2 = g2_ref[...].reshape(1, C)

    def arrived(a):
        for i in range(3):
            exchange(a, i).wait_recv()
        return dot(order, arrive[a].reshape(4 * SLOT, C))

    tokens = arrived(0)
    normed, hat1, inv1 = normalize(tokens, gain1)
    first = normed.astype(BF16)
    qkv = (dot(first, wqkv_ref[...]) + bqkv_ref[...].reshape(1, 3 * C)).astype(BF16)
    queries = qkv[:, 0:C]
    keys = qkv[:, C : 2 * C]
    values = qkv[:, 2 * C : 3 * C]
    queries_t = queries.T
    mixed = jnp.zeros((T, C), F32)
    for head in range(HEADS):
        q = queries * ones[head]
        scores = dot_nt(q, keys) * FACTOR + bias[head]
        top = jnp.max(scores, -1, keepdims=True)
        raised = jnp.exp(scores - top)
        probs = raised * (1.0 / jnp.sum(raised, -1, keepdims=True))
        prob[head] = probs
        probs_low = probs.astype(BF16)
        plow[head] = probs_low
        mixed = jnp.where(masks[head], dot(probs_low, values), mixed)
    mixed = mixed.astype(BF16)
    inner = tokens + dot(mixed, wproj_ref[...]).astype(BF16).astype(F32)

    cot = arrived(1)
    cot_low = cot.astype(BF16)
    normed, hat2, inv2 = normalize(inner, gain2)
    second = normed.astype(BF16)
    second_t = second.T
    cot_t = cot_low.T
    total = inner
    grad_second = jnp.zeros((T, C), F32)
    bfc1 = bfc1_ref[...].reshape(1, HID)
    vec[...] = jnp.zeros_like(vec)
    for n in range(3):
        cols = slice(256 * n, 256 * (n + 1))
        pre = dot(second, wfc1_ref[:, cols]) + bfc1[:, cols]
        cdf = 0.5 * (1.0 + lax.erf(pre * 0.7071067811865476))
        density = jnp.exp(-0.5 * pre * pre) * 0.3989422804014327
        act = (pre * cdf).astype(BF16)
        total = total + dot_nt(act, wfc2_ref[:, cols])
        grad_pre = (dot(cot_low, wfc2_ref[:, cols]) * (cdf + pre * density)).astype(BF16)
        grad_second = grad_second + dot_nt(grad_pre, wfc1_ref[:, cols])
        parts_fc[0, 12 * n : 12 * (n + 1)] = dot(second_t, grad_pre).astype(BF16).reshape(12, 16, 256)
        parts_fc[1, 12 * n : 12 * (n + 1)] = dot(cot_t, act).astype(BF16).reshape(12, 16, 256)
        vec[n : n + 1, :] = jnp.sum(grad_pre.astype(F32), 0, keepdims=True)

    def remote(src, dst, send_sem, recv_sem, target):
        return pltpu.make_async_remote_copy(
            src_ref=src, dst_ref=dst, send_sem=send_sem, recv_sem=recv_sem,
            device_id=target, device_id_type=MESH,
        )

    def wait_bytes(ref, sem):
        pltpu.make_async_copy(ref, ref, sem).wait()

    def add(*terms):
        total = terms[0].astype(F32)
        for term in terms[1:]:
            total = total + term.astype(F32)
        return total.astype(BF16)

    axes = [(n, (n + 1) % 3, (n + 2) % 3) for n in range(3)]
    places = [tuple(spot[axis] for axis in order) for order in axes]

    def block(n, i):
        return pl.ds(n * 16 + i * 4, 4)

    def unit(n):
        return n * 16 + places[n][0] * 4 + places[n][1]

    def to_line(stage_no, which, src, dst):
        for n in range(3):
            for d in range(1, 4):
                at = lax.rem(places[n][which] + d, 4)
                remote(
                    src(n, at), dst(n, d), f_send.at[stage_no], f_recv.at[stage_no],
                    on_axis(axes[n][which], at),
                ).start()

    pair_fc = remote(parts_fc.at[other], core_fc, f_send.at[0], f_recv.at[0], sibling)
    swap_fc = remote(gath_fc.at[core], gath_fc.at[core], f_send.at[6], f_recv.at[6], sibling)
    pair_att = remote(parts_att.at[other], core_att, a_send.at[0], a_recv.at[0], sibling)
    swap_att = remote(gath_att.at[core], gath_att.at[core], a_send.at[4], a_recv.at[4], sibling)

    def early1():
        pair_fc.wait_recv()
        parts_fc[core] = add(parts_fc[core], core_fc[...])
        to_line(
            1, 0, lambda n, at: parts_fc.at[core, block(n, at)], lambda n, d: fold1.at[n, d - 1]
        )

    def early2():
        wait_bytes(fold1, f_recv.at[1])
        for n in range(3):
            own = parts_fc[core, block(n, places[n][0])]
            sum1[n] = add(own, fold1[n, 0], fold1[n, 1], fold1[n, 2])
        to_line(2, 1, lambda n, at: sum1.at[n, at], lambda n, d: fold2.at[n, d - 1])

    def early3():
        wait_bytes(fold2, f_recv.at[2])
        for n in range(3):
            own = sum1[n, places[n][1]]
            sum2[n] = add(own, fold2[n, 0], fold2[n, 1], fold2[n, 2])
            fold3[n, places[n][2]] = sum2[n]
        to_line(3, 2, lambda n, at: sum2.at[n], lambda n, d: fold3.at[n, places[n][2]])

    def early4():
        wait_bytes(fold2, f_recv.at[3])
        for n in range(3):
            gath_fc[core, unit(n)] = add(*[fold3[n, i] for i in range(4)])
        to_line(
            4, 1, lambda n, at: gath_fc.at[core, unit(n)], lambda n, d: gath_fc.at[core, unit(n)]
        )

    def early5():
        wait_bytes(fold2, f_recv.at[4])
        to_line(
            5, 0,
            lambda n, at: gath_fc.at[core, block(n, places[n][0])],
            lambda n, d: gath_fc.at[core, block(n, places[n][0])],
        )

    def early6():
        wait_bytes(fold1, f_recv.at[5])
        swap_fc.start()

    own_rows = pl.ds(pair_row * 4, 4)

    def late1():
        pair_att.wait_recv()
        parts_att[core] = add(parts_att[core], core_att[...])
        for d in range(1, ROWS):
            remote(
                parts_att.at[core, pl.ds(row_of(d) * 4, 4)], fold_att.at[d - 1],
                a_send.at[1], a_recv.at[1], (lon, row_of(d) * 2 + core),
            ).start()

    def late2():
        wait_bytes(fold_att, a_recv.at[1])
        sum_att[...] = add(parts_att[core, own_rows], *[fold_att[d] for d in range(ROWS - 1)])
        mid_att[lon] = sum_att[...]
        for d in range(1, STRIPS):
            remote(
                sum_att, mid_att.at[lon], a_send.at[2], a_recv.at[2], (strip(d), lat)
            ).start()

    def late3():
        wait_bytes(fold_att, a_recv.at[2])
        gath_att[core, own_rows] = add(*[mid_att[i] for i in range(STRIPS)])
        for d in range(1, ROWS):
            remote(
                gath_att.at[core, own_rows], gath_att.at[core, own_rows],
                a_send.at[3], a_recv.at[3], (lon, row_of(d) * 2 + core),
            ).start()

    def late4():
        wait_bytes(fold_att, a_recv.at[3])
        swap_att.start()

    def give_back(a, i):
        return pltpu.make_async_remote_copy(
            src_ref=out_stage.at[a, 2 - i],
            dst_ref=ret_ref.at[a, i + 1],
            send_sem=rt_send.at[a, i],
            recv_sem=rt_recv.at[a, i],
            device_id=behind[i],
            device_id_type=MESH,
        )

    def hand_out(a, field):
        out_stage[a] = dot(back, field).astype(BF16).reshape(4, SLOT, C)
        for i in range(3):
            give_back(a, i).start()
        ret_ref[a, 0] = out_stage[a, 3]

    grad_inner = cot + norm_back(hat2, inv2, gain2, grad_second)
    grad_att = grad_inner.astype(BF16)
    proj_grad = dot_tn(mixed, grad_att).astype(BF16)
    proj_grad = jnp.concatenate([proj_grad, jnp.zeros((C, 64), BF16)], -1).reshape(12, 16, 256)
    parts_fc[0, 36:42] = proj_grad[:6]
    parts_fc[1, 36:42] = proj_grad[6:]
    vec[3:4, 0:C] = jnp.sum(grad_second * hat2, 0, keepdims=True)
    parts_fc[0, 42] = vec[...].astype(BF16)
    parts_fc[1, 42] = jnp.zeros((16, 256), BF16)
    parts_fc[:, 43:] = jnp.zeros((2, FC - 43, 16, 256), BF16)
    pair_fc.start()
    hand_out(0, total.astype(BF16))

    grad_mixed = dot_nt(grad_att, wproj_ref[...]).astype(BF16)
    grad_mixed_t = grad_mixed.T
    dsc[...] = jnp.zeros_like(dsc)
    grad_q = jnp.zeros((T, C), F32)
    grad_k_t = []
    grad_v_t = []
    for head in range(HEADS):
        rows = slice(HEAD * head, HEAD * (head + 1))
        gm = grad_mixed * ones[head]
        probs = prob[head]
        grad_probs = dot_nt(gm, values)
        inside = jnp.sum(probs * grad_probs, -1, keepdims=True)
        grad_scores = probs * (grad_probs - inside)
        dsc[head, 0:T, 0:T] = grad_scores
        scaled = (grad_scores * FACTOR).astype(BF16)
        grad_q = jnp.where(masks[head], dot(scaled, keys), grad_q)
        grad_k_t.append(dot(queries_t[rows], scaled))
        grad_v_t.append(dot(grad_mixed_t[rows], plow[head]))
        if head == 2:
            early1()
    grad_k = jnp.concatenate(grad_k_t, 0).T
    grad_v = jnp.concatenate(grad_v_t, 0).T

    grad_qkv = jnp.concatenate([grad_q, grad_k, grad_v], -1).astype(BF16)
    wide = dot_tn(first, grad_qkv).astype(BF16)
    for n in range(4):
        parts_att[n // 2, n % 2 * 12 : n % 2 * 12 + 12] = (
            wide[:, 128 * n : 128 * (n + 1)].reshape(12, 16, 128)
        )
    edge = jnp.concatenate([wide[:96, 512:576], wide[96:, 512:576]], -1).reshape(6, 16, 128)
    parts_att[0, 24:27] = edge[:3]
    parts_att[1, 24:27] = edge[3:]
    grad_first = dot_nt(grad_qkv, wqkv_ref[...]).astype(BF16).astype(F32)
    vec[...] = jnp.zeros_like(vec)
    sums = jnp.sum(grad_qkv.astype(F32), 0, keepdims=True)
    sums = [sums[:, C * n : C * (n + 1)] for n in range(3)]
    sums.append(jnp.sum(grad_first * hat1, 0, keepdims=True))
    for n in range(4):
        vec[2 * n : 2 * n + 1, 0:128] = sums[n][:, 0:128]
        vec[2 * n + 1 : 2 * n + 2, 0:64] = sums[n][:, 128:C]
    parts_att[0, 27] = vec[:, 0:128].astype(BF16)
    parts_att[1, 27] = jnp.zeros((16, 128), BF16)
    parts_att[:, 28:] = jnp.zeros((2, ATT - 28, 16, 128), BF16)
    pair_att.start()
    early2()
    d_tokens = grad_inner + norm_back(hat1, inv1, gain1, grad_first)
    hand_out(1, d_tokens.astype(BF16))
    late1()
    early3()

    dmat[...] = jnp.zeros_like(dmat)
    for head in range(HEADS):
        acc = jnp.zeros((16, 384), F32)
        for w in range(WIN_W):
            acc = acc + pltpu.roll(
                dsc[head, w * GROUPS : w * GROUPS + 16, :], (WIN_W - 1 - w) * GROUPS, axis=1
            )
        for n in range(3):
            dmat[n, pl.ds(head, 16, stride=8), :] = acc[:, 128 * n : 128 * (n + 1)]

    def table_grad():
        return jnp.concatenate([dmat[n, 0:96, :] for n in range(3)], -1)

    def keep_table(field):
        for n in range(3):
            dmat[n, 0:96, :] = field[:, 128 * n : 128 * (n + 1)]

    def edge_copy():
        return pltpu.make_async_remote_copy(
            src_ref=bbs,
            dst_ref=bbr,
            send_sem=one_send.at[1],
            recv_sem=one_recv.at[1],
            device_id=(lon, north),
            device_id_type=MESH,
        )

    @pl.when(lat == 0)
    def _():
        row = lax.broadcasted_iota(jnp.int32, (96, 384), 0)
        upper = (row < 24) | ((row >= 48) & (row < 72))
        full = table_grad()
        bbs[...] = jnp.where(upper, full, 0.0).astype(BF16)
        edge_copy().start()
        keep_table(jnp.where(upper, 0.0, full))

    @pl.when(lat == BANDS - 1)
    def _():
        edge_copy().wait_recv()
        keep_table(table_grad() + bbr[...].astype(F32))

    bsend[...] = table_grad().astype(BF16).reshape(PARTS, 16, 384)

    for owner in range(PARTS):
        @pl.when(lon != owner)
        def _():
            pltpu.make_async_remote_copy(
                src_ref=bsend.at[owner],
                dst_ref=brecv.at[lon],
                send_sem=b_send.at[0],
                recv_sem=b_recv.at[0],
                device_id=(owner, lat),
                device_id_type=MESH,
            ).start()

    early4()
    late2()
    seven = brecv.at[pl.ds(0, STRIPS - 1)]

    @pl.when(lon < PARTS)
    def _():
        brecv[lon] = bsend[lon]
        wait_bytes(seven, b_recv.at[0])
        bfin[lon] = jnp.sum(brecv[...].astype(F32), 0).astype(BF16)
        for d in range(1, STRIPS):
            pltpu.make_async_remote_copy(
                src_ref=bfin.at[lon],
                dst_ref=bfin.at[lon],
                send_sem=b_send.at[1],
                recv_sem=b_recv.at[1],
                device_id=(strip(d), lat),
                device_id_type=MESH,
            ).start()

    early5()
    late3()

    @pl.when(lon < PARTS)
    def _():
        wait_bytes(bfin.at[pl.ds(0, PARTS - 1)], b_recv.at[1])

    @pl.when(lon >= PARTS)
    def _():
        wait_bytes(bfin, b_recv.at[1])

    tin[...] = dot(bfin[...].reshape(96, 384), unperm_ref[...])
    dtab_ref[...] = jnp.zeros_like(dtab_ref)
    for zp in range(WIN_Z):
        for zq in range(WIN_Z):
            for hp in range(WIN_H):
                j = (zp * WIN_Z + zq) * WIN_H + hp
                first_lane = j * WIN_H * SPAN
                base = first_lane // 128 * 128
                g = zp * WIN_H + hp
                piece = tin[g * 8 : g * 8 + 8, zq * 256 : zq * 256 + 256]
                piece = jnp.concatenate([piece, jnp.zeros((8, 128), F32)], -1)
                moved = pltpu.roll(piece, first_lane - base, axis=1)
                dtab_ref[:, base : base + 384] = dtab_ref[:, base : base + 384] + moved

    early6()
    late4()

    for a in range(2):
        for i in range(3):
            exchange(a, i).wait_send()
            give_back(a, i).wait()

    @pl.when(lat == BANDS - 1)
    def _():
        table_copy().wait_send()

    @pl.when(lat == 0)
    def _():
        edge_copy().wait_send()

    pair_fc.wait_send()
    for stage_no, ref in ((1, fold1), (2, fold2), (3, fold2), (4, fold2), (5, fold1)):
        wait_bytes(ref, f_send.at[stage_no])
    pair_att.wait_send()
    for stage_no in (1, 2, 3):
        wait_bytes(fold_att, a_send.at[stage_no])

    @pl.when(lon < PARTS)
    def _():
        wait_bytes(bsend.at[pl.ds(0, PARTS - 1)], b_send.at[0])
        wait_bytes(seven, b_send.at[1])

    @pl.when(lon >= PARTS)
    def _():
        wait_bytes(bsend, b_send.at[0])

    swap_fc.wait()
    swap_att.wait()


def output_kernel(
    gath_ref, gath_att, ret_ref, dtab_ref,
    out_ref, dtok_ref, dln1_ref, dwqkv_ref, dbqkv_ref, dbias_ref, dwproj_ref, dln2_ref,
    dwfc1_ref, dbfc1_ref, dwfc2_ref,
    stage,
):
    for a, dst in enumerate((out_ref, dtok_ref)):
        stage[...] = ret_ref[a].reshape(4 * SLOT, C).astype(F32)
        for h in range(WIN_H):
            for w in range(WIN_W):
                dst[h, w] = stage[slot_rows(h, w), :].astype(BF16)
    for n in range(3):
        cols = slice(256 * n, 256 * (n + 1))
        rows = slice(12 * n, 12 * (n + 1))
        dwfc1_ref[:, cols] = gath_ref[0, rows].reshape(C, 256).astype(F32)
        dwfc2_ref[:, cols] = gath_ref[1, rows].reshape(C, 256).astype(F32)
    for k in range(2):
        dwproj_ref[96 * k : 96 * (k + 1), :] = (
            gath_ref[k, 36:42].reshape(96, 256)[:, 0:C].astype(F32)
        )
        for n in range(2):
            cols = slice(256 * k + 128 * n, 256 * k + 128 * (n + 1))
            dwqkv_ref[:, cols] = gath_att[k, 12 * n : 12 * (n + 1)].reshape(C, 128).astype(F32)
        edge = gath_att[k, 24:27].reshape(48, 128).astype(F32)
        for n in range(2):
            at = 96 * n + 48 * k
            dwqkv_ref[at : at + 48, 512:576] = edge[:, 64 * n : 64 * (n + 1)]
    vec = gath_ref[0, 42].astype(F32)
    dbfc1_ref[...] = jnp.concatenate([vec[n : n + 1] for n in range(3)], -1).reshape(HID)
    dln2_ref[...] = vec[3:4, :C].reshape(C)
    vec = gath_att[0, 27].astype(F32)
    sums = [
        jnp.concatenate([vec[2 * n : 2 * n + 1], vec[2 * n + 1 : 2 * n + 2, :64]], -1)
        for n in range(4)
    ]
    dbqkv_ref[...] = jnp.concatenate(sums[:3], -1).reshape(3 * C)
    dln1_ref[...] = sums[3].reshape(C)
    for head in range(HEADS):
        dbias_ref[0, head] = dtab_ref[head : head + 1, 0:NREL]


def per_device(
    tokens, cotangent, ln1_gain, w_qkv, b_qkv, bias_table, w_proj, ln2_gain, w_fc1, b_fc1, w_fc2
):
    vmem = pl.BlockSpec(memory_space=pltpu.VMEM)
    order = window_order()
    perm = table_order()
    dma = pltpu.SemaphoreType.DMA
    args = (
        tokens.transpose(1, 2, 0, 3), cotangent.transpose(1, 2, 0, 3), ln1_gain, w_qkv, b_qkv,
        bias_table.transpose(0, 2, 1, 3), w_proj, ln2_gain, w_fc1, b_fc1, w_fc2.T,
        jnp.asarray(order, BF16), jnp.asarray(order.T, BF16),
        jnp.asarray(perm, BF16), jnp.asarray(perm.T, BF16),
        jnp.asarray(cross_pairs()),
    )
    results = pl.pallas_call(
        block_kernel,
        out_shape=(
            jax.ShapeDtypeStruct((2, FC, 16, 256), BF16),
            jax.ShapeDtypeStruct((2, ATT, 16, 128), BF16),
            jax.ShapeDtypeStruct((2, 4, SLOT, C), BF16),
            jax.ShapeDtypeStruct((8, 3456), F32),
        ),
        in_specs=[pl.BlockSpec(memory_space=pl.ANY)] * len(args),
        out_specs=(vmem,) * 4,
        scratch_shapes=[pltpu.VMEM(a.shape, a.dtype) for a in args]
        + [
            pltpu.VMEM((4 * SLOT, C), F32),
            pltpu.VMEM((2, 4, SLOT, C), BF16),
            pltpu.VMEM((2, 4, SLOT, C), BF16),
            pltpu.VMEM((2, 4, SLOT, C), BF16),
            pltpu.VMEM((8, 3456), F32),
            pltpu.VMEM((8, 3456), F32),
            pltpu.VMEM((96, 512), F32),
            pltpu.VMEM((3, 128, 128), F32),
            pltpu.VMEM((HEADS, T, T), F32),
            pltpu.VMEM((HEADS, T, T), F32),
            pltpu.VMEM((HEADS, T, T), BF16),
            pltpu.VMEM((HEADS, 160, 384), F32),
            pltpu.VMEM((3, 128, 128), F32),
            pltpu.VMEM((16, 256), F32),
            pltpu.VMEM((PARTS, 16, 384), BF16),
            pltpu.VMEM((STRIPS, 16, 384), BF16),
            pltpu.VMEM((PARTS, 16, 384), BF16),
            pltpu.VMEM((96, 384), BF16),
            pltpu.VMEM((96, 384), BF16),
            pltpu.VMEM((2, FC, 16, 256), BF16),
            pltpu.VMEM((2, ATT, 16, 128), BF16),
            pltpu.VMEM((FC, 16, 256), BF16),
            pltpu.VMEM((ATT, 16, 128), BF16),
            pltpu.VMEM((3, 3, 4, 16, 256), BF16),
            pltpu.VMEM((3, 4, 16, 256), BF16),
            pltpu.VMEM((3, 3, 16, 256), BF16),
            pltpu.VMEM((3, 16, 256), BF16),
            pltpu.VMEM((3, 4, 16, 256), BF16),
            pltpu.VMEM((ROWS - 1, 4, 16, 128), BF16),
            pltpu.VMEM((4, 16, 128), BF16),
            pltpu.VMEM((STRIPS, 4, 16, 128), BF16),
            dma((len(args),)),
            dma((2, 3)), dma((2, 3)), dma((2, 3)), dma((2, 3)),
            dma((2,)), dma((2,)), dma((7,)), dma((7,)),
            dma((5,)), dma((5,)), dma((2,)), dma((2,)),
        ],
        compiler_params=pltpu.CompilerParams(
            collective_id=0, has_side_effects=True, vmem_limit_bytes=VMEM_LIMIT
        ),
    )(*args)
    shape = jax.ShapeDtypeStruct
    grid_shape = (WIN_H, WIN_W, WIN_Z, C)
    outs = pl.pallas_call(
        output_kernel,
        out_shape=(
            shape(grid_shape, BF16), shape(grid_shape, BF16),
            shape((C,), F32), shape((C, 3 * C), F32), shape((3 * C,), F32),
            shape((1, HEADS, 1, NREL), F32), shape((C, C), F32), shape((C,), F32),
            shape((C, HID), F32), shape((HID,), F32), shape((C, HID), F32),
        ),
        in_specs=[vmem] * 4,
        out_specs=(vmem,) * 11,
        scratch_shapes=[pltpu.VMEM((4 * SLOT, C), F32)],
        compiler_params=pltpu.CompilerParams(vmem_limit_bytes=VMEM_LIMIT),
    )(*results)
    out, d_tok, d_ln1, d_wqkv, d_bqkv, d_bias, d_wproj, d_ln2, d_wfc1, d_bfc1, d_wfc2 = outs
    return (
        out.transpose(2, 0, 1, 3), d_tok.transpose(2, 0, 1, 3), d_ln1, d_wqkv, d_bqkv,
        d_bias.transpose(0, 2, 1, 3), d_wproj, d_ln2, d_wfc1, d_bfc1, d_wfc2.T,
    )


def solution(mesh):
    grid = P(None, "lat", "lon", None)
    rows = P(None, "lat", None, None)
    return jax.shard_map(
        per_device,
        mesh=mesh,
        in_specs=(grid, grid, P(), P(), P(), rows, P(), P(), P(), P(), P()),
        out_specs=(grid, grid, P(), P(), P(), rows, P(), P(), P(), P(), P()),
        check_vma=False,
    )
```

```python
import jax
import jax.numpy as jnp
import numpy as np
from jax import lax
from jax.experimental import pallas as pl
from jax.experimental.pallas import tpu as pltpu
from jax.sharding import PartitionSpec as P

HEADS = 6
WIN_Z = 2
WIN_H = 6
WIN_W = 12
SPAN = 2 * WIN_W - 1
GROUPS = WIN_Z * WIN_H
T = GROUPS * WIN_W
C = 192
HID = 768
HEAD = C // HEADS
NREL = GROUPS * GROUPS * SPAN
SLOT = 48
FC = 48
ATT = 32
ROWS = 8
BANDS = 16
STRIPS = 8
PARTS = 6
EPSILON = 1e-05
VMEM_LIMIT = 56 * 1024 * 1024
FACTOR = HEAD ** (-0.5)
F32 = jnp.float32
BF16 = jnp.bfloat16
MESH = pl.DeviceIdType.MESH


def window_order():
    grid = np.zeros((T, 4 * SLOT), np.float32)
    for w in range(WIN_W):
        for z in range(WIN_Z):
            for h in range(WIN_H):
                slot = (h // 3) * 2 + w // 6
                grid[w * GROUPS + z * WIN_H + h, slot * SLOT + (h % 3) * 12 + (w % 6) * 2 + z] = 1
    return grid


def table_order():
    grid = np.zeros((512, 384), np.float32)
    for z in range(WIN_Z):
        for h in range(WIN_H):
            for i in range(SPAN):
                grid[z * 256 + h * SPAN + i, (SPAN - 1 - i) * GROUPS + z * WIN_H + h] = 1
    return grid


def cross_pairs():
    g = np.arange(96)[:, None] // 8 % WIN_H
    q = np.arange(384)[None, :] % GROUPS % WIN_H
    return np.where((g < 3) != (q < 3), -1e30, 0.0).astype(np.float32)


def dot(a, b):
    return jnp.dot(a, b, preferred_element_type=F32)


def dot_nt(a, b):
    return lax.dot_general(a, b, (((1,), (1,)), ((), ())), preferred_element_type=F32)


def dot_tn(a, b):
    return lax.dot_general(a, b, (((0,), (0,)), ((), ())), preferred_element_type=F32)


def normalize(values, gain):
    average = jnp.mean(values, -1, keepdims=True)
    centered = values - average
    inv = lax.rsqrt(jnp.mean(centered * centered, -1, keepdims=True) + EPSILON)
    hat = centered * inv
    return hat * gain, hat, inv


def norm_back(hat, inv, gain, grad):
    scaled = grad * gain
    return inv * (
        scaled
        - jnp.mean(scaled, -1, keepdims=True)
        - hat * jnp.mean(scaled * hat, -1, keepdims=True)
    )


def slot_rows(h, w):
    at = ((h // 3) * 2 + w // 6) * SLOT + (h % 3) * 12 + (w % 6) * 2
    return slice(at, at + 2)


def block_kernel(
    tok_any, cot_any, g1_any, wqkv_any, bqkv_any, table_any, wproj_any, g2_any, wfc1_any,
    bfc1_any, wfc2_any, order_any, back_any, perm_any, unperm_any, cross_any,
    gath_fc_out, gath_att_out, ret_out, dtab_out,
    tok_ref, cot_ref, g1_ref, wqkv_ref, bqkv_ref, table_ref, wproj_ref, g2_ref, wfc1_ref,
    bfc1_ref, wfc2_ref, order_ref, back_ref, perm_ref, unperm_ref, cross_ref,
    stage, send, arrive, out_stage,
    tabw, tab15, tin, ymat, bias, prob, plow, dsc, dmat, vec,
    bsend, brecv, bfin, bbs, bbr,
    parts_fc, parts_att, core_fc, core_att, fold1, sum1, fold2, sum2, fold3, fold_att, sum_att,
    mid_att, gath_fc, gath_att, dtab_ref,
    in_sem, out_sem,
    ex_send, ex_recv, rt_send, rt_recv, one_send, one_recv, f_send, f_recv,
    a_send, a_recv, b_send, b_recv,
):
    places = (
        (table_any, table_ref), (tok_any, tok_ref), (perm_any, perm_ref), (cot_any, cot_ref),
        (cross_any, cross_ref), (order_any, order_ref), (g1_any, g1_ref), (wqkv_any, wqkv_ref),
        (bqkv_any, bqkv_ref), (wproj_any, wproj_ref), (g2_any, g2_ref), (wfc1_any, wfc1_ref),
        (bfc1_any, bfc1_ref), (wfc2_any, wfc2_ref), (back_any, back_ref),
        (unperm_any, unperm_ref),
    )
    loads = [pltpu.make_async_copy(src, dst, in_sem.at[n]) for n, (src, dst) in enumerate(places)]
    for load in loads:
        load.start()
    lon = lax.axis_index("lon")
    lat = lax.axis_index("lat")
    core = lax.rem(lat, 2)
    other = 1 - core
    pair_row = lat // 2
    east = lax.rem(lon + 1, STRIPS)
    west = lax.rem(lon + STRIPS - 1, STRIPS)
    south = lax.rem(lat + 1, BANDS)
    north = lax.rem(lat + BANDS - 1, BANDS)
    sibling = (lon, lat - core + other)

    spot = (lax.rem(pair_row, 4), lon // 2, lax.rem(lon, 2) * 2 + lat // 8)

    def on_axis(axis, at):
        if axis == 0:
            return (lon, lat // 8 * 8 + at * 2 + core)
        if axis == 1:
            return (at * 2 + lax.rem(lon, 2), lat)
        return (spot[1] * 2 + at // 2, lax.rem(at, 2) * 8 + spot[0] * 2 + core)

    def strip(d):
        return lax.rem(lon + d, STRIPS)

    def row_of(d):
        return lax.rem(pair_row + d, ROWS)

    barrier = pltpu.get_barrier_semaphore()

    def greet(target):
        pl.semaphore_signal(barrier, inc=1, device_id=target, device_id_type=MESH)

    for target in ((lon, south), (lon, north), (east, south), (west, north), sibling):
        greet(target)
    greet(on_axis(2, 3 - spot[2]))
    for d in range(1, 8):
        greet((strip(d), lat))
        greet((lon, row_of(d) * 2 + core))

    stage[...] = jnp.zeros_like(stage)

    def quadrants(a, src):
        loads[(1, 3)[a]].wait()
        for h in range(WIN_H):
            for w in range(WIN_W):
                stage[slot_rows(h, w), :] = src[h, w].astype(F32)
        send[a] = stage[...].astype(BF16).reshape(4, SLOT, C)
        arrive[a, 3] = send[a, 0]

    quadrants(0, tok_ref)
    pl.semaphore_wait(barrier, 20)

    ahead = ((east, lat), (lon, south), (east, south))
    behind = ((west, lat), (lon, north), (west, north))

    def exchange(a, i):
        return pltpu.make_async_remote_copy(
            src_ref=send.at[a, i + 1],
            dst_ref=arrive.at[a, 2 - i],
            send_sem=ex_send.at[a, i],
            recv_sem=ex_recv.at[a, i],
            device_id=ahead[i],
            device_id_type=MESH,
        )

    def table_copy():
        return pltpu.make_async_remote_copy(
            src_ref=tabw,
            dst_ref=tab15,
            send_sem=one_send.at[0],
            recv_sem=one_recv.at[0],
            device_id=(lon, south),
            device_id_type=MESH,
        )

    for i in range(3):
        exchange(0, i).start()

    tabw[...] = jnp.zeros_like(tabw)
    loads[0].wait()
    for head in range(HEADS):
        tabw[head : head + 1, 0:NREL] = table_ref[0, head]

    @pl.when(lat == BANDS - 1)
    def _():
        table_copy().start()

    quadrants(1, cot_ref)
    for i in range(3):
        exchange(1, i).start()

    tin[...] = jnp.zeros_like(tin)

    def spread(src, zp, zq, hp, width):
        j = (zp * WIN_Z + zq) * WIN_H + hp
        first = j * WIN_H * SPAN
        base = first // 128 * 128
        wide = src[:, base : base + 384]
        moved = pltpu.roll(wide, (384 - (first - base)) % 384, axis=1)
        g = zp * WIN_H + hp
        tin[g * 8 : g * 8 + 8, zq * 256 : zq * 256 + width] = moved[:, :width]

    for zp in range(WIN_Z):
        for zq in range(WIN_Z):
            for hp in range(WIN_H):
                spread(tabw, zp, zq, hp, WIN_H * SPAN)

    @pl.when(lat == 0)
    def _():
        table_copy().wait_recv()
        for zp in range(WIN_Z):
            for zq in range(WIN_Z):
                for hp in range(3):
                    spread(tab15, zp, zq, hp, 3 * SPAN)

    whole = tin[...]
    high = whole.astype(BF16)
    rest = whole - high.astype(F32)
    middle = rest.astype(BF16)
    low = (rest - middle.astype(F32)).astype(BF16)
    loads[2].wait()
    perm = perm_ref[...]
    spread_rows = dot(high, perm) + dot(middle, perm) + dot(low, perm)
    for n in range(3):
        ymat[n, 0:96, :] = spread_rows[:, 128 * n : 128 * (n + 1)]
        ymat[n, 96:128, :] = jnp.zeros((32, 128), F32)
    loads[4].wait()

    @pl.when(lat == 0)
    def _():
        for n in range(3):
            ymat[n, 0:96, :] = ymat[n, 0:96, :] + cross_ref[:, 128 * n : 128 * (n + 1)]

    for head in range(HEADS):
        rows = jnp.concatenate(
            [ymat[n, pl.ds(head, 16, stride=8), :] for n in range(3)], -1
        )
        for w in range(WIN_W):
            moved = pltpu.roll(rows, (384 - (WIN_W - 1 - w) * GROUPS) % 384, axis=1)
            bias[head, w * GROUPS : (w + 1) * GROUPS, :] = moved[:GROUPS, :T]

    for n in range(5, 16):
        loads[n].wait()
    lane = lax.broadcasted_iota(jnp.int32, (T, C), 1)
    masks = [(lane >= HEAD * i) & (lane < HEAD * (i + 1)) for i in range(HEADS)]
    ones = [jnp.where(mask[0:16], 1.0, 0.0).astype(BF16)[0:1] for mask in masks]
    order = order_ref[...]
    back = back_ref[...]
    gain1 = g1_ref[...].reshape(1, C)
    gain2 = g2_ref[...].reshape(1, C)

    def arrived(a):
        for i in range(3):
            exchange(a, i).wait_recv()
        return dot(order, arrive[a].reshape(4 * SLOT, C))

    tokens = arrived(0)
    normed, hat1, inv1 = normalize(tokens, gain1)
    first = normed.astype(BF16)
    qkv = (dot(first, wqkv_ref[...]) + bqkv_ref[...].reshape(1, 3 * C)).astype(BF16)
    queries = qkv[:, 0:C]
    keys = qkv[:, C : 2 * C]
    values = qkv[:, 2 * C : 3 * C]
    queries_t = queries.T
    mixed = jnp.zeros((T, C), F32)
    for head in range(HEADS):
        q = queries * ones[head]
        scores = dot_nt(q, keys) * FACTOR + bias[head]
        top = jnp.max(scores, -1, keepdims=True)
        raised = jnp.exp(scores - top)
        probs = raised * (1.0 / jnp.sum(raised, -1, keepdims=True))
        prob[head] = probs
        probs_low = probs.astype(BF16)
        plow[head] = probs_low
        mixed = jnp.where(masks[head], dot(probs_low, values), mixed)
    mixed = mixed.astype(BF16)
    inner = tokens + dot(mixed, wproj_ref[...]).astype(BF16).astype(F32)

    cot = arrived(1)
    cot_low = cot.astype(BF16)
    normed, hat2, inv2 = normalize(inner, gain2)
    second = normed.astype(BF16)
    second_t = second.T
    cot_t = cot_low.T
    total = inner
    grad_second = jnp.zeros((T, C), F32)
    bfc1 = bfc1_ref[...].reshape(1, HID)
    vec[...] = jnp.zeros_like(vec)
    for n in range(3):
        cols = slice(256 * n, 256 * (n + 1))
        pre = dot(second, wfc1_ref[:, cols]) + bfc1[:, cols]
        cdf = 0.5 * (1.0 + lax.erf(pre * 0.7071067811865476))
        density = jnp.exp(-0.5 * pre * pre) * 0.3989422804014327
        act = (pre * cdf).astype(BF16)
        total = total + dot_nt(act, wfc2_ref[:, cols])
        grad_pre = (dot(cot_low, wfc2_ref[:, cols]) * (cdf + pre * density)).astype(BF16)
        grad_second = grad_second + dot_nt(grad_pre, wfc1_ref[:, cols])
        parts_fc[0, 12 * n : 12 * (n + 1)] = dot(second_t, grad_pre).astype(BF16).reshape(12, 16, 256)
        parts_fc[1, 12 * n : 12 * (n + 1)] = dot(cot_t, act).astype(BF16).reshape(12, 16, 256)
        vec[n : n + 1, :] = jnp.sum(grad_pre.astype(F32), 0, keepdims=True)

    def remote(src, dst, send_sem, recv_sem, target):
        return pltpu.make_async_remote_copy(
            src_ref=src, dst_ref=dst, send_sem=send_sem, recv_sem=recv_sem,
            device_id=target, device_id_type=MESH,
        )

    def wait_bytes(ref, sem):
        pltpu.make_async_copy(ref, ref, sem).wait()

    def add(*terms):
        total = terms[0].astype(F32)
        for term in terms[1:]:
            total = total + term.astype(F32)
        return total.astype(BF16)

    axes = [(n, (n + 1) % 3, (n + 2) % 3) for n in range(3)]
    places = [tuple(spot[axis] for axis in order) for order in axes]

    def block(n, i):
        return pl.ds(n * 16 + i * 4, 4)

    def unit(n):
        return n * 16 + places[n][0] * 4 + places[n][1]

    def to_line(stage_no, which, src, dst):
        for n in range(3):
            for d in range(1, 4):
                at = lax.rem(places[n][which] + d, 4)
                remote(
                    src(n, at), dst(n, d), f_send.at[stage_no], f_recv.at[stage_no],
                    on_axis(axes[n][which], at),
                ).start()

    pair_fc = remote(parts_fc.at[other], core_fc, f_send.at[0], f_recv.at[0], sibling)
    swap_fc = remote(
        gath_fc.at[core], gath_fc_out.at[core], f_send.at[6], f_recv.at[6], sibling
    )
    pair_att = remote(parts_att.at[other], core_att, a_send.at[0], a_recv.at[0], sibling)
    swap_att = remote(
        gath_att.at[core], gath_att_out.at[core], a_send.at[4], a_recv.at[4], sibling
    )
    keep = [
        pltpu.make_async_copy(src, dst, out_sem.at[n])
        for n, (src, dst) in enumerate((
            (out_stage.at[0, 3], ret_out.at[0, 0]), (out_stage.at[1, 3], ret_out.at[1, 0]),
            (dtab_ref, dtab_out), (gath_fc.at[core], gath_fc_out.at[core]),
            (gath_att.at[core], gath_att_out.at[core]),
        ))
    ]

    def early1():
        pair_fc.wait_recv()
        parts_fc[core] = add(parts_fc[core], core_fc[...])
        to_line(
            1, 0, lambda n, at: parts_fc.at[core, block(n, at)], lambda n, d: fold1.at[n, d - 1]
        )

    def early2():
        wait_bytes(fold1, f_recv.at[1])
        for n in range(3):
            own = parts_fc[core, block(n, places[n][0])]
            sum1[n] = add(own, fold1[n, 0], fold1[n, 1], fold1[n, 2])
        to_line(2, 1, lambda n, at: sum1.at[n, at], lambda n, d: fold2.at[n, d - 1])

    def early3():
        wait_bytes(fold2, f_recv.at[2])
        for n in range(3):
            own = sum1[n, places[n][1]]
            sum2[n] = add(own, fold2[n, 0], fold2[n, 1], fold2[n, 2])
            fold3[n, places[n][2]] = sum2[n]
        to_line(3, 2, lambda n, at: sum2.at[n], lambda n, d: fold3.at[n, places[n][2]])

    def early4():
        wait_bytes(fold2, f_recv.at[3])
        for n in range(3):
            gath_fc[core, unit(n)] = add(*[fold3[n, i] for i in range(4)])
        to_line(
            4, 1, lambda n, at: gath_fc.at[core, unit(n)], lambda n, d: gath_fc.at[core, unit(n)]
        )

    def early5():
        wait_bytes(fold2, f_recv.at[4])
        to_line(
            5, 0,
            lambda n, at: gath_fc.at[core, block(n, places[n][0])],
            lambda n, d: gath_fc.at[core, block(n, places[n][0])],
        )

    def early6():
        wait_bytes(fold1, f_recv.at[5])
        swap_fc.start()
        keep[3].start()

    own_rows = pl.ds(pair_row * 4, 4)

    def late1():
        pair_att.wait_recv()
        parts_att[core] = add(parts_att[core], core_att[...])
        for d in range(1, ROWS):
            remote(
                parts_att.at[core, pl.ds(row_of(d) * 4, 4)], fold_att.at[d - 1],
                a_send.at[1], a_recv.at[1], (lon, row_of(d) * 2 + core),
            ).start()

    def late2():
        wait_bytes(fold_att, a_recv.at[1])
        sum_att[...] = add(parts_att[core, own_rows], *[fold_att[d] for d in range(ROWS - 1)])
        mid_att[lon] = sum_att[...]
        for d in range(1, STRIPS):
            remote(
                sum_att, mid_att.at[lon], a_send.at[2], a_recv.at[2], (strip(d), lat)
            ).start()

    def late3():
        wait_bytes(fold_att, a_recv.at[2])
        gath_att[core, own_rows] = add(*[mid_att[i] for i in range(STRIPS)])
        for d in range(1, ROWS):
            remote(
                gath_att.at[core, own_rows], gath_att.at[core, own_rows],
                a_send.at[3], a_recv.at[3], (lon, row_of(d) * 2 + core),
            ).start()

    def late4():
        wait_bytes(fold_att, a_recv.at[3])
        swap_att.start()
        keep[4].start()

    def give_back(a, i):
        return pltpu.make_async_remote_copy(
            src_ref=out_stage.at[a, 2 - i],
            dst_ref=ret_out.at[a, i + 1],
            send_sem=rt_send.at[a, i],
            recv_sem=rt_recv.at[a, i],
            device_id=behind[i],
            device_id_type=MESH,
        )

    def hand_out(a, field):
        out_stage[a] = dot(back, field).astype(BF16).reshape(4, SLOT, C)
        for i in range(3):
            give_back(a, i).start()
        keep[a].start()

    grad_inner = cot + norm_back(hat2, inv2, gain2, grad_second)
    grad_att = grad_inner.astype(BF16)
    proj_grad = dot_tn(mixed, grad_att).astype(BF16)
    proj_grad = jnp.concatenate([proj_grad, jnp.zeros((C, 64), BF16)], -1).reshape(12, 16, 256)
    parts_fc[0, 36:42] = proj_grad[:6]
    parts_fc[1, 36:42] = proj_grad[6:]
    vec[3:4, 0:C] = jnp.sum(grad_second * hat2, 0, keepdims=True)
    parts_fc[0, 42] = vec[...].astype(BF16)
    parts_fc[1, 42] = jnp.zeros((16, 256), BF16)
    parts_fc[:, 43:] = jnp.zeros((2, FC - 43, 16, 256), BF16)
    pair_fc.start()
    hand_out(0, total.astype(BF16))

    grad_mixed = dot_nt(grad_att, wproj_ref[...]).astype(BF16)
    grad_mixed_t = grad_mixed.T
    dsc[...] = jnp.zeros_like(dsc)
    grad_q = jnp.zeros((T, C), F32)
    grad_k_t = []
    grad_v_t = []
    for head in range(HEADS):
        rows = slice(HEAD * head, HEAD * (head + 1))
        gm = grad_mixed * ones[head]
        probs = prob[head]
        grad_probs = dot_nt(gm, values)
        inside = jnp.sum(probs * grad_probs, -1, keepdims=True)
        grad_scores = probs * (grad_probs - inside)
        dsc[head, 0:T, 0:T] = grad_scores
        scaled = (grad_scores * FACTOR).astype(BF16)
        grad_q = jnp.where(masks[head], dot(scaled, keys), grad_q)
        grad_k_t.append(dot(queries_t[rows], scaled))
        grad_v_t.append(dot(grad_mixed_t[rows], plow[head]))
        if head == 2:
            early1()
    grad_k = jnp.concatenate(grad_k_t, 0).T
    grad_v = jnp.concatenate(grad_v_t, 0).T

    grad_qkv = jnp.concatenate([grad_q, grad_k, grad_v], -1).astype(BF16)
    wide = dot_tn(first, grad_qkv).astype(BF16)
    for n in range(4):
        parts_att[n // 2, n % 2 * 12 : n % 2 * 12 + 12] = (
            wide[:, 128 * n : 128 * (n + 1)].reshape(12, 16, 128)
        )
    edge = jnp.concatenate([wide[:96, 512:576], wide[96:, 512:576]], -1).reshape(6, 16, 128)
    parts_att[0, 24:27] = edge[:3]
    parts_att[1, 24:27] = edge[3:]
    grad_first = dot_nt(grad_qkv, wqkv_ref[...]).astype(BF16).astype(F32)
    vec[...] = jnp.zeros_like(vec)
    sums = jnp.sum(grad_qkv.astype(F32), 0, keepdims=True)
    sums = [sums[:, C * n : C * (n + 1)] for n in range(3)]
    sums.append(jnp.sum(grad_first * hat1, 0, keepdims=True))
    for n in range(4):
        vec[2 * n : 2 * n + 1, 0:128] = sums[n][:, 0:128]
        vec[2 * n + 1 : 2 * n + 2, 0:64] = sums[n][:, 128:C]
    parts_att[0, 27] = vec[:, 0:128].astype(BF16)
    parts_att[1, 27] = jnp.zeros((16, 128), BF16)
    parts_att[:, 28:] = jnp.zeros((2, ATT - 28, 16, 128), BF16)
    pair_att.start()
    d_tokens = grad_inner + norm_back(hat1, inv1, gain1, grad_first)
    hand_out(1, d_tokens.astype(BF16))

    dmat[...] = jnp.zeros_like(dmat)
    for head in range(HEADS):
        if head == 3:
            early2()
            late1()
        acc = jnp.zeros((16, 384), F32)
        for w in range(WIN_W):
            acc = acc + pltpu.roll(
                dsc[head, w * GROUPS : w * GROUPS + 16, :], (WIN_W - 1 - w) * GROUPS, axis=1
            )
        for n in range(3):
            dmat[n, pl.ds(head, 16, stride=8), :] = acc[:, 128 * n : 128 * (n + 1)]

    def table_grad():
        return jnp.concatenate([dmat[n, 0:96, :] for n in range(3)], -1)

    def keep_table(field):
        for n in range(3):
            dmat[n, 0:96, :] = field[:, 128 * n : 128 * (n + 1)]

    def edge_copy():
        return pltpu.make_async_remote_copy(
            src_ref=bbs,
            dst_ref=bbr,
            send_sem=one_send.at[1],
            recv_sem=one_recv.at[1],
            device_id=(lon, north),
            device_id_type=MESH,
        )

    @pl.when(lat == 0)
    def _():
        row = lax.broadcasted_iota(jnp.int32, (96, 384), 0)
        upper = (row < 24) | ((row >= 48) & (row < 72))
        full = table_grad()
        bbs[...] = jnp.where(upper, full, 0.0).astype(BF16)
        edge_copy().start()
        keep_table(jnp.where(upper, 0.0, full))

    @pl.when(lat == BANDS - 1)
    def _():
        edge_copy().wait_recv()
        keep_table(table_grad() + bbr[...].astype(F32))

    bsend[...] = table_grad().astype(BF16).reshape(PARTS, 16, 384)

    for owner in range(PARTS):
        @pl.when(lon != owner)
        def _():
            pltpu.make_async_remote_copy(
                src_ref=bsend.at[owner],
                dst_ref=brecv.at[lon],
                send_sem=b_send.at[0],
                recv_sem=b_recv.at[0],
                device_id=(owner, lat),
                device_id_type=MESH,
            ).start()

    early3()
    late2()
    early4()
    seven = brecv.at[pl.ds(0, STRIPS - 1)]

    @pl.when(lon < PARTS)
    def _():
        brecv[lon] = bsend[lon]
        wait_bytes(seven, b_recv.at[0])
        bfin[lon] = jnp.sum(brecv[...].astype(F32), 0).astype(BF16)
        for d in range(1, STRIPS):
            pltpu.make_async_remote_copy(
                src_ref=bfin.at[lon],
                dst_ref=bfin.at[lon],
                send_sem=b_send.at[1],
                recv_sem=b_recv.at[1],
                device_id=(strip(d), lat),
                device_id_type=MESH,
            ).start()

    early5()
    late3()

    @pl.when(lon < PARTS)
    def _():
        wait_bytes(bfin.at[pl.ds(0, PARTS - 1)], b_recv.at[1])

    @pl.when(lon >= PARTS)
    def _():
        wait_bytes(bfin, b_recv.at[1])

    tin[...] = dot(bfin[...].reshape(96, 384), unperm_ref[...])
    dtab_ref[...] = jnp.zeros_like(dtab_ref)
    for zp in range(WIN_Z):
        for zq in range(WIN_Z):
            for hp in range(WIN_H):
                j = (zp * WIN_Z + zq) * WIN_H + hp
                first_lane = j * WIN_H * SPAN
                base = first_lane // 128 * 128
                g = zp * WIN_H + hp
                piece = tin[g * 8 : g * 8 + 8, zq * 256 : zq * 256 + 256]
                piece = jnp.concatenate([piece, jnp.zeros((8, 128), F32)], -1)
                moved = pltpu.roll(piece, first_lane - base, axis=1)
                dtab_ref[:, base : base + 384] = dtab_ref[:, base : base + 384] + moved

    keep[2].start()
    early6()
    late4()

    for a in range(2):
        for i in range(3):
            exchange(a, i).wait_send()
            give_back(a, i).wait()

    @pl.when(lat == BANDS - 1)
    def _():
        table_copy().wait_send()

    @pl.when(lat == 0)
    def _():
        edge_copy().wait_send()

    pair_fc.wait_send()
    for stage_no, ref in ((1, fold1), (2, fold2), (3, fold2), (4, fold2), (5, fold1)):
        wait_bytes(ref, f_send.at[stage_no])
    pair_att.wait_send()
    for stage_no in (1, 2, 3):
        wait_bytes(fold_att, a_send.at[stage_no])

    @pl.when(lon < PARTS)
    def _():
        wait_bytes(bsend.at[pl.ds(0, PARTS - 1)], b_send.at[0])
        wait_bytes(seven, b_send.at[1])

    @pl.when(lon >= PARTS)
    def _():
        wait_bytes(bsend, b_send.at[0])

    for copy in keep:
        copy.wait()
    swap_fc.wait()
    swap_att.wait()


def output_kernel(*refs):
    ins, outs = refs[:4], refs[4:15]
    in_bufs, out_bufs = refs[15:19], refs[19:30]
    stage, in_sem, out_sem = refs[30:]
    loads = [
        pltpu.make_async_copy(src, dst, in_sem.at[n])
        for n, (src, dst) in enumerate(zip(ins, in_bufs))
    ]
    stores = [
        pltpu.make_async_copy(src, dst, out_sem.at[n])
        for n, (src, dst) in enumerate(zip(out_bufs, outs))
    ]
    gath_ref, gath_att, ret_ref, dtab_ref = in_bufs
    (
        out_ref, dtok_ref, dln1_ref, dwqkv_ref, dbqkv_ref, dbias_ref, dwproj_ref, dln2_ref,
        dwfc1_ref, dbfc1_ref, dwfc2_ref,
    ) = out_bufs
    for n in (0, 2, 1, 3):
        loads[n].start()
    loads[0].wait()
    for n in range(3):
        cols = slice(256 * n, 256 * (n + 1))
        rows = slice(12 * n, 12 * (n + 1))
        dwfc1_ref[:, cols] = gath_ref[0, rows].reshape(C, 256).astype(F32)
    stores[8].start()
    for n in range(3):
        cols = slice(256 * n, 256 * (n + 1))
        rows = slice(12 * n, 12 * (n + 1))
        dwfc2_ref[:, cols] = gath_ref[1, rows].reshape(C, 256).astype(F32)
    stores[10].start()
    for k in range(2):
        dwproj_ref[96 * k : 96 * (k + 1), :] = (
            gath_ref[k, 36:42].reshape(96, 256)[:, 0:C].astype(F32)
        )
    vec = gath_ref[0, 42].astype(F32)
    dbfc1_ref[...] = jnp.concatenate([vec[n : n + 1] for n in range(3)], -1).reshape(HID)
    dln2_ref[...] = vec[3:4, :C].reshape(C)
    for n in (6, 9, 7):
        stores[n].start()
    loads[2].wait()
    for a, dst in enumerate((out_ref, dtok_ref)):
        stage[...] = ret_ref[a].reshape(4 * SLOT, C).astype(F32)
        for h in range(WIN_H):
            for w in range(WIN_W):
                dst[h, w] = stage[slot_rows(h, w), :].astype(BF16)
        stores[a].start()
    loads[1].wait()
    for k in range(2):
        for n in range(2):
            cols = slice(256 * k + 128 * n, 256 * k + 128 * (n + 1))
            dwqkv_ref[:, cols] = gath_att[k, 12 * n : 12 * (n + 1)].reshape(C, 128).astype(F32)
        edge = gath_att[k, 24:27].reshape(48, 128).astype(F32)
        for n in range(2):
            at = 96 * n + 48 * k
            dwqkv_ref[at : at + 48, 512:576] = edge[:, 64 * n : 64 * (n + 1)]
    vec = gath_att[0, 27].astype(F32)
    sums = [
        jnp.concatenate([vec[2 * n : 2 * n + 1], vec[2 * n + 1 : 2 * n + 2, :64]], -1)
        for n in range(4)
    ]
    dbqkv_ref[...] = jnp.concatenate(sums[:3], -1).reshape(3 * C)
    dln1_ref[...] = sums[3].reshape(C)
    for n in (3, 4, 2):
        stores[n].start()
    loads[3].wait()
    for head in range(HEADS):
        dbias_ref[0, head] = dtab_ref[head : head + 1, 0:NREL]
    stores[5].start()
    for store in stores:
        store.wait()


def per_device(
    tokens, cotangent, ln1_gain, w_qkv, b_qkv, bias_table, w_proj, ln2_gain, w_fc1, b_fc1, w_fc2
):
    hbm = pl.BlockSpec(memory_space=pl.ANY)
    order = window_order()
    perm = table_order()
    dma = pltpu.SemaphoreType.DMA
    args = (
        tokens.transpose(1, 2, 0, 3), cotangent.transpose(1, 2, 0, 3), ln1_gain, w_qkv, b_qkv,
        bias_table.transpose(0, 2, 1, 3), w_proj, ln2_gain, w_fc1, b_fc1, w_fc2.T,
        jnp.asarray(order, BF16), jnp.asarray(order.T, BF16),
        jnp.asarray(perm, BF16), jnp.asarray(perm.T, BF16),
        jnp.asarray(cross_pairs()),
    )
    results = pl.pallas_call(
        block_kernel,
        out_shape=(
            jax.ShapeDtypeStruct((2, FC, 16, 256), BF16),
            jax.ShapeDtypeStruct((2, ATT, 16, 128), BF16),
            jax.ShapeDtypeStruct((2, 4, SLOT, C), BF16),
            jax.ShapeDtypeStruct((8, 3456), F32),
        ),
        in_specs=[hbm] * len(args),
        out_specs=(hbm,) * 4,
        scratch_shapes=[pltpu.VMEM(a.shape, a.dtype) for a in args]
        + [
            pltpu.VMEM((4 * SLOT, C), F32),
            pltpu.VMEM((2, 4, SLOT, C), BF16),
            pltpu.VMEM((2, 4, SLOT, C), BF16),
            pltpu.VMEM((2, 4, SLOT, C), BF16),
            pltpu.VMEM((8, 3456), F32),
            pltpu.VMEM((8, 3456), F32),
            pltpu.VMEM((96, 512), F32),
            pltpu.VMEM((3, 128, 128), F32),
            pltpu.VMEM((HEADS, T, T), F32),
            pltpu.VMEM((HEADS, T, T), F32),
            pltpu.VMEM((HEADS, T, T), BF16),
            pltpu.VMEM((HEADS, 160, 384), F32),
            pltpu.VMEM((3, 128, 128), F32),
            pltpu.VMEM((16, 256), F32),
            pltpu.VMEM((PARTS, 16, 384), BF16),
            pltpu.VMEM((STRIPS, 16, 384), BF16),
            pltpu.VMEM((PARTS, 16, 384), BF16),
            pltpu.VMEM((96, 384), BF16),
            pltpu.VMEM((96, 384), BF16),
            pltpu.VMEM((2, FC, 16, 256), BF16),
            pltpu.VMEM((2, ATT, 16, 128), BF16),
            pltpu.VMEM((FC, 16, 256), BF16),
            pltpu.VMEM((ATT, 16, 128), BF16),
            pltpu.VMEM((3, 3, 4, 16, 256), BF16),
            pltpu.VMEM((3, 4, 16, 256), BF16),
            pltpu.VMEM((3, 3, 16, 256), BF16),
            pltpu.VMEM((3, 16, 256), BF16),
            pltpu.VMEM((3, 4, 16, 256), BF16),
            pltpu.VMEM((ROWS - 1, 4, 16, 128), BF16),
            pltpu.VMEM((4, 16, 128), BF16),
            pltpu.VMEM((STRIPS, 4, 16, 128), BF16),
            pltpu.VMEM((2, FC, 16, 256), BF16),
            pltpu.VMEM((2, ATT, 16, 128), BF16),
            pltpu.VMEM((8, 3456), F32),
            dma((len(args),)), dma((5,)),
            dma((2, 3)), dma((2, 3)), dma((2, 3)), dma((2, 3)),
            dma((2,)), dma((2,)), dma((7,)), dma((7,)),
            dma((5,)), dma((5,)), dma((2,)), dma((2,)),
        ],
        compiler_params=pltpu.CompilerParams(
            collective_id=0, has_side_effects=True, vmem_limit_bytes=VMEM_LIMIT
        ),
    )(*args)
    shape = jax.ShapeDtypeStruct
    grid_shape = (WIN_H, WIN_W, WIN_Z, C)
    results_out = (
        shape(grid_shape, BF16), shape(grid_shape, BF16),
        shape((C,), F32), shape((C, 3 * C), F32), shape((3 * C,), F32),
        shape((1, HEADS, 1, NREL), F32), shape((C, C), F32), shape((C,), F32),
        shape((C, HID), F32), shape((HID,), F32), shape((C, HID), F32),
    )
    outs = pl.pallas_call(
        output_kernel,
        out_shape=results_out,
        in_specs=[hbm] * 4,
        out_specs=(hbm,) * 11,
        scratch_shapes=[pltpu.VMEM(a.shape, a.dtype) for a in tuple(results) + results_out]
        + [pltpu.VMEM((4 * SLOT, C), F32), dma((4,)), dma((11,))],
        compiler_params=pltpu.CompilerParams(vmem_limit_bytes=VMEM_LIMIT),
    )(*results)
    out, d_tok, d_ln1, d_wqkv, d_bqkv, d_bias, d_wproj, d_ln2, d_wfc1, d_bfc1, d_wfc2 = outs
    return (
        out.transpose(2, 0, 1, 3), d_tok.transpose(2, 0, 1, 3), d_ln1, d_wqkv, d_bqkv,
        d_bias.transpose(0, 2, 1, 3), d_wproj, d_ln2, d_wfc1, d_bfc1, d_wfc2.T,
    )


def solution(mesh):
    grid = P(None, "lat", "lon", None)
    rows = P(None, "lat", None, None)
    return jax.shard_map(
        per_device,
        mesh=mesh,
        in_specs=(grid, grid, P(), P(), P(), rows, P(), P(), P(), P(), P()),
        out_specs=(grid, grid, P(), P(), P(), rows, P(), P(), P(), P(), P()),
        check_vma=False,
    )
```

```python
import jax
import jax.numpy as jnp
import numpy as np
from jax import lax
from jax.experimental import pallas as pl
from jax.experimental.pallas import tpu as pltpu
from jax.sharding import PartitionSpec as P

HEADS = 6
WIN_Z = 2
WIN_H = 6
WIN_W = 12
SPAN = 2 * WIN_W - 1
GROUPS = WIN_Z * WIN_H
T = GROUPS * WIN_W
C = 192
HID = 768
HEAD = C // HEADS
NREL = GROUPS * GROUPS * SPAN
SLOT = 48
FC = 48
ATT = 32
ROWS = 8
BANDS = 16
STRIPS = 8
PARTS = 6
EPSILON = 1e-05
VMEM_LIMIT = 56 * 1024 * 1024
FACTOR = HEAD ** (-0.5)
LOG2E = 1.4426950408889634
F32 = jnp.float32
BF16 = jnp.bfloat16
MESH = pl.DeviceIdType.MESH


def window_order():
    grid = np.zeros((T, 4 * SLOT), np.float32)
    for w in range(WIN_W):
        for z in range(WIN_Z):
            for h in range(WIN_H):
                slot = (h // 3) * 2 + w // 6
                grid[w * GROUPS + z * WIN_H + h, slot * SLOT + (h % 3) * 12 + (w % 6) * 2 + z] = 1
    return grid


def table_order():
    grid = np.zeros((512, 384), np.float32)
    for z in range(WIN_Z):
        for h in range(WIN_H):
            for i in range(SPAN):
                grid[z * 256 + h * SPAN + i, (SPAN - 1 - i) * GROUPS + z * WIN_H + h] = 1
    return grid


def cross_pairs():
    g = np.arange(96)[:, None] // 8 % WIN_H
    q = np.arange(384)[None, :] % GROUPS % WIN_H
    return np.where((g < 3) != (q < 3), -1e30, 0.0).astype(np.float32)


def dot(a, b):
    return jnp.dot(a, b, preferred_element_type=F32)


def dot_nt(a, b):
    return lax.dot_general(a, b, (((1,), (1,)), ((), ())), preferred_element_type=F32)


def dot_tn(a, b):
    return lax.dot_general(a, b, (((0,), (0,)), ((), ())), preferred_element_type=F32)


def normalize(values, gain):
    average = jnp.mean(values, -1, keepdims=True)
    centered = values - average
    inv = lax.rsqrt(jnp.mean(centered * centered, -1, keepdims=True) + EPSILON)
    hat = centered * inv
    return hat * gain, hat, inv


def norm_back(hat, inv, gain, grad):
    scaled = grad * gain
    return inv * (
        scaled
        - jnp.mean(scaled, -1, keepdims=True)
        - hat * jnp.mean(scaled * hat, -1, keepdims=True)
    )


def slot_rows(h, w):
    at = ((h // 3) * 2 + w // 6) * SLOT + (h % 3) * 12 + (w % 6) * 2
    return slice(at, at + 2)


def block_kernel(
    tok_any, cot_any, g1_any, wqkv_any, bqkv_any, table_any, wproj_any, g2_any, wfc1_any,
    bfc1_any, wfc2_any, order_any, perm_any, cross_any,
    gath_fc_out, gath_att_out, ret_out, dtab_out,
    tok_ref, cot_ref, g1_ref, wqkv_ref, bqkv_ref, table_ref, wproj_ref, g2_ref, wfc1_ref,
    bfc1_ref, wfc2_ref, order_ref, perm_ref, cross_ref,
    stage, send, arrive, out_stage,
    tabw, tab15, tin, ymat, bias, prob, wide_rows, wide_cols, dsc, dmat, vec,
    bsend, brecv, bfin, bbs, bbr,
    parts_fc, parts_att, core_fc, core_att, fold1, sum1, fold2, sum2, fold3, fold_att, sum_att,
    mid_att, gath_fc, gath_att, dtab_ref,
    in_sem, out_sem,
    ex_send, ex_recv, rt_send, rt_recv, one_send, one_recv, p_send, p_recv, f_send, f_recv,
    a_send, a_recv, b_send, b_recv,
):
    places = (
        (table_any, table_ref), (tok_any, tok_ref), (perm_any, perm_ref), (cot_any, cot_ref),
        (cross_any, cross_ref), (order_any, order_ref), (g1_any, g1_ref), (wqkv_any, wqkv_ref),
        (bqkv_any, bqkv_ref), (wproj_any, wproj_ref), (g2_any, g2_ref), (wfc1_any, wfc1_ref),
        (bfc1_any, bfc1_ref), (wfc2_any, wfc2_ref),
    )
    loads = [pltpu.make_async_copy(src, dst, in_sem.at[n]) for n, (src, dst) in enumerate(places)]
    loads[1].start()
    lon = lax.axis_index("lon")
    lat = lax.axis_index("lat")
    core = lax.rem(lat, 2)
    other = 1 - core
    pair_row = lat // 2
    east = lax.rem(lon + 1, STRIPS)
    west = lax.rem(lon + STRIPS - 1, STRIPS)
    south = lax.rem(lat + 1, BANDS)
    north = lax.rem(lat + BANDS - 1, BANDS)
    sibling = (lon, lat - core + other)

    spot = (lax.rem(pair_row, 4), lon // 2, lax.rem(lon, 2) * 2 + lat // 8)

    def on_axis(axis, at):
        if axis == 0:
            return (lon, lat // 8 * 8 + at * 2 + core)
        if axis == 1:
            return (at * 2 + lax.rem(lon, 2), lat)
        return (spot[1] * 2 + at // 2, lax.rem(at, 2) * 8 + spot[0] * 2 + core)

    def strip(d):
        return lax.rem(lon + d, STRIPS)

    def row_of(d):
        return lax.rem(pair_row + d, ROWS)

    barrier = pltpu.get_barrier_semaphore()

    def greet(target):
        pl.semaphore_signal(barrier, inc=1, device_id=target, device_id_type=MESH)

    for target in ((lon, south), (lon, north), (east, south), (west, north), sibling):
        greet(target)
    greet(on_axis(2, 3 - spot[2]))
    for d in range(1, 8):
        greet((strip(d), lat))
        greet((lon, row_of(d) * 2 + core))
    loads[0].start()
    for load in loads[2:]:
        load.start()

    stage[...] = jnp.zeros_like(stage)

    def quadrants(a, src):
        loads[(1, 3)[a]].wait()
        for h in range(WIN_H):
            for w in range(WIN_W):
                stage[slot_rows(h, w), :] = src[h, w].astype(F32)
        send[a] = stage[...].astype(BF16).reshape(4, SLOT, C)
        arrive[a, 3] = send[a, 0]

    quadrants(0, tok_ref)
    pl.semaphore_wait(barrier, 20)

    ahead = ((east, lat), (lon, south), (east, south))
    behind = ((west, lat), (lon, north), (west, north))

    def exchange(a, i):
        return pltpu.make_async_remote_copy(
            src_ref=send.at[a, i + 1],
            dst_ref=arrive.at[a, 2 - i],
            send_sem=ex_send.at[a, i],
            recv_sem=ex_recv.at[a, i],
            device_id=ahead[i],
            device_id_type=MESH,
        )

    def table_copy():
        return pltpu.make_async_remote_copy(
            src_ref=tabw,
            dst_ref=tab15,
            send_sem=one_send.at[0],
            recv_sem=one_recv.at[0],
            device_id=(lon, south),
            device_id_type=MESH,
        )

    for i in range(3):
        exchange(0, i).start()

    tabw[...] = jnp.zeros_like(tabw)
    loads[0].wait()
    for head in range(HEADS):
        tabw[head : head + 1, 0:NREL] = table_ref[0, head]

    @pl.when(lat == BANDS - 1)
    def _():
        table_copy().start()

    quadrants(1, cot_ref)
    for i in range(3):
        exchange(1, i).start()

    tin[...] = jnp.zeros_like(tin)

    def spread(src, zp, zq, hp, width):
        j = (zp * WIN_Z + zq) * WIN_H + hp
        first = j * WIN_H * SPAN
        base = first // 128 * 128
        wide = src[:, base : base + 384]
        moved = pltpu.roll(wide, (384 - (first - base)) % 384, axis=1)
        g = zp * WIN_H + hp
        tin[g * 8 : g * 8 + 8, zq * 256 : zq * 256 + width] = moved[:, :width]

    for zp in range(WIN_Z):
        for zq in range(WIN_Z):
            for hp in range(WIN_H):
                spread(tabw, zp, zq, hp, WIN_H * SPAN)

    @pl.when(lat == 0)
    def _():
        table_copy().wait_recv()
        for zp in range(WIN_Z):
            for zq in range(WIN_Z):
                for hp in range(3):
                    spread(tab15, zp, zq, hp, 3 * SPAN)

    whole = tin[...]
    high = whole.astype(BF16)
    rest = whole - high.astype(F32)
    middle = rest.astype(BF16)
    low = (rest - middle.astype(F32)).astype(BF16)
    loads[2].wait()
    perm = perm_ref[...]
    spread_rows = (dot(high, perm) + dot(middle, perm) + dot(low, perm)) * LOG2E
    for n in range(3):
        ymat[n, 0:96, :] = spread_rows[:, 128 * n : 128 * (n + 1)]
        ymat[n, 96:128, :] = jnp.zeros((32, 128), F32)
    loads[4].wait()

    @pl.when(lat == 0)
    def _():
        for n in range(3):
            ymat[n, 0:96, :] = ymat[n, 0:96, :] + cross_ref[:, 128 * n : 128 * (n + 1)]

    for head in range(HEADS):
        rows = jnp.concatenate(
            [ymat[n, pl.ds(head, 16, stride=8), :] for n in range(3)], -1
        )
        for w in range(WIN_W):
            moved = pltpu.roll(rows, (384 - (WIN_W - 1 - w) * GROUPS) % 384, axis=1)
            bias[head, w * GROUPS : (w + 1) * GROUPS, :] = moved[:GROUPS, :T]

    for n in range(5, 14):
        loads[n].wait()
    lane = lax.broadcasted_iota(jnp.int32, (16, C), 1)
    ones = [
        jnp.where((lane >= HEAD * i) & (lane < HEAD * (i + 1)), 1.0, 0.0).astype(BF16)[0:1]
        for i in range(HEADS)
    ]
    order = order_ref[...]
    back = order.T
    gain1 = g1_ref[...].reshape(1, C)
    gain2 = g2_ref[...].reshape(1, C)

    def arrived(a):
        for i in range(3):
            exchange(a, i).wait_recv()
        return dot(order, arrive[a].reshape(4 * SLOT, C))

    tokens = arrived(0)
    normed, hat1, inv1 = normalize(tokens, gain1)
    first = normed.astype(BF16)
    qkv = (dot(first, wqkv_ref[...]) + bqkv_ref[...].reshape(1, 3 * C)).astype(BF16)
    queries = qkv[:, 0:C]
    keys = qkv[:, C : 2 * C]
    values = qkv[:, 2 * C : 3 * C]
    queries_t = queries.T
    wide_rows[...] = jnp.zeros_like(wide_rows)
    wide_cols[...] = jnp.zeros_like(wide_cols)
    for head in range(HEADS):
        wide_cols[256 * head : 256 * head + T, :] = values * ones[head]
    for head in range(HEADS):
        q = queries * ones[head]
        scores = dot_nt(q, keys) * (FACTOR * LOG2E) + bias[head]
        top = jnp.max(scores, -1, keepdims=True)
        raised = jnp.exp2(scores - top)
        probs = raised * (1.0 / jnp.sum(raised, -1, keepdims=True))
        prob[head] = probs
        probs_low = probs.astype(BF16)
        wide_rows[:, 256 * head : 256 * head + T] = probs_low
    mixed = dot(wide_rows[...], wide_cols[...]).astype(BF16)
    inner = tokens + dot(mixed, wproj_ref[...]).astype(BF16).astype(F32)

    def remote(src, dst, send_sem, recv_sem, target):
        return pltpu.make_async_remote_copy(
            src_ref=src, dst_ref=dst, send_sem=send_sem, recv_sem=recv_sem,
            device_id=target, device_id_type=MESH,
        )

    def wait_bytes(ref, sem):
        pltpu.make_async_copy(ref, ref, sem).wait()

    def add(*terms):
        total = terms[0].astype(F32)
        for term in terms[1:]:
            total = total + term.astype(F32)
        return total.astype(BF16)

    axes = [(n, (n + 1) % 3, (n + 2) % 3) for n in range(3)]
    places = [tuple(spot[axis] for axis in order) for order in axes]

    def block(n, i):
        return pl.ds(n * 16 + i * 4, 4)

    def unit(n):
        return n * 16 + places[n][0] * 4 + places[n][1]

    def part_to_line(n, stage_no, which, src, dst):
        for d in range(1, 4):
            at = lax.rem(places[n][which] + d, 4)
            remote(
                src(n, at), dst(n, d), f_send.at[stage_no], f_recv.at[stage_no],
                on_axis(axes[n][which], at),
            ).start()

    def to_line(stage_no, which, src, dst):
        for n in range(3):
            part_to_line(n, stage_no, which, src, dst)

    pair_fc = [
        remote(
            parts_fc.at[other, pl.ds(12 * n, 12)], core_fc.at[pl.ds(12 * n, 12)],
            p_send.at[n], p_recv.at[n], sibling,
        )
        for n in range(4)
    ]
    swap_fc = remote(
        gath_fc.at[core], gath_fc_out.at[core], f_send.at[6], f_recv.at[6], sibling
    )
    pair_att = remote(parts_att.at[other], core_att, a_send.at[0], a_recv.at[0], sibling)
    swap_att = remote(
        gath_att.at[core], gath_att_out.at[core], a_send.at[4], a_recv.at[4], sibling
    )
    keep = [
        pltpu.make_async_copy(src, dst, out_sem.at[n])
        for n, (src, dst) in enumerate((
            (out_stage.at[0, 3], ret_out.at[0, 0]), (out_stage.at[1, 3], ret_out.at[1, 0]),
            (dtab_ref, dtab_out), (gath_fc.at[core], gath_fc_out.at[core]),
            (gath_att.at[core], gath_att_out.at[core]),
        ))
    ]

    def early1():
        for n in range(3):
            if n == 0:
                pair_fc[0].wait_recv()
            pair_fc[n + 1].wait_recv()
            rows = pl.ds(16 * n, 16)
            parts_fc[core, rows] = add(parts_fc[core, rows], core_fc[rows])
            part_to_line(
                n, 1, 0, lambda n, at: parts_fc.at[core, block(n, at)],
                lambda n, d: fold1.at[n, d - 1],
            )

    def early2():
        wait_bytes(fold1, f_recv.at[1])
        for n in range(3):
            own = parts_fc[core, block(n, places[n][0])]
            sum1[n] = add(own, fold1[n, 0], fold1[n, 1], fold1[n, 2])
        to_line(2, 1, lambda n, at: sum1.at[n, at], lambda n, d: fold2.at[n, d - 1])

    def early3():
        wait_bytes(fold2, f_recv.at[2])
        for n in range(3):
            own = sum1[n, places[n][1]]
            sum2[n] = add(own, fold2[n, 0], fold2[n, 1], fold2[n, 2])
            fold3[n, places[n][2]] = sum2[n]
        to_line(3, 2, lambda n, at: sum2.at[n], lambda n, d: fold3.at[n, places[n][2]])

    def early4():
        wait_bytes(fold2, f_recv.at[3])
        for n in range(3):
            gath_fc[core, unit(n)] = add(*[fold3[n, i] for i in range(4)])
        to_line(
            4, 1, lambda n, at: gath_fc.at[core, unit(n)], lambda n, d: gath_fc.at[core, unit(n)]
        )

    def early5():
        wait_bytes(fold2, f_recv.at[4])
        to_line(
            5, 0,
            lambda n, at: gath_fc.at[core, block(n, places[n][0])],
            lambda n, d: gath_fc.at[core, block(n, places[n][0])],
        )

    def early6():
        wait_bytes(fold1, f_recv.at[5])
        swap_fc.start()
        keep[3].start()

    own_rows = pl.ds(pair_row * 4, 4)

    def late1():
        pair_att.wait_recv()
        parts_att[core] = add(parts_att[core], core_att[...])
        for d in range(1, ROWS):
            remote(
                parts_att.at[core, pl.ds(row_of(d) * 4, 4)], fold_att.at[d - 1],
                a_send.at[1], a_recv.at[1], (lon, row_of(d) * 2 + core),
            ).start()

    def late2():
        wait_bytes(fold_att, a_recv.at[1])
        sum_att[...] = add(parts_att[core, own_rows], *[fold_att[d] for d in range(ROWS - 1)])
        mid_att[lon] = sum_att[...]
        for d in range(1, STRIPS):
            remote(
                sum_att, mid_att.at[lon], a_send.at[2], a_recv.at[2], (strip(d), lat)
            ).start()

    def late3():
        wait_bytes(fold_att, a_recv.at[2])
        gath_att[core, own_rows] = add(*[mid_att[i] for i in range(STRIPS)])
        for d in range(1, ROWS):
            remote(
                gath_att.at[core, own_rows], gath_att.at[core, own_rows],
                a_send.at[3], a_recv.at[3], (lon, row_of(d) * 2 + core),
            ).start()

    def late4():
        wait_bytes(fold_att, a_recv.at[3])
        swap_att.start()
        keep[4].start()

    cot = arrived(1)
    cot_low = cot.astype(BF16)
    normed, hat2, inv2 = normalize(inner, gain2)
    second = normed.astype(BF16)
    second_t = second.T
    cot_t = cot_low.T
    total = inner
    grad_second = jnp.zeros((T, C), F32)
    bfc1 = bfc1_ref[...].reshape(1, HID)
    vec[...] = jnp.zeros_like(vec)
    for n in range(3):
        cols = slice(256 * n, 256 * (n + 1))
        pre = dot(second, wfc1_ref[:, cols]) + bfc1[:, cols]
        cdf = 0.5 * (1.0 + lax.erf(pre * 0.7071067811865476))
        density = jnp.exp(-0.5 * pre * pre) * 0.3989422804014327
        act = (pre * cdf).astype(BF16)
        total = total + dot_nt(act, wfc2_ref[:, cols])
        grad_pre = (dot(cot_low, wfc2_ref[:, cols]) * (cdf + pre * density)).astype(BF16)
        grad_second = grad_second + dot_nt(grad_pre, wfc1_ref[:, cols])
        parts_fc[0, 12 * n : 12 * (n + 1)] = dot(second_t, grad_pre).astype(BF16).reshape(12, 16, 256)
        parts_fc[1, 12 * n : 12 * (n + 1)] = dot(cot_t, act).astype(BF16).reshape(12, 16, 256)
        vec[n : n + 1, :] = jnp.sum(grad_pre.astype(F32), 0, keepdims=True)
        pair_fc[n].start()

    def give_back(a, i):
        return pltpu.make_async_remote_copy(
            src_ref=out_stage.at[a, 2 - i],
            dst_ref=ret_out.at[a, i + 1],
            send_sem=rt_send.at[a, i],
            recv_sem=rt_recv.at[a, i],
            device_id=behind[i],
            device_id_type=MESH,
        )

    def hand_out(a, field):
        out_stage[a] = dot(back, field).astype(BF16).reshape(4, SLOT, C)
        for i in range(3):
            give_back(a, i).start()
        keep[a].start()

    grad_inner = cot + norm_back(hat2, inv2, gain2, grad_second)
    grad_att = grad_inner.astype(BF16)
    proj_grad = dot_tn(mixed, grad_att).astype(BF16)
    proj_grad = jnp.concatenate([proj_grad, jnp.zeros((C, 64), BF16)], -1).reshape(12, 16, 256)
    parts_fc[0, 36:42] = proj_grad[:6]
    parts_fc[1, 36:42] = proj_grad[6:]
    vec[3:4, 0:C] = jnp.sum(grad_second * hat2, 0, keepdims=True)
    parts_fc[0, 42] = vec[...].astype(BF16)
    parts_fc[1, 42] = jnp.zeros((16, 256), BF16)
    parts_fc[:, 43:] = jnp.zeros((2, FC - 43, 16, 256), BF16)
    pair_fc[3].start()
    hand_out(0, total.astype(BF16))

    grad_mixed = dot_nt(grad_att, wproj_ref[...]).astype(BF16)
    grad_mixed_t = grad_mixed.T
    dsc[...] = jnp.zeros_like(dsc)
    for head in range(HEADS):
        wide_cols[256 * head : 256 * head + T, :] = keys * ones[head]
    grad_k_t = []
    grad_v_t = []
    for head in range(HEADS):
        rows = slice(HEAD * head, HEAD * (head + 1))
        gm = grad_mixed * ones[head]
        probs = prob[head]
        grad_probs = dot_nt(gm, values)
        inside = jnp.sum(probs * grad_probs, -1, keepdims=True)
        grad_scores = probs * (grad_probs - inside)
        dsc[head, 0:T, 0:T] = grad_scores
        scaled = (grad_scores * FACTOR).astype(BF16)
        grad_v_t.append(
            dot(grad_mixed_t[rows], wide_rows[:, 256 * head : 256 * head + T])
        )
        wide_rows[:, 256 * head : 256 * head + T] = scaled
        grad_k_t.append(dot(queries_t[rows], scaled))
        if head == 1:
            early1()
    grad_q = dot(wide_rows[...], wide_cols[...])
    grad_k = jnp.concatenate(grad_k_t, 0).T
    grad_v = jnp.concatenate(grad_v_t, 0).T

    grad_qkv = jnp.concatenate([grad_q, grad_k, grad_v], -1).astype(BF16)
    wide = dot_tn(first, grad_qkv).astype(BF16)
    for n in range(4):
        parts_att[n // 2, n % 2 * 12 : n % 2 * 12 + 12] = (
            wide[:, 128 * n : 128 * (n + 1)].reshape(12, 16, 128)
        )
    edge = jnp.concatenate([wide[:96, 512:576], wide[96:, 512:576]], -1).reshape(6, 16, 128)
    parts_att[0, 24:27] = edge[:3]
    parts_att[1, 24:27] = edge[3:]
    grad_first = dot_nt(grad_qkv, wqkv_ref[...]).astype(BF16).astype(F32)
    vec[...] = jnp.zeros_like(vec)
    sums = jnp.sum(grad_qkv.astype(F32), 0, keepdims=True)
    sums = [sums[:, C * n : C * (n + 1)] for n in range(3)]
    sums.append(jnp.sum(grad_first * hat1, 0, keepdims=True))
    for n in range(4):
        vec[2 * n : 2 * n + 1, 0:128] = sums[n][:, 0:128]
        vec[2 * n + 1 : 2 * n + 2, 0:64] = sums[n][:, 128:C]
    parts_att[0, 27] = vec[:, 0:128].astype(BF16)
    parts_att[1, 27] = jnp.zeros((16, 128), BF16)
    parts_att[:, 28:] = jnp.zeros((2, ATT - 28, 16, 128), BF16)
    pair_att.start()
    d_tokens = grad_inner + norm_back(hat1, inv1, gain1, grad_first)
    hand_out(1, d_tokens.astype(BF16))
    early2()

    dmat[...] = jnp.zeros_like(dmat)
    for head in range(HEADS):
        if head == 3:
            late1()
        acc = jnp.zeros((16, 384), F32)
        for w in range(WIN_W):
            acc = acc + pltpu.roll(
                dsc[head, w * GROUPS : w * GROUPS + 16, :], (WIN_W - 1 - w) * GROUPS, axis=1
            )
        for n in range(3):
            dmat[n, pl.ds(head, 16, stride=8), :] = acc[:, 128 * n : 128 * (n + 1)]

    def table_grad():
        return jnp.concatenate([dmat[n, 0:96, :] for n in range(3)], -1)

    def keep_table(field):
        for n in range(3):
            dmat[n, 0:96, :] = field[:, 128 * n : 128 * (n + 1)]

    def edge_copy():
        return pltpu.make_async_remote_copy(
            src_ref=bbs,
            dst_ref=bbr,
            send_sem=one_send.at[1],
            recv_sem=one_recv.at[1],
            device_id=(lon, north),
            device_id_type=MESH,
        )

    @pl.when(lat == 0)
    def _():
        row = lax.broadcasted_iota(jnp.int32, (96, 384), 0)
        upper = (row < 24) | ((row >= 48) & (row < 72))
        full = table_grad()
        bbs[...] = jnp.where(upper, full, 0.0).astype(BF16)
        edge_copy().start()
        keep_table(jnp.where(upper, 0.0, full))

    @pl.when(lat == BANDS - 1)
    def _():
        edge_copy().wait_recv()
        keep_table(table_grad() + bbr[...].astype(F32))

    bsend[...] = table_grad().astype(BF16).reshape(PARTS, 16, 384)

    for owner in range(PARTS):
        @pl.when(lon != owner)
        def _():
            pltpu.make_async_remote_copy(
                src_ref=bsend.at[owner],
                dst_ref=brecv.at[lon],
                send_sem=b_send.at[0],
                recv_sem=b_recv.at[0],
                device_id=(owner, lat),
                device_id_type=MESH,
            ).start()

    early3()
    late2()
    early4()
    seven = brecv.at[pl.ds(0, STRIPS - 1)]

    @pl.when(lon < PARTS)
    def _():
        brecv[lon] = bsend[lon]
        wait_bytes(seven, b_recv.at[0])
        bfin[lon] = jnp.sum(brecv[...].astype(F32), 0).astype(BF16)
        for d in range(1, STRIPS):
            pltpu.make_async_remote_copy(
                src_ref=bfin.at[lon],
                dst_ref=bfin.at[lon],
                send_sem=b_send.at[1],
                recv_sem=b_recv.at[1],
                device_id=(strip(d), lat),
                device_id_type=MESH,
            ).start()

    early5()
    late3()

    @pl.when(lon < PARTS)
    def _():
        wait_bytes(bfin.at[pl.ds(0, PARTS - 1)], b_recv.at[1])

    @pl.when(lon >= PARTS)
    def _():
        wait_bytes(bfin, b_recv.at[1])

    tin[...] = dot_nt(bfin[...].reshape(96, 384), perm_ref[...])
    dtab_ref[...] = jnp.zeros_like(dtab_ref)
    for zp in range(WIN_Z):
        for zq in range(WIN_Z):
            for hp in range(WIN_H):
                j = (zp * WIN_Z + zq) * WIN_H + hp
                first_lane = j * WIN_H * SPAN
                base = first_lane // 128 * 128
                g = zp * WIN_H + hp
                piece = tin[g * 8 : g * 8 + 8, zq * 256 : zq * 256 + 256]
                piece = jnp.concatenate([piece, jnp.zeros((8, 128), F32)], -1)
                moved = pltpu.roll(piece, first_lane - base, axis=1)
                dtab_ref[:, base : base + 384] = dtab_ref[:, base : base + 384] + moved

    keep[2].start()
    early6()
    late4()

    for a in range(2):
        for i in range(3):
            exchange(a, i).wait_send()
            give_back(a, i).wait()

    @pl.when(lat == BANDS - 1)
    def _():
        table_copy().wait_send()

    @pl.when(lat == 0)
    def _():
        edge_copy().wait_send()

    for copy in pair_fc:
        copy.wait_send()
    for stage_no, ref in ((1, fold1), (2, fold2), (3, fold2), (4, fold2), (5, fold1)):
        wait_bytes(ref, f_send.at[stage_no])
    pair_att.wait_send()
    for stage_no in (1, 2, 3):
        wait_bytes(fold_att, a_send.at[stage_no])

    @pl.when(lon < PARTS)
    def _():
        wait_bytes(bsend.at[pl.ds(0, PARTS - 1)], b_send.at[0])
        wait_bytes(seven, b_send.at[1])

    @pl.when(lon >= PARTS)
    def _():
        wait_bytes(bsend, b_send.at[0])

    for copy in keep:
        copy.wait()
    swap_fc.wait()
    swap_att.wait()


def output_kernel(*refs):
    ins, outs = refs[:4], refs[4:15]
    in_bufs, out_bufs = refs[15:19], refs[19:30]
    stage, in_sem, out_sem = refs[30:]
    loads = [
        pltpu.make_async_copy(src, dst, in_sem.at[n])
        for n, (src, dst) in enumerate(zip(ins, in_bufs))
    ]
    stores = [
        pltpu.make_async_copy(src, dst, out_sem.at[n])
        for n, (src, dst) in enumerate(zip(out_bufs, outs))
    ]
    gath_ref, gath_att, ret_ref, dtab_ref = in_bufs
    (
        out_ref, dtok_ref, dln1_ref, dwqkv_ref, dbqkv_ref, dbias_ref, dwproj_ref, dln2_ref,
        dwfc1_ref, dbfc1_ref, dwfc2_ref,
    ) = out_bufs
    for n in (0, 2, 1, 3):
        loads[n].start()
    loads[0].wait()
    for n in range(3):
        cols = slice(256 * n, 256 * (n + 1))
        rows = slice(12 * n, 12 * (n + 1))
        dwfc1_ref[:, cols] = gath_ref[0, rows].reshape(C, 256).astype(F32)
    stores[8].start()
    for n in range(3):
        cols = slice(256 * n, 256 * (n + 1))
        rows = slice(12 * n, 12 * (n + 1))
        dwfc2_ref[:, cols] = gath_ref[1, rows].reshape(C, 256).astype(F32)
    stores[10].start()
    for k in range(2):
        dwproj_ref[96 * k : 96 * (k + 1), :] = (
            gath_ref[k, 36:42].reshape(96, 256)[:, 0:C].astype(F32)
        )
    vec = gath_ref[0, 42].astype(F32)
    dbfc1_ref[...] = jnp.concatenate([vec[n : n + 1] for n in range(3)], -1).reshape(HID)
    dln2_ref[...] = vec[3:4, :C].reshape(C)
    for n in (6, 9, 7):
        stores[n].start()
    loads[2].wait()
    for a, dst in enumerate((out_ref, dtok_ref)):
        stage[...] = ret_ref[a].reshape(4 * SLOT, C).astype(F32)
        for h in range(WIN_H):
            for w in range(WIN_W):
                dst[h, w] = stage[slot_rows(h, w), :].astype(BF16)
        stores[a].start()
    loads[1].wait()
    for k in range(2):
        for n in range(2):
            cols = slice(256 * k + 128 * n, 256 * k + 128 * (n + 1))
            dwqkv_ref[:, cols] = gath_att[k, 12 * n : 12 * (n + 1)].reshape(C, 128).astype(F32)
        edge = gath_att[k, 24:27].reshape(48, 128).astype(F32)
        for n in range(2):
            at = 96 * n + 48 * k
            dwqkv_ref[at : at + 48, 512:576] = edge[:, 64 * n : 64 * (n + 1)]
    vec = gath_att[0, 27].astype(F32)
    sums = [
        jnp.concatenate([vec[2 * n : 2 * n + 1], vec[2 * n + 1 : 2 * n + 2, :64]], -1)
        for n in range(4)
    ]
    dbqkv_ref[...] = jnp.concatenate(sums[:3], -1).reshape(3 * C)
    dln1_ref[...] = sums[3].reshape(C)
    for n in (3, 4, 2):
        stores[n].start()
    loads[3].wait()
    for head in range(HEADS):
        dbias_ref[0, head] = dtab_ref[head : head + 1, 0:NREL]
    stores[5].start()
    for store in stores:
        store.wait()


def per_device(
    tokens, cotangent, ln1_gain, w_qkv, b_qkv, bias_table, w_proj, ln2_gain, w_fc1, b_fc1, w_fc2
):
    hbm = pl.BlockSpec(memory_space=pl.ANY)
    order = window_order()
    perm = table_order()
    dma = pltpu.SemaphoreType.DMA
    args = (
        tokens.transpose(1, 2, 0, 3), cotangent.transpose(1, 2, 0, 3), ln1_gain, w_qkv, b_qkv,
        bias_table.transpose(0, 2, 1, 3), w_proj, ln2_gain, w_fc1, b_fc1, w_fc2.T,
        jnp.asarray(order, BF16), jnp.asarray(perm, BF16), jnp.asarray(cross_pairs()),
    )
    results = pl.pallas_call(
        block_kernel,
        out_shape=(
            jax.ShapeDtypeStruct((2, FC, 16, 256), BF16),
            jax.ShapeDtypeStruct((2, ATT, 16, 128), BF16),
            jax.ShapeDtypeStruct((2, 4, SLOT, C), BF16),
            jax.ShapeDtypeStruct((8, 3456), F32),
        ),
        in_specs=[hbm] * len(args),
        out_specs=(hbm,) * 4,
        scratch_shapes=[pltpu.VMEM(a.shape, a.dtype) for a in args]
        + [
            pltpu.VMEM((4 * SLOT, C), F32),
            pltpu.VMEM((2, 4, SLOT, C), BF16),
            pltpu.VMEM((2, 4, SLOT, C), BF16),
            pltpu.VMEM((2, 4, SLOT, C), BF16),
            pltpu.VMEM((8, 3456), F32),
            pltpu.VMEM((8, 3456), F32),
            pltpu.VMEM((96, 512), F32),
            pltpu.VMEM((3, 128, 128), F32),
            pltpu.VMEM((HEADS, T, T), F32),
            pltpu.VMEM((HEADS, T, T), F32),
            pltpu.VMEM((T, HEADS * 256), BF16),
            pltpu.VMEM((HEADS * 256, C), BF16),
            pltpu.VMEM((HEADS, 160, 384), F32),
            pltpu.VMEM((3, 128, 128), F32),
            pltpu.VMEM((16, 256), F32),
            pltpu.VMEM((PARTS, 16, 384), BF16),
            pltpu.VMEM((STRIPS, 16, 384), BF16),
            pltpu.VMEM((PARTS, 16, 384), BF16),
            pltpu.VMEM((96, 384), BF16),
            pltpu.VMEM((96, 384), BF16),
            pltpu.VMEM((2, FC, 16, 256), BF16),
            pltpu.VMEM((2, ATT, 16, 128), BF16),
            pltpu.VMEM((FC, 16, 256), BF16),
            pltpu.VMEM((ATT, 16, 128), BF16),
            pltpu.VMEM((3, 3, 4, 16, 256), BF16),
            pltpu.VMEM((3, 4, 16, 256), BF16),
            pltpu.VMEM((3, 3, 16, 256), BF16),
            pltpu.VMEM((3, 16, 256), BF16),
            pltpu.VMEM((3, 4, 16, 256), BF16),
            pltpu.VMEM((ROWS - 1, 4, 16, 128), BF16),
            pltpu.VMEM((4, 16, 128), BF16),
            pltpu.VMEM((STRIPS, 4, 16, 128), BF16),
            pltpu.VMEM((2, FC, 16, 256), BF16),
            pltpu.VMEM((2, ATT, 16, 128), BF16),
            pltpu.VMEM((8, 3456), F32),
            dma((len(args),)), dma((5,)),
            dma((2, 3)), dma((2, 3)), dma((2, 3)), dma((2, 3)),
            dma((2,)), dma((2,)), dma((4,)), dma((4,)), dma((7,)), dma((7,)),
            dma((5,)), dma((5,)), dma((2,)), dma((2,)),
        ],
        compiler_params=pltpu.CompilerParams(
            collective_id=0, has_side_effects=True, vmem_limit_bytes=VMEM_LIMIT
        ),
    )(*args)
    shape = jax.ShapeDtypeStruct
    grid_shape = (WIN_H, WIN_W, WIN_Z, C)
    results_out = (
        shape(grid_shape, BF16), shape(grid_shape, BF16),
        shape((C,), F32), shape((C, 3 * C), F32), shape((3 * C,), F32),
        shape((1, HEADS, 1, NREL), F32), shape((C, C), F32), shape((C,), F32),
        shape((C, HID), F32), shape((HID,), F32), shape((C, HID), F32),
    )
    outs = pl.pallas_call(
        output_kernel,
        out_shape=results_out,
        in_specs=[hbm] * 4,
        out_specs=(hbm,) * 11,
        scratch_shapes=[pltpu.VMEM(a.shape, a.dtype) for a in tuple(results) + results_out]
        + [pltpu.VMEM((4 * SLOT, C), F32), dma((4,)), dma((11,))],
        compiler_params=pltpu.CompilerParams(vmem_limit_bytes=VMEM_LIMIT),
    )(*results)
    out, d_tok, d_ln1, d_wqkv, d_bqkv, d_bias, d_wproj, d_ln2, d_wfc1, d_bfc1, d_wfc2 = outs
    return (
        out.transpose(2, 0, 1, 3), d_tok.transpose(2, 0, 1, 3), d_ln1, d_wqkv, d_bqkv,
        d_bias.transpose(0, 2, 1, 3), d_wproj, d_ln2, d_wfc1, d_bfc1, d_wfc2.T,
    )


def solution(mesh):
    grid = P(None, "lat", "lon", None)
    rows = P(None, "lat", None, None)
    return jax.shard_map(
        per_device,
        mesh=mesh,
        in_specs=(grid, grid, P(), P(), P(), rows, P(), P(), P(), P(), P()),
        out_specs=(grid, grid, P(), P(), P(), rows, P(), P(), P(), P(), P()),
        check_vma=False,
    )
```

```python
import jax
import jax.numpy as jnp
import numpy as np
from jax import lax
from jax.experimental import pallas as pl
from jax.experimental.pallas import tpu as pltpu
from jax.sharding import PartitionSpec as P

HEADS = 6
WIN_Z = 2
WIN_H = 6
WIN_W = 12
SPAN = 2 * WIN_W - 1
GROUPS = WIN_Z * WIN_H
T = GROUPS * WIN_W
C = 192
HID = 768
HEAD = C // HEADS
NREL = GROUPS * GROUPS * SPAN
SLOT = 48
FC = 48
ATT = 32
ROWS = 8
BANDS = 16
STRIPS = 8
PARTS = 6
EPSILON = 1e-05
VMEM_LIMIT = 56 * 1024 * 1024
FACTOR = HEAD ** (-0.5)
LOG2E = 1.4426950408889634
F32 = jnp.float32
BF16 = jnp.bfloat16
MESH = pl.DeviceIdType.MESH


def table_order():
    grid = np.zeros((512, 384), np.float32)
    for z in range(WIN_Z):
        for h in range(WIN_H):
            for i in range(SPAN):
                grid[z * 256 + h * SPAN + i, (SPAN - 1 - i) * GROUPS + h * WIN_Z + z] = 1
    return grid


def cross_pairs():
    g = np.arange(96)[:, None] // 8 // WIN_Z
    q = np.arange(384)[None, :] % GROUPS // WIN_Z
    return np.where((g < 3) != (q < 3), -1e30, 0.0).astype(np.float32)


def dot(a, b):
    return jnp.dot(a, b, preferred_element_type=F32)


def dot_nt(a, b):
    return lax.dot_general(a, b, (((1,), (1,)), ((), ())), preferred_element_type=F32)


def dot_tn(a, b):
    return lax.dot_general(a, b, (((0,), (0,)), ((), ())), preferred_element_type=F32)


def normalize(values, gain):
    average = jnp.mean(values, -1, keepdims=True)
    centered = values - average
    inv = lax.rsqrt(jnp.mean(centered * centered, -1, keepdims=True) + EPSILON)
    hat = centered * inv
    return hat * gain, hat, inv


def norm_back(hat, inv, gain, grad):
    scaled = grad * gain
    return inv * (
        scaled
        - jnp.mean(scaled, -1, keepdims=True)
        - hat * jnp.mean(scaled * hat, -1, keepdims=True)
    )


def pieces():
    for h in range(WIN_H):
        for w in range(WIN_W):
            at = w * GROUPS + h * WIN_Z
            yield (h // 3) * 2 + w // 6, h % 3, w % 6, slice(at, at + WIN_Z)


def quadrant(ref, q):
    return ref.at[pl.ds(q // 2 * 3, 3), pl.ds(q % 2 * 6, 6)]


def block_kernel(
    tok_any, cot_any, g1_any, wqkv_any, bqkv_any, table_any, wproj_any, g2_any, wfc1_any,
    bfc1_any, wfc2_any, perm_any, cross_any,
    gath_fc_out, gath_att_out, block_out, dtok_out, dtab_out,
    g1_ref, wqkv_ref, bqkv_ref, table_ref, wproj_ref, g2_ref, wfc1_ref,
    bfc1_ref, wfc2_ref, perm_ref, cross_ref,
    stage, arrive, out_stage,
    tabw, tab15, tin, ymat, bias, prob, wide_rows, wide_cols, dsc, dmat, vec,
    bsend, brecv, bfin, bbs, bbr,
    parts_fc, parts_att, core_fc, core_att, fold1, sum1, fold2, sum2, fold3, fold_att, sum_att,
    mid_att, gath_fc, gath_att, dtab_ref,
    in_sem, own_sem, out_sem,
    ex_send, ex_recv, rt_send, rt_recv, one_send, one_recv, p_send, p_recv, f_send, f_recv,
    a_send, a_recv, b_send, b_recv,
):
    sources = (
        (table_any, table_ref), (perm_any, perm_ref), (cross_any, cross_ref), (g1_any, g1_ref),
        (wqkv_any, wqkv_ref), (bqkv_any, bqkv_ref), (wproj_any, wproj_ref), (g2_any, g2_ref),
        (wfc1_any, wfc1_ref), (bfc1_any, bfc1_ref), (wfc2_any, wfc2_ref),
    )
    loads = [pltpu.make_async_copy(src, dst, in_sem.at[n]) for n, (src, dst) in enumerate(sources)]
    lon = lax.axis_index("lon")
    lat = lax.axis_index("lat")
    core = lax.rem(lat, 2)
    other = 1 - core
    pair_row = lat // 2
    east = lax.rem(lon + 1, STRIPS)
    west = lax.rem(lon + STRIPS - 1, STRIPS)
    south = lax.rem(lat + 1, BANDS)
    north = lax.rem(lat + BANDS - 1, BANDS)
    sibling = (lon, lat - core + other)

    spot = (lax.rem(pair_row, 4), lon // 2, lax.rem(lon, 2) * 2 + lat // 8)

    def on_axis(axis, at):
        if axis == 0:
            return (lon, lat // 8 * 8 + at * 2 + core)
        if axis == 1:
            return (at * 2 + lax.rem(lon, 2), lat)
        return (spot[1] * 2 + at // 2, lax.rem(at, 2) * 8 + spot[0] * 2 + core)

    def strip(d):
        return lax.rem(lon + d, STRIPS)

    def row_of(d):
        return lax.rem(pair_row + d, ROWS)

    barrier = pltpu.get_barrier_semaphore()

    def greet(target):
        pl.semaphore_signal(barrier, inc=1, device_id=target, device_id_type=MESH)

    for target in ((lon, south), (lon, north), (east, south), (west, north), sibling):
        greet(target)
    greet(on_axis(2, 3 - spot[2]))
    for d in range(1, 8):
        greet((strip(d), lat))
        greet((lon, row_of(d) * 2 + core))
    loads[0].start()
    own = [
        pltpu.make_async_copy(quadrant(src, 0), arrive.at[a, 3], own_sem.at[a])
        for a, src in enumerate((tok_any, cot_any))
    ]
    own[0].start()
    pl.semaphore_wait(barrier, 20)

    ahead = ((east, lat), (lon, south), (east, south))
    behind = ((west, lat), (lon, north), (west, north))

    def exchange(a, i):
        return pltpu.make_async_remote_copy(
            src_ref=quadrant((tok_any, cot_any)[a], i + 1),
            dst_ref=arrive.at[a, 2 - i],
            send_sem=ex_send.at[a, i],
            recv_sem=ex_recv.at[a, i],
            device_id=ahead[i],
            device_id_type=MESH,
        )

    def table_copy():
        return pltpu.make_async_remote_copy(
            src_ref=tabw,
            dst_ref=tab15,
            send_sem=one_send.at[0],
            recv_sem=one_recv.at[0],
            device_id=(lon, south),
            device_id_type=MESH,
        )

    for a in range(2):
        for i in range(3):
            exchange(a, i).start()
    for load in loads[1:]:
        load.start()
    own[1].start()

    tabw[...] = jnp.zeros_like(tabw)
    loads[0].wait()
    for head in range(HEADS):
        tabw[head : head + 1, 0:NREL] = table_ref[0, head]

    @pl.when(lat == BANDS - 1)
    def _():
        table_copy().start()


    tin[...] = jnp.zeros_like(tin)

    def spread(src, zp, zq, hp, width):
        j = (zp * WIN_Z + zq) * WIN_H + hp
        first = j * WIN_H * SPAN
        base = first // 128 * 128
        wide = src[:, base : base + 384]
        moved = pltpu.roll(wide, (384 - (first - base)) % 384, axis=1)
        g = hp * WIN_Z + zp
        tin[g * 8 : g * 8 + 8, zq * 256 : zq * 256 + width] = moved[:, :width]

    for zp in range(WIN_Z):
        for zq in range(WIN_Z):
            for hp in range(WIN_H):
                spread(tabw, zp, zq, hp, WIN_H * SPAN)

    @pl.when(lat == 0)
    def _():
        table_copy().wait_recv()
        for zp in range(WIN_Z):
            for zq in range(WIN_Z):
                for hp in range(3):
                    spread(tab15, zp, zq, hp, 3 * SPAN)

    whole = tin[...]
    high = whole.astype(BF16)
    rest = whole - high.astype(F32)
    middle = rest.astype(BF16)
    low = (rest - middle.astype(F32)).astype(BF16)
    loads[1].wait()
    perm = perm_ref[...]
    spread_rows = (dot(high, perm) + dot(middle, perm) + dot(low, perm)) * LOG2E
    for n in range(3):
        ymat[n, 0:96, :] = spread_rows[:, 128 * n : 128 * (n + 1)]
        ymat[n, 96:128, :] = jnp.zeros((32, 128), F32)
    loads[2].wait()

    @pl.when(lat == 0)
    def _():
        for n in range(3):
            ymat[n, 0:96, :] = ymat[n, 0:96, :] + cross_ref[:, 128 * n : 128 * (n + 1)]

    for head in range(HEADS):
        rows = jnp.concatenate(
            [ymat[n, pl.ds(head, 16, stride=8), :] for n in range(3)], -1
        )
        for w in range(WIN_W):
            moved = pltpu.roll(rows, (384 - (WIN_W - 1 - w) * GROUPS) % 384, axis=1)
            bias[head, w * GROUPS : (w + 1) * GROUPS, :] = moved[:GROUPS, :T]

    for n in range(3, 11):
        loads[n].wait()
    lane = lax.broadcasted_iota(jnp.int32, (16, C), 1)
    ones = [
        jnp.where((lane >= HEAD * i) & (lane < HEAD * (i + 1)), 1.0, 0.0).astype(BF16)[0:1]
        for i in range(HEADS)
    ]
    gain1 = g1_ref[...].reshape(1, C)
    gain2 = g2_ref[...].reshape(1, C)

    def arrived(a):
        for i in range(3):
            exchange(a, i).wait_recv()
        own[a].wait()
        for slot, row, col, rows in pieces():
            stage[a, rows, :] = arrive[a, slot, row, col].astype(F32)
        return stage[a]

    tokens = arrived(0)
    normed, hat1, inv1 = normalize(tokens, gain1)
    first = normed.astype(BF16)
    qkv = (dot(first, wqkv_ref[...]) + bqkv_ref[...].reshape(1, 3 * C)).astype(BF16)
    queries = qkv[:, 0:C]
    keys = qkv[:, C : 2 * C]
    values = qkv[:, 2 * C : 3 * C]
    queries_t = queries.T
    wide_rows[...] = jnp.zeros_like(wide_rows)
    wide_cols[...] = jnp.zeros_like(wide_cols)
    for head in range(HEADS):
        wide_cols[256 * head : 256 * head + T, :] = values * ones[head]
    for head in range(HEADS):
        q = queries * ones[head]
        scores = dot_nt(q, keys) * (FACTOR * LOG2E) + bias[head]
        top = jnp.max(scores, -1, keepdims=True)
        raised = jnp.exp2(scores - top)
        probs = raised * (1.0 / jnp.sum(raised, -1, keepdims=True))
        prob[head] = probs
        probs_low = probs.astype(BF16)
        wide_rows[:, 256 * head : 256 * head + T] = probs_low
    mixed = dot(wide_rows[...], wide_cols[...]).astype(BF16)
    inner = tokens + dot(mixed, wproj_ref[...]).astype(BF16).astype(F32)

    def remote(src, dst, send_sem, recv_sem, target):
        return pltpu.make_async_remote_copy(
            src_ref=src, dst_ref=dst, send_sem=send_sem, recv_sem=recv_sem,
            device_id=target, device_id_type=MESH,
        )

    def wait_bytes(ref, sem):
        pltpu.make_async_copy(ref, ref, sem).wait()

    def add(*terms):
        total = terms[0].astype(F32)
        for term in terms[1:]:
            total = total + term.astype(F32)
        return total.astype(BF16)

    axes = [(n, (n + 1) % 3, (n + 2) % 3) for n in range(3)]
    places = [tuple(spot[axis] for axis in order) for order in axes]

    def block(n, i):
        return pl.ds(n * 16 + i * 4, 4)

    def unit(n):
        return n * 16 + places[n][0] * 4 + places[n][1]

    def part_to_line(n, stage_no, which, src, dst):
        for d in range(1, 4):
            at = lax.rem(places[n][which] + d, 4)
            remote(
                src(n, at), dst(n, d), f_send.at[stage_no], f_recv.at[stage_no],
                on_axis(axes[n][which], at),
            ).start()

    def to_line(stage_no, which, src, dst):
        for n in range(3):
            part_to_line(n, stage_no, which, src, dst)

    pair_fc = [
        remote(
            parts_fc.at[other, pl.ds(12 * n, 12)], core_fc.at[pl.ds(12 * n, 12)],
            p_send.at[n], p_recv.at[n], sibling,
        )
        for n in range(4)
    ]
    swap_fc = remote(
        gath_fc.at[core], gath_fc_out.at[core], f_send.at[6], f_recv.at[6], sibling
    )
    pair_att = remote(parts_att.at[other], core_att, a_send.at[0], a_recv.at[0], sibling)
    swap_att = remote(
        gath_att.at[core], gath_att_out.at[core], a_send.at[4], a_recv.at[4], sibling
    )
    keep = [
        pltpu.make_async_copy(src, dst, out_sem.at[n])
        for n, (src, dst) in enumerate((
            (out_stage.at[0, 3], quadrant(block_out, 0)),
            (out_stage.at[1, 3], quadrant(dtok_out, 0)),
            (dtab_ref, dtab_out), (gath_fc.at[core], gath_fc_out.at[core]),
            (gath_att.at[core], gath_att_out.at[core]),
        ))
    ]

    def early1():
        for n in range(3):
            if n == 0:
                pair_fc[0].wait_recv()
            pair_fc[n + 1].wait_recv()
            rows = pl.ds(16 * n, 16)
            parts_fc[core, rows] = add(parts_fc[core, rows], core_fc[rows])
            part_to_line(
                n, 1, 0, lambda n, at: parts_fc.at[core, block(n, at)],
                lambda n, d: fold1.at[n, d - 1],
            )

    def early2():
        wait_bytes(fold1, f_recv.at[1])
        for n in range(3):
            own = parts_fc[core, block(n, places[n][0])]
            sum1[n] = add(own, fold1[n, 0], fold1[n, 1], fold1[n, 2])
        to_line(2, 1, lambda n, at: sum1.at[n, at], lambda n, d: fold2.at[n, d - 1])

    def early3():
        wait_bytes(fold2, f_recv.at[2])
        for n in range(3):
            own = sum1[n, places[n][1]]
            sum2[n] = add(own, fold2[n, 0], fold2[n, 1], fold2[n, 2])
            fold3[n, places[n][2]] = sum2[n]
        to_line(3, 2, lambda n, at: sum2.at[n], lambda n, d: fold3.at[n, places[n][2]])

    def early4():
        wait_bytes(fold2, f_recv.at[3])
        for n in range(3):
            gath_fc[core, unit(n)] = add(*[fold3[n, i] for i in range(4)])
        to_line(
            4, 1, lambda n, at: gath_fc.at[core, unit(n)], lambda n, d: gath_fc.at[core, unit(n)]
        )

    def early5():
        wait_bytes(fold2, f_recv.at[4])
        to_line(
            5, 0,
            lambda n, at: gath_fc.at[core, block(n, places[n][0])],
            lambda n, d: gath_fc.at[core, block(n, places[n][0])],
        )

    def early6():
        wait_bytes(fold1, f_recv.at[5])
        swap_fc.start()
        keep[3].start()

    own_rows = pl.ds(pair_row * 4, 4)

    def late1():
        pair_att.wait_recv()
        parts_att[core] = add(parts_att[core], core_att[...])
        for d in range(1, ROWS):
            remote(
                parts_att.at[core, pl.ds(row_of(d) * 4, 4)], fold_att.at[d - 1],
                a_send.at[1], a_recv.at[1], (lon, row_of(d) * 2 + core),
            ).start()

    def late2():
        wait_bytes(fold_att, a_recv.at[1])
        sum_att[...] = add(parts_att[core, own_rows], *[fold_att[d] for d in range(ROWS - 1)])
        mid_att[lon] = sum_att[...]
        for d in range(1, STRIPS):
            remote(
                sum_att, mid_att.at[lon], a_send.at[2], a_recv.at[2], (strip(d), lat)
            ).start()

    def late3():
        wait_bytes(fold_att, a_recv.at[2])
        gath_att[core, own_rows] = add(*[mid_att[i] for i in range(STRIPS)])
        for d in range(1, ROWS):
            remote(
                gath_att.at[core, own_rows], gath_att.at[core, own_rows],
                a_send.at[3], a_recv.at[3], (lon, row_of(d) * 2 + core),
            ).start()

    def late4():
        wait_bytes(fold_att, a_recv.at[3])
        swap_att.start()
        keep[4].start()

    cot = arrived(1)
    cot_low = cot.astype(BF16)
    normed, hat2, inv2 = normalize(inner, gain2)
    second = normed.astype(BF16)
    second_t = second.T
    cot_t = cot_low.T
    total = inner
    grad_second = jnp.zeros((T, C), F32)
    bfc1 = bfc1_ref[...].reshape(1, HID)
    vec[...] = jnp.zeros_like(vec)
    for n in range(3):
        cols = slice(256 * n, 256 * (n + 1))
        pre = dot(second, wfc1_ref[:, cols]) + bfc1[:, cols]
        cdf = 0.5 * (1.0 + lax.erf(pre * 0.7071067811865476))
        density = jnp.exp(-0.5 * pre * pre) * 0.3989422804014327
        act = (pre * cdf).astype(BF16)
        total = total + dot_nt(act, wfc2_ref[:, cols])
        grad_pre = (dot(cot_low, wfc2_ref[:, cols]) * (cdf + pre * density)).astype(BF16)
        grad_second = grad_second + dot_nt(grad_pre, wfc1_ref[:, cols])
        parts_fc[0, 12 * n : 12 * (n + 1)] = dot(second_t, grad_pre).astype(BF16).reshape(12, 16, 256)
        parts_fc[1, 12 * n : 12 * (n + 1)] = dot(cot_t, act).astype(BF16).reshape(12, 16, 256)
        vec[n : n + 1, :] = jnp.sum(grad_pre.astype(F32), 0, keepdims=True)
        pair_fc[n].start()

    def give_back(a, i):
        return pltpu.make_async_remote_copy(
            src_ref=out_stage.at[a, 2 - i],
            dst_ref=quadrant((block_out, dtok_out)[a], i + 1),
            send_sem=rt_send.at[a, i],
            recv_sem=rt_recv.at[a, i],
            device_id=behind[i],
            device_id_type=MESH,
        )

    def hand_out(a, field):
        stage[a] = field
        for slot, row, col, rows in pieces():
            out_stage[a, slot, row, col] = stage[a, rows, :].astype(BF16)
        for i in range(3):
            give_back(a, i).start()
        keep[a].start()

    grad_inner = cot + norm_back(hat2, inv2, gain2, grad_second)
    grad_att = grad_inner.astype(BF16)
    proj_grad = dot_tn(mixed, grad_att).astype(BF16)
    proj_grad = jnp.concatenate([proj_grad, jnp.zeros((C, 64), BF16)], -1).reshape(12, 16, 256)
    parts_fc[0, 36:42] = proj_grad[:6]
    parts_fc[1, 36:42] = proj_grad[6:]
    vec[3:4, 0:C] = jnp.sum(grad_second * hat2, 0, keepdims=True)
    parts_fc[0, 42] = vec[...].astype(BF16)
    parts_fc[1, 42] = jnp.zeros((16, 256), BF16)
    parts_fc[:, 43:] = jnp.zeros((2, FC - 43, 16, 256), BF16)
    pair_fc[3].start()
    hand_out(0, total)

    grad_mixed = dot_nt(grad_att, wproj_ref[...]).astype(BF16)
    grad_mixed_t = grad_mixed.T
    dsc[...] = jnp.zeros_like(dsc)
    for head in range(HEADS):
        wide_cols[256 * head : 256 * head + T, :] = keys * ones[head]
    grad_k_t = []
    grad_v_t = []
    for head in range(HEADS):
        rows = slice(HEAD * head, HEAD * (head + 1))
        gm = grad_mixed * ones[head]
        probs = prob[head]
        grad_probs = dot_nt(gm, values)
        inside = jnp.sum(probs * grad_probs, -1, keepdims=True)
        grad_scores = probs * (grad_probs - inside)
        dsc[head, 0:T, 0:T] = grad_scores
        scaled = (grad_scores * FACTOR).astype(BF16)
        grad_v_t.append(
            dot(grad_mixed_t[rows], wide_rows[:, 256 * head : 256 * head + T])
        )
        wide_rows[:, 256 * head : 256 * head + T] = scaled
        grad_k_t.append(dot(queries_t[rows], scaled))
        if head == 2:
            early1()
    grad_q = dot(wide_rows[...], wide_cols[...])
    grad_k = jnp.concatenate(grad_k_t, 0).T
    grad_v = jnp.concatenate(grad_v_t, 0).T

    grad_qkv = jnp.concatenate([grad_q, grad_k, grad_v], -1).astype(BF16)
    wide = dot_tn(first, grad_qkv).astype(BF16)
    for n in range(4):
        parts_att[n // 2, n % 2 * 12 : n % 2 * 12 + 12] = (
            wide[:, 128 * n : 128 * (n + 1)].reshape(12, 16, 128)
        )
    edge = jnp.concatenate([wide[:96, 512:576], wide[96:, 512:576]], -1).reshape(6, 16, 128)
    parts_att[0, 24:27] = edge[:3]
    parts_att[1, 24:27] = edge[3:]
    grad_first = dot_nt(grad_qkv, wqkv_ref[...]).astype(BF16).astype(F32)
    vec[...] = jnp.zeros_like(vec)
    sums = jnp.sum(grad_qkv.astype(F32), 0, keepdims=True)
    sums = [sums[:, C * n : C * (n + 1)] for n in range(3)]
    sums.append(jnp.sum(grad_first * hat1, 0, keepdims=True))
    for n in range(4):
        vec[2 * n : 2 * n + 1, 0:128] = sums[n][:, 0:128]
        vec[2 * n + 1 : 2 * n + 2, 0:64] = sums[n][:, 128:C]
    parts_att[0, 27] = vec[:, 0:128].astype(BF16)
    parts_att[1, 27] = jnp.zeros((16, 128), BF16)
    parts_att[:, 28:] = jnp.zeros((2, ATT - 28, 16, 128), BF16)
    pair_att.start()
    d_tokens = grad_inner + norm_back(hat1, inv1, gain1, grad_first)
    hand_out(1, d_tokens)

    dmat[...] = jnp.zeros_like(dmat)
    for head in range(HEADS):
        if head == 3:
            late1()
            early2()
        acc = jnp.zeros((16, 384), F32)
        for w in range(WIN_W):
            acc = acc + pltpu.roll(
                dsc[head, w * GROUPS : w * GROUPS + 16, :], (WIN_W - 1 - w) * GROUPS, axis=1
            )
        for n in range(3):
            dmat[n, pl.ds(head, 16, stride=8), :] = acc[:, 128 * n : 128 * (n + 1)]

    def table_grad():
        return jnp.concatenate([dmat[n, 0:96, :] for n in range(3)], -1)

    def keep_table(field):
        for n in range(3):
            dmat[n, 0:96, :] = field[:, 128 * n : 128 * (n + 1)]

    def edge_copy():
        return pltpu.make_async_remote_copy(
            src_ref=bbs,
            dst_ref=bbr,
            send_sem=one_send.at[1],
            recv_sem=one_recv.at[1],
            device_id=(lon, north),
            device_id_type=MESH,
        )

    @pl.when(lat == 0)
    def _():
        upper = lax.broadcasted_iota(jnp.int32, (96, 384), 0) < 48
        full = table_grad()
        bbs[...] = jnp.where(upper, full, 0.0).astype(BF16)
        edge_copy().start()
        keep_table(jnp.where(upper, 0.0, full))

    @pl.when(lat == BANDS - 1)
    def _():
        edge_copy().wait_recv()
        keep_table(table_grad() + bbr[...].astype(F32))

    bsend[...] = table_grad().astype(BF16).reshape(PARTS, 16, 384)

    for owner in range(PARTS):
        @pl.when(lon != owner)
        def _():
            pltpu.make_async_remote_copy(
                src_ref=bsend.at[owner],
                dst_ref=brecv.at[lon],
                send_sem=b_send.at[0],
                recv_sem=b_recv.at[0],
                device_id=(owner, lat),
                device_id_type=MESH,
            ).start()

    early3()
    late2()
    early4()
    seven = brecv.at[pl.ds(0, STRIPS - 1)]

    @pl.when(lon < PARTS)
    def _():
        brecv[lon] = bsend[lon]
        wait_bytes(seven, b_recv.at[0])
        bfin[lon] = jnp.sum(brecv[...].astype(F32), 0).astype(BF16)
        for d in range(1, STRIPS):
            pltpu.make_async_remote_copy(
                src_ref=bfin.at[lon],
                dst_ref=bfin.at[lon],
                send_sem=b_send.at[1],
                recv_sem=b_recv.at[1],
                device_id=(strip(d), lat),
                device_id_type=MESH,
            ).start()

    early5()
    late3()

    @pl.when(lon < PARTS)
    def _():
        wait_bytes(bfin.at[pl.ds(0, PARTS - 1)], b_recv.at[1])

    @pl.when(lon >= PARTS)
    def _():
        wait_bytes(bfin, b_recv.at[1])

    tin[...] = dot_nt(bfin[...].reshape(96, 384), perm_ref[...])
    dtab_ref[...] = jnp.zeros_like(dtab_ref)
    for zp in range(WIN_Z):
        for zq in range(WIN_Z):
            for hp in range(WIN_H):
                j = (zp * WIN_Z + zq) * WIN_H + hp
                first_lane = j * WIN_H * SPAN
                base = first_lane // 128 * 128
                g = hp * WIN_Z + zp
                piece = tin[g * 8 : g * 8 + 8, zq * 256 : zq * 256 + 256]
                piece = jnp.concatenate([piece, jnp.zeros((8, 128), F32)], -1)
                moved = pltpu.roll(piece, first_lane - base, axis=1)
                dtab_ref[:, base : base + 384] = dtab_ref[:, base : base + 384] + moved

    keep[2].start()
    early6()
    late4()

    for a in range(2):
        for i in range(3):
            exchange(a, i).wait_send()
            give_back(a, i).wait()

    @pl.when(lat == BANDS - 1)
    def _():
        table_copy().wait_send()

    @pl.when(lat == 0)
    def _():
        edge_copy().wait_send()

    for copy in pair_fc:
        copy.wait_send()
    for stage_no, ref in ((1, fold1), (2, fold2), (3, fold2), (4, fold2), (5, fold1)):
        wait_bytes(ref, f_send.at[stage_no])
    pair_att.wait_send()
    for stage_no in (1, 2, 3):
        wait_bytes(fold_att, a_send.at[stage_no])

    @pl.when(lon < PARTS)
    def _():
        wait_bytes(bsend.at[pl.ds(0, PARTS - 1)], b_send.at[0])
        wait_bytes(seven, b_send.at[1])

    @pl.when(lon >= PARTS)
    def _():
        wait_bytes(bsend, b_send.at[0])

    for copy in keep:
        copy.wait()
    swap_fc.wait()
    swap_att.wait()


def output_kernel(*refs):
    ins, outs = refs[:5], refs[5:16]
    in_bufs, out_bufs = refs[16:19], refs[19:28]
    in_sem, out_sem = refs[28:]
    loads = [
        pltpu.make_async_copy(src, dst, in_sem.at[n])
        for n, (src, dst) in enumerate(zip(ins[2:], in_bufs))
    ]
    stores = [
        pltpu.make_async_copy(src, dst, out_sem.at[n])
        for n, (src, dst) in enumerate(zip(ins[:2] + out_bufs, outs))
    ]
    gath_ref, gath_att, dtab_ref = in_bufs
    (
        dln1_ref, dwqkv_ref, dbqkv_ref, dbias_ref, dwproj_ref, dln2_ref,
        dwfc1_ref, dbfc1_ref, dwfc2_ref,
    ) = out_bufs
    for copy in loads + stores[:2]:
        copy.start()
    loads[0].wait()
    for n in range(3):
        cols = slice(256 * n, 256 * (n + 1))
        rows = slice(12 * n, 12 * (n + 1))
        dwfc1_ref[:, cols] = gath_ref[0, rows].reshape(C, 256).astype(F32)
    stores[8].start()
    for n in range(3):
        cols = slice(256 * n, 256 * (n + 1))
        rows = slice(12 * n, 12 * (n + 1))
        dwfc2_ref[:, cols] = gath_ref[1, rows].reshape(C, 256).astype(F32)
    stores[10].start()
    for k in range(2):
        dwproj_ref[96 * k : 96 * (k + 1), :] = (
            gath_ref[k, 36:42].reshape(96, 256)[:, 0:C].astype(F32)
        )
    vec = gath_ref[0, 42].astype(F32)
    dbfc1_ref[...] = jnp.concatenate([vec[n : n + 1] for n in range(3)], -1).reshape(HID)
    dln2_ref[...] = vec[3:4, :C].reshape(C)
    for n in (6, 9, 7):
        stores[n].start()
    loads[1].wait()
    for k in range(2):
        for n in range(2):
            cols = slice(256 * k + 128 * n, 256 * k + 128 * (n + 1))
            dwqkv_ref[:, cols] = gath_att[k, 12 * n : 12 * (n + 1)].reshape(C, 128).astype(F32)
        edge = gath_att[k, 24:27].reshape(48, 128).astype(F32)
        for n in range(2):
            at = 96 * n + 48 * k
            dwqkv_ref[at : at + 48, 512:576] = edge[:, 64 * n : 64 * (n + 1)]
    vec = gath_att[0, 27].astype(F32)
    sums = [
        jnp.concatenate([vec[2 * n : 2 * n + 1], vec[2 * n + 1 : 2 * n + 2, :64]], -1)
        for n in range(4)
    ]
    dbqkv_ref[...] = jnp.concatenate(sums[:3], -1).reshape(3 * C)
    dln1_ref[...] = sums[3].reshape(C)
    for n in (3, 4, 2):
        stores[n].start()
    loads[2].wait()
    for head in range(HEADS):
        dbias_ref[0, head] = dtab_ref[head : head + 1, 0:NREL]
    stores[5].start()
    for store in stores:
        store.wait()


def per_device(
    tokens, cotangent, ln1_gain, w_qkv, b_qkv, bias_table, w_proj, ln2_gain, w_fc1, b_fc1, w_fc2
):
    hbm = pl.BlockSpec(memory_space=pl.ANY)
    perm = table_order()
    dma = pltpu.SemaphoreType.DMA
    args = (
        tokens.transpose(1, 2, 0, 3), cotangent.transpose(1, 2, 0, 3), ln1_gain, w_qkv, b_qkv,
        bias_table.transpose(0, 2, 1, 3), w_proj, ln2_gain, w_fc1, b_fc1, w_fc2.T,
        jnp.asarray(perm, BF16), jnp.asarray(cross_pairs()),
    )
    gathered, gathered_att, block, d_tok, table = pl.pallas_call(
        block_kernel,
        out_shape=(
            jax.ShapeDtypeStruct((2, FC, 16, 256), BF16),
            jax.ShapeDtypeStruct((2, ATT, 16, 128), BF16),
            jax.ShapeDtypeStruct((WIN_H, WIN_W, WIN_Z, C), BF16),
            jax.ShapeDtypeStruct((WIN_H, WIN_W, WIN_Z, C), BF16),
            jax.ShapeDtypeStruct((8, 3456), F32),
        ),
        in_specs=[hbm] * len(args),
        out_specs=(hbm,) * 5,
        scratch_shapes=[pltpu.VMEM(a.shape, a.dtype) for a in args[2:]]
        + [
            pltpu.VMEM((2, T, C), F32),
            pltpu.VMEM((2, 4, 3, 6, WIN_Z, C), BF16),
            pltpu.VMEM((2, 4, 3, 6, WIN_Z, C), BF16),
            pltpu.VMEM((8, 3456), F32),
            pltpu.VMEM((8, 3456), F32),
            pltpu.VMEM((96, 512), F32),
            pltpu.VMEM((3, 128, 128), F32),
            pltpu.VMEM((HEADS, T, T), F32),
            pltpu.VMEM((HEADS, T, T), F32),
            pltpu.VMEM((T, HEADS * 256), BF16),
            pltpu.VMEM((HEADS * 256, C), BF16),
            pltpu.VMEM((HEADS, 160, 384), F32),
            pltpu.VMEM((3, 128, 128), F32),
            pltpu.VMEM((16, 256), F32),
            pltpu.VMEM((PARTS, 16, 384), BF16),
            pltpu.VMEM((STRIPS, 16, 384), BF16),
            pltpu.VMEM((PARTS, 16, 384), BF16),
            pltpu.VMEM((96, 384), BF16),
            pltpu.VMEM((96, 384), BF16),
            pltpu.VMEM((2, FC, 16, 256), BF16),
            pltpu.VMEM((2, ATT, 16, 128), BF16),
            pltpu.VMEM((FC, 16, 256), BF16),
            pltpu.VMEM((ATT, 16, 128), BF16),
            pltpu.VMEM((3, 3, 4, 16, 256), BF16),
            pltpu.VMEM((3, 4, 16, 256), BF16),
            pltpu.VMEM((3, 3, 16, 256), BF16),
            pltpu.VMEM((3, 16, 256), BF16),
            pltpu.VMEM((3, 4, 16, 256), BF16),
            pltpu.VMEM((ROWS - 1, 4, 16, 128), BF16),
            pltpu.VMEM((4, 16, 128), BF16),
            pltpu.VMEM((STRIPS, 4, 16, 128), BF16),
            pltpu.VMEM((2, FC, 16, 256), BF16),
            pltpu.VMEM((2, ATT, 16, 128), BF16),
            pltpu.VMEM((8, 3456), F32),
            dma((len(args) - 2,)), dma((2,)), dma((5,)),
            dma((2, 3)), dma((2, 3)), dma((2, 3)), dma((2, 3)),
            dma((2,)), dma((2,)), dma((4,)), dma((4,)), dma((7,)), dma((7,)),
            dma((5,)), dma((5,)), dma((2,)), dma((2,)),
        ],
        compiler_params=pltpu.CompilerParams(
            collective_id=0, has_side_effects=True, vmem_limit_bytes=VMEM_LIMIT
        ),
    )(*args)
    shape = jax.ShapeDtypeStruct
    grid_shape = (WIN_H, WIN_W, WIN_Z, C)
    results_out = (
        shape(grid_shape, BF16), shape(grid_shape, BF16),
        shape((C,), F32), shape((C, 3 * C), F32), shape((3 * C,), F32),
        shape((1, HEADS, 1, NREL), F32), shape((C, C), F32), shape((C,), F32),
        shape((C, HID), F32), shape((HID,), F32), shape((C, HID), F32),
    )
    outs = pl.pallas_call(
        output_kernel,
        out_shape=results_out,
        in_specs=[hbm] * 5,
        out_specs=(hbm,) * 11,
        scratch_shapes=[
            pltpu.VMEM(a.shape, a.dtype)
            for a in (gathered, gathered_att, table) + results_out[2:]
        ]
        + [dma((3,)), dma((11,))],
        compiler_params=pltpu.CompilerParams(vmem_limit_bytes=VMEM_LIMIT),
    )(block, d_tok, gathered, gathered_att, table)
    out, d_tok, d_ln1, d_wqkv, d_bqkv, d_bias, d_wproj, d_ln2, d_wfc1, d_bfc1, d_wfc2 = outs
    return (
        out.transpose(2, 0, 1, 3), d_tok.transpose(2, 0, 1, 3), d_ln1, d_wqkv, d_bqkv,
        d_bias.transpose(0, 2, 1, 3), d_wproj, d_ln2, d_wfc1, d_bfc1, d_wfc2.T,
    )


def solution(mesh):
    grid = P(None, "lat", "lon", None)
    rows = P(None, "lat", None, None)
    return jax.shard_map(
        per_device,
        mesh=mesh,
        in_specs=(grid, grid, P(), P(), P(), rows, P(), P(), P(), P(), P()),
        out_specs=(grid, grid, P(), P(), P(), rows, P(), P(), P(), P(), P()),
        check_vma=False,
    )
```

```python
import jax
import jax.numpy as jnp
import numpy as np
from jax import lax
from jax.experimental import pallas as pl
from jax.experimental.pallas import tpu as pltpu
from jax.sharding import PartitionSpec as P

HEADS = 6
WIN_Z = 2
WIN_H = 6
WIN_W = 12
SPAN = 2 * WIN_W - 1
GROUPS = WIN_Z * WIN_H
T = GROUPS * WIN_W
C = 192
HID = 768
HEAD = C // HEADS
NREL = GROUPS * GROUPS * SPAN
FC = 48
ATT = 32
ROWS = 8
BANDS = 16
STRIPS = 8
PARTS = 6
EPSILON = 1e-05
VMEM_LIMIT = 56 * 1024 * 1024
FACTOR = HEAD ** (-0.5)
LOG2E = 1.4426950408889634
F32 = jnp.float32
BF16 = jnp.bfloat16
MESH = pl.DeviceIdType.MESH


def table_order():
    grid = np.zeros((512, 384), np.float32)
    for z in range(WIN_Z):
        for h in range(WIN_H):
            for i in range(SPAN):
                grid[z * 256 + h * SPAN + i, (SPAN - 1 - i) * GROUPS + h * WIN_Z + z] = 1
    return grid


def cross_pairs():
    g = np.arange(96)[:, None] // 8 // WIN_Z
    q = np.arange(384)[None, :] % GROUPS // WIN_Z
    return np.where((g < 3) != (q < 3), -1e30, 0.0).astype(np.float32)


def dot(a, b):
    return jnp.dot(a, b, preferred_element_type=F32)


def dot_nt(a, b):
    return lax.dot_general(a, b, (((1,), (1,)), ((), ())), preferred_element_type=F32)


def dot_tn(a, b):
    return lax.dot_general(a, b, (((0,), (0,)), ((), ())), preferred_element_type=F32)


def normalize(values, gain):
    average = jnp.mean(values, -1, keepdims=True)
    centered = values - average
    inv = lax.rsqrt(jnp.mean(centered * centered, -1, keepdims=True) + EPSILON)
    hat = centered * inv
    return hat * gain, hat, inv


def norm_back(hat, inv, gain, grad):
    scaled = grad * gain
    return inv * (
        scaled
        - jnp.mean(scaled, -1, keepdims=True)
        - hat * jnp.mean(scaled * hat, -1, keepdims=True)
    )


def pieces():
    for h in range(WIN_H):
        for w in range(WIN_W):
            at = w * GROUPS + h * WIN_Z
            yield (h // 3) * 2 + w // 6, h % 3, w % 6, slice(at, at + WIN_Z)


def quadrant(ref, q):
    return ref.at[pl.ds(q // 2 * 3, 3), pl.ds(q % 2 * 6, 6)]


def block_kernel(
    tok_any, cot_any, g1_any, wqkv_any, bqkv_any, table_any, wproj_any, g2_any, wfc1_any,
    bfc1_any, wfc2_any, perm_any, cross_any,
    gath_fc_out, gath_att_out, block_out, dtok_out, dtab_out,
    g1_ref, wqkv_ref, bqkv_ref, table_ref, wproj_ref, g2_ref, wfc1_ref,
    bfc1_ref, wfc2_ref, perm_ref, cross_ref,
    stage, arrive, out_stage,
    tabw, tab15, tin, ymat, bias, prob, wide_rows, wide_cols, dsc, dmat, vec,
    bsend, brecv, bfin, bbs, bbr,
    parts_fc, parts_att, core_fc, core_att, fold1, sum1, fold2, sum2, fold3, fold_att, sum_att,
    mid_att, gath_fc, gath_att, dtab_ref,
    in_sem, own_sem, out_sem,
    ex_send, ex_recv, rt_send, rt_recv, one_send, one_recv, p_send, p_recv, f_send, f_recv,
    a_send, a_recv, b_send, b_recv,
):
    sources = (
        (table_any, table_ref), (perm_any, perm_ref), (cross_any, cross_ref), (g1_any, g1_ref),
        (wqkv_any, wqkv_ref), (bqkv_any, bqkv_ref), (wproj_any, wproj_ref), (g2_any, g2_ref),
        (wfc1_any, wfc1_ref), (bfc1_any, bfc1_ref), (wfc2_any, wfc2_ref),
    )
    loads = [pltpu.make_async_copy(src, dst, in_sem.at[n]) for n, (src, dst) in enumerate(sources)]
    lon = lax.axis_index("lon")
    lat = lax.axis_index("lat")
    core = lax.rem(lat, 2)
    other = 1 - core
    pair_row = lat // 2
    east = lax.rem(lon + 1, STRIPS)
    west = lax.rem(lon + STRIPS - 1, STRIPS)
    south = lax.rem(lat + 1, BANDS)
    north = lax.rem(lat + BANDS - 1, BANDS)
    sibling = (lon, lat - core + other)

    spot = (lax.rem(pair_row, 4), lon // 2, lax.rem(lon, 2) * 2 + lat // 8)

    def on_axis(axis, at):
        if axis == 0:
            return (lon, lat // 8 * 8 + at * 2 + core)
        if axis == 1:
            return (at * 2 + lax.rem(lon, 2), lat)
        return (spot[1] * 2 + at // 2, lax.rem(at, 2) * 8 + spot[0] * 2 + core)

    def strip(d):
        return lax.rem(lon + d, STRIPS)

    def row_of(d):
        return lax.rem(pair_row + d, ROWS)

    barrier = pltpu.get_barrier_semaphore()

    def greet(target):
        pl.semaphore_signal(barrier, inc=1, device_id=target, device_id_type=MESH)

    for target in ((lon, south), (lon, north), (east, south), (west, north), sibling):
        greet(target)
    greet(on_axis(2, 3 - spot[2]))
    for d in range(1, 8):
        greet((strip(d), lat))
        greet((lon, row_of(d) * 2 + core))
    loads[0].start()
    own = [
        pltpu.make_async_copy(quadrant(src, 0), arrive.at[a, 3], own_sem.at[a])
        for a, src in enumerate((tok_any, cot_any))
    ]
    own[0].start()
    pl.semaphore_wait(barrier, 20)

    ahead = ((east, lat), (lon, south), (east, south))
    behind = ((west, lat), (lon, north), (west, north))

    def exchange(a, i):
        return pltpu.make_async_remote_copy(
            src_ref=quadrant((tok_any, cot_any)[a], i + 1),
            dst_ref=arrive.at[a, 2 - i],
            send_sem=ex_send.at[a, i],
            recv_sem=ex_recv.at[a, i],
            device_id=ahead[i],
            device_id_type=MESH,
        )

    def table_copy():
        return pltpu.make_async_remote_copy(
            src_ref=table_any,
            dst_ref=tab15,
            send_sem=one_send.at[0],
            recv_sem=one_recv.at[0],
            device_id=(lon, south),
            device_id_type=MESH,
        )

    @pl.when(lat == BANDS - 1)
    def _():
        table_copy().start()

    for a in range(2):
        for i in range(3):
            exchange(a, i).start()
    for load in loads[1:]:
        load.start()
    own[1].start()

    tabw[...] = jnp.zeros_like(tabw)
    loads[0].wait()
    for head in range(HEADS):
        tabw[head : head + 1, 0:NREL] = table_ref[0, head]

    tin[...] = jnp.zeros_like(tin)

    def spread(src, zp, zq, hp, width):
        j = (zp * WIN_Z + zq) * WIN_H + hp
        first = j * WIN_H * SPAN
        base = first // 128 * 128
        wide = src[:, base : base + 384]
        moved = pltpu.roll(wide, (384 - (first - base)) % 384, axis=1)
        g = hp * WIN_Z + zp
        tin[g * 8 : g * 8 + 8, zq * 256 : zq * 256 + width] = moved[:, :width]

    for zp in range(WIN_Z):
        for zq in range(WIN_Z):
            for hp in range(WIN_H):
                spread(tabw, zp, zq, hp, WIN_H * SPAN)

    def permuted(whole):
        high = whole.astype(BF16)
        rest = whole - high.astype(F32)
        middle = rest.astype(BF16)
        low = (rest - middle.astype(F32)).astype(BF16)
        perm = perm_ref[...]
        return (dot(high, perm) + dot(middle, perm) + dot(low, perm)) * LOG2E

    loads[1].wait()
    spread_rows = permuted(tin[...])
    for n in range(3):
        ymat[n, 0:96, :] = spread_rows[:, 128 * n : 128 * (n + 1)]
        ymat[n, 96:128, :] = jnp.zeros((32, 128), F32)
    loads[2].wait()

    @pl.when(lat == 0)
    def _():
        for n in range(3):
            ymat[n, 0:96, :] = ymat[n, 0:96, :] + cross_ref[:, 128 * n : 128 * (n + 1)]

    def place_bias(tall, count):
        for head in range(HEADS):
            rows = jnp.concatenate(
                [ymat[n, pl.ds(head, tall, stride=8), :] for n in range(3)], -1
            )
            for w in range(WIN_W):
                moved = pltpu.roll(rows, (384 - (WIN_W - 1 - w) * GROUPS) % 384, axis=1)
                bias[head, w * GROUPS : w * GROUPS + count, :] = moved[:count, :T]

    place_bias(16, GROUPS)
    for n in range(3, 11):
        loads[n].wait()
    lane = lax.broadcasted_iota(jnp.int32, (16, C), 1)
    ones = [
        jnp.where((lane >= HEAD * i) & (lane < HEAD * (i + 1)), 1.0, 0.0).astype(BF16)[0:1]
        for i in range(HEADS)
    ]
    gain1 = g1_ref[...].reshape(1, C)
    gain2 = g2_ref[...].reshape(1, C)

    def arrived(a):
        for i in range(3):
            exchange(a, i).wait_recv()
        own[a].wait()
        for slot, row, col, rows in pieces():
            stage[a, rows, :] = arrive[a, slot, row, col].astype(F32)
        return stage[a]

    tokens = arrived(0)
    normed, hat1, inv1 = normalize(tokens, gain1)
    first = normed.astype(BF16)
    qkv = (dot(first, wqkv_ref[...]) + bqkv_ref[...].reshape(1, 3 * C)).astype(BF16)
    queries = qkv[:, 0:C]
    keys = qkv[:, C : 2 * C]
    values = qkv[:, 2 * C : 3 * C]
    queries_t = queries.T

    @pl.when(lat == 0)
    def _():
        table_copy().wait_recv()
        for head in range(HEADS):
            tabw[head : head + 1, 0:NREL] = tab15[0, head]
        tin[0:48, :] = jnp.zeros((48, 512), F32)
        for zp in range(WIN_Z):
            for zq in range(WIN_Z):
                for hp in range(3):
                    spread(tabw, zp, zq, hp, 3 * SPAN)
        upper_rows = permuted(tin[0:48, :]) + cross_ref[0:48, :]
        for n in range(3):
            ymat[n, 0:48, :] = upper_rows[:, 128 * n : 128 * (n + 1)]
        place_bias(8, 6)

    wide_rows[...] = jnp.zeros_like(wide_rows)
    wide_cols[...] = jnp.zeros_like(wide_cols)
    for head in range(HEADS):
        wide_cols[256 * head : 256 * head + T, :] = values * ones[head]
    for head in range(HEADS):
        q = queries * ones[head]
        scores = dot_nt(q, keys) * (FACTOR * LOG2E) + bias[head]
        top = jnp.max(scores, -1, keepdims=True)
        raised = jnp.exp2(scores - top)
        probs = raised * (1.0 / jnp.sum(raised, -1, keepdims=True))
        prob[head] = probs
        probs_low = probs.astype(BF16)
        wide_rows[:, 256 * head : 256 * head + T] = probs_low
    mixed = dot(wide_rows[...], wide_cols[...]).astype(BF16)
    inner = tokens + dot(mixed, wproj_ref[...]).astype(BF16).astype(F32)

    def remote(src, dst, send_sem, recv_sem, target):
        return pltpu.make_async_remote_copy(
            src_ref=src, dst_ref=dst, send_sem=send_sem, recv_sem=recv_sem,
            device_id=target, device_id_type=MESH,
        )

    def wait_bytes(ref, sem):
        pltpu.make_async_copy(ref, ref, sem).wait()

    def add(*terms):
        total = terms[0].astype(F32)
        for term in terms[1:]:
            total = total + term.astype(F32)
        return total.astype(BF16)

    axes = [(n, (n + 1) % 3, (n + 2) % 3) for n in range(3)]
    places = [tuple(spot[axis] for axis in order) for order in axes]

    def block(n, i):
        return pl.ds(n * 16 + i * 4, 4)

    def unit(n):
        return n * 16 + places[n][0] * 4 + places[n][1]

    def part_to_line(n, stage_no, which, src, dst):
        for d in range(1, 4):
            at = lax.rem(places[n][which] + d, 4)
            remote(
                src(n, at), dst(n, d), f_send.at[stage_no], f_recv.at[stage_no],
                on_axis(axes[n][which], at),
            ).start()

    def to_line(stage_no, which, src, dst):
        for n in range(3):
            part_to_line(n, stage_no, which, src, dst)

    pair_fc = [
        remote(
            parts_fc.at[other, pl.ds(12 * n, 12)], core_fc.at[pl.ds(12 * n, 12)],
            p_send.at[n], p_recv.at[n], sibling,
        )
        for n in range(4)
    ]
    swap_fc = remote(
        gath_fc.at[core], gath_fc_out.at[core], f_send.at[6], f_recv.at[6], sibling
    )
    pair_att = remote(parts_att.at[other], core_att, a_send.at[0], a_recv.at[0], sibling)
    swap_att = remote(
        gath_att.at[core], gath_att_out.at[core], a_send.at[4], a_recv.at[4], sibling
    )
    keep = [
        pltpu.make_async_copy(src, dst, out_sem.at[n])
        for n, (src, dst) in enumerate((
            (out_stage.at[0, 3], quadrant(block_out, 0)),
            (out_stage.at[1, 3], quadrant(dtok_out, 0)),
            (dtab_ref, dtab_out), (gath_fc.at[core], gath_fc_out.at[core]),
            (gath_att.at[core], gath_att_out.at[core]),
        ))
    ]

    def early1():
        for n in range(3):
            if n == 0:
                pair_fc[0].wait_recv()
            pair_fc[n + 1].wait_recv()
            rows = pl.ds(16 * n, 16)
            parts_fc[core, rows] = add(parts_fc[core, rows], core_fc[rows])
            part_to_line(
                n, 1, 0, lambda n, at: parts_fc.at[core, block(n, at)],
                lambda n, d: fold1.at[n, d - 1],
            )

    def early2():
        wait_bytes(fold1, f_recv.at[1])
        for n in range(3):
            own = parts_fc[core, block(n, places[n][0])]
            sum1[n] = add(own, fold1[n, 0], fold1[n, 1], fold1[n, 2])
        to_line(2, 1, lambda n, at: sum1.at[n, at], lambda n, d: fold2.at[n, d - 1])

    def early3():
        wait_bytes(fold2, f_recv.at[2])
        for n in range(3):
            own = sum1[n, places[n][1]]
            sum2[n] = add(own, fold2[n, 0], fold2[n, 1], fold2[n, 2])
            fold3[n, places[n][2]] = sum2[n]
        to_line(3, 2, lambda n, at: sum2.at[n], lambda n, d: fold3.at[n, places[n][2]])

    def early4():
        wait_bytes(fold2, f_recv.at[3])
        for n in range(3):
            gath_fc[core, unit(n)] = add(*[fold3[n, i] for i in range(4)])
        to_line(
            4, 1, lambda n, at: gath_fc.at[core, unit(n)], lambda n, d: gath_fc.at[core, unit(n)]
        )

    def early5():
        wait_bytes(fold2, f_recv.at[4])
        to_line(
            5, 0,
            lambda n, at: gath_fc.at[core, block(n, places[n][0])],
            lambda n, d: gath_fc.at[core, block(n, places[n][0])],
        )

    def early6():
        wait_bytes(fold1, f_recv.at[5])
        swap_fc.start()
        keep[3].start()

    own_rows = pl.ds(pair_row * 4, 4)

    def late1():
        pair_att.wait_recv()
        parts_att[core] = add(parts_att[core], core_att[...])
        for d in range(1, ROWS):
            remote(
                parts_att.at[core, pl.ds(row_of(d) * 4, 4)], fold_att.at[d - 1],
                a_send.at[1], a_recv.at[1], (lon, row_of(d) * 2 + core),
            ).start()

    def late2():
        wait_bytes(fold_att, a_recv.at[1])
        sum_att[...] = add(parts_att[core, own_rows], *[fold_att[d] for d in range(ROWS - 1)])
        mid_att[lon] = sum_att[...]
        for d in range(1, STRIPS):
            remote(
                sum_att, mid_att.at[lon], a_send.at[2], a_recv.at[2], (strip(d), lat)
            ).start()

    def late3():
        wait_bytes(fold_att, a_recv.at[2])
        gath_att[core, own_rows] = add(*[mid_att[i] for i in range(STRIPS)])
        for d in range(1, ROWS):
            remote(
                gath_att.at[core, own_rows], gath_att.at[core, own_rows],
                a_send.at[3], a_recv.at[3], (lon, row_of(d) * 2 + core),
            ).start()

    def late4():
        wait_bytes(fold_att, a_recv.at[3])
        swap_att.start()
        keep[4].start()

    cot = arrived(1)
    cot_low = cot.astype(BF16)
    normed, hat2, inv2 = normalize(inner, gain2)
    second = normed.astype(BF16)
    second_t = second.T
    cot_t = cot_low.T
    total = inner
    grad_second = jnp.zeros((T, C), F32)
    bfc1 = bfc1_ref[...].reshape(1, HID)
    vec[...] = jnp.zeros_like(vec)
    for n in range(3):
        cols = slice(256 * n, 256 * (n + 1))
        pre = dot(second, wfc1_ref[:, cols]) + bfc1[:, cols]
        cdf = 0.5 * (1.0 + lax.erf(pre * 0.7071067811865476))
        density = jnp.exp(-0.5 * pre * pre) * 0.3989422804014327
        act = (pre * cdf).astype(BF16)
        total = total + dot_nt(act, wfc2_ref[:, cols])
        grad_pre = (dot(cot_low, wfc2_ref[:, cols]) * (cdf + pre * density)).astype(BF16)
        grad_second = grad_second + dot_nt(grad_pre, wfc1_ref[:, cols])
        parts_fc[0, 12 * n : 12 * (n + 1)] = dot(second_t, grad_pre).astype(BF16).reshape(12, 16, 256)
        parts_fc[1, 12 * n : 12 * (n + 1)] = dot(cot_t, act).astype(BF16).reshape(12, 16, 256)
        vec[n : n + 1, :] = jnp.sum(grad_pre.astype(F32), 0, keepdims=True)
        pair_fc[n].start()

    def give_back(a, i):
        return pltpu.make_async_remote_copy(
            src_ref=out_stage.at[a, 2 - i],
            dst_ref=quadrant((block_out, dtok_out)[a], i + 1),
            send_sem=rt_send.at[a, i],
            recv_sem=rt_recv.at[a, i],
            device_id=behind[i],
            device_id_type=MESH,
        )

    def hand_out(a, field):
        stage[a] = field
        for slot, row, col, rows in pieces():
            out_stage[a, slot, row, col] = stage[a, rows, :].astype(BF16)
        for i in range(3):
            give_back(a, i).start()
        keep[a].start()

    grad_inner = cot + norm_back(hat2, inv2, gain2, grad_second)
    grad_att = grad_inner.astype(BF16)
    proj_grad = dot_tn(mixed, grad_att).astype(BF16)
    proj_grad = jnp.concatenate([proj_grad, jnp.zeros((C, 64), BF16)], -1).reshape(12, 16, 256)
    parts_fc[0, 36:42] = proj_grad[:6]
    parts_fc[1, 36:42] = proj_grad[6:]
    vec[3:4, 0:C] = jnp.sum(grad_second * hat2, 0, keepdims=True)
    parts_fc[0, 42] = vec[...].astype(BF16)
    parts_fc[1, 42] = jnp.zeros((16, 256), BF16)
    parts_fc[:, 43:] = jnp.zeros((2, FC - 43, 16, 256), BF16)
    pair_fc[3].start()
    hand_out(0, total)

    grad_mixed = dot_nt(grad_att, wproj_ref[...]).astype(BF16)
    grad_mixed_t = grad_mixed.T
    dsc[...] = jnp.zeros_like(dsc)
    for head in range(HEADS):
        wide_cols[256 * head : 256 * head + T, :] = keys * ones[head]
    grad_k_t = []
    grad_v_t = []
    for head in range(HEADS):
        rows = slice(HEAD * head, HEAD * (head + 1))
        gm = grad_mixed * ones[head]
        probs = prob[head]
        grad_probs = dot_nt(gm, values)
        inside = jnp.sum(probs * grad_probs, -1, keepdims=True)
        grad_scores = probs * (grad_probs - inside)
        dsc[head, 0:T, 0:T] = grad_scores
        scaled = (grad_scores * FACTOR).astype(BF16)
        grad_v_t.append(
            dot(grad_mixed_t[rows], wide_rows[:, 256 * head : 256 * head + T])
        )
        wide_rows[:, 256 * head : 256 * head + T] = scaled
        grad_k_t.append(dot(queries_t[rows], scaled))
        if head == 2:
            early1()
    grad_q = dot(wide_rows[...], wide_cols[...])
    grad_k = jnp.concatenate(grad_k_t, 0).T
    grad_v = jnp.concatenate(grad_v_t, 0).T

    grad_qkv = jnp.concatenate([grad_q, grad_k, grad_v], -1).astype(BF16)
    wide = dot_tn(first, grad_qkv).astype(BF16)
    for n in range(4):
        parts_att[n // 2, n % 2 * 12 : n % 2 * 12 + 12] = (
            wide[:, 128 * n : 128 * (n + 1)].reshape(12, 16, 128)
        )
    edge = jnp.concatenate([wide[:96, 512:576], wide[96:, 512:576]], -1).reshape(6, 16, 128)
    parts_att[0, 24:27] = edge[:3]
    parts_att[1, 24:27] = edge[3:]
    grad_first = dot_nt(grad_qkv, wqkv_ref[...]).astype(BF16).astype(F32)
    vec[...] = jnp.zeros_like(vec)
    sums = jnp.sum(grad_qkv.astype(F32), 0, keepdims=True)
    sums = [sums[:, C * n : C * (n + 1)] for n in range(3)]
    sums.append(jnp.sum(grad_first * hat1, 0, keepdims=True))
    for n in range(4):
        vec[2 * n : 2 * n + 1, 0:128] = sums[n][:, 0:128]
        vec[2 * n + 1 : 2 * n + 2, 0:64] = sums[n][:, 128:C]
    parts_att[0, 27] = vec[:, 0:128].astype(BF16)
    parts_att[1, 27] = jnp.zeros((16, 128), BF16)
    parts_att[:, 28:] = jnp.zeros((2, ATT - 28, 16, 128), BF16)
    pair_att.start()
    d_tokens = grad_inner + norm_back(hat1, inv1, gain1, grad_first)
    hand_out(1, d_tokens)

    dmat[...] = jnp.zeros_like(dmat)
    for head in range(HEADS):
        if head == 3:
            late1()
            early2()
        acc = jnp.zeros((16, 384), F32)
        for w in range(WIN_W):
            acc = acc + pltpu.roll(
                dsc[head, w * GROUPS : w * GROUPS + 16, :], (WIN_W - 1 - w) * GROUPS, axis=1
            )
        for n in range(3):
            dmat[n, pl.ds(head, 16, stride=8), :] = acc[:, 128 * n : 128 * (n + 1)]

    def table_grad():
        return jnp.concatenate([dmat[n, 0:96, :] for n in range(3)], -1)

    def keep_table(field):
        for n in range(3):
            dmat[n, 0:96, :] = field[:, 128 * n : 128 * (n + 1)]

    def edge_copy():
        return pltpu.make_async_remote_copy(
            src_ref=bbs,
            dst_ref=bbr,
            send_sem=one_send.at[1],
            recv_sem=one_recv.at[1],
            device_id=(lon, north),
            device_id_type=MESH,
        )

    @pl.when(lat == 0)
    def _():
        upper = lax.broadcasted_iota(jnp.int32, (96, 384), 0) < 48
        full = table_grad()
        bbs[...] = jnp.where(upper, full, 0.0).astype(BF16)
        edge_copy().start()
        keep_table(jnp.where(upper, 0.0, full))

    @pl.when(lat == BANDS - 1)
    def _():
        edge_copy().wait_recv()
        keep_table(table_grad() + bbr[...].astype(F32))

    bsend[...] = table_grad().astype(BF16).reshape(PARTS, 16, 384)

    for owner in range(PARTS):
        @pl.when(lon != owner)
        def _():
            pltpu.make_async_remote_copy(
                src_ref=bsend.at[owner],
                dst_ref=brecv.at[lon],
                send_sem=b_send.at[0],
                recv_sem=b_recv.at[0],
                device_id=(owner, lat),
                device_id_type=MESH,
            ).start()

    early3()
    late2()
    early4()
    seven = brecv.at[pl.ds(0, STRIPS - 1)]

    @pl.when(lon < PARTS)
    def _():
        brecv[lon] = bsend[lon]
        wait_bytes(seven, b_recv.at[0])
        bfin[lon] = jnp.sum(brecv[...].astype(F32), 0).astype(BF16)
        for d in range(1, STRIPS):
            pltpu.make_async_remote_copy(
                src_ref=bfin.at[lon],
                dst_ref=bfin.at[lon],
                send_sem=b_send.at[1],
                recv_sem=b_recv.at[1],
                device_id=(strip(d), lat),
                device_id_type=MESH,
            ).start()

    early5()
    late3()

    @pl.when(lon < PARTS)
    def _():
        wait_bytes(bfin.at[pl.ds(0, PARTS - 1)], b_recv.at[1])

    @pl.when(lon >= PARTS)
    def _():
        wait_bytes(bfin, b_recv.at[1])

    tin[...] = dot_nt(bfin[...].reshape(96, 384), perm_ref[...])
    dtab_ref[...] = jnp.zeros_like(dtab_ref)
    for zp in range(WIN_Z):
        for zq in range(WIN_Z):
            for hp in range(WIN_H):
                j = (zp * WIN_Z + zq) * WIN_H + hp
                first_lane = j * WIN_H * SPAN
                base = first_lane // 128 * 128
                g = hp * WIN_Z + zp
                piece = tin[g * 8 : g * 8 + 8, zq * 256 : zq * 256 + 256]
                piece = jnp.concatenate([piece, jnp.zeros((8, 128), F32)], -1)
                moved = pltpu.roll(piece, first_lane - base, axis=1)
                dtab_ref[:, base : base + 384] = dtab_ref[:, base : base + 384] + moved

    keep[2].start()
    early6()
    late4()

    for a in range(2):
        for i in range(3):
            exchange(a, i).wait_send()
            give_back(a, i).wait()

    @pl.when(lat == BANDS - 1)
    def _():
        table_copy().wait_send()

    @pl.when(lat == 0)
    def _():
        edge_copy().wait_send()

    for copy in pair_fc:
        copy.wait_send()
    for stage_no, ref in ((1, fold1), (2, fold2), (3, fold2), (4, fold2), (5, fold1)):
        wait_bytes(ref, f_send.at[stage_no])
    pair_att.wait_send()
    for stage_no in (1, 2, 3):
        wait_bytes(fold_att, a_send.at[stage_no])

    @pl.when(lon < PARTS)
    def _():
        wait_bytes(bsend.at[pl.ds(0, PARTS - 1)], b_send.at[0])
        wait_bytes(seven, b_send.at[1])

    @pl.when(lon >= PARTS)
    def _():
        wait_bytes(bsend, b_send.at[0])

    for copy in keep:
        copy.wait()
    swap_fc.wait()
    swap_att.wait()


def output_kernel(*refs):
    ins, outs = refs[:5], refs[5:16]
    in_bufs, out_bufs = refs[16:21], refs[21:30]
    in_sem, out_sem = refs[30:]
    loads = [
        pltpu.make_async_copy(src, dst, in_sem.at[n])
        for n, (src, dst) in enumerate(zip(ins, in_bufs))
    ]
    stores = [
        pltpu.make_async_copy(src, dst, out_sem.at[n])
        for n, (src, dst) in enumerate(zip(in_bufs[:2] + out_bufs, outs))
    ]
    gath_ref, gath_att, dtab_ref = in_bufs[2:]
    (
        dln1_ref, dwqkv_ref, dbqkv_ref, dbias_ref, dwproj_ref, dln2_ref,
        dwfc1_ref, dbfc1_ref, dwfc2_ref,
    ) = out_bufs
    for n in (2, 0, 1, 3, 4):
        loads[n].start()
    loads[2].wait()
    for n in range(3):
        cols = slice(256 * n, 256 * (n + 1))
        rows = slice(12 * n, 12 * (n + 1))
        dwfc1_ref[:, cols] = gath_ref[0, rows].reshape(C, 256).astype(F32)
    stores[8].start()
    for n in range(3):
        cols = slice(256 * n, 256 * (n + 1))
        rows = slice(12 * n, 12 * (n + 1))
        dwfc2_ref[:, cols] = gath_ref[1, rows].reshape(C, 256).astype(F32)
    stores[10].start()
    for k in range(2):
        dwproj_ref[96 * k : 96 * (k + 1), :] = (
            gath_ref[k, 36:42].reshape(96, 256)[:, 0:C].astype(F32)
        )
    vec = gath_ref[0, 42].astype(F32)
    dbfc1_ref[...] = jnp.concatenate([vec[n : n + 1] for n in range(3)], -1).reshape(HID)
    dln2_ref[...] = vec[3:4, :C].reshape(C)
    for n in (6, 9, 7):
        stores[n].start()
    for n in range(2):
        loads[n].wait()
        stores[n].start()
    loads[3].wait()
    for k in range(2):
        for n in range(2):
            cols = slice(256 * k + 128 * n, 256 * k + 128 * (n + 1))
            dwqkv_ref[:, cols] = gath_att[k, 12 * n : 12 * (n + 1)].reshape(C, 128).astype(F32)
        edge = gath_att[k, 24:27].reshape(48, 128).astype(F32)
        for n in range(2):
            at = 96 * n + 48 * k
            dwqkv_ref[at : at + 48, 512:576] = edge[:, 64 * n : 64 * (n + 1)]
    vec = gath_att[0, 27].astype(F32)
    sums = [
        jnp.concatenate([vec[2 * n : 2 * n + 1], vec[2 * n + 1 : 2 * n + 2, :64]], -1)
        for n in range(4)
    ]
    dbqkv_ref[...] = jnp.concatenate(sums[:3], -1).reshape(3 * C)
    dln1_ref[...] = sums[3].reshape(C)
    for n in (3, 4, 2):
        stores[n].start()
    loads[4].wait()
    for head in range(HEADS):
        dbias_ref[0, head] = dtab_ref[head : head + 1, 0:NREL]
    stores[5].start()
    for store in stores:
        store.wait()


def per_device(
    tokens, cotangent, ln1_gain, w_qkv, b_qkv, bias_table, w_proj, ln2_gain, w_fc1, b_fc1, w_fc2
):
    hbm = pl.BlockSpec(memory_space=pl.ANY)
    perm = table_order()
    dma = pltpu.SemaphoreType.DMA
    args = (
        tokens.transpose(1, 2, 0, 3), cotangent.transpose(1, 2, 0, 3), ln1_gain, w_qkv, b_qkv,
        bias_table.transpose(0, 2, 1, 3), w_proj, ln2_gain, w_fc1, b_fc1, w_fc2.T,
        jnp.asarray(perm, BF16), jnp.asarray(cross_pairs()),
    )
    gathered, gathered_att, block, d_tok, table = pl.pallas_call(
        block_kernel,
        out_shape=(
            jax.ShapeDtypeStruct((2, FC, 16, 256), BF16),
            jax.ShapeDtypeStruct((2, ATT, 16, 128), BF16),
            jax.ShapeDtypeStruct((WIN_H, WIN_W, WIN_Z, C), BF16),
            jax.ShapeDtypeStruct((WIN_H, WIN_W, WIN_Z, C), BF16),
            jax.ShapeDtypeStruct((8, 3456), F32),
        ),
        in_specs=[hbm] * len(args),
        out_specs=(hbm,) * 5,
        scratch_shapes=[pltpu.VMEM(a.shape, a.dtype) for a in args[2:]]
        + [
            pltpu.VMEM((2, T, C), F32),
            pltpu.VMEM((2, 4, 3, 6, WIN_Z, C), BF16),
            pltpu.VMEM((2, 4, 3, 6, WIN_Z, C), BF16),
            pltpu.VMEM((8, 3456), F32),
            pltpu.VMEM((1, HEADS, 1, NREL), F32),
            pltpu.VMEM((96, 512), F32),
            pltpu.VMEM((3, 128, 128), F32),
            pltpu.VMEM((HEADS, T, T), F32),
            pltpu.VMEM((HEADS, T, T), F32),
            pltpu.VMEM((T, HEADS * 256), BF16),
            pltpu.VMEM((HEADS * 256, C), BF16),
            pltpu.VMEM((HEADS, 160, 384), F32),
            pltpu.VMEM((3, 128, 128), F32),
            pltpu.VMEM((16, 256), F32),
            pltpu.VMEM((PARTS, 16, 384), BF16),
            pltpu.VMEM((STRIPS, 16, 384), BF16),
            pltpu.VMEM((PARTS, 16, 384), BF16),
            pltpu.VMEM((96, 384), BF16),
            pltpu.VMEM((96, 384), BF16),
            pltpu.VMEM((2, FC, 16, 256), BF16),
            pltpu.VMEM((2, ATT, 16, 128), BF16),
            pltpu.VMEM((FC, 16, 256), BF16),
            pltpu.VMEM((ATT, 16, 128), BF16),
            pltpu.VMEM((3, 3, 4, 16, 256), BF16),
            pltpu.VMEM((3, 4, 16, 256), BF16),
            pltpu.VMEM((3, 3, 16, 256), BF16),
            pltpu.VMEM((3, 16, 256), BF16),
            pltpu.VMEM((3, 4, 16, 256), BF16),
            pltpu.VMEM((ROWS - 1, 4, 16, 128), BF16),
            pltpu.VMEM((4, 16, 128), BF16),
            pltpu.VMEM((STRIPS, 4, 16, 128), BF16),
            pltpu.VMEM((2, FC, 16, 256), BF16),
            pltpu.VMEM((2, ATT, 16, 128), BF16),
            pltpu.VMEM((8, 3456), F32),
            dma((len(args) - 2,)), dma((2,)), dma((5,)),
            dma((2, 3)), dma((2, 3)), dma((2, 3)), dma((2, 3)),
            dma((2,)), dma((2,)), dma((4,)), dma((4,)), dma((7,)), dma((7,)),
            dma((5,)), dma((5,)), dma((2,)), dma((2,)),
        ],
        compiler_params=pltpu.CompilerParams(
            collective_id=0, has_side_effects=True, vmem_limit_bytes=VMEM_LIMIT
        ),
    )(*args)
    shape = jax.ShapeDtypeStruct
    grid_shape = (WIN_H, WIN_W, WIN_Z, C)
    results_out = (
        shape(grid_shape, BF16), shape(grid_shape, BF16),
        shape((C,), F32), shape((C, 3 * C), F32), shape((3 * C,), F32),
        shape((1, HEADS, 1, NREL), F32), shape((C, C), F32), shape((C,), F32),
        shape((C, HID), F32), shape((HID,), F32), shape((C, HID), F32),
    )
    outs = pl.pallas_call(
        output_kernel,
        out_shape=results_out,
        in_specs=[hbm] * 5,
        out_specs=(hbm,) * 11,
        scratch_shapes=[
            pltpu.VMEM(a.shape, a.dtype)
            for a in (block, d_tok, gathered, gathered_att, table) + results_out[2:]
        ]
        + [dma((5,)), dma((11,))],
        compiler_params=pltpu.CompilerParams(vmem_limit_bytes=VMEM_LIMIT),
    )(block, d_tok, gathered, gathered_att, table)
    out, d_tok, d_ln1, d_wqkv, d_bqkv, d_bias, d_wproj, d_ln2, d_wfc1, d_bfc1, d_wfc2 = outs
    return (
        out.transpose(2, 0, 1, 3), d_tok.transpose(2, 0, 1, 3), d_ln1, d_wqkv, d_bqkv,
        d_bias.transpose(0, 2, 1, 3), d_wproj, d_ln2, d_wfc1, d_bfc1, d_wfc2.T,
    )


def solution(mesh):
    grid = P(None, "lat", "lon", None)
    rows = P(None, "lat", None, None)
    return jax.shard_map(
        per_device,
        mesh=mesh,
        in_specs=(grid, grid, P(), P(), P(), rows, P(), P(), P(), P(), P()),
        out_specs=(grid, grid, P(), P(), P(), rows, P(), P(), P(), P(), P()),
        check_vma=False,
    )
```

```python
import jax
import jax.numpy as jnp
import numpy as np
from jax import lax
from jax.experimental import pallas as pl
from jax.experimental.pallas import tpu as pltpu
from jax.sharding import PartitionSpec as P

HEADS = 6
WIN_Z = 2
WIN_H = 6
WIN_W = 12
SPAN = 2 * WIN_W - 1
GROUPS = WIN_Z * WIN_H
T = GROUPS * WIN_W
C = 192
HID = 768
HEAD = C // HEADS
NREL = GROUPS * GROUPS * SPAN
FC = 48
ATT = 32
ROWS = 8
BANDS = 16
STRIPS = 8
PARTS = 6
EPSILON = 1e-05
VMEM_LIMIT = 56 * 1024 * 1024
FACTOR = HEAD ** (-0.5)
LOG2E = 1.4426950408889634
F32 = jnp.float32
BF16 = jnp.bfloat16
MESH = pl.DeviceIdType.MESH


def table_order():
    grid = np.zeros((512, 384), np.float32)
    for z in range(WIN_Z):
        for h in range(WIN_H):
            for i in range(SPAN):
                grid[z * 256 + h * SPAN + i, (SPAN - 1 - i) * GROUPS + h * WIN_Z + z] = 1
    return grid


def cross_pairs():
    g = np.arange(96)[:, None] // 8 // WIN_Z
    q = np.arange(384)[None, :] % GROUPS // WIN_Z
    return np.where((g < 3) != (q < 3), -1e30, 0.0).astype(np.float32)


def dot(a, b):
    return jnp.dot(a, b, preferred_element_type=F32)


def dot_nt(a, b):
    return lax.dot_general(a, b, (((1,), (1,)), ((), ())), preferred_element_type=F32)


def dot_tn(a, b):
    return lax.dot_general(a, b, (((0,), (0,)), ((), ())), preferred_element_type=F32)


def normalize(values, gain):
    average = jnp.mean(values, -1, keepdims=True)
    centered = values - average
    inv = lax.rsqrt(jnp.mean(centered * centered, -1, keepdims=True) + EPSILON)
    hat = centered * inv
    return hat * gain, hat, inv


def norm_back(hat, inv, gain, grad):
    scaled = grad * gain
    return inv * (
        scaled
        - jnp.mean(scaled, -1, keepdims=True)
        - hat * jnp.mean(scaled * hat, -1, keepdims=True)
    )


def pieces():
    for h in range(WIN_H):
        for w in range(WIN_W):
            at = w * GROUPS + h * WIN_Z
            yield (h // 3) * 2 + w // 6, h % 3, w % 6, slice(at, at + WIN_Z)


def quadrant(ref, q):
    return ref.at[pl.ds(q // 2 * 3, 3), pl.ds(q % 2 * 6, 6)]


def block_kernel(
    tok_any, cot_any, g1_any, wqkv_any, bqkv_any, table_any, wproj_any, g2_any, wfc1_any,
    bfc1_any, wfc2_any, perm_any, cross_any,
    gath_fc_out, gath_att_out, block_out, dtok_out, dtab_out,
    g1_ref, wqkv_ref, bqkv_ref, table_ref, wproj_ref, g2_ref, wfc1_ref,
    bfc1_ref, wfc2_ref, perm_ref, cross_ref,
    stage, arrive, out_stage,
    tabw, tab15, tin, ymat, bias, prob, wide_rows, wide_cols, dsc, dmat, vec,
    bsend, brecv, bfin, bbs, bbr,
    parts_fc, parts_att, fold1, sum1, fold2, sum2, fold3, fold_att, sum_att,
    mid_att, gath_fc, gath_att, dtab_ref,
    in_sem, own_sem, out_sem,
    ex_send, ex_recv, rt_send, rt_recv, one_send, one_recv, f_send, f_recv,
    a_send, a_recv, b_send, b_recv,
):
    sources = (
        (table_any, table_ref), (perm_any, perm_ref), (cross_any, cross_ref), (g1_any, g1_ref),
        (wqkv_any, wqkv_ref), (bqkv_any, bqkv_ref), (wproj_any, wproj_ref), (g2_any, g2_ref),
        (wfc1_any, wfc1_ref), (bfc1_any, bfc1_ref), (wfc2_any, wfc2_ref),
    )
    loads = [pltpu.make_async_copy(src, dst, in_sem.at[n]) for n, (src, dst) in enumerate(sources)]
    lon = lax.axis_index("lon")
    lat = lax.axis_index("lat")
    core = lax.rem(lat, 2)
    other = 1 - core
    pair_row = lat // 2
    east = lax.rem(lon + 1, STRIPS)
    west = lax.rem(lon + STRIPS - 1, STRIPS)
    south = lax.rem(lat + 1, BANDS)
    north = lax.rem(lat + BANDS - 1, BANDS)

    spot = (lax.rem(pair_row, 4), lon // 2, lax.rem(lon, 2) * 2 + lat // 8)

    def on_axis(axis, at, side=core):
        if axis == 0:
            return (lon, lat // 8 * 8 + at * 2 + side)
        if axis == 1:
            return (at * 2 + lax.rem(lon, 2), lat - core + side)
        return (spot[1] * 2 + at // 2, lax.rem(at, 2) * 8 + spot[0] * 2 + side)

    def strip(d):
        return lax.rem(lon + d, STRIPS)

    def row_of(d):
        return lax.rem(pair_row + d, ROWS)

    barrier = pltpu.get_barrier_semaphore()

    def greet(target):
        pl.semaphore_signal(barrier, inc=1, device_id=target, device_id_type=MESH)

    for target in ((east, south), (west, north)):
        greet(target)
    for d in range(1, STRIPS):
        greet((strip(d), lat))
    for d in range(1, BANDS):
        greet((lon, lax.rem(lat + d, BANDS)))
    for d in range(1, 4):
        greet(on_axis(1, lax.rem(spot[1] + d, 4), other))
    across = lax.rem(spot[2] + 2, 4)
    greet(on_axis(2, across, other))
    greet(on_axis(2, 3 - spot[2]))
    greet(on_axis(2, 3 - spot[2], other))
    loads[0].start()
    own = [
        pltpu.make_async_copy(quadrant(src, 0), arrive.at[a, 3], own_sem.at[a])
        for a, src in enumerate((tok_any, cot_any))
    ]
    own[0].start()
    pl.semaphore_wait(barrier, 30)

    ahead = ((east, lat), (lon, south), (east, south))
    behind = ((west, lat), (lon, north), (west, north))

    def exchange(a, i):
        return pltpu.make_async_remote_copy(
            src_ref=quadrant((tok_any, cot_any)[a], i + 1),
            dst_ref=arrive.at[a, 2 - i],
            send_sem=ex_send.at[a, i],
            recv_sem=ex_recv.at[a, i],
            device_id=ahead[i],
            device_id_type=MESH,
        )

    def table_copy():
        return pltpu.make_async_remote_copy(
            src_ref=table_any,
            dst_ref=tab15,
            send_sem=one_send.at[0],
            recv_sem=one_recv.at[0],
            device_id=(lon, south),
            device_id_type=MESH,
        )

    @pl.when(lat == BANDS - 1)
    def _():
        table_copy().start()

    for a in range(2):
        for i in range(3):
            exchange(a, i).start()
    for load in loads[1:]:
        load.start()
    own[1].start()

    tabw[...] = jnp.zeros_like(tabw)
    loads[0].wait()
    for head in range(HEADS):
        tabw[head : head + 1, 0:NREL] = table_ref[0, head]

    tin[...] = jnp.zeros_like(tin)

    def spread(src, zp, zq, hp, width):
        j = (zp * WIN_Z + zq) * WIN_H + hp
        first = j * WIN_H * SPAN
        base = first // 128 * 128
        wide = src[:, base : base + 384]
        moved = pltpu.roll(wide, (384 - (first - base)) % 384, axis=1)
        g = hp * WIN_Z + zp
        tin[g * 8 : g * 8 + 8, zq * 256 : zq * 256 + width] = moved[:, :width]

    for zp in range(WIN_Z):
        for zq in range(WIN_Z):
            for hp in range(WIN_H):
                spread(tabw, zp, zq, hp, WIN_H * SPAN)

    def permuted(whole):
        high = whole.astype(BF16)
        rest = whole - high.astype(F32)
        middle = rest.astype(BF16)
        low = (rest - middle.astype(F32)).astype(BF16)
        perm = perm_ref[...]
        return (dot(high, perm) + dot(middle, perm) + dot(low, perm)) * LOG2E

    loads[1].wait()
    spread_rows = permuted(tin[...])
    for n in range(3):
        ymat[n, 0:96, :] = spread_rows[:, 128 * n : 128 * (n + 1)]
        ymat[n, 96:128, :] = jnp.zeros((32, 128), F32)
    loads[2].wait()

    @pl.when(lat == 0)
    def _():
        for n in range(3):
            ymat[n, 0:96, :] = ymat[n, 0:96, :] + cross_ref[:, 128 * n : 128 * (n + 1)]

    def place_bias(tall, count):
        for head in range(HEADS):
            rows = jnp.concatenate(
                [ymat[n, pl.ds(head, tall, stride=8), :] for n in range(3)], -1
            )
            for w in range(WIN_W):
                moved = pltpu.roll(rows, (384 - (WIN_W - 1 - w) * GROUPS) % 384, axis=1)
                bias[head, w * GROUPS : w * GROUPS + count, :] = moved[:count, :T]

    place_bias(16, GROUPS)
    for n in range(3, 11):
        loads[n].wait()
    lane = lax.broadcasted_iota(jnp.int32, (16, C), 1)
    ones = [
        jnp.where((lane >= HEAD * i) & (lane < HEAD * (i + 1)), 1.0, 0.0).astype(BF16)[0:1]
        for i in range(HEADS)
    ]
    gain1 = g1_ref[...].reshape(1, C)
    gain2 = g2_ref[...].reshape(1, C)

    def arrived(a):
        for i in range(3):
            exchange(a, i).wait_recv()
        own[a].wait()
        for slot, row, col, rows in pieces():
            stage[a, rows, :] = arrive[a, slot, row, col].astype(F32)
        return stage[a]

    tokens = arrived(0)
    normed, hat1, inv1 = normalize(tokens, gain1)
    first = normed.astype(BF16)
    qkv = (dot(first, wqkv_ref[...]) + bqkv_ref[...].reshape(1, 3 * C)).astype(BF16)
    queries = qkv[:, 0:C]
    keys = qkv[:, C : 2 * C]
    values = qkv[:, 2 * C : 3 * C]
    queries_t = queries.T

    @pl.when(lat == 0)
    def _():
        table_copy().wait_recv()
        for head in range(HEADS):
            tabw[head : head + 1, 0:NREL] = tab15[0, head]
        tin[0:48, :] = jnp.zeros((48, 512), F32)
        for zp in range(WIN_Z):
            for zq in range(WIN_Z):
                for hp in range(3):
                    spread(tabw, zp, zq, hp, 3 * SPAN)
        upper_rows = permuted(tin[0:48, :]) + cross_ref[0:48, :]
        for n in range(3):
            ymat[n, 0:48, :] = upper_rows[:, 128 * n : 128 * (n + 1)]
        place_bias(8, 6)

    wide_rows[...] = jnp.zeros_like(wide_rows)
    wide_cols[...] = jnp.zeros_like(wide_cols)
    for head in range(HEADS):
        wide_cols[256 * head : 256 * head + T, :] = values * ones[head]
    for head in range(HEADS):
        q = queries * ones[head]
        scores = dot_nt(q, keys) * (FACTOR * LOG2E) + bias[head]
        top = jnp.max(scores, -1, keepdims=True)
        raised = jnp.exp2(scores - top)
        probs = raised * (1.0 / jnp.sum(raised, -1, keepdims=True))
        prob[head] = probs
        probs_low = probs.astype(BF16)
        wide_rows[:, 256 * head : 256 * head + T] = probs_low
    mixed = dot(wide_rows[...], wide_cols[...]).astype(BF16)
    inner = tokens + dot(mixed, wproj_ref[...]).astype(BF16).astype(F32)

    def remote(src, dst, send_sem, recv_sem, target):
        return pltpu.make_async_remote_copy(
            src_ref=src, dst_ref=dst, send_sem=send_sem, recv_sem=recv_sem,
            device_id=target, device_id_type=MESH,
        )

    def wait_bytes(ref, sem):
        pltpu.make_async_copy(ref, ref, sem).wait()

    def add(*terms):
        total = terms[0].astype(F32)
        for term in terms[1:]:
            total = total + term.astype(F32)
        return total.astype(BF16)

    axes = [(n, (n + 1) % 3, (n + 2) % 3) for n in range(3)]
    places = [tuple(spot[axis] for axis in order) for order in axes]

    def block(n, i):
        return pl.ds(n * 16 + i * 4, 4)

    def unit(n):
        return n * 16 + places[n][0] * 4 + places[n][1]

    def part_to_line(n, stage_no, which, src, dst):
        for d in range(1, 4):
            at = lax.rem(places[n][which] + d, 4)
            remote(
                src(n, at), dst(n, d), f_send.at[stage_no], f_recv.at[stage_no],
                on_axis(axes[n][which], at),
            ).start()

    def to_line(stage_no, which, src, dst):
        for n in range(3):
            part_to_line(n, stage_no, which, src, dst)

    def seven(n):
        for d in range(1, 4):
            yield lax.rem(places[n][0] + d, 4), core, d - 1
        for d in range(4):
            yield lax.rem(places[n][0] + d, 4), other, 3 + d

    def early1(n):
        for at, side, slot in seven(n):
            remote(
                parts_fc.at[side, block(n, at)], fold1.at[n, slot], f_send.at[1], f_recv.at[1],
                on_axis(n, at, side),
            ).start()

    def early2():
        wait_bytes(fold1, f_recv.at[1])
        for n in range(3):
            own_block = parts_fc[core, block(n, places[n][0])]
            sum1[n] = add(own_block, *[fold1[n, i] for i in range(7)])
            part_to_line(n, 2, 1, lambda n, at: sum1.at[n, at], lambda n, d: fold2.at[n, d - 1])

    def early3():
        wait_bytes(fold2, f_recv.at[2])
        for n in range(3):
            own_unit = sum1[n, places[n][1]]
            sum2[n] = add(own_unit, fold2[n, 0], fold2[n, 1], fold2[n, 2])
            fold3[n, places[n][2]] = sum2[n]
        to_line(3, 2, lambda n, at: sum2.at[n], lambda n, d: fold3.at[n, places[n][2]])

    def early4():
        wait_bytes(fold2, f_recv.at[3])
        for n in range(3):
            gath_fc[unit(n)] = add(*[fold3[n, i] for i in range(4)])
        to_line(4, 1, lambda n, at: gath_fc.at[unit(n)], lambda n, d: gath_fc.at[unit(n)])

    def early5():
        wait_bytes(fold2, f_recv.at[4])
        for n in range(3):
            rows = block(n, places[n][0])
            for at, side, _ in seven(n):
                remote(
                    gath_fc.at[rows], gath_fc_out.at[core, rows], f_send.at[5], f_recv.at[5],
                    on_axis(n, at, side),
                ).start()
            keep[3 + n].start()

    own_rows = pl.ds(pair_row * 4, 4)

    def fifteen():
        for d in range(1, ROWS):
            yield row_of(d), core, d - 1
        for d in range(ROWS):
            yield row_of(d), other, 7 + d

    def late1():
        for row, side, slot in fifteen():
            remote(
                parts_att.at[side, pl.ds(row * 4, 4)], fold_att.at[slot],
                a_send.at[0], a_recv.at[0], (lon, row * 2 + side),
            ).start()

    def late2():
        wait_bytes(fold_att, a_recv.at[0])
        sum_att[...] = add(parts_att[core, own_rows], *[fold_att[i] for i in range(15)])
        mid_att[lon] = sum_att[...]
        for d in range(1, STRIPS):
            remote(
                sum_att, mid_att.at[lon], a_send.at[1], a_recv.at[1], (strip(d), lat)
            ).start()

    def late3():
        wait_bytes(mid_att.at[pl.ds(0, STRIPS - 1)], a_recv.at[1])
        gath_att[...] = add(*[mid_att[i] for i in range(STRIPS)])
        for row, side, _ in fifteen():
            remote(
                gath_att, gath_att_out.at[core, own_rows],
                a_send.at[2], a_recv.at[2], (lon, row * 2 + side),
            ).start()
        keep[6].start()

    keep = [
        pltpu.make_async_copy(src, dst, out_sem.at[n])
        for n, (src, dst) in enumerate(
            [
                (out_stage.at[0, 3], quadrant(block_out, 0)),
                (out_stage.at[1, 3], quadrant(dtok_out, 0)),
                (dtab_ref, dtab_out),
            ]
            + [
                (gath_fc.at[block(n, places[n][0])], gath_fc_out.at[core, block(n, places[n][0])])
                for n in range(3)
            ]
            + [(gath_att, gath_att_out.at[core, own_rows])]
        )
    ]

    cot = arrived(1)
    cot_low = cot.astype(BF16)
    normed, hat2, inv2 = normalize(inner, gain2)
    second = normed.astype(BF16)
    second_t = second.T
    cot_t = cot_low.T
    total = inner
    grad_second = jnp.zeros((T, C), F32)
    bfc1 = bfc1_ref[...].reshape(1, HID)
    vec[...] = jnp.zeros_like(vec)
    for n in range(3):
        cols = slice(256 * n, 256 * (n + 1))
        pre = dot(second, wfc1_ref[:, cols]) + bfc1[:, cols]
        cdf = 0.5 * (1.0 + lax.erf(pre * 0.7071067811865476))
        density = jnp.exp(-0.5 * pre * pre) * 0.3989422804014327
        act = (pre * cdf).astype(BF16)
        total = total + dot_nt(act, wfc2_ref[:, cols])
        grad_pre = (dot(cot_low, wfc2_ref[:, cols]) * (cdf + pre * density)).astype(BF16)
        grad_second = grad_second + dot_nt(grad_pre, wfc1_ref[:, cols])
        parts_fc[0, 12 * n : 12 * (n + 1)] = dot(second_t, grad_pre).astype(BF16).reshape(12, 16, 256)
        parts_fc[1, 12 * n : 12 * (n + 1)] = dot(cot_t, act).astype(BF16).reshape(12, 16, 256)
        vec[n : n + 1, :] = jnp.sum(grad_pre.astype(F32), 0, keepdims=True)
        if n:
            early1(n - 1)

    def give_back(a, i):
        return pltpu.make_async_remote_copy(
            src_ref=out_stage.at[a, 2 - i],
            dst_ref=quadrant((block_out, dtok_out)[a], i + 1),
            send_sem=rt_send.at[a, i],
            recv_sem=rt_recv.at[a, i],
            device_id=behind[i],
            device_id_type=MESH,
        )

    def hand_out(a, field):
        stage[a] = field
        for slot, row, col, rows in pieces():
            out_stage[a, slot, row, col] = stage[a, rows, :].astype(BF16)
        for i in range(3):
            give_back(a, i).start()
        keep[a].start()

    grad_inner = cot + norm_back(hat2, inv2, gain2, grad_second)
    grad_att = grad_inner.astype(BF16)
    proj_grad = dot_tn(mixed, grad_att).astype(BF16)
    proj_grad = jnp.concatenate([proj_grad, jnp.zeros((C, 64), BF16)], -1).reshape(12, 16, 256)
    parts_fc[0, 36:42] = proj_grad[:6]
    parts_fc[1, 36:42] = proj_grad[6:]
    vec[3:4, 0:C] = jnp.sum(grad_second * hat2, 0, keepdims=True)
    parts_fc[0, 42] = vec[...].astype(BF16)
    parts_fc[1, 42] = jnp.zeros((16, 256), BF16)
    parts_fc[:, 43:] = jnp.zeros((2, FC - 43, 16, 256), BF16)
    early1(2)
    hand_out(0, total)

    grad_mixed = dot_nt(grad_att, wproj_ref[...]).astype(BF16)
    grad_mixed_t = grad_mixed.T
    dsc[...] = jnp.zeros_like(dsc)
    for head in range(HEADS):
        wide_cols[256 * head : 256 * head + T, :] = keys * ones[head]
    grad_k_t = []
    grad_v_t = []
    for head in range(HEADS):
        rows = slice(HEAD * head, HEAD * (head + 1))
        gm = grad_mixed * ones[head]
        probs = prob[head]
        grad_probs = dot_nt(gm, values)
        inside = jnp.sum(probs * grad_probs, -1, keepdims=True)
        grad_scores = probs * (grad_probs - inside)
        dsc[head, 0:T, 0:T] = grad_scores
        scaled = (grad_scores * FACTOR).astype(BF16)
        grad_v_t.append(
            dot(grad_mixed_t[rows], wide_rows[:, 256 * head : 256 * head + T])
        )
        wide_rows[:, 256 * head : 256 * head + T] = scaled
        grad_k_t.append(dot(queries_t[rows], scaled))
    grad_q = dot(wide_rows[...], wide_cols[...])
    grad_k = jnp.concatenate(grad_k_t, 0).T
    grad_v = jnp.concatenate(grad_v_t, 0).T

    grad_qkv = jnp.concatenate([grad_q, grad_k, grad_v], -1).astype(BF16)
    wide = dot_tn(first, grad_qkv).astype(BF16)
    for n in range(4):
        parts_att[n // 2, n % 2 * 12 : n % 2 * 12 + 12] = (
            wide[:, 128 * n : 128 * (n + 1)].reshape(12, 16, 128)
        )
    edge = jnp.concatenate([wide[:96, 512:576], wide[96:, 512:576]], -1).reshape(6, 16, 128)
    parts_att[0, 24:27] = edge[:3]
    parts_att[1, 24:27] = edge[3:]
    grad_first = dot_nt(grad_qkv, wqkv_ref[...]).astype(BF16).astype(F32)
    vec[...] = jnp.zeros_like(vec)
    sums = jnp.sum(grad_qkv.astype(F32), 0, keepdims=True)
    sums = [sums[:, C * n : C * (n + 1)] for n in range(3)]
    sums.append(jnp.sum(grad_first * hat1, 0, keepdims=True))
    for n in range(4):
        vec[2 * n : 2 * n + 1, 0:128] = sums[n][:, 0:128]
        vec[2 * n + 1 : 2 * n + 2, 0:64] = sums[n][:, 128:C]
    parts_att[0, 27] = vec[:, 0:128].astype(BF16)
    parts_att[1, 27] = jnp.zeros((16, 128), BF16)
    parts_att[:, 28:] = jnp.zeros((2, ATT - 28, 16, 128), BF16)
    late1()
    early2()
    d_tokens = grad_inner + norm_back(hat1, inv1, gain1, grad_first)
    hand_out(1, d_tokens)

    dmat[...] = jnp.zeros_like(dmat)
    for head in range(HEADS):
        acc = jnp.zeros((16, 384), F32)
        for w in range(WIN_W):
            acc = acc + pltpu.roll(
                dsc[head, w * GROUPS : w * GROUPS + 16, :], (WIN_W - 1 - w) * GROUPS, axis=1
            )
        for n in range(3):
            dmat[n, pl.ds(head, 16, stride=8), :] = acc[:, 128 * n : 128 * (n + 1)]

    def table_grad():
        return jnp.concatenate([dmat[n, 0:96, :] for n in range(3)], -1)

    def keep_table(field):
        for n in range(3):
            dmat[n, 0:96, :] = field[:, 128 * n : 128 * (n + 1)]

    def edge_copy():
        return pltpu.make_async_remote_copy(
            src_ref=bbs,
            dst_ref=bbr,
            send_sem=one_send.at[1],
            recv_sem=one_recv.at[1],
            device_id=(lon, north),
            device_id_type=MESH,
        )

    @pl.when(lat == 0)
    def _():
        upper = lax.broadcasted_iota(jnp.int32, (96, 384), 0) < 48
        full = table_grad()
        bbs[...] = jnp.where(upper, full, 0.0).astype(BF16)
        edge_copy().start()
        keep_table(jnp.where(upper, 0.0, full))

    @pl.when(lat == BANDS - 1)
    def _():
        edge_copy().wait_recv()
        keep_table(table_grad() + bbr[...].astype(F32))

    bsend[...] = table_grad().astype(BF16).reshape(PARTS, 16, 384)

    for owner in range(PARTS):
        @pl.when(lon != owner)
        def _():
            pltpu.make_async_remote_copy(
                src_ref=bsend.at[owner],
                dst_ref=brecv.at[lon],
                send_sem=b_send.at[0],
                recv_sem=b_recv.at[0],
                device_id=(owner, lat),
                device_id_type=MESH,
            ).start()

    early3()
    late2()
    early4()
    strips = brecv.at[pl.ds(0, STRIPS - 1)]

    @pl.when(lon < PARTS)
    def _():
        brecv[lon] = bsend[lon]
        wait_bytes(strips, b_recv.at[0])
        bfin[lon] = jnp.sum(brecv[...].astype(F32), 0).astype(BF16)
        for d in range(1, STRIPS):
            pltpu.make_async_remote_copy(
                src_ref=bfin.at[lon],
                dst_ref=bfin.at[lon],
                send_sem=b_send.at[1],
                recv_sem=b_recv.at[1],
                device_id=(strip(d), lat),
                device_id_type=MESH,
            ).start()

    early5()
    late3()

    @pl.when(lon < PARTS)
    def _():
        wait_bytes(bfin.at[pl.ds(0, PARTS - 1)], b_recv.at[1])

    @pl.when(lon >= PARTS)
    def _():
        wait_bytes(bfin, b_recv.at[1])

    tin[...] = dot_nt(bfin[...].reshape(96, 384), perm_ref[...])
    dtab_ref[...] = jnp.zeros_like(dtab_ref)
    for zp in range(WIN_Z):
        for zq in range(WIN_Z):
            for hp in range(WIN_H):
                j = (zp * WIN_Z + zq) * WIN_H + hp
                first_lane = j * WIN_H * SPAN
                base = first_lane // 128 * 128
                g = hp * WIN_Z + zp
                piece = tin[g * 8 : g * 8 + 8, zq * 256 : zq * 256 + 256]
                piece = jnp.concatenate([piece, jnp.zeros((8, 128), F32)], -1)
                moved = pltpu.roll(piece, first_lane - base, axis=1)
                dtab_ref[:, base : base + 384] = dtab_ref[:, base : base + 384] + moved

    keep[2].start()

    for a in range(2):
        for i in range(3):
            exchange(a, i).wait_send()
            give_back(a, i).wait()

    @pl.when(lat == BANDS - 1)
    def _():
        table_copy().wait_send()

    @pl.when(lat == 0)
    def _():
        edge_copy().wait_send()

    for stage_no, ref in ((1, fold1), (2, fold2), (3, fold2), (4, fold2), (5, fold1)):
        wait_bytes(ref, f_send.at[stage_no])
    for stage_no, ref in ((0, fold_att), (1, mid_att.at[pl.ds(0, STRIPS - 1)]), (2, fold_att)):
        wait_bytes(ref, a_send.at[stage_no])

    @pl.when(lon < PARTS)
    def _():
        wait_bytes(bsend.at[pl.ds(0, PARTS - 1)], b_send.at[0])
        wait_bytes(strips, b_send.at[1])

    @pl.when(lon >= PARTS)
    def _():
        wait_bytes(bsend, b_send.at[0])

    for copy in keep:
        copy.wait()
    wait_bytes(fold1, f_recv.at[5])
    wait_bytes(fold_att, a_recv.at[2])


def output_kernel(*refs):
    ins, outs = refs[:5], refs[5:16]
    in_bufs, out_bufs = refs[16:21], refs[21:30]
    in_sem, out_sem = refs[30:]
    loads = [
        pltpu.make_async_copy(src, dst, in_sem.at[n])
        for n, (src, dst) in enumerate(zip(ins, in_bufs))
    ]
    stores = [
        pltpu.make_async_copy(src, dst, out_sem.at[n])
        for n, (src, dst) in enumerate(zip(in_bufs[:2] + out_bufs, outs))
    ]
    gath_ref, gath_att, dtab_ref = in_bufs[2:]
    (
        dln1_ref, dwqkv_ref, dbqkv_ref, dbias_ref, dwproj_ref, dln2_ref,
        dwfc1_ref, dbfc1_ref, dwfc2_ref,
    ) = out_bufs
    for n in (2, 0, 1, 3, 4):
        loads[n].start()
    loads[2].wait()
    for n in range(3):
        cols = slice(256 * n, 256 * (n + 1))
        rows = slice(12 * n, 12 * (n + 1))
        dwfc1_ref[:, cols] = gath_ref[0, rows].reshape(C, 256).astype(F32)
    stores[8].start()
    for n in range(3):
        cols = slice(256 * n, 256 * (n + 1))
        rows = slice(12 * n, 12 * (n + 1))
        dwfc2_ref[:, cols] = gath_ref[1, rows].reshape(C, 256).astype(F32)
    stores[10].start()
    for k in range(2):
        dwproj_ref[96 * k : 96 * (k + 1), :] = (
            gath_ref[k, 36:42].reshape(96, 256)[:, 0:C].astype(F32)
        )
    vec = gath_ref[0, 42].astype(F32)
    dbfc1_ref[...] = jnp.concatenate([vec[n : n + 1] for n in range(3)], -1).reshape(HID)
    dln2_ref[...] = vec[3:4, :C].reshape(C)
    for n in (6, 9, 7):
        stores[n].start()
    for n in range(2):
        loads[n].wait()
        stores[n].start()
    loads[3].wait()
    for k in range(2):
        for n in range(2):
            cols = slice(256 * k + 128 * n, 256 * k + 128 * (n + 1))
            dwqkv_ref[:, cols] = gath_att[k, 12 * n : 12 * (n + 1)].reshape(C, 128).astype(F32)
        edge = gath_att[k, 24:27].reshape(48, 128).astype(F32)
        for n in range(2):
            at = 96 * n + 48 * k
            dwqkv_ref[at : at + 48, 512:576] = edge[:, 64 * n : 64 * (n + 1)]
    vec = gath_att[0, 27].astype(F32)
    sums = [
        jnp.concatenate([vec[2 * n : 2 * n + 1], vec[2 * n + 1 : 2 * n + 2, :64]], -1)
        for n in range(4)
    ]
    dbqkv_ref[...] = jnp.concatenate(sums[:3], -1).reshape(3 * C)
    dln1_ref[...] = sums[3].reshape(C)
    for n in (3, 4, 2):
        stores[n].start()
    loads[4].wait()
    for head in range(HEADS):
        dbias_ref[0, head] = dtab_ref[head : head + 1, 0:NREL]
    stores[5].start()
    for store in stores:
        store.wait()


def per_device(
    tokens, cotangent, ln1_gain, w_qkv, b_qkv, bias_table, w_proj, ln2_gain, w_fc1, b_fc1, w_fc2
):
    hbm = pl.BlockSpec(memory_space=pl.ANY)
    perm = table_order()
    dma = pltpu.SemaphoreType.DMA
    args = (
        tokens.transpose(1, 2, 0, 3), cotangent.transpose(1, 2, 0, 3), ln1_gain, w_qkv, b_qkv,
        bias_table.transpose(0, 2, 1, 3), w_proj, ln2_gain, w_fc1, b_fc1, w_fc2.T,
        jnp.asarray(perm, BF16), jnp.asarray(cross_pairs()),
    )
    gathered, gathered_att, block, d_tok, table = pl.pallas_call(
        block_kernel,
        out_shape=(
            jax.ShapeDtypeStruct((2, FC, 16, 256), BF16),
            jax.ShapeDtypeStruct((2, ATT, 16, 128), BF16),
            jax.ShapeDtypeStruct((WIN_H, WIN_W, WIN_Z, C), BF16),
            jax.ShapeDtypeStruct((WIN_H, WIN_W, WIN_Z, C), BF16),
            jax.ShapeDtypeStruct((8, 3456), F32),
        ),
        in_specs=[hbm] * len(args),
        out_specs=(hbm,) * 5,
        scratch_shapes=[pltpu.VMEM(a.shape, a.dtype) for a in args[2:]]
        + [
            pltpu.VMEM((2, T, C), F32),
            pltpu.VMEM((2, 4, 3, 6, WIN_Z, C), BF16),
            pltpu.VMEM((2, 4, 3, 6, WIN_Z, C), BF16),
            pltpu.VMEM((8, 3456), F32),
            pltpu.VMEM((1, HEADS, 1, NREL), F32),
            pltpu.VMEM((96, 512), F32),
            pltpu.VMEM((3, 128, 128), F32),
            pltpu.VMEM((HEADS, T, T), F32),
            pltpu.VMEM((HEADS, T, T), F32),
            pltpu.VMEM((T, HEADS * 256), BF16),
            pltpu.VMEM((HEADS * 256, C), BF16),
            pltpu.VMEM((HEADS, 160, 384), F32),
            pltpu.VMEM((3, 128, 128), F32),
            pltpu.VMEM((16, 256), F32),
            pltpu.VMEM((PARTS, 16, 384), BF16),
            pltpu.VMEM((STRIPS, 16, 384), BF16),
            pltpu.VMEM((PARTS, 16, 384), BF16),
            pltpu.VMEM((96, 384), BF16),
            pltpu.VMEM((96, 384), BF16),
            pltpu.VMEM((2, FC, 16, 256), BF16),
            pltpu.VMEM((2, ATT, 16, 128), BF16),
            pltpu.VMEM((3, 7, 4, 16, 256), BF16),
            pltpu.VMEM((3, 4, 16, 256), BF16),
            pltpu.VMEM((3, 3, 16, 256), BF16),
            pltpu.VMEM((3, 16, 256), BF16),
            pltpu.VMEM((3, 4, 16, 256), BF16),
            pltpu.VMEM((BANDS - 1, 4, 16, 128), BF16),
            pltpu.VMEM((4, 16, 128), BF16),
            pltpu.VMEM((STRIPS, 4, 16, 128), BF16),
            pltpu.VMEM((FC, 16, 256), BF16),
            pltpu.VMEM((4, 16, 128), BF16),
            pltpu.VMEM((8, 3456), F32),
            dma((len(args) - 2,)), dma((2,)), dma((7,)),
            dma((2, 3)), dma((2, 3)), dma((2, 3)), dma((2, 3)),
            dma((2,)), dma((2,)), dma((6,)), dma((6,)),
            dma((3,)), dma((3,)), dma((2,)), dma((2,)),
        ],
        compiler_params=pltpu.CompilerParams(
            collective_id=0, has_side_effects=True, vmem_limit_bytes=VMEM_LIMIT
        ),
    )(*args)
    shape = jax.ShapeDtypeStruct
    grid_shape = (WIN_H, WIN_W, WIN_Z, C)
    results_out = (
        shape(grid_shape, BF16), shape(grid_shape, BF16),
        shape((C,), F32), shape((C, 3 * C), F32), shape((3 * C,), F32),
        shape((1, HEADS, 1, NREL), F32), shape((C, C), F32), shape((C,), F32),
        shape((C, HID), F32), shape((HID,), F32), shape((C, HID), F32),
    )
    outs = pl.pallas_call(
        output_kernel,
        out_shape=results_out,
        in_specs=[hbm] * 5,
        out_specs=(hbm,) * 11,
        scratch_shapes=[
            pltpu.VMEM(a.shape, a.dtype)
            for a in (block, d_tok, gathered, gathered_att, table) + results_out[2:]
        ]
        + [dma((5,)), dma((11,))],
        compiler_params=pltpu.CompilerParams(vmem_limit_bytes=VMEM_LIMIT),
    )(block, d_tok, gathered, gathered_att, table)
    out, d_tok, d_ln1, d_wqkv, d_bqkv, d_bias, d_wproj, d_ln2, d_wfc1, d_bfc1, d_wfc2 = outs
    return (
        out.transpose(2, 0, 1, 3), d_tok.transpose(2, 0, 1, 3), d_ln1, d_wqkv, d_bqkv,
        d_bias.transpose(0, 2, 1, 3), d_wproj, d_ln2, d_wfc1, d_bfc1, d_wfc2.T,
    )


def solution(mesh):
    grid = P(None, "lat", "lon", None)
    rows = P(None, "lat", None, None)
    return jax.shard_map(
        per_device,
        mesh=mesh,
        in_specs=(grid, grid, P(), P(), P(), rows, P(), P(), P(), P(), P()),
        out_specs=(grid, grid, P(), P(), P(), rows, P(), P(), P(), P(), P()),
        check_vma=False,
    )
```

```python
import jax
import jax.numpy as jnp
import numpy as np
from jax import lax
from jax.experimental import pallas as pl
from jax.experimental.pallas import tpu as pltpu
from jax.sharding import PartitionSpec as P

HEADS = 6
WIN_Z = 2
WIN_H = 6
WIN_W = 12
SPAN = 2 * WIN_W - 1
GROUPS = WIN_Z * WIN_H
T = GROUPS * WIN_W
C = 192
HID = 768
HEAD = C // HEADS
NREL = GROUPS * GROUPS * SPAN
FC = 48
ATT = 32
ROWS = 8
BANDS = 16
STRIPS = 8
PARTS = 6
EPSILON = 1e-05
VMEM_LIMIT = 56 * 1024 * 1024
FACTOR = HEAD ** (-0.5)
LOG2E = 1.4426950408889634
F32 = jnp.float32
BF16 = jnp.bfloat16
MESH = pl.DeviceIdType.MESH


def table_order():
    grid = np.zeros((512, 384), np.float32)
    for z in range(WIN_Z):
        for h in range(WIN_H):
            for i in range(SPAN):
                grid[z * 256 + h * SPAN + i, (SPAN - 1 - i) * GROUPS + h * WIN_Z + z] = 1
    return grid


def cross_pairs():
    g = np.arange(96)[:, None] // 8 // WIN_Z
    q = np.arange(384)[None, :] % GROUPS // WIN_Z
    return np.where((g < 3) != (q < 3), -1e30, 0.0).astype(np.float32)


def dot(a, b):
    return jnp.dot(a, b, preferred_element_type=F32)


def dot_nt(a, b):
    return lax.dot_general(a, b, (((1,), (1,)), ((), ())), preferred_element_type=F32)


def dot_tn(a, b):
    return lax.dot_general(a, b, (((0,), (0,)), ((), ())), preferred_element_type=F32)


def normalize(values, gain):
    average = jnp.mean(values, -1, keepdims=True)
    centered = values - average
    inv = lax.rsqrt(jnp.mean(centered * centered, -1, keepdims=True) + EPSILON)
    hat = centered * inv
    return hat * gain, hat, inv


def norm_back(hat, inv, gain, grad):
    scaled = grad * gain
    return inv * (
        scaled
        - jnp.mean(scaled, -1, keepdims=True)
        - hat * jnp.mean(scaled * hat, -1, keepdims=True)
    )


def pieces():
    for h in range(WIN_H):
        for w in range(WIN_W):
            at = w * GROUPS + h * WIN_Z
            yield (h // 3) * 2 + w // 6, h % 3, w % 6, slice(at, at + WIN_Z)


def quadrant(ref, q):
    return ref.at[pl.ds(q // 2 * 3, 3), pl.ds(q % 2 * 6, 6)]


def block_kernel(
    tok_any, cot_any, g1_any, wqkv_any, bqkv_any, table_any, wproj_any, g2_any, wfc1_any,
    bfc1_any, wfc2_any, perm_any, cross_any,
    gath_fc_out, gath_att_out, block_out, dtok_out, dtab_out,
    g1_ref, wqkv_ref, bqkv_ref, table_ref, wproj_ref, g2_ref, wfc1_ref,
    bfc1_ref, wfc2_ref, perm_ref, cross_ref,
    stage, arrive, out_stage,
    tabw, tab15, tin, ymat, bias, prob, wide_rows, wide_cols, dsc, dmat, vec,
    bsend, brecv, bfin, bbs, bbr,
    parts_fc, parts_att, core_fc, core_att, fold1, sum1, fold2, sum2, fold3, fold_att, sum_att,
    mid_att, gath_fc, gath_att, dtab_ref,
    in_sem, own_sem, out_sem,
    ex_send, ex_recv, rt_send, rt_recv, one_send, one_recv, p_send, p_recv, f_send, f_recv,
    a_send, a_recv, b_send, b_recv,
):
    sources = (
        (table_any, table_ref), (perm_any, perm_ref), (cross_any, cross_ref), (g1_any, g1_ref),
        (wqkv_any, wqkv_ref), (bqkv_any, bqkv_ref), (wproj_any, wproj_ref), (g2_any, g2_ref),
        (wfc1_any, wfc1_ref), (bfc1_any, bfc1_ref), (wfc2_any, wfc2_ref),
    )
    loads = [pltpu.make_async_copy(src, dst, in_sem.at[n]) for n, (src, dst) in enumerate(sources)]
    lon = lax.axis_index("lon")
    lat = lax.axis_index("lat")
    core = lax.rem(lat, 2)
    other = 1 - core
    pair_row = lat // 2
    east = lax.rem(lon + 1, STRIPS)
    west = lax.rem(lon + STRIPS - 1, STRIPS)
    south = lax.rem(lat + 1, BANDS)
    north = lax.rem(lat + BANDS - 1, BANDS)
    sibling = (lon, lat - core + other)

    spot = (lax.rem(pair_row, 4), lon // 2, lax.rem(lon, 2) * 2 + lat // 8)

    def on_axis(axis, at):
        if axis == 0:
            return (lon, lat // 8 * 8 + at * 2 + core)
        if axis == 1:
            return (at * 2 + lax.rem(lon, 2), lat)
        return (spot[1] * 2 + at // 2, lax.rem(at, 2) * 8 + spot[0] * 2 + core)

    def strip(d):
        return lax.rem(lon + d, STRIPS)

    def row_of(d):
        return lax.rem(pair_row + d, ROWS)

    barrier = pltpu.get_barrier_semaphore()

    def greet(target):
        pl.semaphore_signal(barrier, inc=1, device_id=target, device_id_type=MESH)

    for target in ((lon, south), (lon, north), (east, south), (west, north), sibling):
        greet(target)
    greet(on_axis(2, 3 - spot[2]))
    for d in range(1, 8):
        greet((strip(d), lat))
        greet((lon, row_of(d) * 2 + core))
    loads[0].start()
    own = [
        pltpu.make_async_copy(quadrant(src, 0), arrive.at[a, 3], own_sem.at[a])
        for a, src in enumerate((tok_any, cot_any))
    ]
    own[0].start()
    pl.semaphore_wait(barrier, 20)

    ahead = ((east, lat), (lon, south), (east, south))
    behind = ((west, lat), (lon, north), (west, north))

    def exchange(a, i):
        return pltpu.make_async_remote_copy(
            src_ref=quadrant((tok_any, cot_any)[a], i + 1),
            dst_ref=arrive.at[a, 2 - i],
            send_sem=ex_send.at[a, i],
            recv_sem=ex_recv.at[a, i],
            device_id=ahead[i],
            device_id_type=MESH,
        )

    def table_copy():
        return pltpu.make_async_remote_copy(
            src_ref=table_any,
            dst_ref=tab15,
            send_sem=one_send.at[0],
            recv_sem=one_recv.at[0],
            device_id=(lon, south),
            device_id_type=MESH,
        )

    @pl.when(lat == BANDS - 1)
    def _():
        table_copy().start()

    for a in range(2):
        for i in range(3):
            exchange(a, i).start()
    for load in loads[1:]:
        load.start()
    own[1].start()

    tabw[...] = jnp.zeros_like(tabw)
    loads[0].wait()
    for head in range(HEADS):
        tabw[head : head + 1, 0:NREL] = table_ref[0, head]

    tin[...] = jnp.zeros_like(tin)

    def spread(src, zp, zq, hp, width):
        j = (zp * WIN_Z + zq) * WIN_H + hp
        first = j * WIN_H * SPAN
        base = first // 128 * 128
        wide = src[:, base : base + 384]
        moved = pltpu.roll(wide, (384 - (first - base)) % 384, axis=1)
        g = hp * WIN_Z + zp
        tin[g * 8 : g * 8 + 8, zq * 256 : zq * 256 + width] = moved[:, :width]

    for zp in range(WIN_Z):
        for zq in range(WIN_Z):
            for hp in range(WIN_H):
                spread(tabw, zp, zq, hp, WIN_H * SPAN)

    def permuted(whole):
        high = whole.astype(BF16)
        rest = whole - high.astype(F32)
        middle = rest.astype(BF16)
        low = (rest - middle.astype(F32)).astype(BF16)
        perm = perm_ref[...]
        return (dot(high, perm) + dot(middle, perm) + dot(low, perm)) * LOG2E

    loads[1].wait()
    spread_rows = permuted(tin[...])
    for n in range(3):
        ymat[n, 0:96, :] = spread_rows[:, 128 * n : 128 * (n + 1)]
        ymat[n, 96:128, :] = jnp.zeros((32, 128), F32)
    loads[2].wait()

    @pl.when(lat == 0)
    def _():
        for n in range(3):
            ymat[n, 0:96, :] = ymat[n, 0:96, :] + cross_ref[:, 128 * n : 128 * (n + 1)]

    def place_bias(tall, count):
        for head in range(HEADS):
            rows = jnp.concatenate(
                [ymat[n, pl.ds(head, tall, stride=8), :] for n in range(3)], -1
            )
            for w in range(WIN_W):
                moved = pltpu.roll(rows, (384 - (WIN_W - 1 - w) * GROUPS) % 384, axis=1)
                bias[head, w * GROUPS : w * GROUPS + count, :] = moved[:count, :T]

    place_bias(16, GROUPS)
    for n in range(3, 11):
        loads[n].wait()
    lane = lax.broadcasted_iota(jnp.int32, (16, C), 1)
    ones = [
        jnp.where((lane >= HEAD * i) & (lane < HEAD * (i + 1)), 1.0, 0.0).astype(BF16)[0:1]
        for i in range(HEADS)
    ]
    gain1 = g1_ref[...].reshape(1, C)
    gain2 = g2_ref[...].reshape(1, C)

    def arrived(a):
        for i in range(3):
            exchange(a, i).wait_recv()
        own[a].wait()
        for slot, row, col, rows in pieces():
            stage[a, rows, :] = arrive[a, slot, row, col].astype(F32)
        return stage[a]

    tokens = arrived(0)
    normed, hat1, inv1 = normalize(tokens, gain1)
    first = normed.astype(BF16)
    qkv = (dot(first, wqkv_ref[...]) + bqkv_ref[...].reshape(1, 3 * C)).astype(BF16)
    queries = qkv[:, 0:C]
    keys = qkv[:, C : 2 * C]
    values = qkv[:, 2 * C : 3 * C]
    queries_t = queries.T

    @pl.when(lat == 0)
    def _():
        table_copy().wait_recv()
        for head in range(HEADS):
            tabw[head : head + 1, 0:NREL] = tab15[0, head]
        tin[0:48, :] = jnp.zeros((48, 512), F32)
        for zp in range(WIN_Z):
            for zq in range(WIN_Z):
                for hp in range(3):
                    spread(tabw, zp, zq, hp, 3 * SPAN)
        upper_rows = permuted(tin[0:48, :]) + cross_ref[0:48, :]
        for n in range(3):
            ymat[n, 0:48, :] = upper_rows[:, 128 * n : 128 * (n + 1)]
        place_bias(8, 6)

    wide_rows[...] = jnp.zeros_like(wide_rows)
    wide_cols[...] = jnp.zeros_like(wide_cols)
    for head in range(HEADS):
        wide_cols[256 * head : 256 * head + T, :] = values * ones[head]
    for head in range(HEADS):
        q = queries * ones[head]
        scores = dot_nt(q, keys) * (FACTOR * LOG2E) + bias[head]
        top = jnp.max(scores, -1, keepdims=True)
        raised = jnp.exp2(scores - top)
        probs = raised * (1.0 / jnp.sum(raised, -1, keepdims=True))
        prob[head] = probs
        probs_low = probs.astype(BF16)
        wide_rows[:, 256 * head : 256 * head + T] = probs_low
    mixed = dot(wide_rows[...], wide_cols[...]).astype(BF16)
    inner = tokens + dot(mixed, wproj_ref[...]).astype(BF16).astype(F32)

    def remote(src, dst, send_sem, recv_sem, target):
        return pltpu.make_async_remote_copy(
            src_ref=src, dst_ref=dst, send_sem=send_sem, recv_sem=recv_sem,
            device_id=target, device_id_type=MESH,
        )

    def wait_bytes(ref, sem):
        pltpu.make_async_copy(ref, ref, sem).wait()

    def add(*terms):
        total = terms[0].astype(F32)
        for term in terms[1:]:
            total = total + term.astype(F32)
        return total.astype(BF16)

    axes = [(n, (n + 1) % 3, (n + 2) % 3) for n in range(3)]
    places = [tuple(spot[axis] for axis in order) for order in axes]

    def block(n, i):
        return pl.ds(n * 16 + i * 4, 4)

    def unit(n):
        return n * 16 + places[n][0] * 4 + places[n][1]

    def part_to_line(n, stage_no, which, src, dst):
        for d in range(1, 4):
            at = lax.rem(places[n][which] + d, 4)
            remote(
                src(n, at), dst(n, d), f_send.at[stage_no], f_recv.at[stage_no],
                on_axis(axes[n][which], at),
            ).start()

    def to_line(stage_no, which, src, dst):
        for n in range(3):
            part_to_line(n, stage_no, which, src, dst)

    pair_fc = [
        remote(
            parts_fc.at[other, pl.ds(12 * n, 12)], core_fc.at[pl.ds(12 * n, 12)],
            p_send.at[n], p_recv.at[n], sibling,
        )
        for n in range(4)
    ]
    swap_fc = remote(
        gath_fc.at[core], gath_fc_out.at[core], f_send.at[6], f_recv.at[6], sibling
    )
    pair_att = remote(parts_att.at[other], core_att, a_send.at[0], a_recv.at[0], sibling)
    swap_att = remote(
        gath_att.at[core], gath_att_out.at[core], a_send.at[4], a_recv.at[4], sibling
    )
    keep = [
        pltpu.make_async_copy(src, dst, out_sem.at[n])
        for n, (src, dst) in enumerate((
            (out_stage.at[0, 3], quadrant(block_out, 0)),
            (out_stage.at[1, 3], quadrant(dtok_out, 0)),
            (dtab_ref, dtab_out), (gath_fc.at[core], gath_fc_out.at[core]),
            (gath_att.at[core], gath_att_out.at[core]),
        ))
    ]

    def early1():
        for n in range(3):
            if n == 0:
                pair_fc[0].wait_recv()
            pair_fc[n + 1].wait_recv()
            rows = pl.ds(16 * n, 16)
            parts_fc[core, rows] = add(parts_fc[core, rows], core_fc[rows])
            part_to_line(
                n, 1, 0, lambda n, at: parts_fc.at[core, block(n, at)],
                lambda n, d: fold1.at[n, d - 1],
            )

    def early2():
        wait_bytes(fold1, f_recv.at[1])
        for n in range(3):
            own = parts_fc[core, block(n, places[n][0])]
            sum1[n] = add(own, fold1[n, 0], fold1[n, 1], fold1[n, 2])
        to_line(2, 1, lambda n, at: sum1.at[n, at], lambda n, d: fold2.at[n, d - 1])

    def early3():
        wait_bytes(fold2, f_recv.at[2])
        for n in range(3):
            own = sum1[n, places[n][1]]
            sum2[n] = add(own, fold2[n, 0], fold2[n, 1], fold2[n, 2])
            fold3[n, places[n][2]] = sum2[n]
        to_line(3, 2, lambda n, at: sum2.at[n], lambda n, d: fold3.at[n, places[n][2]])

    def early4():
        wait_bytes(fold2, f_recv.at[3])
        for n in range(3):
            gath_fc[core, unit(n)] = add(*[fold3[n, i] for i in range(4)])
        to_line(
            4, 1, lambda n, at: gath_fc.at[core, unit(n)], lambda n, d: gath_fc.at[core, unit(n)]
        )

    def early5():
        wait_bytes(fold2, f_recv.at[4])
        to_line(
            5, 0,
            lambda n, at: gath_fc.at[core, block(n, places[n][0])],
            lambda n, d: gath_fc.at[core, block(n, places[n][0])],
        )

    def early6():
        wait_bytes(fold1, f_recv.at[5])
        swap_fc.start()
        keep[3].start()

    own_rows = pl.ds(pair_row * 4, 4)

    def late1():
        pair_att.wait_recv()
        parts_att[core] = add(parts_att[core], core_att[...])
        for d in range(1, ROWS):
            remote(
                parts_att.at[core, pl.ds(row_of(d) * 4, 4)], fold_att.at[d - 1],
                a_send.at[1], a_recv.at[1], (lon, row_of(d) * 2 + core),
            ).start()

    def late2():
        wait_bytes(fold_att, a_recv.at[1])
        sum_att[...] = add(parts_att[core, own_rows], *[fold_att[d] for d in range(ROWS - 1)])
        mid_att[lon] = sum_att[...]
        for d in range(1, STRIPS):
            remote(
                sum_att, mid_att.at[lon], a_send.at[2], a_recv.at[2], (strip(d), lat)
            ).start()

    def late3():
        wait_bytes(fold_att, a_recv.at[2])
        gath_att[core, own_rows] = add(*[mid_att[i] for i in range(STRIPS)])
        for d in range(1, ROWS):
            remote(
                gath_att.at[core, own_rows], gath_att.at[core, own_rows],
                a_send.at[3], a_recv.at[3], (lon, row_of(d) * 2 + core),
            ).start()

    def late4():
        wait_bytes(fold_att, a_recv.at[3])
        swap_att.start()
        keep[4].start()

    cot = arrived(1)
    cot_low = cot.astype(BF16)
    normed, hat2, inv2 = normalize(inner, gain2)
    second = normed.astype(BF16)
    second_t = second.T
    cot_t = cot_low.T
    total = inner
    grad_second = jnp.zeros((T, C), F32)
    bfc1 = bfc1_ref[...].reshape(1, HID)
    vec[...] = jnp.zeros_like(vec)
    for n in range(3):
        cols = slice(256 * n, 256 * (n + 1))
        pre = dot(second, wfc1_ref[:, cols]) + bfc1[:, cols]
        cdf = 0.5 * (1.0 + lax.erf(pre * 0.7071067811865476))
        density = jnp.exp(-0.5 * pre * pre) * 0.3989422804014327
        act = (pre * cdf).astype(BF16)
        total = total + dot_nt(act, wfc2_ref[:, cols])
        grad_pre = (dot(cot_low, wfc2_ref[:, cols]) * (cdf + pre * density)).astype(BF16)
        grad_second = grad_second + dot_nt(grad_pre, wfc1_ref[:, cols])
        parts_fc[0, 12 * n : 12 * (n + 1)] = dot(second_t, grad_pre).astype(BF16).reshape(12, 16, 256)
        parts_fc[1, 12 * n : 12 * (n + 1)] = dot(cot_t, act).astype(BF16).reshape(12, 16, 256)
        vec[n : n + 1, :] = jnp.sum(grad_pre.astype(F32), 0, keepdims=True)
        pair_fc[n].start()

    def give_back(a, i):
        return pltpu.make_async_remote_copy(
            src_ref=out_stage.at[a, 2 - i],
            dst_ref=quadrant((block_out, dtok_out)[a], i + 1),
            send_sem=rt_send.at[a, i],
            recv_sem=rt_recv.at[a, i],
            device_id=behind[i],
            device_id_type=MESH,
        )

    def hand_out(a, field):
        stage[a] = field
        for slot, row, col, rows in pieces():
            out_stage[a, slot, row, col] = stage[a, rows, :].astype(BF16)
        for i in range(3):
            give_back(a, i).start()
        keep[a].start()

    grad_inner = cot + norm_back(hat2, inv2, gain2, grad_second)
    grad_att = grad_inner.astype(BF16)
    proj_grad = dot_tn(mixed, grad_att).astype(BF16)
    proj_grad = jnp.concatenate([proj_grad, jnp.zeros((C, 64), BF16)], -1).reshape(12, 16, 256)
    parts_fc[0, 36:42] = proj_grad[:6]
    parts_fc[1, 36:42] = proj_grad[6:]
    vec[3:4, 0:C] = jnp.sum(grad_second * hat2, 0, keepdims=True)
    parts_fc[0, 42] = vec[...].astype(BF16)
    parts_fc[1, 42] = jnp.zeros((16, 256), BF16)
    parts_fc[:, 43:] = jnp.zeros((2, FC - 43, 16, 256), BF16)
    pair_fc[3].start()
    hand_out(0, total)

    grad_mixed = dot_nt(grad_att, wproj_ref[...]).astype(BF16)
    grad_mixed_t = grad_mixed.T
    dsc[...] = jnp.zeros_like(dsc)
    for head in range(HEADS):
        wide_cols[256 * head : 256 * head + T, :] = keys * ones[head]
    grad_k_t = []
    grad_v_t = []
    for head in range(HEADS):
        rows = slice(HEAD * head, HEAD * (head + 1))
        gm = grad_mixed * ones[head]
        probs = prob[head]
        grad_probs = dot_nt(gm, values)
        inside = jnp.sum(probs * grad_probs, -1, keepdims=True)
        grad_scores = probs * (grad_probs - inside)
        dsc[head, 0:T, 0:T] = grad_scores
        scaled = (grad_scores * FACTOR).astype(BF16)
        grad_v_t.append(
            dot(grad_mixed_t[rows], wide_rows[:, 256 * head : 256 * head + T])
        )
        wide_rows[:, 256 * head : 256 * head + T] = scaled
        grad_k_t.append(dot(queries_t[rows], scaled))
        if head == 2:
            early1()
    grad_q = dot(wide_rows[...], wide_cols[...])
    grad_k = jnp.concatenate(grad_k_t, 0).T
    grad_v = jnp.concatenate(grad_v_t, 0).T

    grad_qkv = jnp.concatenate([grad_q, grad_k, grad_v], -1).astype(BF16)
    wide = dot_tn(first, grad_qkv).astype(BF16)
    for n in range(4):
        parts_att[n // 2, n % 2 * 12 : n % 2 * 12 + 12] = (
            wide[:, 128 * n : 128 * (n + 1)].reshape(12, 16, 128)
        )
    edge = jnp.concatenate([wide[:96, 512:576], wide[96:, 512:576]], -1).reshape(6, 16, 128)
    parts_att[0, 24:27] = edge[:3]
    parts_att[1, 24:27] = edge[3:]
    grad_first = dot_nt(grad_qkv, wqkv_ref[...]).astype(BF16).astype(F32)
    vec[...] = jnp.zeros_like(vec)
    sums = jnp.sum(grad_qkv.astype(F32), 0, keepdims=True)
    sums = [sums[:, C * n : C * (n + 1)] for n in range(3)]
    sums.append(jnp.sum(grad_first * hat1, 0, keepdims=True))
    for n in range(4):
        vec[2 * n : 2 * n + 1, 0:128] = sums[n][:, 0:128]
        vec[2 * n + 1 : 2 * n + 2, 0:64] = sums[n][:, 128:C]
    parts_att[0, 27] = vec[:, 0:128].astype(BF16)
    parts_att[1, 27] = jnp.zeros((16, 128), BF16)
    parts_att[:, 28:] = jnp.zeros((2, ATT - 28, 16, 128), BF16)
    pair_att.start()
    d_tokens = grad_inner + norm_back(hat1, inv1, gain1, grad_first)
    hand_out(1, d_tokens)

    dmat[...] = jnp.zeros_like(dmat)
    for head in range(HEADS):
        if head == 3:
            late1()
            early2()
        acc = jnp.zeros((16, 384), F32)
        for w in range(WIN_W):
            acc = acc + pltpu.roll(
                dsc[head, w * GROUPS : w * GROUPS + 16, :], (WIN_W - 1 - w) * GROUPS, axis=1
            )
        for n in range(3):
            dmat[n, pl.ds(head, 16, stride=8), :] = acc[:, 128 * n : 128 * (n + 1)]

    def table_grad():
        return jnp.concatenate([dmat[n, 0:96, :] for n in range(3)], -1)

    def keep_table(field):
        for n in range(3):
            dmat[n, 0:96, :] = field[:, 128 * n : 128 * (n + 1)]

    def edge_copy():
        return pltpu.make_async_remote_copy(
            src_ref=bbs,
            dst_ref=bbr,
            send_sem=one_send.at[1],
            recv_sem=one_recv.at[1],
            device_id=(lon, north),
            device_id_type=MESH,
        )

    @pl.when(lat == 0)
    def _():
        upper = lax.broadcasted_iota(jnp.int32, (96, 384), 0) < 48
        full = table_grad()
        bbs[...] = jnp.where(upper, full, 0.0).astype(BF16)
        edge_copy().start()
        keep_table(jnp.where(upper, 0.0, full))

    early3()
    late2()

    @pl.when(lat == BANDS - 1)
    def _():
        edge_copy().wait_recv()
        keep_table(table_grad() + bbr[...].astype(F32))

    bsend[...] = table_grad().astype(BF16).reshape(PARTS, 16, 384)

    for owner in range(PARTS):
        @pl.when(lon != owner)
        def _():
            pltpu.make_async_remote_copy(
                src_ref=bsend.at[owner],
                dst_ref=brecv.at[lon],
                send_sem=b_send.at[0],
                recv_sem=b_recv.at[0],
                device_id=(owner, lat),
                device_id_type=MESH,
            ).start()

    early4()
    early5()
    seven = brecv.at[pl.ds(0, STRIPS - 1)]

    @pl.when(lon < PARTS)
    def _():
        brecv[lon] = bsend[lon]
        wait_bytes(seven, b_recv.at[0])
        bfin[lon] = jnp.sum(brecv[...].astype(F32), 0).astype(BF16)
        for d in range(1, STRIPS):
            pltpu.make_async_remote_copy(
                src_ref=bfin.at[lon],
                dst_ref=bfin.at[lon],
                send_sem=b_send.at[1],
                recv_sem=b_recv.at[1],
                device_id=(strip(d), lat),
                device_id_type=MESH,
            ).start()

    late3()
    early6()
    late4()

    @pl.when(lon < PARTS)
    def _():
        wait_bytes(bfin.at[pl.ds(0, PARTS - 1)], b_recv.at[1])

    @pl.when(lon >= PARTS)
    def _():
        wait_bytes(bfin, b_recv.at[1])

    tin[...] = dot_nt(bfin[...].reshape(96, 384), perm_ref[...])
    dtab_ref[...] = jnp.zeros_like(dtab_ref)
    for zp in range(WIN_Z):
        for zq in range(WIN_Z):
            for hp in range(WIN_H):
                j = (zp * WIN_Z + zq) * WIN_H + hp
                first_lane = j * WIN_H * SPAN
                base = first_lane // 128 * 128
                g = hp * WIN_Z + zp
                piece = tin[g * 8 : g * 8 + 8, zq * 256 : zq * 256 + 256]
                piece = jnp.concatenate([piece, jnp.zeros((8, 128), F32)], -1)
                moved = pltpu.roll(piece, first_lane - base, axis=1)
                dtab_ref[:, base : base + 384] = dtab_ref[:, base : base + 384] + moved

    keep[2].start()

    for a in range(2):
        for i in range(3):
            exchange(a, i).wait_send()
            give_back(a, i).wait()

    @pl.when(lat == BANDS - 1)
    def _():
        table_copy().wait_send()

    @pl.when(lat == 0)
    def _():
        edge_copy().wait_send()

    for copy in pair_fc:
        copy.wait_send()
    for stage_no, ref in ((1, fold1), (2, fold2), (3, fold2), (4, fold2), (5, fold1)):
        wait_bytes(ref, f_send.at[stage_no])
    pair_att.wait_send()
    for stage_no in (1, 2, 3):
        wait_bytes(fold_att, a_send.at[stage_no])

    @pl.when(lon < PARTS)
    def _():
        wait_bytes(bsend.at[pl.ds(0, PARTS - 1)], b_send.at[0])
        wait_bytes(seven, b_send.at[1])

    @pl.when(lon >= PARTS)
    def _():
        wait_bytes(bsend, b_send.at[0])

    for copy in keep:
        copy.wait()
    swap_fc.wait()
    swap_att.wait()


def output_kernel(*refs):
    ins, outs = refs[:5], refs[5:16]
    in_bufs, out_bufs = refs[16:21], refs[21:30]
    in_sem, out_sem = refs[30:]
    loads = [
        pltpu.make_async_copy(src, dst, in_sem.at[n])
        for n, (src, dst) in enumerate(zip(ins, in_bufs))
    ]
    stores = [
        pltpu.make_async_copy(src, dst, out_sem.at[n])
        for n, (src, dst) in enumerate(zip(in_bufs[:2] + out_bufs, outs))
    ]
    gath_ref, gath_att, dtab_ref = in_bufs[2:]
    (
        dln1_ref, dwqkv_ref, dbqkv_ref, dbias_ref, dwproj_ref, dln2_ref,
        dwfc1_ref, dbfc1_ref, dwfc2_ref,
    ) = out_bufs
    for n in (2, 0, 1, 3, 4):
        loads[n].start()
    loads[2].wait()
    for n in range(3):
        cols = slice(256 * n, 256 * (n + 1))
        rows = slice(12 * n, 12 * (n + 1))
        dwfc1_ref[:, cols] = gath_ref[0, rows].reshape(C, 256).astype(F32)
    stores[8].start()
    for n in range(3):
        cols = slice(256 * n, 256 * (n + 1))
        rows = slice(12 * n, 12 * (n + 1))
        dwfc2_ref[:, cols] = gath_ref[1, rows].reshape(C, 256).astype(F32)
    stores[10].start()
    for k in range(2):
        dwproj_ref[96 * k : 96 * (k + 1), :] = (
            gath_ref[k, 36:42].reshape(96, 256)[:, 0:C].astype(F32)
        )
    vec = gath_ref[0, 42].astype(F32)
    dbfc1_ref[...] = jnp.concatenate([vec[n : n + 1] for n in range(3)], -1).reshape(HID)
    dln2_ref[...] = vec[3:4, :C].reshape(C)
    for n in (6, 9, 7):
        stores[n].start()
    for n in range(2):
        loads[n].wait()
        stores[n].start()
    loads[3].wait()
    for k in range(2):
        for n in range(2):
            cols = slice(256 * k + 128 * n, 256 * k + 128 * (n + 1))
            dwqkv_ref[:, cols] = gath_att[k, 12 * n : 12 * (n + 1)].reshape(C, 128).astype(F32)
        edge = gath_att[k, 24:27].reshape(48, 128).astype(F32)
        for n in range(2):
            at = 96 * n + 48 * k
            dwqkv_ref[at : at + 48, 512:576] = edge[:, 64 * n : 64 * (n + 1)]
    vec = gath_att[0, 27].astype(F32)
    sums = [
        jnp.concatenate([vec[2 * n : 2 * n + 1], vec[2 * n + 1 : 2 * n + 2, :64]], -1)
        for n in range(4)
    ]
    dbqkv_ref[...] = jnp.concatenate(sums[:3], -1).reshape(3 * C)
    dln1_ref[...] = sums[3].reshape(C)
    for n in (3, 4, 2):
        stores[n].start()
    loads[4].wait()
    for head in range(HEADS):
        dbias_ref[0, head] = dtab_ref[head : head + 1, 0:NREL]
    stores[5].start()
    for store in stores:
        store.wait()


def per_device(
    tokens, cotangent, ln1_gain, w_qkv, b_qkv, bias_table, w_proj, ln2_gain, w_fc1, b_fc1, w_fc2
):
    hbm = pl.BlockSpec(memory_space=pl.ANY)
    perm = table_order()
    dma = pltpu.SemaphoreType.DMA
    args = (
        tokens.transpose(1, 2, 0, 3), cotangent.transpose(1, 2, 0, 3), ln1_gain, w_qkv, b_qkv,
        bias_table.transpose(0, 2, 1, 3), w_proj, ln2_gain, w_fc1, b_fc1, w_fc2.T,
        jnp.asarray(perm, BF16), jnp.asarray(cross_pairs()),
    )
    gathered, gathered_att, block, d_tok, table = pl.pallas_call(
        block_kernel,
        out_shape=(
            jax.ShapeDtypeStruct((2, FC, 16, 256), BF16),
            jax.ShapeDtypeStruct((2, ATT, 16, 128), BF16),
            jax.ShapeDtypeStruct((WIN_H, WIN_W, WIN_Z, C), BF16),
            jax.ShapeDtypeStruct((WIN_H, WIN_W, WIN_Z, C), BF16),
            jax.ShapeDtypeStruct((8, 3456), F32),
        ),
        in_specs=[hbm] * len(args),
        out_specs=(hbm,) * 5,
        scratch_shapes=[pltpu.VMEM(a.shape, a.dtype) for a in args[2:]]
        + [
            pltpu.VMEM((2, T, C), F32),
            pltpu.VMEM((2, 4, 3, 6, WIN_Z, C), BF16),
            pltpu.VMEM((2, 4, 3, 6, WIN_Z, C), BF16),
            pltpu.VMEM((8, 3456), F32),
            pltpu.VMEM((1, HEADS, 1, NREL), F32),
            pltpu.VMEM((96, 512), F32),
            pltpu.VMEM((3, 128, 128), F32),
            pltpu.VMEM((HEADS, T, T), F32),
            pltpu.VMEM((HEADS, T, T), F32),
            pltpu.VMEM((T, HEADS * 256), BF16),
            pltpu.VMEM((HEADS * 256, C), BF16),
            pltpu.VMEM((HEADS, 160, 384), F32),
            pltpu.VMEM((3, 128, 128), F32),
            pltpu.VMEM((16, 256), F32),
            pltpu.VMEM((PARTS, 16, 384), BF16),
            pltpu.VMEM((STRIPS, 16, 384), BF16),
            pltpu.VMEM((PARTS, 16, 384), BF16),
            pltpu.VMEM((96, 384), BF16),
            pltpu.VMEM((96, 384), BF16),
            pltpu.VMEM((2, FC, 16, 256), BF16),
            pltpu.VMEM((2, ATT, 16, 128), BF16),
            pltpu.VMEM((FC, 16, 256), BF16),
            pltpu.VMEM((ATT, 16, 128), BF16),
            pltpu.VMEM((3, 3, 4, 16, 256), BF16),
            pltpu.VMEM((3, 4, 16, 256), BF16),
            pltpu.VMEM((3, 3, 16, 256), BF16),
            pltpu.VMEM((3, 16, 256), BF16),
            pltpu.VMEM((3, 4, 16, 256), BF16),
            pltpu.VMEM((ROWS - 1, 4, 16, 128), BF16),
            pltpu.VMEM((4, 16, 128), BF16),
            pltpu.VMEM((STRIPS, 4, 16, 128), BF16),
            pltpu.VMEM((2, FC, 16, 256), BF16),
            pltpu.VMEM((2, ATT, 16, 128), BF16),
            pltpu.VMEM((8, 3456), F32),
            dma((len(args) - 2,)), dma((2,)), dma((5,)),
            dma((2, 3)), dma((2, 3)), dma((2, 3)), dma((2, 3)),
            dma((2,)), dma((2,)), dma((4,)), dma((4,)), dma((7,)), dma((7,)),
            dma((5,)), dma((5,)), dma((2,)), dma((2,)),
        ],
        compiler_params=pltpu.CompilerParams(
            collective_id=0, has_side_effects=True, vmem_limit_bytes=VMEM_LIMIT
        ),
    )(*args)
    shape = jax.ShapeDtypeStruct
    grid_shape = (WIN_H, WIN_W, WIN_Z, C)
    results_out = (
        shape(grid_shape, BF16), shape(grid_shape, BF16),
        shape((C,), F32), shape((C, 3 * C), F32), shape((3 * C,), F32),
        shape((1, HEADS, 1, NREL), F32), shape((C, C), F32), shape((C,), F32),
        shape((C, HID), F32), shape((HID,), F32), shape((C, HID), F32),
    )
    outs = pl.pallas_call(
        output_kernel,
        out_shape=results_out,
        in_specs=[hbm] * 5,
        out_specs=(hbm,) * 11,
        scratch_shapes=[
            pltpu.VMEM(a.shape, a.dtype)
            for a in (block, d_tok, gathered, gathered_att, table) + results_out[2:]
        ]
        + [dma((5,)), dma((11,))],
        compiler_params=pltpu.CompilerParams(vmem_limit_bytes=VMEM_LIMIT),
    )(block, d_tok, gathered, gathered_att, table)
    out, d_tok, d_ln1, d_wqkv, d_bqkv, d_bias, d_wproj, d_ln2, d_wfc1, d_bfc1, d_wfc2 = outs
    return (
        out.transpose(2, 0, 1, 3), d_tok.transpose(2, 0, 1, 3), d_ln1, d_wqkv, d_bqkv,
        d_bias.transpose(0, 2, 1, 3), d_wproj, d_ln2, d_wfc1, d_bfc1, d_wfc2.T,
    )


def solution(mesh):
    grid = P(None, "lat", "lon", None)
    rows = P(None, "lat", None, None)
    return jax.shard_map(
        per_device,
        mesh=mesh,
        in_specs=(grid, grid, P(), P(), P(), rows, P(), P(), P(), P(), P()),
        out_specs=(grid, grid, P(), P(), P(), rows, P(), P(), P(), P(), P()),
        check_vma=False,
    )
```

```python
import jax
import jax.numpy as jnp
import numpy as np
from jax import lax
from jax.experimental import pallas as pl
from jax.experimental.pallas import tpu as pltpu
from jax.sharding import PartitionSpec as P

HEADS = 6
WIN_Z = 2
WIN_H = 6
WIN_W = 12
SPAN = 2 * WIN_W - 1
GROUPS = WIN_Z * WIN_H
T = GROUPS * WIN_W
C = 192
HID = 768
HEAD = C // HEADS
NREL = GROUPS * GROUPS * SPAN
FC = 48
ATT = 32
ROWS = 8
BANDS = 16
STRIPS = 8
PARTS = 6
EPSILON = 1e-05
VMEM_LIMIT = 56 * 1024 * 1024
FACTOR = HEAD ** (-0.5)
LOG2E = 1.4426950408889634
F32 = jnp.float32
BF16 = jnp.bfloat16
MESH = pl.DeviceIdType.MESH


def table_order():
    grid = np.zeros((512, 384), np.float32)
    for z in range(WIN_Z):
        for h in range(WIN_H):
            for i in range(SPAN):
                grid[z * 256 + h * SPAN + i, (SPAN - 1 - i) * GROUPS + h * WIN_Z + z] = 1
    return grid


def cross_pairs():
    g = np.arange(96)[:, None] // 8 // WIN_Z
    q = np.arange(384)[None, :] % GROUPS // WIN_Z
    return np.where((g < 3) != (q < 3), -1e30, 0.0).astype(np.float32)


def dot(a, b):
    return jnp.dot(a, b, preferred_element_type=F32)


def dot_nt(a, b):
    return lax.dot_general(a, b, (((1,), (1,)), ((), ())), preferred_element_type=F32)


def dot_tn(a, b):
    return lax.dot_general(a, b, (((0,), (0,)), ((), ())), preferred_element_type=F32)


def normalize(values, gain):
    average = jnp.mean(values, -1, keepdims=True)
    centered = values - average
    inv = lax.rsqrt(jnp.mean(centered * centered, -1, keepdims=True) + EPSILON)
    hat = centered * inv
    return hat * gain, hat, inv


def norm_back(hat, inv, gain, grad):
    scaled = grad * gain
    return inv * (
        scaled
        - jnp.mean(scaled, -1, keepdims=True)
        - hat * jnp.mean(scaled * hat, -1, keepdims=True)
    )


def pieces():
    for h in range(WIN_H):
        for w in range(WIN_W):
            at = w * GROUPS + h * WIN_Z
            yield (h // 3) * 2 + w // 6, h % 3, w % 6, slice(at, at + WIN_Z)


def quadrant(ref, q):
    return ref.at[pl.ds(q // 2 * 3, 3), pl.ds(q % 2 * 6, 6)]


def block_kernel(
    tok_any, cot_any, g1_any, wqkv_any, bqkv_any, table_any, wproj_any, g2_any, wfc1_any,
    bfc1_any, wfc2_any, perm_any, cross_any,
    gath_fc_out, gath_att_out, block_out, dtok_out, dtab_out,
    g1_ref, wqkv_ref, bqkv_ref, table_ref, wproj_ref, g2_ref, wfc1_ref,
    bfc1_ref, wfc2_ref, perm_ref, cross_ref,
    stage, arrive, out_stage,
    tabw, tab15, tin, ymat, bias, prob, wide_rows, wide_cols, dsc, dmat, vec,
    bsend, brecv, bfin, bbs, bbr,
    parts_fc, parts_att, core_fc, core_att, fold1, sum1, fold2, sum2, fold3, fold_att, sum_att,
    mid_att, gath_fc, gath_att, dtab_ref,
    in_sem, own_sem, out_sem,
    ex_send, ex_recv, rt_send, rt_recv, one_send, one_recv, p_send, p_recv, f_send, f_recv,
    a_send, a_recv, b_send, b_recv,
):
    sources = (
        (table_any, table_ref), (perm_any, perm_ref), (cross_any, cross_ref), (g1_any, g1_ref),
        (wqkv_any, wqkv_ref), (bqkv_any, bqkv_ref), (wproj_any, wproj_ref), (g2_any, g2_ref),
        (wfc1_any, wfc1_ref), (bfc1_any, bfc1_ref), (wfc2_any, wfc2_ref),
    )
    loads = [pltpu.make_async_copy(src, dst, in_sem.at[n]) for n, (src, dst) in enumerate(sources)]
    lon = lax.axis_index("lon")
    lat = lax.axis_index("lat")
    core = lax.rem(lat, 2)
    other = 1 - core
    pair_row = lat // 2
    east = lax.rem(lon + 1, STRIPS)
    west = lax.rem(lon + STRIPS - 1, STRIPS)
    south = lax.rem(lat + 1, BANDS)
    north = lax.rem(lat + BANDS - 1, BANDS)
    sibling = (lon, lat - core + other)

    spot = (lax.rem(pair_row, 4), lon // 2, lax.rem(lon, 2) * 2 + lat // 8)

    def on_axis(axis, at):
        if axis == 0:
            return (lon, lat // 8 * 8 + at * 2 + core)
        if axis == 1:
            return (at * 2 + lax.rem(lon, 2), lat)
        return (spot[1] * 2 + at // 2, lax.rem(at, 2) * 8 + spot[0] * 2 + core)

    def strip(d):
        return lax.rem(lon + d, STRIPS)

    def row_of(d):
        return lax.rem(pair_row + d, ROWS)

    barrier = pltpu.get_barrier_semaphore()

    def greet(target):
        pl.semaphore_signal(barrier, inc=1, device_id=target, device_id_type=MESH)

    for target in ((lon, south), (lon, north), (east, south), (west, north), sibling):
        greet(target)
    greet(on_axis(2, 3 - spot[2]))
    for d in range(1, 8):
        greet((strip(d), lat))
        greet((lon, row_of(d) * 2 + core))
    loads[0].start()
    own = [
        pltpu.make_async_copy(quadrant(src, 0), arrive.at[a, 3], own_sem.at[a])
        for a, src in enumerate((tok_any, cot_any))
    ]
    own[0].start()
    pl.semaphore_wait(barrier, 20)

    ahead = ((east, lat), (lon, south), (east, south))
    behind = ((west, lat), (lon, north), (west, north))

    def exchange(a, i):
        return pltpu.make_async_remote_copy(
            src_ref=quadrant((tok_any, cot_any)[a], i + 1),
            dst_ref=arrive.at[a, 2 - i],
            send_sem=ex_send.at[a, i],
            recv_sem=ex_recv.at[a, i],
            device_id=ahead[i],
            device_id_type=MESH,
        )

    def table_copy():
        return pltpu.make_async_remote_copy(
            src_ref=table_any,
            dst_ref=tab15,
            send_sem=one_send.at[0],
            recv_sem=one_recv.at[0],
            device_id=(lon, south),
            device_id_type=MESH,
        )

    @pl.when(lat == BANDS - 1)
    def _():
        table_copy().start()

    for a in range(2):
        for i in range(3):
            exchange(a, i).start()
    for load in loads[1:]:
        load.start()
    own[1].start()

    tabw[...] = jnp.zeros_like(tabw)
    loads[0].wait()
    for head in range(HEADS):
        tabw[head : head + 1, 0:NREL] = table_ref[0, head]

    tin[...] = jnp.zeros_like(tin)

    def spread(src, zp, zq, hp, width):
        j = (zp * WIN_Z + zq) * WIN_H + hp
        first = j * WIN_H * SPAN
        base = first // 128 * 128
        wide = src[:, base : base + 384]
        moved = pltpu.roll(wide, (384 - (first - base)) % 384, axis=1)
        g = hp * WIN_Z + zp
        tin[g * 8 : g * 8 + 8, zq * 256 : zq * 256 + width] = moved[:, :width]

    for zp in range(WIN_Z):
        for zq in range(WIN_Z):
            for hp in range(WIN_H):
                spread(tabw, zp, zq, hp, WIN_H * SPAN)

    def permuted(whole):
        high = whole.astype(BF16)
        rest = whole - high.astype(F32)
        middle = rest.astype(BF16)
        low = (rest - middle.astype(F32)).astype(BF16)
        perm = perm_ref[...]
        return (dot(high, perm) + dot(middle, perm) + dot(low, perm)) * LOG2E

    loads[1].wait()
    spread_rows = permuted(tin[...])
    for n in range(3):
        ymat[n, 0:96, :] = spread_rows[:, 128 * n : 128 * (n + 1)]
        ymat[n, 96:128, :] = jnp.zeros((32, 128), F32)
    loads[2].wait()

    @pl.when(lat == 0)
    def _():
        for n in range(3):
            ymat[n, 0:96, :] = ymat[n, 0:96, :] + cross_ref[:, 128 * n : 128 * (n + 1)]

    def place_bias(tall, count):
        for head in range(HEADS):
            rows = jnp.concatenate(
                [ymat[n, pl.ds(head, tall, stride=8), :] for n in range(3)], -1
            )
            for w in range(WIN_W):
                moved = pltpu.roll(rows, (384 - (WIN_W - 1 - w) * GROUPS) % 384, axis=1)
                bias[head, w * GROUPS : w * GROUPS + count, :] = moved[:count, :T]

    place_bias(16, GROUPS)
    for n in range(3, 11):
        loads[n].wait()
    lane = lax.broadcasted_iota(jnp.int32, (16, C), 1)
    ones = [
        jnp.where((lane >= HEAD * i) & (lane < HEAD * (i + 1)), 1.0, 0.0).astype(BF16)[0:1]
        for i in range(HEADS)
    ]
    gain1 = g1_ref[...].reshape(1, C)
    gain2 = g2_ref[...].reshape(1, C)

    def arrived(a):
        for i in range(3):
            exchange(a, i).wait_recv()
        own[a].wait()
        for slot, row, col, rows in pieces():
            stage[a, rows, :] = arrive[a, slot, row, col].astype(F32)
        return stage[a]

    tokens = arrived(0)
    normed, hat1, inv1 = normalize(tokens, gain1)
    first = normed.astype(BF16)
    qkv = (dot(first, wqkv_ref[...]) + bqkv_ref[...].reshape(1, 3 * C)).astype(BF16)
    queries = qkv[:, 0:C]
    keys = qkv[:, C : 2 * C]
    values = qkv[:, 2 * C : 3 * C]
    queries_t = queries.T

    @pl.when(lat == 0)
    def _():
        table_copy().wait_recv()
        for head in range(HEADS):
            tabw[head : head + 1, 0:NREL] = tab15[0, head]
        tin[0:48, :] = jnp.zeros((48, 512), F32)
        for zp in range(WIN_Z):
            for zq in range(WIN_Z):
                for hp in range(3):
                    spread(tabw, zp, zq, hp, 3 * SPAN)
        upper_rows = permuted(tin[0:48, :]) + cross_ref[0:48, :]
        for n in range(3):
            ymat[n, 0:48, :] = upper_rows[:, 128 * n : 128 * (n + 1)]
        place_bias(8, 6)

    wide_rows[...] = jnp.zeros_like(wide_rows)
    wide_cols[...] = jnp.zeros_like(wide_cols)
    for head in range(HEADS):
        wide_cols[256 * head : 256 * head + T, :] = values * ones[head]
    for head in range(HEADS):
        q = queries * ones[head]
        scores = dot_nt(q, keys) * (FACTOR * LOG2E) + bias[head]
        top = jnp.max(scores, -1, keepdims=True)
        raised = jnp.exp2(scores - top)
        probs = raised * (1.0 / jnp.sum(raised, -1, keepdims=True))
        prob[head] = probs
        probs_low = probs.astype(BF16)
        wide_rows[:, 256 * head : 256 * head + T] = probs_low
    mixed = dot(wide_rows[...], wide_cols[...]).astype(BF16)
    inner = tokens + dot(mixed, wproj_ref[...]).astype(BF16).astype(F32)

    def remote(src, dst, send_sem, recv_sem, target):
        return pltpu.make_async_remote_copy(
            src_ref=src, dst_ref=dst, send_sem=send_sem, recv_sem=recv_sem,
            device_id=target, device_id_type=MESH,
        )

    def wait_bytes(ref, sem):
        pltpu.make_async_copy(ref, ref, sem).wait()

    def add(*terms):
        total = terms[0].astype(F32)
        for term in terms[1:]:
            total = total + term.astype(F32)
        return total.astype(BF16)

    axes = [(n, (n + 1) % 3, (n + 2) % 3) for n in range(3)]
    places = [tuple(spot[axis] for axis in order) for order in axes]

    def block(n, i):
        return pl.ds(n * 16 + i * 4, 4)

    def unit(n):
        return n * 16 + places[n][0] * 4 + places[n][1]

    def part_to_line(n, stage_no, which, src, dst):
        for d in range(1, 4):
            at = lax.rem(places[n][which] + d, 4)
            remote(
                src(n, at), dst(n, d), f_send.at[stage_no, n], f_recv.at[stage_no, n],
                on_axis(axes[n][which], at),
            ).start()

    pair_fc = [
        remote(
            parts_fc.at[other, pl.ds(12 * n, 12)], core_fc.at[pl.ds(12 * n, 12)],
            p_send.at[n], p_recv.at[n], sibling,
        )
        for n in range(4)
    ]
    def third(n):
        return pl.ds(16 * n, 16)

    swap_fc = [
        remote(
            gath_fc.at[core, third(n)], gath_fc_out.at[core, third(n)],
            f_send.at[6, n], f_recv.at[6, n], sibling,
        )
        for n in range(3)
    ]
    pair_att = remote(parts_att.at[other], core_att, a_send.at[0], a_recv.at[0], sibling)
    swap_att = remote(
        gath_att.at[core], gath_att_out.at[core], a_send.at[4], a_recv.at[4], sibling
    )
    kept = [
        (out_stage.at[0, 3], quadrant(block_out, 0)),
        (out_stage.at[1, 3], quadrant(dtok_out, 0)),
        (dtab_ref, dtab_out),
        (gath_att.at[core], gath_att_out.at[core]),
    ] + [(gath_fc.at[core, third(n)], gath_fc_out.at[core, third(n)]) for n in range(3)]
    keep = [
        pltpu.make_async_copy(src, dst, out_sem.at[n]) for n, (src, dst) in enumerate(kept)
    ]

    def early1(n):
        if n == 0:
            pair_fc[0].wait_recv()
        pair_fc[n + 1].wait_recv()
        parts_fc[core, third(n)] = add(parts_fc[core, third(n)], core_fc[third(n)])
        part_to_line(
            n, 1, 0, lambda n, at: parts_fc.at[core, block(n, at)],
            lambda n, d: fold1.at[n, d - 1],
        )

    def early2():
        for n in range(3):
            wait_bytes(fold1.at[n], f_recv.at[1, n])
            own_block = parts_fc[core, block(n, places[n][0])]
            sum1[n] = add(own_block, fold1[n, 0], fold1[n, 1], fold1[n, 2])
            part_to_line(
                n, 2, 1, lambda n, at: sum1.at[n, at], lambda n, d: fold2.at[n, d - 1]
            )

    def early3():
        for n in range(3):
            wait_bytes(fold2.at[n], f_recv.at[2, n])
            own_unit = sum1[n, places[n][1]]
            sum2[n] = add(own_unit, fold2[n, 0], fold2[n, 1], fold2[n, 2])
            fold3[n, places[n][2]] = sum2[n]
            part_to_line(
                n, 3, 2, lambda n, at: sum2.at[n], lambda n, d: fold3.at[n, places[n][2]]
            )

    def early4():
        for n in range(3):
            wait_bytes(fold2.at[n], f_recv.at[3, n])
            gath_fc[core, unit(n)] = add(*[fold3[n, i] for i in range(4)])
            part_to_line(
                n, 4, 1, lambda n, at: gath_fc.at[core, unit(n)],
                lambda n, d: gath_fc.at[core, unit(n)],
            )

    def early5():
        for n in range(3):
            wait_bytes(fold2.at[n], f_recv.at[4, n])
            part_to_line(
                n, 5, 0, lambda n, at: gath_fc.at[core, block(n, places[n][0])],
                lambda n, d: gath_fc.at[core, block(n, places[n][0])],
            )

    def early6():
        for n in range(3):
            wait_bytes(fold1.at[n], f_recv.at[5, n])
            swap_fc[n].start()
            keep[4 + n].start()

    own_rows = pl.ds(pair_row * 4, 4)

    def late1():
        pair_att.wait_recv()
        parts_att[core] = add(parts_att[core], core_att[...])
        for d in range(1, ROWS):
            remote(
                parts_att.at[core, pl.ds(row_of(d) * 4, 4)], fold_att.at[d - 1],
                a_send.at[1], a_recv.at[1], (lon, row_of(d) * 2 + core),
            ).start()

    def late2():
        wait_bytes(fold_att, a_recv.at[1])
        sum_att[...] = add(parts_att[core, own_rows], *[fold_att[d] for d in range(ROWS - 1)])
        mid_att[lon] = sum_att[...]
        for d in range(1, STRIPS):
            remote(
                sum_att, mid_att.at[lon], a_send.at[2], a_recv.at[2], (strip(d), lat)
            ).start()

    def late3():
        wait_bytes(fold_att, a_recv.at[2])
        gath_att[core, own_rows] = add(*[mid_att[i] for i in range(STRIPS)])
        for d in range(1, ROWS):
            remote(
                gath_att.at[core, own_rows], gath_att.at[core, own_rows],
                a_send.at[3], a_recv.at[3], (lon, row_of(d) * 2 + core),
            ).start()

    def late4():
        wait_bytes(fold_att, a_recv.at[3])
        swap_att.start()
        keep[3].start()

    cot = arrived(1)
    cot_low = cot.astype(BF16)
    normed, hat2, inv2 = normalize(inner, gain2)
    second = normed.astype(BF16)
    second_t = second.T
    cot_t = cot_low.T
    total = inner
    grad_second = jnp.zeros((T, C), F32)
    bfc1 = bfc1_ref[...].reshape(1, HID)
    vec[...] = jnp.zeros_like(vec)
    for n in range(3):
        cols = slice(256 * n, 256 * (n + 1))
        pre = dot(second, wfc1_ref[:, cols]) + bfc1[:, cols]
        cdf = 0.5 * (1.0 + lax.erf(pre * 0.7071067811865476))
        density = jnp.exp(-0.5 * pre * pre) * 0.3989422804014327
        act = (pre * cdf).astype(BF16)
        total = total + dot_nt(act, wfc2_ref[:, cols])
        grad_pre = (dot(cot_low, wfc2_ref[:, cols]) * (cdf + pre * density)).astype(BF16)
        grad_second = grad_second + dot_nt(grad_pre, wfc1_ref[:, cols])
        parts_fc[0, 12 * n : 12 * (n + 1)] = dot(second_t, grad_pre).astype(BF16).reshape(12, 16, 256)
        parts_fc[1, 12 * n : 12 * (n + 1)] = dot(cot_t, act).astype(BF16).reshape(12, 16, 256)
        vec[n : n + 1, :] = jnp.sum(grad_pre.astype(F32), 0, keepdims=True)
        pair_fc[n].start()

    def give_back(a, i):
        return pltpu.make_async_remote_copy(
            src_ref=out_stage.at[a, 2 - i],
            dst_ref=quadrant((block_out, dtok_out)[a], i + 1),
            send_sem=rt_send.at[a, i],
            recv_sem=rt_recv.at[a, i],
            device_id=behind[i],
            device_id_type=MESH,
        )

    def hand_out(a, field):
        stage[a] = field
        for slot, row, col, rows in pieces():
            out_stage[a, slot, row, col] = stage[a, rows, :].astype(BF16)
        for i in range(3):
            give_back(a, i).start()
        keep[a].start()

    grad_inner = cot + norm_back(hat2, inv2, gain2, grad_second)
    grad_att = grad_inner.astype(BF16)
    proj_grad = dot_tn(mixed, grad_att).astype(BF16)
    proj_grad = jnp.concatenate([proj_grad, jnp.zeros((C, 64), BF16)], -1).reshape(12, 16, 256)
    parts_fc[0, 36:42] = proj_grad[:6]
    parts_fc[1, 36:42] = proj_grad[6:]
    vec[3:4, 0:C] = jnp.sum(grad_second * hat2, 0, keepdims=True)
    parts_fc[0, 42] = vec[...].astype(BF16)
    parts_fc[1, 42] = jnp.zeros((16, 256), BF16)
    parts_fc[:, 43:] = jnp.zeros((2, FC - 43, 16, 256), BF16)
    pair_fc[3].start()
    hand_out(0, total)
    early1(0)

    grad_mixed = dot_nt(grad_att, wproj_ref[...]).astype(BF16)
    grad_mixed_t = grad_mixed.T
    dsc[...] = jnp.zeros_like(dsc)
    for head in range(HEADS):
        wide_cols[256 * head : 256 * head + T, :] = keys * ones[head]
    grad_k_t = []
    grad_v_t = []
    for head in range(HEADS):
        rows = slice(HEAD * head, HEAD * (head + 1))
        gm = grad_mixed * ones[head]
        probs = prob[head]
        grad_probs = dot_nt(gm, values)
        inside = jnp.sum(probs * grad_probs, -1, keepdims=True)
        grad_scores = probs * (grad_probs - inside)
        dsc[head, 0:T, 0:T] = grad_scores
        scaled = (grad_scores * FACTOR).astype(BF16)
        grad_v_t.append(
            dot(grad_mixed_t[rows], wide_rows[:, 256 * head : 256 * head + T])
        )
        wide_rows[:, 256 * head : 256 * head + T] = scaled
        grad_k_t.append(dot(queries_t[rows], scaled))
        if head in (0, 2):
            early1(1 + head // 2)
    grad_q = dot(wide_rows[...], wide_cols[...])
    grad_k = jnp.concatenate(grad_k_t, 0).T
    grad_v = jnp.concatenate(grad_v_t, 0).T

    grad_qkv = jnp.concatenate([grad_q, grad_k, grad_v], -1).astype(BF16)
    wide = dot_tn(first, grad_qkv).astype(BF16)
    for n in range(4):
        parts_att[n // 2, n % 2 * 12 : n % 2 * 12 + 12] = (
            wide[:, 128 * n : 128 * (n + 1)].reshape(12, 16, 128)
        )
    edge = jnp.concatenate([wide[:96, 512:576], wide[96:, 512:576]], -1).reshape(6, 16, 128)
    parts_att[0, 24:27] = edge[:3]
    parts_att[1, 24:27] = edge[3:]
    grad_first = dot_nt(grad_qkv, wqkv_ref[...]).astype(BF16).astype(F32)
    vec[...] = jnp.zeros_like(vec)
    sums = jnp.sum(grad_qkv.astype(F32), 0, keepdims=True)
    sums = [sums[:, C * n : C * (n + 1)] for n in range(3)]
    sums.append(jnp.sum(grad_first * hat1, 0, keepdims=True))
    for n in range(4):
        vec[2 * n : 2 * n + 1, 0:128] = sums[n][:, 0:128]
        vec[2 * n + 1 : 2 * n + 2, 0:64] = sums[n][:, 128:C]
    parts_att[0, 27] = vec[:, 0:128].astype(BF16)
    parts_att[1, 27] = jnp.zeros((16, 128), BF16)
    parts_att[:, 28:] = jnp.zeros((2, ATT - 28, 16, 128), BF16)
    pair_att.start()
    d_tokens = grad_inner + norm_back(hat1, inv1, gain1, grad_first)
    hand_out(1, d_tokens)

    dmat[...] = jnp.zeros_like(dmat)
    for head in range(HEADS):
        if head == 3:
            late1()
            early2()
        acc = jnp.zeros((16, 384), F32)
        for w in range(WIN_W):
            acc = acc + pltpu.roll(
                dsc[head, w * GROUPS : w * GROUPS + 16, :], (WIN_W - 1 - w) * GROUPS, axis=1
            )
        for n in range(3):
            dmat[n, pl.ds(head, 16, stride=8), :] = acc[:, 128 * n : 128 * (n + 1)]

    def table_grad():
        return jnp.concatenate([dmat[n, 0:96, :] for n in range(3)], -1)

    def keep_table(field):
        for n in range(3):
            dmat[n, 0:96, :] = field[:, 128 * n : 128 * (n + 1)]

    def edge_copy():
        return pltpu.make_async_remote_copy(
            src_ref=bbs,
            dst_ref=bbr,
            send_sem=one_send.at[1],
            recv_sem=one_recv.at[1],
            device_id=(lon, north),
            device_id_type=MESH,
        )

    @pl.when(lat == 0)
    def _():
        upper = lax.broadcasted_iota(jnp.int32, (96, 384), 0) < 48
        full = table_grad()
        bbs[...] = jnp.where(upper, full, 0.0).astype(BF16)
        edge_copy().start()
        keep_table(jnp.where(upper, 0.0, full))

    early3()
    late2()

    @pl.when(lat == BANDS - 1)
    def _():
        edge_copy().wait_recv()
        keep_table(table_grad() + bbr[...].astype(F32))

    bsend[...] = table_grad().astype(BF16).reshape(PARTS, 16, 384)

    for owner in range(PARTS):
        @pl.when(lon != owner)
        def _():
            pltpu.make_async_remote_copy(
                src_ref=bsend.at[owner],
                dst_ref=brecv.at[lon],
                send_sem=b_send.at[0],
                recv_sem=b_recv.at[0],
                device_id=(owner, lat),
                device_id_type=MESH,
            ).start()

    early4()
    early5()
    seven = brecv.at[pl.ds(0, STRIPS - 1)]

    @pl.when(lon < PARTS)
    def _():
        brecv[lon] = bsend[lon]
        wait_bytes(seven, b_recv.at[0])
        bfin[lon] = jnp.sum(brecv[...].astype(F32), 0).astype(BF16)
        for d in range(1, STRIPS):
            pltpu.make_async_remote_copy(
                src_ref=bfin.at[lon],
                dst_ref=bfin.at[lon],
                send_sem=b_send.at[1],
                recv_sem=b_recv.at[1],
                device_id=(strip(d), lat),
                device_id_type=MESH,
            ).start()

    late3()
    early6()
    late4()

    @pl.when(lon < PARTS)
    def _():
        wait_bytes(bfin.at[pl.ds(0, PARTS - 1)], b_recv.at[1])

    @pl.when(lon >= PARTS)
    def _():
        wait_bytes(bfin, b_recv.at[1])

    tin[...] = dot_nt(bfin[...].reshape(96, 384), perm_ref[...])
    dtab_ref[...] = jnp.zeros_like(dtab_ref)
    for zp in range(WIN_Z):
        for zq in range(WIN_Z):
            for hp in range(WIN_H):
                j = (zp * WIN_Z + zq) * WIN_H + hp
                first_lane = j * WIN_H * SPAN
                base = first_lane // 128 * 128
                g = hp * WIN_Z + zp
                piece = tin[g * 8 : g * 8 + 8, zq * 256 : zq * 256 + 256]
                piece = jnp.concatenate([piece, jnp.zeros((8, 128), F32)], -1)
                moved = pltpu.roll(piece, first_lane - base, axis=1)
                dtab_ref[:, base : base + 384] = dtab_ref[:, base : base + 384] + moved

    keep[2].start()

    for a in range(2):
        for i in range(3):
            exchange(a, i).wait_send()
            give_back(a, i).wait()

    @pl.when(lat == BANDS - 1)
    def _():
        table_copy().wait_send()

    @pl.when(lat == 0)
    def _():
        edge_copy().wait_send()

    for copy in pair_fc:
        copy.wait_send()
    for stage_no, ref in ((1, fold1), (2, fold2), (3, fold2), (4, fold2), (5, fold1)):
        for n in range(3):
            wait_bytes(ref.at[n], f_send.at[stage_no, n])
    pair_att.wait_send()
    for stage_no in (1, 2, 3):
        wait_bytes(fold_att, a_send.at[stage_no])

    @pl.when(lon < PARTS)
    def _():
        wait_bytes(bsend.at[pl.ds(0, PARTS - 1)], b_send.at[0])
        wait_bytes(seven, b_send.at[1])

    @pl.when(lon >= PARTS)
    def _():
        wait_bytes(bsend, b_send.at[0])

    for copy in keep:
        copy.wait()
    for copy in swap_fc:
        copy.wait()
    swap_att.wait()


def output_kernel(*refs):
    ins, outs = refs[:5], refs[5:16]
    in_bufs, out_bufs = refs[16:21], refs[21:30]
    in_sem, out_sem = refs[30:]
    loads = [
        pltpu.make_async_copy(src, dst, in_sem.at[n])
        for n, (src, dst) in enumerate(zip(ins, in_bufs))
    ]
    stores = [
        pltpu.make_async_copy(src, dst, out_sem.at[n])
        for n, (src, dst) in enumerate(zip(in_bufs[:2] + out_bufs, outs))
    ]
    gath_ref, gath_att, dtab_ref = in_bufs[2:]
    (
        dln1_ref, dwqkv_ref, dbqkv_ref, dbias_ref, dwproj_ref, dln2_ref,
        dwfc1_ref, dbfc1_ref, dwfc2_ref,
    ) = out_bufs
    for n in (2, 0, 1, 3, 4):
        loads[n].start()
    loads[2].wait()
    for n in range(3):
        cols = slice(256 * n, 256 * (n + 1))
        rows = slice(12 * n, 12 * (n + 1))
        dwfc1_ref[:, cols] = gath_ref[0, rows].reshape(C, 256).astype(F32)
    stores[8].start()
    for n in range(3):
        cols = slice(256 * n, 256 * (n + 1))
        rows = slice(12 * n, 12 * (n + 1))
        dwfc2_ref[:, cols] = gath_ref[1, rows].reshape(C, 256).astype(F32)
    stores[10].start()
    for k in range(2):
        dwproj_ref[96 * k : 96 * (k + 1), :] = (
            gath_ref[k, 36:42].reshape(96, 256)[:, 0:C].astype(F32)
        )
    vec = gath_ref[0, 42].astype(F32)
    dbfc1_ref[...] = jnp.concatenate([vec[n : n + 1] for n in range(3)], -1).reshape(HID)
    dln2_ref[...] = vec[3:4, :C].reshape(C)
    for n in (6, 9, 7):
        stores[n].start()
    for n in range(2):
        loads[n].wait()
        stores[n].start()
    loads[3].wait()
    for k in range(2):
        for n in range(2):
            cols = slice(256 * k + 128 * n, 256 * k + 128 * (n + 1))
            dwqkv_ref[:, cols] = gath_att[k, 12 * n : 12 * (n + 1)].reshape(C, 128).astype(F32)
        edge = gath_att[k, 24:27].reshape(48, 128).astype(F32)
        for n in range(2):
            at = 96 * n + 48 * k
            dwqkv_ref[at : at + 48, 512:576] = edge[:, 64 * n : 64 * (n + 1)]
    vec = gath_att[0, 27].astype(F32)
    sums = [
        jnp.concatenate([vec[2 * n : 2 * n + 1], vec[2 * n + 1 : 2 * n + 2, :64]], -1)
        for n in range(4)
    ]
    dbqkv_ref[...] = jnp.concatenate(sums[:3], -1).reshape(3 * C)
    dln1_ref[...] = sums[3].reshape(C)
    for n in (3, 4, 2):
        stores[n].start()
    loads[4].wait()
    for head in range(HEADS):
        dbias_ref[0, head] = dtab_ref[head : head + 1, 0:NREL]
    stores[5].start()
    for store in stores:
        store.wait()


def per_device(
    tokens, cotangent, ln1_gain, w_qkv, b_qkv, bias_table, w_proj, ln2_gain, w_fc1, b_fc1, w_fc2
):
    hbm = pl.BlockSpec(memory_space=pl.ANY)
    perm = table_order()
    dma = pltpu.SemaphoreType.DMA
    args = (
        tokens.transpose(1, 2, 0, 3), cotangent.transpose(1, 2, 0, 3), ln1_gain, w_qkv, b_qkv,
        bias_table.transpose(0, 2, 1, 3), w_proj, ln2_gain, w_fc1, b_fc1, w_fc2.T,
        jnp.asarray(perm, BF16), jnp.asarray(cross_pairs()),
    )
    gathered, gathered_att, block, d_tok, table = pl.pallas_call(
        block_kernel,
        out_shape=(
            jax.ShapeDtypeStruct((2, FC, 16, 256), BF16),
            jax.ShapeDtypeStruct((2, ATT, 16, 128), BF16),
            jax.ShapeDtypeStruct((WIN_H, WIN_W, WIN_Z, C), BF16),
            jax.ShapeDtypeStruct((WIN_H, WIN_W, WIN_Z, C), BF16),
            jax.ShapeDtypeStruct((8, 3456), F32),
        ),
        in_specs=[hbm] * len(args),
        out_specs=(hbm,) * 5,
        scratch_shapes=[pltpu.VMEM(a.shape, a.dtype) for a in args[2:]]
        + [
            pltpu.VMEM((2, T, C), F32),
            pltpu.VMEM((2, 4, 3, 6, WIN_Z, C), BF16),
            pltpu.VMEM((2, 4, 3, 6, WIN_Z, C), BF16),
            pltpu.VMEM((8, 3456), F32),
            pltpu.VMEM((1, HEADS, 1, NREL), F32),
            pltpu.VMEM((96, 512), F32),
            pltpu.VMEM((3, 128, 128), F32),
            pltpu.VMEM((HEADS, T, T), F32),
            pltpu.VMEM((HEADS, T, T), F32),
            pltpu.VMEM((T, HEADS * 256), BF16),
            pltpu.VMEM((HEADS * 256, C), BF16),
            pltpu.VMEM((HEADS, 160, 384), F32),
            pltpu.VMEM((3, 128, 128), F32),
            pltpu.VMEM((16, 256), F32),
            pltpu.VMEM((PARTS, 16, 384), BF16),
            pltpu.VMEM((STRIPS, 16, 384), BF16),
            pltpu.VMEM((PARTS, 16, 384), BF16),
            pltpu.VMEM((96, 384), BF16),
            pltpu.VMEM((96, 384), BF16),
            pltpu.VMEM((2, FC, 16, 256), BF16),
            pltpu.VMEM((2, ATT, 16, 128), BF16),
            pltpu.VMEM((FC, 16, 256), BF16),
            pltpu.VMEM((ATT, 16, 128), BF16),
            pltpu.VMEM((3, 3, 4, 16, 256), BF16),
            pltpu.VMEM((3, 4, 16, 256), BF16),
            pltpu.VMEM((3, 3, 16, 256), BF16),
            pltpu.VMEM((3, 16, 256), BF16),
            pltpu.VMEM((3, 4, 16, 256), BF16),
            pltpu.VMEM((ROWS - 1, 4, 16, 128), BF16),
            pltpu.VMEM((4, 16, 128), BF16),
            pltpu.VMEM((STRIPS, 4, 16, 128), BF16),
            pltpu.VMEM((2, FC, 16, 256), BF16),
            pltpu.VMEM((2, ATT, 16, 128), BF16),
            pltpu.VMEM((8, 3456), F32),
            dma((len(args) - 2,)), dma((2,)), dma((7,)),
            dma((2, 3)), dma((2, 3)), dma((2, 3)), dma((2, 3)),
            dma((2,)), dma((2,)), dma((4,)), dma((4,)), dma((7, 3)), dma((7, 3)),
            dma((5,)), dma((5,)), dma((2,)), dma((2,)),
        ],
        compiler_params=pltpu.CompilerParams(
            collective_id=0, has_side_effects=True, vmem_limit_bytes=VMEM_LIMIT
        ),
    )(*args)
    shape = jax.ShapeDtypeStruct
    grid_shape = (WIN_H, WIN_W, WIN_Z, C)
    results_out = (
        shape(grid_shape, BF16), shape(grid_shape, BF16),
        shape((C,), F32), shape((C, 3 * C), F32), shape((3 * C,), F32),
        shape((1, HEADS, 1, NREL), F32), shape((C, C), F32), shape((C,), F32),
        shape((C, HID), F32), shape((HID,), F32), shape((C, HID), F32),
    )
    outs = pl.pallas_call(
        output_kernel,
        out_shape=results_out,
        in_specs=[hbm] * 5,
        out_specs=(hbm,) * 11,
        scratch_shapes=[
            pltpu.VMEM(a.shape, a.dtype)
            for a in (block, d_tok, gathered, gathered_att, table) + results_out[2:]
        ]
        + [dma((5,)), dma((11,))],
        compiler_params=pltpu.CompilerParams(vmem_limit_bytes=VMEM_LIMIT),
    )(block, d_tok, gathered, gathered_att, table)
    out, d_tok, d_ln1, d_wqkv, d_bqkv, d_bias, d_wproj, d_ln2, d_wfc1, d_bfc1, d_wfc2 = outs
    return (
        out.transpose(2, 0, 1, 3), d_tok.transpose(2, 0, 1, 3), d_ln1, d_wqkv, d_bqkv,
        d_bias.transpose(0, 2, 1, 3), d_wproj, d_ln2, d_wfc1, d_bfc1, d_wfc2.T,
    )


def solution(mesh):
    grid = P(None, "lat", "lon", None)
    rows = P(None, "lat", None, None)
    return jax.shard_map(
        per_device,
        mesh=mesh,
        in_specs=(grid, grid, P(), P(), P(), rows, P(), P(), P(), P(), P()),
        out_specs=(grid, grid, P(), P(), P(), rows, P(), P(), P(), P(), P()),
        check_vma=False,
    )
```

```python
import jax
import jax.numpy as jnp
import numpy as np
from jax import lax
from jax.experimental import pallas as pl
from jax.experimental.pallas import tpu as pltpu
from jax.sharding import PartitionSpec as P

HEADS = 6
WIN_Z = 2
WIN_H = 6
WIN_W = 12
SPAN = 2 * WIN_W - 1
GROUPS = WIN_Z * WIN_H
T = GROUPS * WIN_W
C = 192
HID = 768
HEAD = C // HEADS
NREL = GROUPS * GROUPS * SPAN
FC = 48
ATT = 24
TALL = 3
ROWS = 8
BANDS = 16
STRIPS = 8
PARTS = 6
EPSILON = 1e-05
VMEM_LIMIT = 56 * 1024 * 1024
FACTOR = HEAD ** (-0.5)
LOG2E = 1.4426950408889634
F32 = jnp.float32
BF16 = jnp.bfloat16
MESH = pl.DeviceIdType.MESH


def table_order():
    grid = np.zeros((512, 384), np.float32)
    for z in range(WIN_Z):
        for h in range(WIN_H):
            for i in range(SPAN):
                grid[z * 256 + h * SPAN + i, (SPAN - 1 - i) * GROUPS + h * WIN_Z + z] = 1
    return grid


def cross_pairs():
    g = np.arange(96)[:, None] // 8 // WIN_Z
    q = np.arange(384)[None, :] % GROUPS // WIN_Z
    return np.where((g < 3) != (q < 3), -1e30, 0.0).astype(np.float32)


def dot(a, b):
    return jnp.dot(a, b, preferred_element_type=F32)


def dot_nt(a, b):
    return lax.dot_general(a, b, (((1,), (1,)), ((), ())), preferred_element_type=F32)


def dot_tn(a, b):
    return lax.dot_general(a, b, (((0,), (0,)), ((), ())), preferred_element_type=F32)


def normalize(values, gain):
    average = jnp.mean(values, -1, keepdims=True)
    centered = values - average
    inv = lax.rsqrt(jnp.mean(centered * centered, -1, keepdims=True) + EPSILON)
    hat = centered * inv
    return hat * gain, hat, inv


def norm_back(hat, inv, gain, grad):
    scaled = grad * gain
    return inv * (
        scaled
        - jnp.mean(scaled, -1, keepdims=True)
        - hat * jnp.mean(scaled * hat, -1, keepdims=True)
    )


def pieces():
    for h in range(WIN_H):
        for w in range(WIN_W):
            at = w * GROUPS + h * WIN_Z
            yield (h // 3) * 2 + w // 6, h % 3, w % 6, slice(at, at + WIN_Z)


def quadrant(ref, q):
    return ref.at[pl.ds(q // 2 * 3, 3), pl.ds(q % 2 * 6, 6)]


def block_kernel(
    tok_any, cot_any, g1_any, wqkv_any, bqkv_any, table_any, wproj_any, g2_any, wfc1_any,
    bfc1_any, wfc2_any, perm_any, cross_any,
    gath_fc_out, gath_att_out, block_out, dtok_out, dtab_out,
    g1_ref, wqkv_ref, bqkv_ref, table_ref, wproj_ref, g2_ref, wfc1_ref,
    bfc1_ref, wfc2_ref, perm_ref, cross_ref,
    stage, arrive, out_stage,
    tabw, tab15, tin, ymat, bias, prob, wide_rows, wide_cols, dsc, dmat, vec,
    bsend, brecv, bfin, bbs, bbr,
    parts_fc, parts_att, core_att, fold1, sum1, fold2, sum2, fold3, fold_att, sum_att,
    mid_att, gath_fc, gath_att, dtab_ref,
    in_sem, own_sem, out_sem,
    ex_send, ex_recv, rt_send, rt_recv, one_send, one_recv, f_send, f_recv,
    a_send, a_recv, b_send, b_recv,
):
    sources = (
        (table_any, table_ref), (perm_any, perm_ref), (cross_any, cross_ref), (g1_any, g1_ref),
        (wqkv_any, wqkv_ref), (bqkv_any, bqkv_ref), (wproj_any, wproj_ref), (g2_any, g2_ref),
        (wfc1_any, wfc1_ref), (bfc1_any, bfc1_ref), (wfc2_any, wfc2_ref),
    )
    loads = [pltpu.make_async_copy(src, dst, in_sem.at[n]) for n, (src, dst) in enumerate(sources)]
    lon = lax.axis_index("lon")
    lat = lax.axis_index("lat")
    core = lax.rem(lat, 2)
    other = 1 - core
    pair_row = lat // 2
    east = lax.rem(lon + 1, STRIPS)
    west = lax.rem(lon + STRIPS - 1, STRIPS)
    south = lax.rem(lat + 1, BANDS)
    north = lax.rem(lat + BANDS - 1, BANDS)
    sibling = (lon, lat - core + other)

    spot = (lax.rem(pair_row, 4), lon // 2, lax.rem(lon, 2) * 2 + lat // 8)

    def on_axis(axis, at, side=core):
        if axis == 0:
            return (lon, lat // 8 * 8 + at * 2 + side)
        if axis == 1:
            return (at * 2 + lax.rem(lon, 2), lat - core + side)
        return (spot[1] * 2 + at // 2, lax.rem(at, 2) * 8 + spot[0] * 2 + side)

    def strip(d):
        return lax.rem(lon + d, STRIPS)

    def row_of(d):
        return lax.rem(pair_row + d, ROWS)

    barrier = pltpu.get_barrier_semaphore()

    def greet(target):
        pl.semaphore_signal(barrier, inc=1, device_id=target, device_id_type=MESH)

    for target in ((east, south), (west, north)):
        greet(target)
    for d in range(1, STRIPS):
        greet((strip(d), lat))
    for d in range(1, BANDS):
        greet((lon, lax.rem(lat + d, BANDS)))
    for d in range(1, 4):
        greet(on_axis(1, lax.rem(spot[1] + d, 4), other))
    across = lax.rem(spot[2] + 2, 4)
    greet(on_axis(2, across, other))
    greet(on_axis(2, 3 - spot[2]))
    greet(on_axis(2, 3 - spot[2], other))
    loads[0].start()
    own = [
        pltpu.make_async_copy(quadrant(src, 0), arrive.at[a, 3], own_sem.at[a])
        for a, src in enumerate((tok_any, cot_any))
    ]
    own[0].start()
    pl.semaphore_wait(barrier, 30)

    ahead = ((east, lat), (lon, south), (east, south))
    behind = ((west, lat), (lon, north), (west, north))

    def exchange(a, i):
        return pltpu.make_async_remote_copy(
            src_ref=quadrant((tok_any, cot_any)[a], i + 1),
            dst_ref=arrive.at[a, 2 - i],
            send_sem=ex_send.at[a, i],
            recv_sem=ex_recv.at[a, i],
            device_id=ahead[i],
            device_id_type=MESH,
        )

    def table_copy():
        return pltpu.make_async_remote_copy(
            src_ref=table_any,
            dst_ref=tab15,
            send_sem=one_send.at[0],
            recv_sem=one_recv.at[0],
            device_id=(lon, south),
            device_id_type=MESH,
        )

    @pl.when(lat == BANDS - 1)
    def _():
        table_copy().start()

    for a in range(2):
        for i in range(3):
            exchange(a, i).start()
    for load in loads[1:]:
        load.start()
    own[1].start()

    tabw[...] = jnp.zeros_like(tabw)
    loads[0].wait()
    for head in range(HEADS):
        tabw[head : head + 1, 0:NREL] = table_ref[0, head]

    tin[...] = jnp.zeros_like(tin)

    def spread(src, zp, zq, hp, width):
        j = (zp * WIN_Z + zq) * WIN_H + hp
        first = j * WIN_H * SPAN
        base = first // 128 * 128
        wide = src[:, base : base + 384]
        moved = pltpu.roll(wide, (384 - (first - base)) % 384, axis=1)
        g = hp * WIN_Z + zp
        tin[g * 8 : g * 8 + 8, zq * 256 : zq * 256 + width] = moved[:, :width]

    for zp in range(WIN_Z):
        for zq in range(WIN_Z):
            for hp in range(WIN_H):
                spread(tabw, zp, zq, hp, WIN_H * SPAN)

    def permuted(whole):
        high = whole.astype(BF16)
        rest = whole - high.astype(F32)
        middle = rest.astype(BF16)
        low = (rest - middle.astype(F32)).astype(BF16)
        perm = perm_ref[...]
        return (dot(high, perm) + dot(middle, perm) + dot(low, perm)) * LOG2E

    loads[1].wait()
    spread_rows = permuted(tin[...])
    for n in range(3):
        ymat[n, 0:96, :] = spread_rows[:, 128 * n : 128 * (n + 1)]
        ymat[n, 96:128, :] = jnp.zeros((32, 128), F32)
    loads[2].wait()

    @pl.when(lat == 0)
    def _():
        for n in range(3):
            ymat[n, 0:96, :] = ymat[n, 0:96, :] + cross_ref[:, 128 * n : 128 * (n + 1)]

    def place_bias(tall, count):
        for head in range(HEADS):
            rows = jnp.concatenate(
                [ymat[n, pl.ds(head, tall, stride=8), :] for n in range(3)], -1
            )
            for w in range(WIN_W):
                moved = pltpu.roll(rows, (384 - (WIN_W - 1 - w) * GROUPS) % 384, axis=1)
                bias[head, w * GROUPS : w * GROUPS + count, :] = moved[:count, :T]

    place_bias(16, GROUPS)
    for n in range(3, 11):
        loads[n].wait()
    lane = lax.broadcasted_iota(jnp.int32, (16, C), 1)
    ones = [
        jnp.where((lane >= HEAD * i) & (lane < HEAD * (i + 1)), 1.0, 0.0).astype(BF16)[0:1]
        for i in range(HEADS)
    ]
    gain1 = g1_ref[...].reshape(1, C)
    gain2 = g2_ref[...].reshape(1, C)

    def arrived(a):
        for i in range(3):
            exchange(a, i).wait_recv()
        own[a].wait()
        for slot, row, col, rows in pieces():
            stage[a, rows, :] = arrive[a, slot, row, col].astype(F32)
        return stage[a]

    tokens = arrived(0)
    normed, hat1, inv1 = normalize(tokens, gain1)
    first = normed.astype(BF16)
    qkv = (dot(first, wqkv_ref[...]) + bqkv_ref[...].reshape(1, 3 * C)).astype(BF16)
    queries = qkv[:, 0:C]
    keys = qkv[:, C : 2 * C]
    values = qkv[:, 2 * C : 3 * C]
    queries_t = queries.T

    @pl.when(lat == 0)
    def _():
        table_copy().wait_recv()
        for head in range(HEADS):
            tabw[head : head + 1, 0:NREL] = tab15[0, head]
        tin[0:48, :] = jnp.zeros((48, 512), F32)
        for zp in range(WIN_Z):
            for zq in range(WIN_Z):
                for hp in range(3):
                    spread(tabw, zp, zq, hp, 3 * SPAN)
        upper_rows = permuted(tin[0:48, :]) + cross_ref[0:48, :]
        for n in range(3):
            ymat[n, 0:48, :] = upper_rows[:, 128 * n : 128 * (n + 1)]
        place_bias(8, 6)

    wide_rows[...] = jnp.zeros_like(wide_rows)
    wide_cols[...] = jnp.zeros_like(wide_cols)
    for head in range(HEADS):
        wide_cols[256 * head : 256 * head + T, :] = values * ones[head]
    for head in range(HEADS):
        q = queries * ones[head]
        scores = dot_nt(q, keys) * (FACTOR * LOG2E) + bias[head]
        top = jnp.max(scores, -1, keepdims=True)
        raised = jnp.exp2(scores - top)
        probs = raised * (1.0 / jnp.sum(raised, -1, keepdims=True))
        prob[head] = probs
        probs_low = probs.astype(BF16)
        wide_rows[:, 256 * head : 256 * head + T] = probs_low
    mixed = dot(wide_rows[...], wide_cols[...]).astype(BF16)
    inner = tokens + dot(mixed, wproj_ref[...]).astype(BF16).astype(F32)

    def remote(src, dst, send_sem, recv_sem, target):
        return pltpu.make_async_remote_copy(
            src_ref=src, dst_ref=dst, send_sem=send_sem, recv_sem=recv_sem,
            device_id=target, device_id_type=MESH,
        )

    def wait_bytes(ref, sem):
        pltpu.make_async_copy(ref, ref, sem).wait()

    def add(*terms):
        total = terms[0].astype(F32)
        for term in terms[1:]:
            total = total + term.astype(F32)
        return total.astype(BF16)

    axes = [(n, (n + 1) % 3, (n + 2) % 3) for n in range(3)]
    places = [tuple(spot[axis] for axis in order) for order in axes]

    def block(n, i):
        return pl.ds(n * 16 + i * 4, 4)

    def unit(n):
        return n * 16 + places[n][0] * 4 + places[n][1]

    def part_to_line(n, stage_no, which, src, dst):
        for d in range(1, 4):
            at = lax.rem(places[n][which] + d, 4)
            remote(
                src(n, at), dst(n, d), f_send.at[stage_no, n], f_recv.at[stage_no, n],
                on_axis(axes[n][which], at),
            ).start()

    def third(n):
        return pl.ds(16 * n, 16)

    swap_fc = [
        remote(
            gath_fc.at[core, third(n)], gath_fc_out.at[core, third(n)],
            f_send.at[6, n], f_recv.at[6, n], sibling,
        )
        for n in range(3)
    ]
    pair_att = remote(parts_att.at[other], core_att, a_send.at[0], a_recv.at[0], sibling)
    swap_att = remote(
        gath_att.at[core], gath_att_out.at[core], a_send.at[4], a_recv.at[4], sibling
    )
    kept = [
        (out_stage.at[0, 3], quadrant(block_out, 0)),
        (out_stage.at[1, 3], quadrant(dtok_out, 0)),
        (dtab_ref, dtab_out),
        (gath_att.at[core], gath_att_out.at[core]),
    ] + [(gath_fc.at[core, third(n)], gath_fc_out.at[core, third(n)]) for n in range(3)]
    keep = [
        pltpu.make_async_copy(src, dst, out_sem.at[n]) for n, (src, dst) in enumerate(kept)
    ]

    def early1(n):
        for side, first, slot in ((core, 1, -1), (other, 0, 3)):
            for d in range(first, 4):
                at = lax.rem(places[n][0] + d, 4)
                remote(
                    parts_fc.at[side, block(n, at)], fold1.at[n, slot + d],
                    f_send.at[1, n], f_recv.at[1, n], on_axis(n, at, side),
                ).start()

    def early2():
        for n in range(3):
            wait_bytes(fold1.at[n], f_recv.at[1, n])
            own_block = parts_fc[core, block(n, places[n][0])]
            sum1[n] = add(own_block, *[fold1[n, i] for i in range(7)])
            part_to_line(
                n, 2, 1, lambda n, at: sum1.at[n, at], lambda n, d: fold2.at[n, d - 1]
            )

    def early3():
        for n in range(3):
            wait_bytes(fold2.at[n], f_recv.at[2, n])
            own_unit = sum1[n, places[n][1]]
            sum2[n] = add(own_unit, fold2[n, 0], fold2[n, 1], fold2[n, 2])
            fold3[n, places[n][2]] = sum2[n]
            part_to_line(
                n, 3, 2, lambda n, at: sum2.at[n], lambda n, d: fold3.at[n, places[n][2]]
            )

    def early4():
        for n in range(3):
            wait_bytes(fold2.at[n], f_recv.at[3, n])
            gath_fc[core, unit(n)] = add(*[fold3[n, i] for i in range(4)])
            part_to_line(
                n, 4, 1, lambda n, at: gath_fc.at[core, unit(n)],
                lambda n, d: gath_fc.at[core, unit(n)],
            )

    def early5():
        for n in range(3):
            wait_bytes(fold2.at[n], f_recv.at[4, n])
            part_to_line(
                n, 5, 0, lambda n, at: gath_fc.at[core, block(n, places[n][0])],
                lambda n, d: gath_fc.at[core, block(n, places[n][0])],
            )

    def early6():
        for n in range(3):
            wait_bytes(fold1.at[n, pl.ds(0, 3)], f_recv.at[5, n])
            swap_fc[n].start()
            keep[4 + n].start()

    own_rows = pl.ds(pair_row * TALL, TALL)

    def late1():
        pair_att.wait_recv()
        parts_att[core] = add(parts_att[core], core_att[...])
        for d in range(1, ROWS):
            remote(
                parts_att.at[core, pl.ds(row_of(d) * TALL, TALL)], fold_att.at[d - 1],
                a_send.at[1], a_recv.at[1], (lon, row_of(d) * 2 + core),
            ).start()

    def late2():
        wait_bytes(fold_att, a_recv.at[1])
        sum_att[...] = add(parts_att[core, own_rows], *[fold_att[d] for d in range(ROWS - 1)])
        mid_att[lon] = sum_att[...]
        for d in range(1, STRIPS):
            remote(
                sum_att, mid_att.at[lon], a_send.at[2], a_recv.at[2], (strip(d), lat)
            ).start()

    def late3():
        wait_bytes(fold_att, a_recv.at[2])
        gath_att[core, own_rows] = add(*[mid_att[i] for i in range(STRIPS)])
        for d in range(1, ROWS):
            remote(
                gath_att.at[core, own_rows], gath_att.at[core, own_rows],
                a_send.at[3], a_recv.at[3], (lon, row_of(d) * 2 + core),
            ).start()

    def late4():
        wait_bytes(fold_att, a_recv.at[3])
        swap_att.start()
        keep[3].start()

    cot = arrived(1)
    cot_low = cot.astype(BF16)
    normed, hat2, inv2 = normalize(inner, gain2)
    second = normed.astype(BF16)
    second_t = second.T
    cot_t = cot_low.T
    total = inner
    grad_second = jnp.zeros((T, C), F32)
    bfc1 = bfc1_ref[...].reshape(1, HID)
    vec[...] = jnp.zeros_like(vec)
    for n in range(3):
        cols = slice(256 * n, 256 * (n + 1))
        pre = dot(second, wfc1_ref[:, cols]) + bfc1[:, cols]
        cdf = 0.5 * (1.0 + lax.erf(pre * 0.7071067811865476))
        density = jnp.exp(-0.5 * pre * pre) * 0.3989422804014327
        act = (pre * cdf).astype(BF16)
        total = total + dot_nt(act, wfc2_ref[:, cols])
        grad_pre = (dot(cot_low, wfc2_ref[:, cols]) * (cdf + pre * density)).astype(BF16)
        grad_second = grad_second + dot_nt(grad_pre, wfc1_ref[:, cols])
        parts_fc[0, 12 * n : 12 * (n + 1)] = dot(second_t, grad_pre).astype(BF16).reshape(12, 16, 256)
        parts_fc[1, 12 * n : 12 * (n + 1)] = dot(cot_t, act).astype(BF16).reshape(12, 16, 256)
        vec[n : n + 1, :] = jnp.sum(grad_pre.astype(F32), 0, keepdims=True)
        if n:
            early1(n - 1)

    def give_back(a, i):
        return pltpu.make_async_remote_copy(
            src_ref=out_stage.at[a, 2 - i],
            dst_ref=quadrant((block_out, dtok_out)[a], i + 1),
            send_sem=rt_send.at[a, i],
            recv_sem=rt_recv.at[a, i],
            device_id=behind[i],
            device_id_type=MESH,
        )

    def hand_out(a, field):
        stage[a] = field
        for slot, row, col, rows in pieces():
            out_stage[a, slot, row, col] = stage[a, rows, :].astype(BF16)
        for i in range(3):
            give_back(a, i).start()
        keep[a].start()

    grad_inner = cot + norm_back(hat2, inv2, gain2, grad_second)
    grad_att = grad_inner.astype(BF16)
    hand_out(0, total)
    grad_mixed = dot_nt(grad_att, wproj_ref[...]).astype(BF16)
    grad_mixed_t = grad_mixed.T
    grad_v_t = [
        dot(
            grad_mixed_t[HEAD * head : HEAD * (head + 1)],
            wide_rows[:, 256 * head : 256 * head + T],
        )
        for head in range(HEADS)
    ]
    grad_v = jnp.concatenate(grad_v_t, 0).T.astype(BF16)
    first_t = first.T
    value_grad = dot(first_t, grad_v).astype(BF16)
    proj_grad = dot_tn(mixed, grad_att).astype(BF16)
    last = value_grad[176:C]
    last = jnp.concatenate(
        [last[:, 0:64], last[:, 64:128], last[:, 128:C], jnp.zeros((144, 64), BF16)], 0
    )
    proj_grad = jnp.concatenate([proj_grad, last], -1).reshape(12, 16, 256)
    value_grad = jnp.concatenate([value_grad, jnp.zeros((C, 64), BF16)], -1).reshape(12, 16, 256)
    parts_fc[0, 36:42] = proj_grad[:6]
    parts_fc[1, 36:42] = proj_grad[6:]
    parts_fc[0, 43:48] = value_grad[0:5]
    parts_fc[1, 42:48] = value_grad[5:11]
    vec[3:4, 0:C] = jnp.sum(grad_second * hat2, 0, keepdims=True)
    vec[4:5, 0:C] = jnp.sum(grad_v.astype(F32), 0, keepdims=True)
    parts_fc[0, 42] = vec[...].astype(BF16)
    early1(2)

    dsc[...] = jnp.zeros_like(dsc)
    for head in range(HEADS):
        wide_cols[256 * head : 256 * head + T, :] = keys * ones[head]
    grad_k_t = []
    for head in range(HEADS):
        rows = slice(HEAD * head, HEAD * (head + 1))
        gm = grad_mixed * ones[head]
        probs = prob[head]
        grad_probs = dot_nt(gm, values)
        inside = jnp.sum(probs * grad_probs, -1, keepdims=True)
        grad_scores = probs * (grad_probs - inside)
        dsc[head, 0:T, 0:T] = grad_scores
        scaled = (grad_scores * FACTOR).astype(BF16)
        wide_rows[:, 256 * head : 256 * head + T] = scaled
        grad_k_t.append(dot(queries_t[rows], scaled))
    grad_q = dot(wide_rows[...], wide_cols[...])
    grad_k = jnp.concatenate(grad_k_t, 0).T

    grad_qk = jnp.concatenate([grad_q, grad_k], -1).astype(BF16)
    wide = dot(first_t, grad_qk).astype(BF16)
    wide = [wide[:, 128 * n : 128 * (n + 1)].reshape(12, 16, 128) for n in range(3)]
    parts_att[0, 0:12] = wide[0]
    parts_att[0, 12:18] = wide[1][:6]
    parts_att[1, 0:6] = wide[1][6:]
    parts_att[1, 6:18] = wide[2]
    grad_first = dot_nt(grad_qk, wqkv_ref[:, 0 : 2 * C])
    grad_first = grad_first + dot_nt(grad_v, wqkv_ref[:, 2 * C : 3 * C])
    grad_first = grad_first.astype(BF16).astype(F32)
    vec[...] = jnp.zeros_like(vec)
    sums = jnp.sum(grad_qk.astype(F32), 0, keepdims=True)
    sums = [sums[:, C * n : C * (n + 1)] for n in range(2)]
    sums.append(jnp.sum(grad_first * hat1, 0, keepdims=True))
    for n in range(3):
        vec[2 * n : 2 * n + 1, 0:128] = sums[n][:, 0:128]
        vec[2 * n + 1 : 2 * n + 2, 0:64] = sums[n][:, 128:C]
    parts_att[0, 18] = vec[:, 0:128].astype(BF16)
    parts_att[1, 18] = jnp.zeros((16, 128), BF16)
    parts_att[:, 19:] = jnp.zeros((2, ATT - 19, 16, 128), BF16)
    pair_att.start()
    d_tokens = grad_inner + norm_back(hat1, inv1, gain1, grad_first)
    hand_out(1, d_tokens)

    dmat[...] = jnp.zeros_like(dmat)
    for head in range(HEADS):
        if head == 3:
            late1()
            early2()
        acc = jnp.zeros((16, 384), F32)
        for w in range(WIN_W):
            acc = acc + pltpu.roll(
                dsc[head, w * GROUPS : w * GROUPS + 16, :], (WIN_W - 1 - w) * GROUPS, axis=1
            )
        for n in range(3):
            dmat[n, pl.ds(head, 16, stride=8), :] = acc[:, 128 * n : 128 * (n + 1)]

    def table_grad():
        return jnp.concatenate([dmat[n, 0:96, :] for n in range(3)], -1)

    def keep_table(field):
        for n in range(3):
            dmat[n, 0:96, :] = field[:, 128 * n : 128 * (n + 1)]

    def edge_copy():
        return pltpu.make_async_remote_copy(
            src_ref=bbs,
            dst_ref=bbr,
            send_sem=one_send.at[1],
            recv_sem=one_recv.at[1],
            device_id=(lon, north),
            device_id_type=MESH,
        )

    @pl.when(lat == 0)
    def _():
        upper = lax.broadcasted_iota(jnp.int32, (96, 384), 0) < 48
        full = table_grad()
        bbs[...] = jnp.where(upper, full, 0.0).astype(BF16)
        edge_copy().start()
        keep_table(jnp.where(upper, 0.0, full))

    late2()
    early3()

    @pl.when(lat == BANDS - 1)
    def _():
        edge_copy().wait_recv()
        keep_table(table_grad() + bbr[...].astype(F32))

    bsend[...] = table_grad().astype(BF16).reshape(PARTS, 16, 384)

    for owner in range(PARTS):
        @pl.when(lon != owner)
        def _():
            pltpu.make_async_remote_copy(
                src_ref=bsend.at[owner],
                dst_ref=brecv.at[lon],
                send_sem=b_send.at[0],
                recv_sem=b_recv.at[0],
                device_id=(owner, lat),
                device_id_type=MESH,
            ).start()

    early4()
    late3()
    early5()
    seven = brecv.at[pl.ds(0, STRIPS - 1)]

    @pl.when(lon < PARTS)
    def _():
        brecv[lon] = bsend[lon]
        wait_bytes(seven, b_recv.at[0])
        bfin[lon] = jnp.sum(brecv[...].astype(F32), 0).astype(BF16)
        for d in range(1, STRIPS):
            pltpu.make_async_remote_copy(
                src_ref=bfin.at[lon],
                dst_ref=bfin.at[lon],
                send_sem=b_send.at[1],
                recv_sem=b_recv.at[1],
                device_id=(strip(d), lat),
                device_id_type=MESH,
            ).start()

    late4()
    early6()

    @pl.when(lon < PARTS)
    def _():
        wait_bytes(bfin.at[pl.ds(0, PARTS - 1)], b_recv.at[1])

    @pl.when(lon >= PARTS)
    def _():
        wait_bytes(bfin, b_recv.at[1])

    tin[...] = dot_nt(bfin[...].reshape(96, 384), perm_ref[...])
    dtab_ref[...] = jnp.zeros_like(dtab_ref)
    for zp in range(WIN_Z):
        for zq in range(WIN_Z):
            for hp in range(WIN_H):
                j = (zp * WIN_Z + zq) * WIN_H + hp
                first_lane = j * WIN_H * SPAN
                base = first_lane // 128 * 128
                g = hp * WIN_Z + zp
                piece = tin[g * 8 : g * 8 + 8, zq * 256 : zq * 256 + 256]
                piece = jnp.concatenate([piece, jnp.zeros((8, 128), F32)], -1)
                moved = pltpu.roll(piece, first_lane - base, axis=1)
                dtab_ref[:, base : base + 384] = dtab_ref[:, base : base + 384] + moved

    keep[2].start()

    for a in range(2):
        for i in range(3):
            exchange(a, i).wait_send()
            give_back(a, i).wait()

    @pl.when(lat == BANDS - 1)
    def _():
        table_copy().wait_send()

    @pl.when(lat == 0)
    def _():
        edge_copy().wait_send()

    for n in range(3):
        wait_bytes(fold1.at[n], f_send.at[1, n])
        for stage_no in (2, 3, 4):
            wait_bytes(fold2.at[n], f_send.at[stage_no, n])
        wait_bytes(fold1.at[n, pl.ds(0, 3)], f_send.at[5, n])
    pair_att.wait_send()
    for stage_no in (1, 2, 3):
        wait_bytes(fold_att, a_send.at[stage_no])

    @pl.when(lon < PARTS)
    def _():
        wait_bytes(bsend.at[pl.ds(0, PARTS - 1)], b_send.at[0])
        wait_bytes(seven, b_send.at[1])

    @pl.when(lon >= PARTS)
    def _():
        wait_bytes(bsend, b_send.at[0])

    for copy in keep:
        copy.wait()
    for copy in swap_fc:
        copy.wait()
    swap_att.wait()


def output_kernel(*refs):
    ins, outs = refs[:5], refs[5:16]
    in_bufs, out_bufs = refs[16:21], refs[21:30]
    in_sem, out_sem = refs[30:]
    loads = [
        pltpu.make_async_copy(src, dst, in_sem.at[n])
        for n, (src, dst) in enumerate(zip(ins, in_bufs))
    ]
    stores = [
        pltpu.make_async_copy(src, dst, out_sem.at[n])
        for n, (src, dst) in enumerate(zip(in_bufs[:2] + out_bufs, outs))
    ]
    gath_ref, gath_att, dtab_ref = in_bufs[2:]
    (
        dln1_ref, dwqkv_ref, dbqkv_ref, dbias_ref, dwproj_ref, dln2_ref,
        dwfc1_ref, dbfc1_ref, dwfc2_ref,
    ) = out_bufs
    for n in (2, 0, 1, 3, 4):
        loads[n].start()
    loads[2].wait()
    for n in range(3):
        cols = slice(256 * n, 256 * (n + 1))
        rows = slice(12 * n, 12 * (n + 1))
        dwfc1_ref[:, cols] = gath_ref[0, rows].reshape(C, 256).astype(F32)
    stores[8].start()
    for n in range(3):
        cols = slice(256 * n, 256 * (n + 1))
        rows = slice(12 * n, 12 * (n + 1))
        dwfc2_ref[:, cols] = gath_ref[1, rows].reshape(C, 256).astype(F32)
    stores[10].start()
    for k in range(2):
        dwproj_ref[96 * k : 96 * (k + 1), :] = (
            gath_ref[k, 36:42].reshape(96, 256)[:, 0:C].astype(F32)
        )
    vec = gath_ref[0, 42].astype(F32)
    dbfc1_ref[...] = jnp.concatenate([vec[n : n + 1] for n in range(3)], -1).reshape(HID)
    dln2_ref[...] = vec[3:4, :C].reshape(C)
    for n in (6, 9, 7):
        stores[n].start()
    for n in range(2):
        loads[n].wait()
        stores[n].start()
    loads[3].wait()
    dwqkv_ref[:, 0:128] = gath_att[0, 0:12].reshape(C, 128).astype(F32)
    dwqkv_ref[0:96, 128:256] = gath_att[0, 12:18].reshape(96, 128).astype(F32)
    dwqkv_ref[96:C, 128:256] = gath_att[1, 0:6].reshape(96, 128).astype(F32)
    dwqkv_ref[:, 256:384] = gath_att[1, 6:18].reshape(C, 128).astype(F32)
    dwqkv_ref[0:80, 384:576] = gath_ref[0, 43:48].reshape(80, 256)[:, 0:C].astype(F32)
    dwqkv_ref[80:176, 384:576] = gath_ref[1, 42:48].reshape(96, 256)[:, 0:C].astype(F32)
    last = [gath_ref[0, 36 + n][:, C:256].astype(F32) for n in range(3)]
    dwqkv_ref[176:C, 384:576] = jnp.concatenate(last, -1)
    value_bias = vec[4:5, :C]
    vec = gath_att[0, 18].astype(F32)
    sums = [
        jnp.concatenate([vec[2 * n : 2 * n + 1], vec[2 * n + 1 : 2 * n + 2, :64]], -1)
        for n in range(3)
    ]
    dbqkv_ref[...] = jnp.concatenate(sums[:2] + [value_bias], -1).reshape(3 * C)
    dln1_ref[...] = sums[2].reshape(C)
    for n in (3, 4, 2):
        stores[n].start()
    loads[4].wait()
    for head in range(HEADS):
        dbias_ref[0, head] = dtab_ref[head : head + 1, 0:NREL]
    stores[5].start()
    for store in stores:
        store.wait()


def per_device(
    tokens, cotangent, ln1_gain, w_qkv, b_qkv, bias_table, w_proj, ln2_gain, w_fc1, b_fc1, w_fc2
):
    hbm = pl.BlockSpec(memory_space=pl.ANY)
    perm = table_order()
    dma = pltpu.SemaphoreType.DMA
    args = (
        tokens.transpose(1, 2, 0, 3), cotangent.transpose(1, 2, 0, 3), ln1_gain, w_qkv, b_qkv,
        bias_table.transpose(0, 2, 1, 3), w_proj, ln2_gain, w_fc1, b_fc1, w_fc2.T,
        jnp.asarray(perm, BF16), jnp.asarray(cross_pairs()),
    )
    gathered, gathered_att, block, d_tok, table = pl.pallas_call(
        block_kernel,
        out_shape=(
            jax.ShapeDtypeStruct((2, FC, 16, 256), BF16),
            jax.ShapeDtypeStruct((2, ATT, 16, 128), BF16),
            jax.ShapeDtypeStruct((WIN_H, WIN_W, WIN_Z, C), BF16),
            jax.ShapeDtypeStruct((WIN_H, WIN_W, WIN_Z, C), BF16),
            jax.ShapeDtypeStruct((8, 3456), F32),
        ),
        in_specs=[hbm] * len(args),
        out_specs=(hbm,) * 5,
        scratch_shapes=[pltpu.VMEM(a.shape, a.dtype) for a in args[2:]]
        + [
            pltpu.VMEM((2, T, C), F32),
            pltpu.VMEM((2, 4, 3, 6, WIN_Z, C), BF16),
            pltpu.VMEM((2, 4, 3, 6, WIN_Z, C), BF16),
            pltpu.VMEM((8, 3456), F32),
            pltpu.VMEM((1, HEADS, 1, NREL), F32),
            pltpu.VMEM((96, 512), F32),
            pltpu.VMEM((3, 128, 128), F32),
            pltpu.VMEM((HEADS, T, T), F32),
            pltpu.VMEM((HEADS, T, T), F32),
            pltpu.VMEM((T, HEADS * 256), BF16),
            pltpu.VMEM((HEADS * 256, C), BF16),
            pltpu.VMEM((HEADS, 160, 384), F32),
            pltpu.VMEM((3, 128, 128), F32),
            pltpu.VMEM((16, 256), F32),
            pltpu.VMEM((PARTS, 16, 384), BF16),
            pltpu.VMEM((STRIPS, 16, 384), BF16),
            pltpu.VMEM((PARTS, 16, 384), BF16),
            pltpu.VMEM((96, 384), BF16),
            pltpu.VMEM((96, 384), BF16),
            pltpu.VMEM((2, FC, 16, 256), BF16),
            pltpu.VMEM((2, ATT, 16, 128), BF16),
            pltpu.VMEM((ATT, 16, 128), BF16),
            pltpu.VMEM((3, 7, 4, 16, 256), BF16),
            pltpu.VMEM((3, 4, 16, 256), BF16),
            pltpu.VMEM((3, 3, 16, 256), BF16),
            pltpu.VMEM((3, 16, 256), BF16),
            pltpu.VMEM((3, 4, 16, 256), BF16),
            pltpu.VMEM((ROWS - 1, TALL, 16, 128), BF16),
            pltpu.VMEM((TALL, 16, 128), BF16),
            pltpu.VMEM((STRIPS, TALL, 16, 128), BF16),
            pltpu.VMEM((2, FC, 16, 256), BF16),
            pltpu.VMEM((2, ATT, 16, 128), BF16),
            pltpu.VMEM((8, 3456), F32),
            dma((len(args) - 2,)), dma((2,)), dma((7,)),
            dma((2, 3)), dma((2, 3)), dma((2, 3)), dma((2, 3)),
            dma((2,)), dma((2,)), dma((7, 3)), dma((7, 3)),
            dma((5,)), dma((5,)), dma((2,)), dma((2,)),
        ],
        compiler_params=pltpu.CompilerParams(
            collective_id=0, has_side_effects=True, vmem_limit_bytes=VMEM_LIMIT
        ),
    )(*args)
    shape = jax.ShapeDtypeStruct
    grid_shape = (WIN_H, WIN_W, WIN_Z, C)
    results_out = (
        shape(grid_shape, BF16), shape(grid_shape, BF16),
        shape((C,), F32), shape((C, 3 * C), F32), shape((3 * C,), F32),
        shape((1, HEADS, 1, NREL), F32), shape((C, C), F32), shape((C,), F32),
        shape((C, HID), F32), shape((HID,), F32), shape((C, HID), F32),
    )
    outs = pl.pallas_call(
        output_kernel,
        out_shape=results_out,
        in_specs=[hbm] * 5,
        out_specs=(hbm,) * 11,
        scratch_shapes=[
            pltpu.VMEM(a.shape, a.dtype)
            for a in (block, d_tok, gathered, gathered_att, table) + results_out[2:]
        ]
        + [dma((5,)), dma((11,))],
        compiler_params=pltpu.CompilerParams(vmem_limit_bytes=VMEM_LIMIT),
    )(block, d_tok, gathered, gathered_att, table)
    out, d_tok, d_ln1, d_wqkv, d_bqkv, d_bias, d_wproj, d_ln2, d_wfc1, d_bfc1, d_wfc2 = outs
    return (
        out.transpose(2, 0, 1, 3), d_tok.transpose(2, 0, 1, 3), d_ln1, d_wqkv, d_bqkv,
        d_bias.transpose(0, 2, 1, 3), d_wproj, d_ln2, d_wfc1, d_bfc1, d_wfc2.T,
    )


def solution(mesh):
    grid = P(None, "lat", "lon", None)
    rows = P(None, "lat", None, None)
    return jax.shard_map(
        per_device,
        mesh=mesh,
        in_specs=(grid, grid, P(), P(), P(), rows, P(), P(), P(), P(), P()),
        out_specs=(grid, grid, P(), P(), P(), rows, P(), P(), P(), P(), P()),
        check_vma=False,
    )
```

```python
import jax
import jax.numpy as jnp
import numpy as np
from jax import lax
from jax.experimental import pallas as pl
from jax.experimental.pallas import tpu as pltpu
from jax.sharding import PartitionSpec as P

HEADS = 6
WIN_Z = 2
WIN_H = 6
WIN_W = 12
SPAN = 2 * WIN_W - 1
GROUPS = WIN_Z * WIN_H
T = GROUPS * WIN_W
C = 192
HID = 768
HEAD = C // HEADS
NREL = GROUPS * GROUPS * SPAN
FC = 48
ATT = 24
TALL = 3
ROWS = 8
BANDS = 16
STRIPS = 8
PARTS = 6
EPSILON = 1e-05
VMEM_LIMIT = 56 * 1024 * 1024
FACTOR = HEAD ** (-0.5)
LOG2E = 1.4426950408889634
F32 = jnp.float32
BF16 = jnp.bfloat16
MESH = pl.DeviceIdType.MESH


def table_order():
    grid = np.zeros((512, 384), np.float32)
    for z in range(WIN_Z):
        for h in range(WIN_H):
            for i in range(SPAN):
                grid[z * 256 + h * SPAN + i, (SPAN - 1 - i) * GROUPS + h * WIN_Z + z] = 1
    return grid


def cross_pairs():
    g = np.arange(96)[:, None] // 8 // WIN_Z
    q = np.arange(384)[None, :] % GROUPS // WIN_Z
    return np.where((g < 3) != (q < 3), -1e30, 0.0).astype(np.float32)


def dot(a, b):
    return jnp.dot(a, b, preferred_element_type=F32)


def dot_nt(a, b):
    return lax.dot_general(a, b, (((1,), (1,)), ((), ())), preferred_element_type=F32)


def dot_tn(a, b):
    return lax.dot_general(a, b, (((0,), (0,)), ((), ())), preferred_element_type=F32)


def normalize(values, gain):
    average = jnp.mean(values, -1, keepdims=True)
    centered = values - average
    inv = lax.rsqrt(jnp.mean(centered * centered, -1, keepdims=True) + EPSILON)
    hat = centered * inv
    return hat * gain, hat, inv


def norm_back(hat, inv, gain, grad):
    scaled = grad * gain
    return inv * (
        scaled
        - jnp.mean(scaled, -1, keepdims=True)
        - hat * jnp.mean(scaled * hat, -1, keepdims=True)
    )


def pieces():
    for h in range(WIN_H):
        for w in range(WIN_W):
            at = w * GROUPS + h * WIN_Z
            yield (h // 3) * 2 + w // 6, h % 3, w % 6, slice(at, at + WIN_Z)


def quadrant(ref, q):
    return ref.at[pl.ds(q // 2 * 3, 3), pl.ds(q % 2 * 6, 6)]


def block_kernel(
    tok_any, cot_any, g1_any, wqkv_any, bqkv_any, table_any, wproj_any, g2_any, wfc1_any,
    bfc1_any, wfc2_any, perm_any, cross_any,
    gath_fc_out, gath_att_out, block_out, dtok_out, dtab_out,
    g1_ref, wqkv_ref, bqkv_ref, table_ref, wproj_ref, g2_ref, wfc1_ref,
    bfc1_ref, wfc2_ref, perm_ref, cross_ref,
    stage, arrive, out_stage,
    tabw, tab15, tin, ymat, bias, prob, wide_rows, wide_cols, dsc, dmat, vec,
    bsend, brecv, bfin, bbs, bbr,
    parts_fc, parts_att, core_att, fold1, sum1, fold2, sum2, fold3, fold_att, sum_att,
    mid_att, gath_fc, gath_att, dtab_ref,
    in_sem, own_sem, out_sem,
    ex_send, ex_recv, rt_send, rt_recv, one_send, one_recv, f_send, f_recv,
    a_send, a_recv, b_send, b_recv,
):
    sources = (
        (table_any, table_ref), (perm_any, perm_ref), (cross_any, cross_ref), (g1_any, g1_ref),
        (wqkv_any, wqkv_ref), (bqkv_any, bqkv_ref), (wproj_any, wproj_ref), (g2_any, g2_ref),
        (wfc1_any, wfc1_ref), (bfc1_any, bfc1_ref), (wfc2_any, wfc2_ref),
    )
    loads = [pltpu.make_async_copy(src, dst, in_sem.at[n]) for n, (src, dst) in enumerate(sources)]
    lon = lax.axis_index("lon")
    lat = lax.axis_index("lat")
    core = lax.rem(lat, 2)
    other = 1 - core
    pair_row = lat // 2
    east = lax.rem(lon + 1, STRIPS)
    west = lax.rem(lon + STRIPS - 1, STRIPS)
    south = lax.rem(lat + 1, BANDS)
    north = lax.rem(lat + BANDS - 1, BANDS)
    sibling = (lon, lat - core + other)

    spot = (lax.rem(pair_row, 4), lon // 2, lax.rem(lon, 2) * 2 + lat // 8)

    def on_axis(axis, at, side=core):
        if axis == 0:
            return (lon, lat // 8 * 8 + at * 2 + side)
        if axis == 1:
            return (at * 2 + lax.rem(lon, 2), lat - core + side)
        return (spot[1] * 2 + at // 2, lax.rem(at, 2) * 8 + spot[0] * 2 + side)

    def strip(d):
        return lax.rem(lon + d, STRIPS)

    def row_of(d):
        return lax.rem(pair_row + d, ROWS)

    barrier = pltpu.get_barrier_semaphore()

    def greet(target):
        pl.semaphore_signal(barrier, inc=1, device_id=target, device_id_type=MESH)

    for target in ((east, south), (west, north)):
        greet(target)
    for d in range(1, STRIPS):
        greet((strip(d), lat))
    for d in range(1, BANDS):
        greet((lon, lax.rem(lat + d, BANDS)))
    for d in range(1, 4):
        greet(on_axis(1, lax.rem(spot[1] + d, 4), other))
    across = lax.rem(spot[2] + 2, 4)
    greet(on_axis(2, across, other))
    greet(on_axis(2, 3 - spot[2]))
    greet(on_axis(2, 3 - spot[2], other))
    loads[0].start()
    own = [
        pltpu.make_async_copy(quadrant(src, 0), arrive.at[a, 3], own_sem.at[a])
        for a, src in enumerate((tok_any, cot_any))
    ]
    own[0].start()
    pl.semaphore_wait(barrier, 30)

    ahead = ((east, lat), (lon, south), (east, south))
    behind = ((west, lat), (lon, north), (west, north))

    def exchange(a, i):
        return pltpu.make_async_remote_copy(
            src_ref=quadrant((tok_any, cot_any)[a], i + 1),
            dst_ref=arrive.at[a, 2 - i],
            send_sem=ex_send.at[a, i],
            recv_sem=ex_recv.at[a, i],
            device_id=ahead[i],
            device_id_type=MESH,
        )

    def table_copy():
        return pltpu.make_async_remote_copy(
            src_ref=table_any,
            dst_ref=tab15,
            send_sem=one_send.at[0],
            recv_sem=one_recv.at[0],
            device_id=(lon, south),
            device_id_type=MESH,
        )

    @pl.when(lat == BANDS - 1)
    def _():
        table_copy().start()

    for a in range(2):
        for i in range(3):
            exchange(a, i).start()
    for load in loads[1:]:
        load.start()
    own[1].start()

    tabw[...] = jnp.zeros_like(tabw)
    loads[0].wait()
    for head in range(HEADS):
        tabw[head : head + 1, 0:NREL] = table_ref[0, head]

    tin[...] = jnp.zeros_like(tin)
    for ref in (dsc, wide_rows, wide_cols, dmat):
        ref[...] = jnp.zeros_like(ref)

    def spread(src, zp, zq, hp, width):
        j = (zp * WIN_Z + zq) * WIN_H + hp
        first = j * WIN_H * SPAN
        base = first // 128 * 128
        wide = src[:, base : base + 384]
        moved = pltpu.roll(wide, (384 - (first - base)) % 384, axis=1)
        g = hp * WIN_Z + zp
        tin[g * 8 : g * 8 + 8, zq * 256 : zq * 256 + width] = moved[:, :width]

    for zp in range(WIN_Z):
        for zq in range(WIN_Z):
            for hp in range(WIN_H):
                spread(tabw, zp, zq, hp, WIN_H * SPAN)

    def permuted(whole):
        high = whole.astype(BF16)
        rest = whole - high.astype(F32)
        middle = rest.astype(BF16)
        low = (rest - middle.astype(F32)).astype(BF16)
        count = whole.shape[0]
        terms = dot(jnp.concatenate([high, middle, low], 0), perm_ref[...])
        return (terms[:count] + terms[count : 2 * count] + terms[2 * count :]) * LOG2E

    loads[1].wait()
    spread_rows = permuted(tin[...])
    for n in range(3):
        ymat[n, 0:96, :] = spread_rows[:, 128 * n : 128 * (n + 1)]
        ymat[n, 96:128, :] = jnp.zeros((32, 128), F32)
    loads[2].wait()

    @pl.when(lat == 0)
    def _():
        for n in range(3):
            ymat[n, 0:96, :] = ymat[n, 0:96, :] + cross_ref[:, 128 * n : 128 * (n + 1)]

    def place_bias(tall, count):
        for head in range(HEADS):
            rows = jnp.concatenate(
                [ymat[n, pl.ds(head, tall, stride=8), :] for n in range(3)], -1
            )
            for w in range(WIN_W):
                moved = pltpu.roll(rows, (384 - (WIN_W - 1 - w) * GROUPS) % 384, axis=1)
                bias[head, w * GROUPS : w * GROUPS + count, :] = moved[:count, :T]

    place_bias(16, GROUPS)
    for n in range(3, 11):
        loads[n].wait()
    lane = lax.broadcasted_iota(jnp.int32, (16, C), 1)
    ones = [
        jnp.where((lane >= HEAD * i) & (lane < HEAD * (i + 1)), 1.0, 0.0).astype(BF16)[0:1]
        for i in range(HEADS)
    ]
    gain1 = g1_ref[...].reshape(1, C)
    gain2 = g2_ref[...].reshape(1, C)

    def arrived(a):
        for i in range(3):
            exchange(a, i).wait_recv()
        own[a].wait()
        for slot, row, col, rows in pieces():
            stage[a, rows, :] = arrive[a, slot, row, col].astype(F32)
        return stage[a]

    tokens = arrived(0)
    normed, hat1, inv1 = normalize(tokens, gain1)
    first = normed.astype(BF16)
    qkv = (dot(first, wqkv_ref[...]) + bqkv_ref[...].reshape(1, 3 * C)).astype(BF16)
    queries = qkv[:, 0:C]
    keys = qkv[:, C : 2 * C]
    values = qkv[:, 2 * C : 3 * C]
    queries_t = queries.T

    @pl.when(lat == 0)
    def _():
        table_copy().wait_recv()
        for head in range(HEADS):
            tabw[head : head + 1, 0:NREL] = tab15[0, head]
        tin[0:48, :] = jnp.zeros((48, 512), F32)
        for zp in range(WIN_Z):
            for zq in range(WIN_Z):
                for hp in range(3):
                    spread(tabw, zp, zq, hp, 3 * SPAN)
        upper_rows = permuted(tin[0:48, :]) + cross_ref[0:48, :]
        for n in range(3):
            ymat[n, 0:48, :] = upper_rows[:, 128 * n : 128 * (n + 1)]
        place_bias(8, 6)

    cot = arrived(1)
    cot_low = cot.astype(BF16)
    cot_t = cot_low.T

    for head in range(HEADS):
        wide_cols[256 * head : 256 * head + T, :] = values * ones[head]
    for head in range(HEADS):
        q = queries * ones[head]
        scores = dot_nt(q, keys) * (FACTOR * LOG2E) + bias[head]
        top = jnp.max(scores, -1, keepdims=True)
        raised = jnp.exp2(scores - top)
        probs = raised * (1.0 / jnp.sum(raised, -1, keepdims=True))
        prob[head] = probs
        probs_low = probs.astype(BF16)
        wide_rows[:, 256 * head : 256 * head + T] = probs_low
    mixed = dot(wide_rows[...], wide_cols[...]).astype(BF16)
    inner = tokens + dot(mixed, wproj_ref[...]).astype(BF16).astype(F32)

    def remote(src, dst, send_sem, recv_sem, target):
        return pltpu.make_async_remote_copy(
            src_ref=src, dst_ref=dst, send_sem=send_sem, recv_sem=recv_sem,
            device_id=target, device_id_type=MESH,
        )

    def wait_bytes(ref, sem):
        pltpu.make_async_copy(ref, ref, sem).wait()

    def add(*terms):
        total = terms[0].astype(F32)
        for term in terms[1:]:
            total = total + term.astype(F32)
        return total.astype(BF16)

    axes = [(n, (n + 1) % 3, (n + 2) % 3) for n in range(3)]
    places = [tuple(spot[axis] for axis in order) for order in axes]

    def block(n, i):
        return pl.ds(n * 16 + i * 4, 4)

    def unit(n):
        return n * 16 + places[n][0] * 4 + places[n][1]

    def part_to_line(n, stage_no, which, src, dst):
        for d in range(1, 4):
            at = lax.rem(places[n][which] + d, 4)
            remote(
                src(n, at), dst(n, d), f_send.at[stage_no, n], f_recv.at[stage_no, n],
                on_axis(axes[n][which], at),
            ).start()

    def third(n):
        return pl.ds(16 * n, 16)

    swap_fc = [
        remote(
            gath_fc.at[core, third(n)], gath_fc_out.at[core, third(n)],
            f_send.at[6, n], f_recv.at[6, n], sibling,
        )
        for n in range(3)
    ]
    pair_att = remote(parts_att.at[other], core_att, a_send.at[0], a_recv.at[0], sibling)
    swap_att = remote(
        gath_att.at[core], gath_att_out.at[core], a_send.at[4], a_recv.at[4], sibling
    )
    kept = [
        (out_stage.at[0, 3], quadrant(block_out, 0)),
        (out_stage.at[1, 3], quadrant(dtok_out, 0)),
        (dtab_ref, dtab_out),
        (gath_att.at[core], gath_att_out.at[core]),
    ] + [(gath_fc.at[core, third(n)], gath_fc_out.at[core, third(n)]) for n in range(3)]
    keep = [
        pltpu.make_async_copy(src, dst, out_sem.at[n]) for n, (src, dst) in enumerate(kept)
    ]

    def early1(n):
        for side, first, slot in ((core, 1, -1), (other, 0, 3)):
            for d in range(first, 4):
                at = lax.rem(places[n][0] + d, 4)
                remote(
                    parts_fc.at[side, block(n, at)], fold1.at[n, slot + d],
                    f_send.at[1, n], f_recv.at[1, n], on_axis(n, at, side),
                ).start()

    def early2():
        for n in range(3):
            wait_bytes(fold1.at[n], f_recv.at[1, n])
            own_block = parts_fc[core, block(n, places[n][0])]
            sum1[n] = add(own_block, *[fold1[n, i] for i in range(7)])
            part_to_line(
                n, 2, 1, lambda n, at: sum1.at[n, at], lambda n, d: fold2.at[n, d - 1]
            )

    def early3():
        for n in range(3):
            wait_bytes(fold2.at[n], f_recv.at[2, n])
            own_unit = sum1[n, places[n][1]]
            sum2[n] = add(own_unit, fold2[n, 0], fold2[n, 1], fold2[n, 2])
            fold3[n, places[n][2]] = sum2[n]
            part_to_line(
                n, 3, 2, lambda n, at: sum2.at[n], lambda n, d: fold3.at[n, places[n][2]]
            )

    def early4():
        for n in range(3):
            wait_bytes(fold2.at[n], f_recv.at[3, n])
            gath_fc[core, unit(n)] = add(*[fold3[n, i] for i in range(4)])
            part_to_line(
                n, 4, 1, lambda n, at: gath_fc.at[core, unit(n)],
                lambda n, d: gath_fc.at[core, unit(n)],
            )

    def early5():
        for n in range(3):
            wait_bytes(fold2.at[n], f_recv.at[4, n])
            part_to_line(
                n, 5, 0, lambda n, at: gath_fc.at[core, block(n, places[n][0])],
                lambda n, d: gath_fc.at[core, block(n, places[n][0])],
            )

    def early6():
        for n in range(3):
            wait_bytes(fold1.at[n, pl.ds(0, 3)], f_recv.at[5, n])
            swap_fc[n].start()
            keep[4 + n].start()

    own_rows = pl.ds(pair_row * TALL, TALL)

    def late1():
        pair_att.wait_recv()
        parts_att[core] = add(parts_att[core], core_att[...])
        for d in range(1, ROWS):
            remote(
                parts_att.at[core, pl.ds(row_of(d) * TALL, TALL)], fold_att.at[d - 1],
                a_send.at[1], a_recv.at[1], (lon, row_of(d) * 2 + core),
            ).start()

    def late2():
        wait_bytes(fold_att, a_recv.at[1])
        sum_att[...] = add(parts_att[core, own_rows], *[fold_att[d] for d in range(ROWS - 1)])
        mid_att[lon] = sum_att[...]
        for d in range(1, STRIPS):
            remote(
                sum_att, mid_att.at[lon], a_send.at[2], a_recv.at[2], (strip(d), lat)
            ).start()

    def late3():
        wait_bytes(fold_att, a_recv.at[2])
        gath_att[core, own_rows] = add(*[mid_att[i] for i in range(STRIPS)])
        for d in range(1, ROWS):
            remote(
                gath_att.at[core, own_rows], gath_att.at[core, own_rows],
                a_send.at[3], a_recv.at[3], (lon, row_of(d) * 2 + core),
            ).start()

    def late4():
        wait_bytes(fold_att, a_recv.at[3])
        swap_att.start()
        keep[3].start()

    normed, hat2, inv2 = normalize(inner, gain2)
    second = normed.astype(BF16)
    second_t = second.T
    total = inner
    grad_second = jnp.zeros((T, C), F32)
    bfc1 = bfc1_ref[...].reshape(1, HID)
    vec[...] = jnp.zeros_like(vec)
    for n in range(3):
        cols = slice(256 * n, 256 * (n + 1))
        pre = dot(second, wfc1_ref[:, cols]) + bfc1[:, cols]
        cdf = 0.5 * (1.0 + lax.erf(pre * 0.7071067811865476))
        density = jnp.exp(-0.5 * pre * pre) * 0.3989422804014327
        act = (pre * cdf).astype(BF16)
        total = total + dot_nt(act, wfc2_ref[:, cols])
        grad_pre = (dot(cot_low, wfc2_ref[:, cols]) * (cdf + pre * density)).astype(BF16)
        grad_second = grad_second + dot_nt(grad_pre, wfc1_ref[:, cols])
        parts_fc[0, 12 * n : 12 * (n + 1)] = dot(second_t, grad_pre).astype(BF16).reshape(12, 16, 256)
        parts_fc[1, 12 * n : 12 * (n + 1)] = dot(cot_t, act).astype(BF16).reshape(12, 16, 256)
        vec[n : n + 1, :] = jnp.sum(grad_pre.astype(F32), 0, keepdims=True)
        if n:
            early1(n - 1)

    def give_back(a, i):
        return pltpu.make_async_remote_copy(
            src_ref=out_stage.at[a, 2 - i],
            dst_ref=quadrant((block_out, dtok_out)[a], i + 1),
            send_sem=rt_send.at[a, i],
            recv_sem=rt_recv.at[a, i],
            device_id=behind[i],
            device_id_type=MESH,
        )

    def hand_out(a):
        for slot, row, col, rows in pieces():
            out_stage[a, slot, row, col] = stage[a, rows, :].astype(BF16)
        for i in range(3):
            give_back(a, i).start()
        keep[a].start()

    grad_inner = cot + norm_back(hat2, inv2, gain2, grad_second)
    grad_att = grad_inner.astype(BF16)
    stage[0] = total
    grad_mixed = dot_nt(grad_att, wproj_ref[...]).astype(BF16)
    grad_mixed_t = grad_mixed.T
    grad_v_t = [
        dot(
            grad_mixed_t[HEAD * head : HEAD * (head + 1)],
            wide_rows[:, 256 * head : 256 * head + T],
        )
        for head in range(HEADS)
    ]
    grad_v = jnp.concatenate(grad_v_t, 0).T.astype(BF16)
    first_t = first.T
    value_grad = dot(first_t, grad_v).astype(BF16)
    proj_grad = dot_tn(mixed, grad_att).astype(BF16)
    last = value_grad[176:C]
    last = jnp.concatenate(
        [last[:, 0:64], last[:, 64:128], last[:, 128:C], jnp.zeros((144, 64), BF16)], 0
    )
    proj_grad = jnp.concatenate([proj_grad, last], -1).reshape(12, 16, 256)
    value_grad = jnp.concatenate([value_grad, jnp.zeros((C, 64), BF16)], -1).reshape(12, 16, 256)
    parts_fc[0, 36:42] = proj_grad[:6]
    parts_fc[1, 36:42] = proj_grad[6:]
    parts_fc[0, 43:48] = value_grad[0:5]
    parts_fc[1, 42:48] = value_grad[5:11]
    vec[3:4, 0:C] = jnp.sum(grad_second * hat2, 0, keepdims=True)
    vec[4:5, 0:C] = jnp.sum(grad_v.astype(F32), 0, keepdims=True)
    parts_fc[0, 42] = vec[...].astype(BF16)
    early1(2)

    for head in range(HEADS):
        wide_cols[256 * head : 256 * head + T, :] = keys * ones[head]
    grad_k_t = []
    for head in range(HEADS):
        rows = slice(HEAD * head, HEAD * (head + 1))
        gm = grad_mixed * ones[head]
        probs = prob[head]
        grad_probs = dot_nt(gm, values)
        inside = jnp.sum(probs * grad_probs, -1, keepdims=True)
        grad_scores = probs * (grad_probs - inside)
        dsc[head, 0:T, 0:T] = grad_scores
        scaled = (grad_scores * FACTOR).astype(BF16)
        wide_rows[:, 256 * head : 256 * head + T] = scaled
        grad_k_t.append(dot(queries_t[rows], scaled))
    grad_q = dot(wide_rows[...], wide_cols[...])
    grad_k = jnp.concatenate(grad_k_t, 0).T

    grad_qk = jnp.concatenate([grad_q, grad_k], -1).astype(BF16)
    wide = dot(first_t, grad_qk).astype(BF16)
    wide = [wide[:, 128 * n : 128 * (n + 1)].reshape(12, 16, 128) for n in range(3)]
    parts_att[0, 0:12] = wide[0]
    parts_att[0, 12:18] = wide[1][:6]
    parts_att[1, 0:6] = wide[1][6:]
    parts_att[1, 6:18] = wide[2]
    grad_first = dot_nt(grad_qk, wqkv_ref[:, 0 : 2 * C])
    grad_first = grad_first + dot_nt(grad_v, wqkv_ref[:, 2 * C : 3 * C])
    grad_first = grad_first.astype(BF16).astype(F32)
    vec[...] = jnp.zeros_like(vec)
    sums = jnp.sum(grad_qk.astype(F32), 0, keepdims=True)
    sums = [sums[:, C * n : C * (n + 1)] for n in range(2)]
    sums.append(jnp.sum(grad_first * hat1, 0, keepdims=True))
    for n in range(3):
        vec[2 * n : 2 * n + 1, 0:128] = sums[n][:, 0:128]
        vec[2 * n + 1 : 2 * n + 2, 0:64] = sums[n][:, 128:C]
    parts_att[0, 18] = vec[:, 0:128].astype(BF16)
    parts_att[1, 18] = jnp.zeros((16, 128), BF16)
    parts_att[:, 19:] = jnp.zeros((2, ATT - 19, 16, 128), BF16)
    pair_att.start()
    d_tokens = grad_inner + norm_back(hat1, inv1, gain1, grad_first)
    stage[1] = d_tokens
    hand_out(1)
    hand_out(0)

    for head in range(HEADS):
        if head == 3:
            late1()
            early2()
        acc = jnp.zeros((16, 384), F32)
        for w in range(WIN_W):
            acc = acc + pltpu.roll(
                dsc[head, w * GROUPS : w * GROUPS + 16, :], (WIN_W - 1 - w) * GROUPS, axis=1
            )
        for n in range(3):
            dmat[n, pl.ds(head, 16, stride=8), :] = acc[:, 128 * n : 128 * (n + 1)]

    def table_grad():
        return jnp.concatenate([dmat[n, 0:96, :] for n in range(3)], -1)

    def keep_table(field):
        for n in range(3):
            dmat[n, 0:96, :] = field[:, 128 * n : 128 * (n + 1)]

    def edge_copy():
        return pltpu.make_async_remote_copy(
            src_ref=bbs,
            dst_ref=bbr,
            send_sem=one_send.at[1],
            recv_sem=one_recv.at[1],
            device_id=(lon, north),
            device_id_type=MESH,
        )

    @pl.when(lat == 0)
    def _():
        upper = lax.broadcasted_iota(jnp.int32, (96, 384), 0) < 48
        full = table_grad()
        bbs[...] = jnp.where(upper, full, 0.0).astype(BF16)
        edge_copy().start()
        keep_table(jnp.where(upper, 0.0, full))

    late2()
    early3()

    @pl.when(lat == BANDS - 1)
    def _():
        edge_copy().wait_recv()
        keep_table(table_grad() + bbr[...].astype(F32))

    bsend[...] = table_grad().astype(BF16).reshape(PARTS, 16, 384)

    for owner in range(PARTS):
        @pl.when(lon != owner)
        def _():
            pltpu.make_async_remote_copy(
                src_ref=bsend.at[owner],
                dst_ref=brecv.at[lon],
                send_sem=b_send.at[0],
                recv_sem=b_recv.at[0],
                device_id=(owner, lat),
                device_id_type=MESH,
            ).start()

    early4()
    late3()
    early5()
    seven = brecv.at[pl.ds(0, STRIPS - 1)]

    @pl.when(lon < PARTS)
    def _():
        brecv[lon] = bsend[lon]
        wait_bytes(seven, b_recv.at[0])
        bfin[lon] = jnp.sum(brecv[...].astype(F32), 0).astype(BF16)
        for d in range(1, STRIPS):
            pltpu.make_async_remote_copy(
                src_ref=bfin.at[lon],
                dst_ref=bfin.at[lon],
                send_sem=b_send.at[1],
                recv_sem=b_recv.at[1],
                device_id=(strip(d), lat),
                device_id_type=MESH,
            ).start()

    late4()
    early6()

    @pl.when(lon < PARTS)
    def _():
        wait_bytes(bfin.at[pl.ds(0, PARTS - 1)], b_recv.at[1])

    @pl.when(lon >= PARTS)
    def _():
        wait_bytes(bfin, b_recv.at[1])

    tin[...] = dot_nt(bfin[...].reshape(96, 384), perm_ref[...])
    dtab_ref[...] = jnp.zeros_like(dtab_ref)
    for zp in range(WIN_Z):
        for zq in range(WIN_Z):
            for hp in range(WIN_H):
                j = (zp * WIN_Z + zq) * WIN_H + hp
                first_lane = j * WIN_H * SPAN
                base = first_lane // 128 * 128
                g = hp * WIN_Z + zp
                piece = tin[g * 8 : g * 8 + 8, zq * 256 : zq * 256 + 256]
                piece = jnp.concatenate([piece, jnp.zeros((8, 128), F32)], -1)
                moved = pltpu.roll(piece, first_lane - base, axis=1)
                dtab_ref[:, base : base + 384] = dtab_ref[:, base : base + 384] + moved

    keep[2].start()

    for a in range(2):
        for i in range(3):
            exchange(a, i).wait_send()
            give_back(a, i).wait()

    @pl.when(lat == BANDS - 1)
    def _():
        table_copy().wait_send()

    @pl.when(lat == 0)
    def _():
        edge_copy().wait_send()

    for n in range(3):
        wait_bytes(fold1.at[n], f_send.at[1, n])
        for stage_no in (2, 3, 4):
            wait_bytes(fold2.at[n], f_send.at[stage_no, n])
        wait_bytes(fold1.at[n, pl.ds(0, 3)], f_send.at[5, n])
    pair_att.wait_send()
    for stage_no in (1, 2, 3):
        wait_bytes(fold_att, a_send.at[stage_no])

    @pl.when(lon < PARTS)
    def _():
        wait_bytes(bsend.at[pl.ds(0, PARTS - 1)], b_send.at[0])
        wait_bytes(seven, b_send.at[1])

    @pl.when(lon >= PARTS)
    def _():
        wait_bytes(bsend, b_send.at[0])

    for copy in keep:
        copy.wait()
    for copy in swap_fc:
        copy.wait()
    swap_att.wait()


def output_kernel(*refs):
    ins, outs = refs[:5], refs[5:16]
    in_bufs, out_bufs = refs[16:21], refs[21:30]
    in_sem, out_sem = refs[30:]
    loads = [
        pltpu.make_async_copy(src, dst, in_sem.at[n])
        for n, (src, dst) in enumerate(zip(ins, in_bufs))
    ]
    stores = [
        pltpu.make_async_copy(src, dst, out_sem.at[n])
        for n, (src, dst) in enumerate(zip(in_bufs[:2] + out_bufs, outs))
    ]
    gath_ref, gath_att, dtab_ref = in_bufs[2:]
    (
        dln1_ref, dwqkv_ref, dbqkv_ref, dbias_ref, dwproj_ref, dln2_ref,
        dwfc1_ref, dbfc1_ref, dwfc2_ref,
    ) = out_bufs
    for n in (2, 0, 1, 3, 4):
        loads[n].start()
    loads[2].wait()
    for n in range(3):
        cols = slice(256 * n, 256 * (n + 1))
        rows = slice(12 * n, 12 * (n + 1))
        dwfc1_ref[:, cols] = gath_ref[0, rows].reshape(C, 256).astype(F32)
    stores[8].start()
    for n in range(3):
        cols = slice(256 * n, 256 * (n + 1))
        rows = slice(12 * n, 12 * (n + 1))
        dwfc2_ref[:, cols] = gath_ref[1, rows].reshape(C, 256).astype(F32)
    stores[10].start()
    for k in range(2):
        dwproj_ref[96 * k : 96 * (k + 1), :] = (
            gath_ref[k, 36:42].reshape(96, 256)[:, 0:C].astype(F32)
        )
    vec = gath_ref[0, 42].astype(F32)
    dbfc1_ref[...] = jnp.concatenate([vec[n : n + 1] for n in range(3)], -1).reshape(HID)
    dln2_ref[...] = vec[3:4, :C].reshape(C)
    for n in (6, 9, 7):
        stores[n].start()
    for n in range(2):
        loads[n].wait()
        stores[n].start()
    loads[3].wait()
    dwqkv_ref[:, 0:128] = gath_att[0, 0:12].reshape(C, 128).astype(F32)
    dwqkv_ref[0:96, 128:256] = gath_att[0, 12:18].reshape(96, 128).astype(F32)
    dwqkv_ref[96:C, 128:256] = gath_att[1, 0:6].reshape(96, 128).astype(F32)
    dwqkv_ref[:, 256:384] = gath_att[1, 6:18].reshape(C, 128).astype(F32)
    dwqkv_ref[0:80, 384:576] = gath_ref[0, 43:48].reshape(80, 256)[:, 0:C].astype(F32)
    dwqkv_ref[80:176, 384:576] = gath_ref[1, 42:48].reshape(96, 256)[:, 0:C].astype(F32)
    last = [gath_ref[0, 36 + n][:, C:256].astype(F32) for n in range(3)]
    dwqkv_ref[176:C, 384:576] = jnp.concatenate(last, -1)
    value_bias = vec[4:5, :C]
    vec = gath_att[0, 18].astype(F32)
    sums = [
        jnp.concatenate([vec[2 * n : 2 * n + 1], vec[2 * n + 1 : 2 * n + 2, :64]], -1)
        for n in range(3)
    ]
    dbqkv_ref[...] = jnp.concatenate(sums[:2] + [value_bias], -1).reshape(3 * C)
    dln1_ref[...] = sums[2].reshape(C)
    for n in (3, 4, 2):
        stores[n].start()
    loads[4].wait()
    for head in range(HEADS):
        dbias_ref[0, head] = dtab_ref[head : head + 1, 0:NREL]
    stores[5].start()
    for store in stores:
        store.wait()


def per_device(
    tokens, cotangent, ln1_gain, w_qkv, b_qkv, bias_table, w_proj, ln2_gain, w_fc1, b_fc1, w_fc2
):
    hbm = pl.BlockSpec(memory_space=pl.ANY)
    perm = table_order()
    dma = pltpu.SemaphoreType.DMA
    args = (
        tokens.transpose(1, 2, 0, 3), cotangent.transpose(1, 2, 0, 3), ln1_gain, w_qkv, b_qkv,
        bias_table.transpose(0, 2, 1, 3), w_proj, ln2_gain, w_fc1, b_fc1, w_fc2.T,
        jnp.asarray(perm, BF16), jnp.asarray(cross_pairs()),
    )
    gathered, gathered_att, block, d_tok, table = pl.pallas_call(
        block_kernel,
        out_shape=(
            jax.ShapeDtypeStruct((2, FC, 16, 256), BF16),
            jax.ShapeDtypeStruct((2, ATT, 16, 128), BF16),
            jax.ShapeDtypeStruct((WIN_H, WIN_W, WIN_Z, C), BF16),
            jax.ShapeDtypeStruct((WIN_H, WIN_W, WIN_Z, C), BF16),
            jax.ShapeDtypeStruct((8, 3456), F32),
        ),
        in_specs=[hbm] * len(args),
        out_specs=(hbm,) * 5,
        scratch_shapes=[pltpu.VMEM(a.shape, a.dtype) for a in args[2:]]
        + [
            pltpu.VMEM((2, T, C), F32),
            pltpu.VMEM((2, 4, 3, 6, WIN_Z, C), BF16),
            pltpu.VMEM((2, 4, 3, 6, WIN_Z, C), BF16),
            pltpu.VMEM((8, 3456), F32),
            pltpu.VMEM((1, HEADS, 1, NREL), F32),
            pltpu.VMEM((96, 512), F32),
            pltpu.VMEM((3, 128, 128), F32),
            pltpu.VMEM((HEADS, T, T), F32),
            pltpu.VMEM((HEADS, T, T), F32),
            pltpu.VMEM((T, HEADS * 256), BF16),
            pltpu.VMEM((HEADS * 256, C), BF16),
            pltpu.VMEM((HEADS, 160, 384), F32),
            pltpu.VMEM((3, 128, 128), F32),
            pltpu.VMEM((16, 256), F32),
            pltpu.VMEM((PARTS, 16, 384), BF16),
            pltpu.VMEM((STRIPS, 16, 384), BF16),
            pltpu.VMEM((PARTS, 16, 384), BF16),
            pltpu.VMEM((96, 384), BF16),
            pltpu.VMEM((96, 384), BF16),
            pltpu.VMEM((2, FC, 16, 256), BF16),
            pltpu.VMEM((2, ATT, 16, 128), BF16),
            pltpu.VMEM((ATT, 16, 128), BF16),
            pltpu.VMEM((3, 7, 4, 16, 256), BF16),
            pltpu.VMEM((3, 4, 16, 256), BF16),
            pltpu.VMEM((3, 3, 16, 256), BF16),
            pltpu.VMEM((3, 16, 256), BF16),
            pltpu.VMEM((3, 4, 16, 256), BF16),
            pltpu.VMEM((ROWS - 1, TALL, 16, 128), BF16),
            pltpu.VMEM((TALL, 16, 128), BF16),
            pltpu.VMEM((STRIPS, TALL, 16, 128), BF16),
            pltpu.VMEM((2, FC, 16, 256), BF16),
            pltpu.VMEM((2, ATT, 16, 128), BF16),
            pltpu.VMEM((8, 3456), F32),
            dma((len(args) - 2,)), dma((2,)), dma((7,)),
            dma((2, 3)), dma((2, 3)), dma((2, 3)), dma((2, 3)),
            dma((2,)), dma((2,)), dma((7, 3)), dma((7, 3)),
            dma((5,)), dma((5,)), dma((2,)), dma((2,)),
        ],
        compiler_params=pltpu.CompilerParams(
            collective_id=0, has_side_effects=True, vmem_limit_bytes=VMEM_LIMIT
        ),
    )(*args)
    shape = jax.ShapeDtypeStruct
    grid_shape = (WIN_H, WIN_W, WIN_Z, C)
    results_out = (
        shape(grid_shape, BF16), shape(grid_shape, BF16),
        shape((C,), F32), shape((C, 3 * C), F32), shape((3 * C,), F32),
        shape((1, HEADS, 1, NREL), F32), shape((C, C), F32), shape((C,), F32),
        shape((C, HID), F32), shape((HID,), F32), shape((C, HID), F32),
    )
    outs = pl.pallas_call(
        output_kernel,
        out_shape=results_out,
        in_specs=[hbm] * 5,
        out_specs=(hbm,) * 11,
        scratch_shapes=[
            pltpu.VMEM(a.shape, a.dtype)
            for a in (block, d_tok, gathered, gathered_att, table) + results_out[2:]
        ]
        + [dma((5,)), dma((11,))],
        compiler_params=pltpu.CompilerParams(vmem_limit_bytes=VMEM_LIMIT),
    )(block, d_tok, gathered, gathered_att, table)
    out, d_tok, d_ln1, d_wqkv, d_bqkv, d_bias, d_wproj, d_ln2, d_wfc1, d_bfc1, d_wfc2 = outs
    return (
        out.transpose(2, 0, 1, 3), d_tok.transpose(2, 0, 1, 3), d_ln1, d_wqkv, d_bqkv,
        d_bias.transpose(0, 2, 1, 3), d_wproj, d_ln2, d_wfc1, d_bfc1, d_wfc2.T,
    )


def solution(mesh):
    grid = P(None, "lat", "lon", None)
    rows = P(None, "lat", None, None)
    return jax.shard_map(
        per_device,
        mesh=mesh,
        in_specs=(grid, grid, P(), P(), P(), rows, P(), P(), P(), P(), P()),
        out_specs=(grid, grid, P(), P(), P(), rows, P(), P(), P(), P(), P()),
        check_vma=False,
    )
```

```python
import jax
import jax.numpy as jnp
import numpy as np
from jax import lax
from jax.experimental import pallas as pl
from jax.experimental.pallas import tpu as pltpu
from jax.sharding import PartitionSpec as P

HEADS = 6
WIN_Z = 2
WIN_H = 6
WIN_W = 12
SPAN = 2 * WIN_W - 1
GROUPS = WIN_Z * WIN_H
T = GROUPS * WIN_W
C = 192
HID = 768
HEAD = C // HEADS
NREL = GROUPS * GROUPS * SPAN
FC = 48
ATT = 24
TALL = 3
ROWS = 8
BANDS = 16
STRIPS = 8
PARTS = 6
EPSILON = 1e-05
VMEM_LIMIT = 56 * 1024 * 1024
FACTOR = HEAD ** (-0.5)
LOG2E = 1.4426950408889634
F32 = jnp.float32
BF16 = jnp.bfloat16
MESH = pl.DeviceIdType.MESH


def table_order():
    grid = np.zeros((512, 384), np.float32)
    for z in range(WIN_Z):
        for h in range(WIN_H):
            for i in range(SPAN):
                grid[z * 256 + h * SPAN + i, (SPAN - 1 - i) * GROUPS + h * WIN_Z + z] = 1
    return grid


def cross_pairs():
    g = np.arange(96)[:, None] // 8 // WIN_Z
    q = np.arange(384)[None, :] % GROUPS // WIN_Z
    return np.where((g < 3) != (q < 3), -1e30, 0.0).astype(np.float32)


def dot(a, b):
    return jnp.dot(a, b, preferred_element_type=F32)


def dot_nt(a, b):
    return lax.dot_general(a, b, (((1,), (1,)), ((), ())), preferred_element_type=F32)


def dot_tn(a, b):
    return lax.dot_general(a, b, (((0,), (0,)), ((), ())), preferred_element_type=F32)


def normalize(values, gain):
    average = jnp.mean(values, -1, keepdims=True)
    centered = values - average
    inv = lax.rsqrt(jnp.mean(centered * centered, -1, keepdims=True) + EPSILON)
    hat = centered * inv
    return hat * gain, hat, inv


def norm_back(hat, inv, gain, grad):
    scaled = grad * gain
    return inv * (
        scaled
        - jnp.mean(scaled, -1, keepdims=True)
        - hat * jnp.mean(scaled * hat, -1, keepdims=True)
    )


def pieces():
    for h in range(WIN_H):
        for w in range(WIN_W):
            at = w * GROUPS + h * WIN_Z
            yield (h // 3) * 2 + w // 6, h % 3, w % 6, slice(at, at + WIN_Z)


def quadrant(ref, q):
    return ref.at[pl.ds(q // 2 * 3, 3), pl.ds(q % 2 * 6, 6)]


def block_kernel(
    tok_any, cot_any, g1_any, wqkv_any, bqkv_any, table_any, wproj_any, g2_any, wfc1_any,
    bfc1_any, wfc2_any, perm_any, cross_any,
    gath_fc_out, gath_att_out, block_out, dtok_out, dtab_out,
    g1_ref, wqkv_ref, bqkv_ref, table_ref, wproj_ref, g2_ref, wfc1_ref,
    bfc1_ref, wfc2_ref, perm_ref, cross_ref,
    stage, arrive, out_stage,
    tabw, tab15, tin, ymat, bias, prob, wide_rows, wide_cols, dsc, dmat, vec,
    bsend, brecv, bfin, bbs, bbr,
    parts_fc, parts_att, core_att, fold1, sum1, fold2, sum2, fold3, fold_att, sum_att,
    mid_att, gath_fc, gath_att, dtab_ref,
    in_sem, own_sem, out_sem,
    ex_send, ex_recv, rt_send, rt_recv, one_send, one_recv, f_send, f_recv,
    a_send, a_recv, b_send, b_recv,
):
    sources = (
        (table_any, table_ref), (perm_any, perm_ref), (cross_any, cross_ref), (g1_any, g1_ref),
        (wqkv_any, wqkv_ref), (bqkv_any, bqkv_ref), (wproj_any, wproj_ref), (g2_any, g2_ref),
        (wfc1_any, wfc1_ref), (bfc1_any, bfc1_ref), (wfc2_any, wfc2_ref),
    )
    loads = [pltpu.make_async_copy(src, dst, in_sem.at[n]) for n, (src, dst) in enumerate(sources)]
    lon = lax.axis_index("lon")
    lat = lax.axis_index("lat")
    core = lax.rem(lat, 2)
    other = 1 - core
    pair_row = lat // 2
    east = lax.rem(lon + 1, STRIPS)
    west = lax.rem(lon + STRIPS - 1, STRIPS)
    south = lax.rem(lat + 1, BANDS)
    north = lax.rem(lat + BANDS - 1, BANDS)
    sibling = (lon, lat - core + other)

    spot = (lax.rem(pair_row, 4), lon // 2, lax.rem(lon, 2) * 2 + lat // 8)

    def on_axis(axis, at, side=core):
        if axis == 0:
            return (lon, lat // 8 * 8 + at * 2 + side)
        if axis == 1:
            return (at * 2 + lax.rem(lon, 2), lat - core + side)
        return (spot[1] * 2 + at // 2, lax.rem(at, 2) * 8 + spot[0] * 2 + side)

    def strip(d):
        return lax.rem(lon + d, STRIPS)

    def row_of(d):
        return lax.rem(pair_row + d, ROWS)

    barrier = pltpu.get_barrier_semaphore()

    def greet(target):
        pl.semaphore_signal(barrier, inc=1, device_id=target, device_id_type=MESH)

    for target in ((east, south), (west, north)):
        greet(target)
    for d in range(1, STRIPS):
        greet((strip(d), lat))
    for d in range(1, BANDS):
        greet((lon, lax.rem(lat + d, BANDS)))
    for d in range(1, 4):
        greet(on_axis(1, lax.rem(spot[1] + d, 4), other))
    across = lax.rem(spot[2] + 2, 4)
    greet(on_axis(2, across, other))
    greet(on_axis(2, 3 - spot[2]))
    greet(on_axis(2, 3 - spot[2], other))
    loads[0].start()
    own = [
        pltpu.make_async_copy(quadrant(src, 0), arrive.at[a, 3], own_sem.at[a])
        for a, src in enumerate((tok_any, cot_any))
    ]
    own[0].start()
    pl.semaphore_wait(barrier, 30)

    ahead = ((east, lat), (lon, south), (east, south))
    behind = ((west, lat), (lon, north), (west, north))

    def exchange(a, i):
        return pltpu.make_async_remote_copy(
            src_ref=quadrant((tok_any, cot_any)[a], i + 1),
            dst_ref=arrive.at[a, 2 - i],
            send_sem=ex_send.at[a, i],
            recv_sem=ex_recv.at[a, i],
            device_id=ahead[i],
            device_id_type=MESH,
        )

    def table_copy():
        return pltpu.make_async_remote_copy(
            src_ref=table_any,
            dst_ref=tab15,
            send_sem=one_send.at[0],
            recv_sem=one_recv.at[0],
            device_id=(lon, south),
            device_id_type=MESH,
        )

    @pl.when(lat == BANDS - 1)
    def _():
        table_copy().start()

    for a in range(2):
        for i in range(3):
            exchange(a, i).start()
    for load in loads[1:]:
        load.start()
    own[1].start()

    tabw[...] = jnp.zeros_like(tabw)
    loads[0].wait()
    for head in range(HEADS):
        tabw[head : head + 1, 0:NREL] = table_ref[0, head]

    tin[...] = jnp.zeros_like(tin)
    for ref in (dsc, wide_rows, wide_cols, dmat):
        ref[...] = jnp.zeros_like(ref)

    def spread(src, zp, zq, hp, width):
        j = (zp * WIN_Z + zq) * WIN_H + hp
        first = j * WIN_H * SPAN
        base = first // 128 * 128
        wide = src[:, base : base + 384]
        moved = pltpu.roll(wide, (384 - (first - base)) % 384, axis=1)
        g = hp * WIN_Z + zp
        tin[g * 8 : g * 8 + 8, zq * 256 : zq * 256 + width] = moved[:, :width]

    for zp in range(WIN_Z):
        for zq in range(WIN_Z):
            for hp in range(WIN_H):
                spread(tabw, zp, zq, hp, WIN_H * SPAN)

    def permuted(whole):
        high = whole.astype(BF16)
        rest = whole - high.astype(F32)
        middle = rest.astype(BF16)
        low = (rest - middle.astype(F32)).astype(BF16)
        count = whole.shape[0]
        terms = dot(jnp.concatenate([high, middle, low], 0), perm_ref[...])
        return (terms[:count] + terms[count : 2 * count] + terms[2 * count :]) * LOG2E

    loads[1].wait()
    spread_rows = permuted(tin[...])
    for n in range(3):
        ymat[n, 0:96, :] = spread_rows[:, 128 * n : 128 * (n + 1)]
        ymat[n, 96:128, :] = jnp.zeros((32, 128), F32)
    loads[2].wait()

    @pl.when(lat == 0)
    def _():
        for n in range(3):
            ymat[n, 0:96, :] = ymat[n, 0:96, :] + cross_ref[:, 128 * n : 128 * (n + 1)]

    def place_bias(tall, count):
        for head in range(HEADS):
            rows = jnp.concatenate(
                [ymat[n, pl.ds(head, tall, stride=8), :] for n in range(3)], -1
            )
            for w in range(WIN_W):
                moved = pltpu.roll(rows, (384 - (WIN_W - 1 - w) * GROUPS) % 384, axis=1)
                bias[head, w * GROUPS : w * GROUPS + count, :] = moved[:count, :T]

    place_bias(16, GROUPS)
    for n in range(3, 11):
        loads[n].wait()
    lane = lax.broadcasted_iota(jnp.int32, (16, C), 1)
    ones = [
        jnp.where((lane >= HEAD * i) & (lane < HEAD * (i + 1)), 1.0, 0.0).astype(BF16)[0:1]
        for i in range(HEADS)
    ]
    gain1 = g1_ref[...].reshape(1, C)
    gain2 = g2_ref[...].reshape(1, C)

    def arrived(a):
        for i in range(3):
            exchange(a, i).wait_recv()
        own[a].wait()
        for slot, row, col, rows in pieces():
            stage[a, rows, :] = arrive[a, slot, row, col].astype(F32)
        return stage[a]

    tokens = arrived(0)
    normed, hat1, inv1 = normalize(tokens, gain1)
    first = normed.astype(BF16)
    qkv = (dot(first, wqkv_ref[...]) + bqkv_ref[...].reshape(1, 3 * C)).astype(BF16)
    queries = qkv[:, 0:C]
    keys = qkv[:, C : 2 * C]
    values = qkv[:, 2 * C : 3 * C]
    queries_t = queries.T

    @pl.when(lat == 0)
    def _():
        table_copy().wait_recv()
        for head in range(HEADS):
            tabw[head : head + 1, 0:NREL] = tab15[0, head]
        tin[0:48, :] = jnp.zeros((48, 512), F32)
        for zp in range(WIN_Z):
            for zq in range(WIN_Z):
                for hp in range(3):
                    spread(tabw, zp, zq, hp, 3 * SPAN)
        upper_rows = permuted(tin[0:48, :]) + cross_ref[0:48, :]
        for n in range(3):
            ymat[n, 0:48, :] = upper_rows[:, 128 * n : 128 * (n + 1)]
        place_bias(8, 6)

    cot = arrived(1)
    cot_low = cot.astype(BF16)
    cot_t = cot_low.T

    for head in range(HEADS):
        wide_cols[256 * head : 256 * head + T, :] = values * ones[head]
    for head in range(HEADS):
        q = queries * ones[head]
        scores = dot_nt(q, keys) * (FACTOR * LOG2E) + bias[head]
        top = jnp.max(scores, -1, keepdims=True)
        raised = jnp.exp2(scores - top)
        probs = raised * (1.0 / jnp.sum(raised, -1, keepdims=True))
        prob[head] = probs
        probs_low = probs.astype(BF16)
        wide_rows[:, 256 * head : 256 * head + T] = probs_low
    mixed = dot(wide_rows[...], wide_cols[...]).astype(BF16)
    inner = tokens + dot(mixed, wproj_ref[...]).astype(BF16).astype(F32)

    def remote(src, dst, send_sem, recv_sem, target):
        return pltpu.make_async_remote_copy(
            src_ref=src, dst_ref=dst, send_sem=send_sem, recv_sem=recv_sem,
            device_id=target, device_id_type=MESH,
        )

    def wait_bytes(ref, sem):
        pltpu.make_async_copy(ref, ref, sem).wait()

    def add(*terms):
        total = terms[0].astype(F32)
        for term in terms[1:]:
            total = total + term.astype(F32)
        return total.astype(BF16)

    axes = [(n, (n + 1) % 3, (n + 2) % 3) for n in range(3)]
    places = [tuple(spot[axis] for axis in order) for order in axes]

    def block(n, i):
        return pl.ds(n * 16 + i * 4, 4)

    def unit(n):
        return n * 16 + places[n][0] * 4 + places[n][1]

    def part_to_line(n, stage_no, which, src, dst):
        for d in range(1, 4):
            at = lax.rem(places[n][which] + d, 4)
            remote(
                src(n, at), dst(n, d), f_send.at[stage_no, n], f_recv.at[stage_no, n],
                on_axis(axes[n][which], at),
            ).start()

    def third(n):
        return pl.ds(16 * n, 16)

    swap_fc = [
        remote(
            gath_fc.at[core, third(n)], gath_fc_out.at[core, third(n)],
            f_send.at[6, n], f_recv.at[6, n], sibling,
        )
        for n in range(3)
    ]
    pair_att = remote(parts_att.at[other], core_att, a_send.at[0], a_recv.at[0], sibling)
    swap_att = remote(
        gath_att.at[core], gath_att_out.at[core], a_send.at[4], a_recv.at[4], sibling
    )
    kept = [
        (out_stage.at[0, 3], quadrant(block_out, 0)),
        (out_stage.at[1, 3], quadrant(dtok_out, 0)),
        (dtab_ref, dtab_out),
        (gath_att.at[core], gath_att_out.at[core]),
    ] + [(gath_fc.at[core, third(n)], gath_fc_out.at[core, third(n)]) for n in range(3)]
    keep = [
        pltpu.make_async_copy(src, dst, out_sem.at[n]) for n, (src, dst) in enumerate(kept)
    ]

    def early1(n):
        for side, first, slot in ((core, 1, -1), (other, 0, 3)):
            for d in range(first, 4):
                at = lax.rem(places[n][0] + d, 4)
                remote(
                    parts_fc.at[side, block(n, at)], fold1.at[n, slot + d],
                    f_send.at[1, n], f_recv.at[1, n], on_axis(n, at, side),
                ).start()

    def early2(n):
        wait_bytes(fold1.at[n], f_recv.at[1, n])
        own_block = parts_fc[core, block(n, places[n][0])]
        sum1[n] = add(own_block, *[fold1[n, i] for i in range(7)])
        part_to_line(
            n, 2, 1, lambda n, at: sum1.at[n, at], lambda n, d: fold2.at[n, d - 1]
        )

    def early3(n):
        wait_bytes(fold2.at[n], f_recv.at[2, n])
        own_unit = sum1[n, places[n][1]]
        sum2[n] = add(own_unit, fold2[n, 0], fold2[n, 1], fold2[n, 2])
        fold3[n, places[n][2]] = sum2[n]
        part_to_line(
            n, 3, 2, lambda n, at: sum2.at[n], lambda n, d: fold3.at[n, places[n][2]]
        )

    def early4(n):
        wait_bytes(fold2.at[n], f_recv.at[3, n])
        gath_fc[core, unit(n)] = add(*[fold3[n, i] for i in range(4)])
        part_to_line(
            n, 4, 1, lambda n, at: gath_fc.at[core, unit(n)],
            lambda n, d: gath_fc.at[core, unit(n)],
        )

    def early5(n):
        wait_bytes(fold2.at[n], f_recv.at[4, n])
        part_to_line(
            n, 5, 0, lambda n, at: gath_fc.at[core, block(n, places[n][0])],
            lambda n, d: gath_fc.at[core, block(n, places[n][0])],
        )

    def early6(n):
        wait_bytes(fold1.at[n, pl.ds(0, 3)], f_recv.at[5, n])
        swap_fc[n].start()
        keep[4 + n].start()

    own_rows = pl.ds(pair_row * TALL, TALL)

    def late1():
        pair_att.wait_recv()
        parts_att[core] = add(parts_att[core], core_att[...])
        for d in range(1, ROWS):
            remote(
                parts_att.at[core, pl.ds(row_of(d) * TALL, TALL)], fold_att.at[d - 1],
                a_send.at[1], a_recv.at[1], (lon, row_of(d) * 2 + core),
            ).start()

    def late2():
        wait_bytes(fold_att, a_recv.at[1])
        sum_att[...] = add(parts_att[core, own_rows], *[fold_att[d] for d in range(ROWS - 1)])
        mid_att[lon] = sum_att[...]
        for d in range(1, STRIPS):
            remote(
                sum_att, mid_att.at[lon], a_send.at[2], a_recv.at[2], (strip(d), lat)
            ).start()

    def late3():
        wait_bytes(fold_att, a_recv.at[2])
        gath_att[core, own_rows] = add(*[mid_att[i] for i in range(STRIPS)])
        for d in range(1, ROWS):
            remote(
                gath_att.at[core, own_rows], gath_att.at[core, own_rows],
                a_send.at[3], a_recv.at[3], (lon, row_of(d) * 2 + core),
            ).start()

    def late4():
        wait_bytes(fold_att, a_recv.at[3])
        swap_att.start()
        keep[3].start()

    normed, hat2, inv2 = normalize(inner, gain2)
    second = normed.astype(BF16)
    second_t = second.T
    total = inner
    grad_second = jnp.zeros((T, C), F32)
    bfc1 = bfc1_ref[...].reshape(1, HID)
    vec[...] = jnp.zeros_like(vec)
    for n in range(3):
        cols = slice(256 * n, 256 * (n + 1))
        pre = dot(second, wfc1_ref[:, cols]) + bfc1[:, cols]
        cdf = 0.5 * (1.0 + lax.erf(pre * 0.7071067811865476))
        density = jnp.exp(-0.5 * pre * pre) * 0.3989422804014327
        act = (pre * cdf).astype(BF16)
        total = total + dot_nt(act, wfc2_ref[:, cols])
        grad_pre = (dot(cot_low, wfc2_ref[:, cols]) * (cdf + pre * density)).astype(BF16)
        grad_second = grad_second + dot_nt(grad_pre, wfc1_ref[:, cols])
        parts_fc[0, 12 * n : 12 * (n + 1)] = dot(second_t, grad_pre).astype(BF16).reshape(12, 16, 256)
        parts_fc[1, 12 * n : 12 * (n + 1)] = dot(cot_t, act).astype(BF16).reshape(12, 16, 256)
        vec[n : n + 1, :] = jnp.sum(grad_pre.astype(F32), 0, keepdims=True)
        if n:
            early1(n - 1)

    def give_back(a, i):
        return pltpu.make_async_remote_copy(
            src_ref=out_stage.at[a, 2 - i],
            dst_ref=quadrant((block_out, dtok_out)[a], i + 1),
            send_sem=rt_send.at[a, i],
            recv_sem=rt_recv.at[a, i],
            device_id=behind[i],
            device_id_type=MESH,
        )

    def hand_out(a):
        for slot, row, col, rows in pieces():
            out_stage[a, slot, row, col] = stage[a, rows, :].astype(BF16)
        for i in range(3):
            give_back(a, i).start()
        keep[a].start()

    grad_inner = cot + norm_back(hat2, inv2, gain2, grad_second)
    grad_att = grad_inner.astype(BF16)
    stage[0] = total
    grad_mixed = dot_nt(grad_att, wproj_ref[...]).astype(BF16)
    grad_mixed_t = grad_mixed.T
    grad_v_t = [
        dot(
            grad_mixed_t[HEAD * head : HEAD * (head + 1)],
            wide_rows[:, 256 * head : 256 * head + T],
        )
        for head in range(HEADS)
    ]
    grad_v = jnp.concatenate(grad_v_t, 0).T.astype(BF16)
    first_t = first.T
    value_grad = dot(first_t, grad_v).astype(BF16)
    proj_grad = dot_tn(mixed, grad_att).astype(BF16)
    last = value_grad[176:C]
    last = jnp.concatenate(
        [last[:, 0:64], last[:, 64:128], last[:, 128:C], jnp.zeros((144, 64), BF16)], 0
    )
    proj_grad = jnp.concatenate([proj_grad, last], -1).reshape(12, 16, 256)
    value_grad = jnp.concatenate([value_grad, jnp.zeros((C, 64), BF16)], -1).reshape(12, 16, 256)
    parts_fc[0, 36:42] = proj_grad[:6]
    parts_fc[1, 36:42] = proj_grad[6:]
    parts_fc[0, 43:48] = value_grad[0:5]
    parts_fc[1, 42:48] = value_grad[5:11]
    vec[3:4, 0:C] = jnp.sum(grad_second * hat2, 0, keepdims=True)
    vec[4:5, 0:C] = jnp.sum(grad_v.astype(F32), 0, keepdims=True)
    parts_fc[0, 42] = vec[...].astype(BF16)
    early1(2)

    for head in range(HEADS):
        wide_cols[256 * head : 256 * head + T, :] = keys * ones[head]
    grad_k_t = []
    for head in range(HEADS):
        rows = slice(HEAD * head, HEAD * (head + 1))
        gm = grad_mixed * ones[head]
        probs = prob[head]
        grad_probs = dot_nt(gm, values)
        inside = jnp.sum(probs * grad_probs, -1, keepdims=True)
        grad_scores = probs * (grad_probs - inside)
        dsc[head, 0:T, 0:T] = grad_scores
        scaled = (grad_scores * FACTOR).astype(BF16)
        wide_rows[:, 256 * head : 256 * head + T] = scaled
        grad_k_t.append(dot(queries_t[rows], scaled))
    grad_q = dot(wide_rows[...], wide_cols[...])
    grad_k = jnp.concatenate(grad_k_t, 0).T

    grad_qk = jnp.concatenate([grad_q, grad_k], -1).astype(BF16)
    wide = dot(first_t, grad_qk).astype(BF16)
    wide = [wide[:, 128 * n : 128 * (n + 1)].reshape(12, 16, 128) for n in range(3)]
    parts_att[0, 0:12] = wide[0]
    parts_att[0, 12:18] = wide[1][:6]
    parts_att[1, 0:6] = wide[1][6:]
    parts_att[1, 6:18] = wide[2]
    grad_first = dot_nt(grad_qk, wqkv_ref[:, 0 : 2 * C])
    grad_first = grad_first + dot_nt(grad_v, wqkv_ref[:, 2 * C : 3 * C])
    grad_first = grad_first.astype(BF16).astype(F32)
    vec[...] = jnp.zeros_like(vec)
    sums = jnp.sum(grad_qk.astype(F32), 0, keepdims=True)
    sums = [sums[:, C * n : C * (n + 1)] for n in range(2)]
    sums.append(jnp.sum(grad_first * hat1, 0, keepdims=True))
    for n in range(3):
        vec[2 * n : 2 * n + 1, 0:128] = sums[n][:, 0:128]
        vec[2 * n + 1 : 2 * n + 2, 0:64] = sums[n][:, 128:C]
    parts_att[0, 18] = vec[:, 0:128].astype(BF16)
    parts_att[1, 18] = jnp.zeros((16, 128), BF16)
    parts_att[:, 19:] = jnp.zeros((2, ATT - 19, 16, 128), BF16)
    pair_att.start()
    early2(0)
    early2(1)
    d_tokens = grad_inner + norm_back(hat1, inv1, gain1, grad_first)
    stage[1] = d_tokens
    hand_out(1)

    for head in range(HEADS):
        if head == 3:
            late1()
            early2(2)
            early3(0)
            early3(1)
        acc = jnp.zeros((16, 384), F32)
        for w in range(WIN_W):
            acc = acc + pltpu.roll(
                dsc[head, w * GROUPS : w * GROUPS + 16, :], (WIN_W - 1 - w) * GROUPS, axis=1
            )
        for n in range(3):
            dmat[n, pl.ds(head, 16, stride=8), :] = acc[:, 128 * n : 128 * (n + 1)]

    def table_grad():
        return jnp.concatenate([dmat[n, 0:96, :] for n in range(3)], -1)

    def keep_table(field):
        for n in range(3):
            dmat[n, 0:96, :] = field[:, 128 * n : 128 * (n + 1)]

    def edge_copy():
        return pltpu.make_async_remote_copy(
            src_ref=bbs,
            dst_ref=bbr,
            send_sem=one_send.at[1],
            recv_sem=one_recv.at[1],
            device_id=(lon, north),
            device_id_type=MESH,
        )

    @pl.when(lat == 0)
    def _():
        upper = lax.broadcasted_iota(jnp.int32, (96, 384), 0) < 48
        full = table_grad()
        bbs[...] = jnp.where(upper, full, 0.0).astype(BF16)
        edge_copy().start()
        keep_table(jnp.where(upper, 0.0, full))

    hand_out(0)
    early3(2)
    early4(0)
    early4(1)
    late2()

    @pl.when(lat == BANDS - 1)
    def _():
        edge_copy().wait_recv()
        keep_table(table_grad() + bbr[...].astype(F32))

    bsend[...] = table_grad().astype(BF16).reshape(PARTS, 16, 384)

    for owner in range(PARTS):
        @pl.when(lon != owner)
        def _():
            pltpu.make_async_remote_copy(
                src_ref=bsend.at[owner],
                dst_ref=brecv.at[lon],
                send_sem=b_send.at[0],
                recv_sem=b_recv.at[0],
                device_id=(owner, lat),
                device_id_type=MESH,
            ).start()

    early4(2)
    early5(0)
    early5(1)
    late3()
    early5(2)
    seven = brecv.at[pl.ds(0, STRIPS - 1)]

    @pl.when(lon < PARTS)
    def _():
        brecv[lon] = bsend[lon]
        wait_bytes(seven, b_recv.at[0])
        bfin[lon] = jnp.sum(brecv[...].astype(F32), 0).astype(BF16)
        for d in range(1, STRIPS):
            pltpu.make_async_remote_copy(
                src_ref=bfin.at[lon],
                dst_ref=bfin.at[lon],
                send_sem=b_send.at[1],
                recv_sem=b_recv.at[1],
                device_id=(strip(d), lat),
                device_id_type=MESH,
            ).start()

    late4()
    for n in range(3):
        early6(n)

    @pl.when(lon < PARTS)
    def _():
        wait_bytes(bfin.at[pl.ds(0, PARTS - 1)], b_recv.at[1])

    @pl.when(lon >= PARTS)
    def _():
        wait_bytes(bfin, b_recv.at[1])

    tin[...] = dot_nt(bfin[...].reshape(96, 384), perm_ref[...])
    dtab_ref[...] = jnp.zeros_like(dtab_ref)
    for zp in range(WIN_Z):
        for zq in range(WIN_Z):
            for hp in range(WIN_H):
                j = (zp * WIN_Z + zq) * WIN_H + hp
                first_lane = j * WIN_H * SPAN
                base = first_lane // 128 * 128
                g = hp * WIN_Z + zp
                piece = tin[g * 8 : g * 8 + 8, zq * 256 : zq * 256 + 256]
                piece = jnp.concatenate([piece, jnp.zeros((8, 128), F32)], -1)
                moved = pltpu.roll(piece, first_lane - base, axis=1)
                dtab_ref[:, base : base + 384] = dtab_ref[:, base : base + 384] + moved

    keep[2].start()

    for a in range(2):
        for i in range(3):
            exchange(a, i).wait_send()
            give_back(a, i).wait()

    @pl.when(lat == BANDS - 1)
    def _():
        table_copy().wait_send()

    @pl.when(lat == 0)
    def _():
        edge_copy().wait_send()

    for n in range(3):
        wait_bytes(fold1.at[n], f_send.at[1, n])
        for stage_no in (2, 3, 4):
            wait_bytes(fold2.at[n], f_send.at[stage_no, n])
        wait_bytes(fold1.at[n, pl.ds(0, 3)], f_send.at[5, n])
    pair_att.wait_send()
    for stage_no in (1, 2, 3):
        wait_bytes(fold_att, a_send.at[stage_no])

    @pl.when(lon < PARTS)
    def _():
        wait_bytes(bsend.at[pl.ds(0, PARTS - 1)], b_send.at[0])
        wait_bytes(seven, b_send.at[1])

    @pl.when(lon >= PARTS)
    def _():
        wait_bytes(bsend, b_send.at[0])

    for copy in keep:
        copy.wait()
    for copy in swap_fc:
        copy.wait()
    swap_att.wait()


def output_kernel(*refs):
    ins, outs = refs[:5], refs[5:16]
    in_bufs, out_bufs = refs[16:21], refs[21:30]
    in_sem, out_sem = refs[30:]
    loads = [
        pltpu.make_async_copy(src, dst, in_sem.at[n])
        for n, (src, dst) in enumerate(zip(ins, in_bufs))
    ]
    stores = [
        pltpu.make_async_copy(src, dst, out_sem.at[n])
        for n, (src, dst) in enumerate(zip(in_bufs[:2] + out_bufs, outs))
    ]
    gath_ref, gath_att, dtab_ref = in_bufs[2:]
    (
        dln1_ref, dwqkv_ref, dbqkv_ref, dbias_ref, dwproj_ref, dln2_ref,
        dwfc1_ref, dbfc1_ref, dwfc2_ref,
    ) = out_bufs
    for n in (2, 0, 1, 3, 4):
        loads[n].start()
    loads[2].wait()
    for n in range(3):
        cols = slice(256 * n, 256 * (n + 1))
        rows = slice(12 * n, 12 * (n + 1))
        dwfc1_ref[:, cols] = gath_ref[0, rows].reshape(C, 256).astype(F32)
    stores[8].start()
    for n in range(3):
        cols = slice(256 * n, 256 * (n + 1))
        rows = slice(12 * n, 12 * (n + 1))
        dwfc2_ref[:, cols] = gath_ref[1, rows].reshape(C, 256).astype(F32)
    stores[10].start()
    for k in range(2):
        dwproj_ref[96 * k : 96 * (k + 1), :] = (
            gath_ref[k, 36:42].reshape(96, 256)[:, 0:C].astype(F32)
        )
    vec = gath_ref[0, 42].astype(F32)
    dbfc1_ref[...] = jnp.concatenate([vec[n : n + 1] for n in range(3)], -1).reshape(HID)
    dln2_ref[...] = vec[3:4, :C].reshape(C)
    for n in (6, 9, 7):
        stores[n].start()
    for n in range(2):
        loads[n].wait()
        stores[n].start()
    loads[3].wait()
    dwqkv_ref[:, 0:128] = gath_att[0, 0:12].reshape(C, 128).astype(F32)
    dwqkv_ref[0:96, 128:256] = gath_att[0, 12:18].reshape(96, 128).astype(F32)
    dwqkv_ref[96:C, 128:256] = gath_att[1, 0:6].reshape(96, 128).astype(F32)
    dwqkv_ref[:, 256:384] = gath_att[1, 6:18].reshape(C, 128).astype(F32)
    dwqkv_ref[0:80, 384:576] = gath_ref[0, 43:48].reshape(80, 256)[:, 0:C].astype(F32)
    dwqkv_ref[80:176, 384:576] = gath_ref[1, 42:48].reshape(96, 256)[:, 0:C].astype(F32)
    last = [gath_ref[0, 36 + n][:, C:256].astype(F32) for n in range(3)]
    dwqkv_ref[176:C, 384:576] = jnp.concatenate(last, -1)
    value_bias = vec[4:5, :C]
    vec = gath_att[0, 18].astype(F32)
    sums = [
        jnp.concatenate([vec[2 * n : 2 * n + 1], vec[2 * n + 1 : 2 * n + 2, :64]], -1)
        for n in range(3)
    ]
    dbqkv_ref[...] = jnp.concatenate(sums[:2] + [value_bias], -1).reshape(3 * C)
    dln1_ref[...] = sums[2].reshape(C)
    for n in (3, 4, 2):
        stores[n].start()
    loads[4].wait()
    for head in range(HEADS):
        dbias_ref[0, head] = dtab_ref[head : head + 1, 0:NREL]
    stores[5].start()
    for store in stores:
        store.wait()


def per_device(
    tokens, cotangent, ln1_gain, w_qkv, b_qkv, bias_table, w_proj, ln2_gain, w_fc1, b_fc1, w_fc2
):
    hbm = pl.BlockSpec(memory_space=pl.ANY)
    perm = table_order()
    dma = pltpu.SemaphoreType.DMA
    args = (
        tokens.transpose(1, 2, 0, 3), cotangent.transpose(1, 2, 0, 3), ln1_gain, w_qkv, b_qkv,
        bias_table.transpose(0, 2, 1, 3), w_proj, ln2_gain, w_fc1, b_fc1, w_fc2.T,
        jnp.asarray(perm, BF16), jnp.asarray(cross_pairs()),
    )
    gathered, gathered_att, block, d_tok, table = pl.pallas_call(
        block_kernel,
        out_shape=(
            jax.ShapeDtypeStruct((2, FC, 16, 256), BF16),
            jax.ShapeDtypeStruct((2, ATT, 16, 128), BF16),
            jax.ShapeDtypeStruct((WIN_H, WIN_W, WIN_Z, C), BF16),
            jax.ShapeDtypeStruct((WIN_H, WIN_W, WIN_Z, C), BF16),
            jax.ShapeDtypeStruct((8, 3456), F32),
        ),
        in_specs=[hbm] * len(args),
        out_specs=(hbm,) * 5,
        scratch_shapes=[pltpu.VMEM(a.shape, a.dtype) for a in args[2:]]
        + [
            pltpu.VMEM((2, T, C), F32),
            pltpu.VMEM((2, 4, 3, 6, WIN_Z, C), BF16),
            pltpu.VMEM((2, 4, 3, 6, WIN_Z, C), BF16),
            pltpu.VMEM((8, 3456), F32),
            pltpu.VMEM((1, HEADS, 1, NREL), F32),
            pltpu.VMEM((96, 512), F32),
            pltpu.VMEM((3, 128, 128), F32),
            pltpu.VMEM((HEADS, T, T), F32),
            pltpu.VMEM((HEADS, T, T), F32),
            pltpu.VMEM((T, HEADS * 256), BF16),
            pltpu.VMEM((HEADS * 256, C), BF16),
            pltpu.VMEM((HEADS, 160, 384), F32),
            pltpu.VMEM((3, 128, 128), F32),
            pltpu.VMEM((16, 256), F32),
            pltpu.VMEM((PARTS, 16, 384), BF16),
            pltpu.VMEM((STRIPS, 16, 384), BF16),
            pltpu.VMEM((PARTS, 16, 384), BF16),
            pltpu.VMEM((96, 384), BF16),
            pltpu.VMEM((96, 384), BF16),
            pltpu.VMEM((2, FC, 16, 256), BF16),
            pltpu.VMEM((2, ATT, 16, 128), BF16),
            pltpu.VMEM((ATT, 16, 128), BF16),
            pltpu.VMEM((3, 7, 4, 16, 256), BF16),
            pltpu.VMEM((3, 4, 16, 256), BF16),
            pltpu.VMEM((3, 3, 16, 256), BF16),
            pltpu.VMEM((3, 16, 256), BF16),
            pltpu.VMEM((3, 4, 16, 256), BF16),
            pltpu.VMEM((ROWS - 1, TALL, 16, 128), BF16),
            pltpu.VMEM((TALL, 16, 128), BF16),
            pltpu.VMEM((STRIPS, TALL, 16, 128), BF16),
            pltpu.VMEM((2, FC, 16, 256), BF16),
            pltpu.VMEM((2, ATT, 16, 128), BF16),
            pltpu.VMEM((8, 3456), F32),
            dma((len(args) - 2,)), dma((2,)), dma((7,)),
            dma((2, 3)), dma((2, 3)), dma((2, 3)), dma((2, 3)),
            dma((2,)), dma((2,)), dma((7, 3)), dma((7, 3)),
            dma((5,)), dma((5,)), dma((2,)), dma((2,)),
        ],
        compiler_params=pltpu.CompilerParams(
            collective_id=0, has_side_effects=True, vmem_limit_bytes=VMEM_LIMIT
        ),
    )(*args)
    shape = jax.ShapeDtypeStruct
    grid_shape = (WIN_H, WIN_W, WIN_Z, C)
    results_out = (
        shape(grid_shape, BF16), shape(grid_shape, BF16),
        shape((C,), F32), shape((C, 3 * C), F32), shape((3 * C,), F32),
        shape((1, HEADS, 1, NREL), F32), shape((C, C), F32), shape((C,), F32),
        shape((C, HID), F32), shape((HID,), F32), shape((C, HID), F32),
    )
    outs = pl.pallas_call(
        output_kernel,
        out_shape=results_out,
        in_specs=[hbm] * 5,
        out_specs=(hbm,) * 11,
        scratch_shapes=[
            pltpu.VMEM(a.shape, a.dtype)
            for a in (block, d_tok, gathered, gathered_att, table) + results_out[2:]
        ]
        + [dma((5,)), dma((11,))],
        compiler_params=pltpu.CompilerParams(vmem_limit_bytes=VMEM_LIMIT),
    )(block, d_tok, gathered, gathered_att, table)
    out, d_tok, d_ln1, d_wqkv, d_bqkv, d_bias, d_wproj, d_ln2, d_wfc1, d_bfc1, d_wfc2 = outs
    return (
        out.transpose(2, 0, 1, 3), d_tok.transpose(2, 0, 1, 3), d_ln1, d_wqkv, d_bqkv,
        d_bias.transpose(0, 2, 1, 3), d_wproj, d_ln2, d_wfc1, d_bfc1, d_wfc2.T,
    )


def solution(mesh):
    grid = P(None, "lat", "lon", None)
    rows = P(None, "lat", None, None)
    return jax.shard_map(
        per_device,
        mesh=mesh,
        in_specs=(grid, grid, P(), P(), P(), rows, P(), P(), P(), P(), P()),
        out_specs=(grid, grid, P(), P(), P(), rows, P(), P(), P(), P(), P()),
        check_vma=False,
    )
```

```python
import jax
import jax.numpy as jnp
import numpy as np
from jax import lax
from jax.experimental import pallas as pl
from jax.experimental.pallas import tpu as pltpu
from jax.sharding import PartitionSpec as P

HEADS = 6
WIN_Z = 2
WIN_H = 6
WIN_W = 12
SPAN = 2 * WIN_W - 1
GROUPS = WIN_Z * WIN_H
T = GROUPS * WIN_W
C = 192
HID = 768
HEAD = C // HEADS
NREL = GROUPS * GROUPS * SPAN
FC = 48
ATT = 24
TALL = 3
ROWS = 8
BANDS = 16
STRIPS = 8
PARTS = 6
EPSILON = 1e-05
VMEM_LIMIT = 56 * 1024 * 1024
FACTOR = HEAD ** (-0.5)
LOG2E = 1.4426950408889634
F32 = jnp.float32
BF16 = jnp.bfloat16
MESH = pl.DeviceIdType.MESH


def table_order():
    grid = np.zeros((512, 384), np.float32)
    for z in range(WIN_Z):
        for h in range(WIN_H):
            for i in range(SPAN):
                grid[z * 256 + h * SPAN + i, (SPAN - 1 - i) * GROUPS + h * WIN_Z + z] = 1
    return grid


def cross_pairs():
    g = np.arange(96)[:, None] // 8 // WIN_Z
    q = np.arange(384)[None, :] % GROUPS // WIN_Z
    return np.where((g < 3) != (q < 3), -1e30, 0.0).astype(np.float32)


def dot(a, b):
    return jnp.dot(a, b, preferred_element_type=F32)


def dot_nt(a, b):
    return lax.dot_general(a, b, (((1,), (1,)), ((), ())), preferred_element_type=F32)


def dot_tn(a, b):
    return lax.dot_general(a, b, (((0,), (0,)), ((), ())), preferred_element_type=F32)


def normalize(values, gain):
    average = jnp.mean(values, -1, keepdims=True)
    centered = values - average
    inv = lax.rsqrt(jnp.mean(centered * centered, -1, keepdims=True) + EPSILON)
    hat = centered * inv
    return hat * gain, hat, inv


def norm_back(hat, inv, gain, grad):
    scaled = grad * gain
    return inv * (
        scaled
        - jnp.mean(scaled, -1, keepdims=True)
        - hat * jnp.mean(scaled * hat, -1, keepdims=True)
    )


def pieces():
    for h in range(WIN_H):
        for w in range(WIN_W):
            at = w * GROUPS + h * WIN_Z
            yield (h // 3) * 2 + w // 6, h % 3, w % 6, slice(at, at + WIN_Z)


def quadrant(ref, q):
    return ref.at[pl.ds(q // 2 * 3, 3), pl.ds(q % 2 * 6, 6)]


def block_kernel(
    tok_any, cot_any, g1_any, wqkv_any, bqkv_any, table_any, wproj_any, g2_any, wfc1_any,
    bfc1_any, wfc2_any, perm_any, cross_any,
    gath_fc_out, gath_att_out, block_out, dtok_out, dtab_out,
    g1_ref, wqkv_ref, bqkv_ref, table_ref, wproj_ref, g2_ref, wfc1_ref,
    bfc1_ref, wfc2_ref, perm_ref, cross_ref,
    stage, arrive, out_stage,
    tabw, tab15, tin, ymat, bias, prob, wide_rows, wide_cols, dsc, dmat, vec,
    bsend, brecv, bfin, bbs, bbr,
    parts_fc, parts_att, fold1, sum1, fold2, sum2, fold3, fold_att, sum_att,
    mid_att, gath_fc, gath_att, dtab_ref,
    in_sem, own_sem, out_sem,
    ex_send, ex_recv, rt_send, rt_recv, one_send, one_recv, f_send, f_recv,
    a_send, a_recv, b_send, b_recv,
):
    sources = (
        (table_any, table_ref), (perm_any, perm_ref), (cross_any, cross_ref), (g1_any, g1_ref),
        (wqkv_any, wqkv_ref), (bqkv_any, bqkv_ref), (wproj_any, wproj_ref), (g2_any, g2_ref),
        (wfc1_any, wfc1_ref), (bfc1_any, bfc1_ref), (wfc2_any, wfc2_ref),
    )
    loads = [pltpu.make_async_copy(src, dst, in_sem.at[n]) for n, (src, dst) in enumerate(sources)]
    lon = lax.axis_index("lon")
    lat = lax.axis_index("lat")
    core = lax.rem(lat, 2)
    other = 1 - core
    pair_row = lat // 2
    east = lax.rem(lon + 1, STRIPS)
    west = lax.rem(lon + STRIPS - 1, STRIPS)
    south = lax.rem(lat + 1, BANDS)
    north = lax.rem(lat + BANDS - 1, BANDS)
    sibling = (lon, lat - core + other)

    spot = (lax.rem(pair_row, 4), lon // 2, lax.rem(lon, 2) * 2 + lat // 8)

    def on_axis(axis, at, side=core):
        if axis == 0:
            return (lon, lat // 8 * 8 + at * 2 + side)
        if axis == 1:
            return (at * 2 + lax.rem(lon, 2), lat - core + side)
        return (spot[1] * 2 + at // 2, lax.rem(at, 2) * 8 + spot[0] * 2 + side)

    def strip(d):
        return lax.rem(lon + d, STRIPS)

    def row_of(d):
        return lax.rem(pair_row + d, ROWS)

    barrier = pltpu.get_barrier_semaphore()

    def greet(target):
        pl.semaphore_signal(barrier, inc=1, device_id=target, device_id_type=MESH)

    for target in ((east, south), (west, north)):
        greet(target)
    for d in range(1, STRIPS):
        greet((strip(d), lat))
    for d in range(1, BANDS):
        greet((lon, lax.rem(lat + d, BANDS)))
    for d in range(1, 4):
        greet(on_axis(1, lax.rem(spot[1] + d, 4), other))
    across = lax.rem(spot[2] + 2, 4)
    greet(on_axis(2, across, other))
    greet(on_axis(2, 3 - spot[2]))
    greet(on_axis(2, 3 - spot[2], other))
    loads[0].start()
    own = [
        pltpu.make_async_copy(quadrant(src, 0), arrive.at[a, 3], own_sem.at[a])
        for a, src in enumerate((tok_any, cot_any))
    ]
    own[0].start()
    pl.semaphore_wait(barrier, 30)

    ahead = ((east, lat), (lon, south), (east, south))
    behind = ((west, lat), (lon, north), (west, north))

    def exchange(a, i):
        return pltpu.make_async_remote_copy(
            src_ref=quadrant((tok_any, cot_any)[a], i + 1),
            dst_ref=arrive.at[a, 2 - i],
            send_sem=ex_send.at[a, i],
            recv_sem=ex_recv.at[a, i],
            device_id=ahead[i],
            device_id_type=MESH,
        )

    def table_copy():
        return pltpu.make_async_remote_copy(
            src_ref=table_any,
            dst_ref=tab15,
            send_sem=one_send.at[0],
            recv_sem=one_recv.at[0],
            device_id=(lon, south),
            device_id_type=MESH,
        )

    @pl.when(lat == BANDS - 1)
    def _():
        table_copy().start()

    for a in range(2):
        for i in range(3):
            exchange(a, i).start()
    for load in loads[1:]:
        load.start()
    own[1].start()

    tabw[...] = jnp.zeros_like(tabw)
    loads[0].wait()
    for head in range(HEADS):
        tabw[head : head + 1, 0:NREL] = table_ref[0, head]

    tin[...] = jnp.zeros_like(tin)
    for ref in (dsc, wide_rows, wide_cols, dmat):
        ref[...] = jnp.zeros_like(ref)

    def spread(src, zp, zq, hp, width):
        j = (zp * WIN_Z + zq) * WIN_H + hp
        first = j * WIN_H * SPAN
        base = first // 128 * 128
        wide = src[:, base : base + 384]
        moved = pltpu.roll(wide, (384 - (first - base)) % 384, axis=1)
        g = hp * WIN_Z + zp
        tin[g * 8 : g * 8 + 8, zq * 256 : zq * 256 + width] = moved[:, :width]

    for zp in range(WIN_Z):
        for zq in range(WIN_Z):
            for hp in range(WIN_H):
                spread(tabw, zp, zq, hp, WIN_H * SPAN)

    def permuted(whole):
        high = whole.astype(BF16)
        rest = whole - high.astype(F32)
        middle = rest.astype(BF16)
        low = (rest - middle.astype(F32)).astype(BF16)
        count = whole.shape[0]
        terms = dot(jnp.concatenate([high, middle, low], 0), perm_ref[...])
        return (terms[:count] + terms[count : 2 * count] + terms[2 * count :]) * LOG2E

    loads[1].wait()
    spread_rows = permuted(tin[...])
    for n in range(3):
        ymat[n, 0:96, :] = spread_rows[:, 128 * n : 128 * (n + 1)]
        ymat[n, 96:128, :] = jnp.zeros((32, 128), F32)
    loads[2].wait()

    @pl.when(lat == 0)
    def _():
        for n in range(3):
            ymat[n, 0:96, :] = ymat[n, 0:96, :] + cross_ref[:, 128 * n : 128 * (n + 1)]

    def place_bias(tall, count):
        for head in range(HEADS):
            rows = jnp.concatenate(
                [ymat[n, pl.ds(head, tall, stride=8), :] for n in range(3)], -1
            )
            for w in range(WIN_W):
                moved = pltpu.roll(rows, (384 - (WIN_W - 1 - w) * GROUPS) % 384, axis=1)
                bias[head, w * GROUPS : w * GROUPS + count, :] = moved[:count, :T]

    place_bias(16, GROUPS)
    for n in range(3, 11):
        loads[n].wait()
    lane = lax.broadcasted_iota(jnp.int32, (16, C), 1)
    ones = [
        jnp.where((lane >= HEAD * i) & (lane < HEAD * (i + 1)), 1.0, 0.0).astype(BF16)[0:1]
        for i in range(HEADS)
    ]
    gain1 = g1_ref[...].reshape(1, C)
    gain2 = g2_ref[...].reshape(1, C)

    def arrived(a):
        for i in range(3):
            exchange(a, i).wait_recv()
        own[a].wait()
        for slot, row, col, rows in pieces():
            stage[a, rows, :] = arrive[a, slot, row, col].astype(F32)
        return stage[a]

    tokens = arrived(0)
    normed, hat1, inv1 = normalize(tokens, gain1)
    first = normed.astype(BF16)
    qkv = (dot(first, wqkv_ref[...]) + bqkv_ref[...].reshape(1, 3 * C)).astype(BF16)
    queries = qkv[:, 0:C]
    keys = qkv[:, C : 2 * C]
    values = qkv[:, 2 * C : 3 * C]
    queries_t = queries.T

    @pl.when(lat == 0)
    def _():
        table_copy().wait_recv()
        for head in range(HEADS):
            tabw[head : head + 1, 0:NREL] = tab15[0, head]
        tin[0:48, :] = jnp.zeros((48, 512), F32)
        for zp in range(WIN_Z):
            for zq in range(WIN_Z):
                for hp in range(3):
                    spread(tabw, zp, zq, hp, 3 * SPAN)
        upper_rows = permuted(tin[0:48, :]) + cross_ref[0:48, :]
        for n in range(3):
            ymat[n, 0:48, :] = upper_rows[:, 128 * n : 128 * (n + 1)]
        place_bias(8, 6)

    cot = arrived(1)
    cot_low = cot.astype(BF16)
    cot_t = cot_low.T

    for head in range(HEADS):
        wide_cols[256 * head : 256 * head + T, :] = values * ones[head]
    for head in range(HEADS):
        q = queries * ones[head]
        scores = dot_nt(q, keys) * (FACTOR * LOG2E) + bias[head]
        top = jnp.max(scores, -1, keepdims=True)
        raised = jnp.exp2(scores - top)
        probs = raised * (1.0 / jnp.sum(raised, -1, keepdims=True))
        prob[head] = probs
        probs_low = probs.astype(BF16)
        wide_rows[:, 256 * head : 256 * head + T] = probs_low
    mixed = dot(wide_rows[...], wide_cols[...]).astype(BF16)
    inner = tokens + dot(mixed, wproj_ref[...]).astype(BF16).astype(F32)

    def remote(src, dst, send_sem, recv_sem, target):
        return pltpu.make_async_remote_copy(
            src_ref=src, dst_ref=dst, send_sem=send_sem, recv_sem=recv_sem,
            device_id=target, device_id_type=MESH,
        )

    def wait_bytes(ref, sem):
        pltpu.make_async_copy(ref, ref, sem).wait()

    def add(*terms):
        total = terms[0].astype(F32)
        for term in terms[1:]:
            total = total + term.astype(F32)
        return total.astype(BF16)

    axes = [(n, (n + 1) % 3, (n + 2) % 3) for n in range(3)]
    places = [tuple(spot[axis] for axis in order) for order in axes]

    def block(n, i):
        return pl.ds(n * 16 + i * 4, 4)

    def unit(n):
        return n * 16 + places[n][0] * 4 + places[n][1]

    def part_to_line(n, stage_no, which, src, dst):
        for d in range(1, 4):
            at = lax.rem(places[n][which] + d, 4)
            remote(
                src(n, at), dst(n, d), f_send.at[stage_no, n], f_recv.at[stage_no, n],
                on_axis(axes[n][which], at),
            ).start()

    def third(n):
        return pl.ds(16 * n, 16)

    swap_fc = [
        remote(
            gath_fc.at[core, third(n)], gath_fc_out.at[core, third(n)],
            f_send.at[6, n], f_recv.at[6, n], sibling,
        )
        for n in range(3)
    ]
    swap_att = remote(
        gath_att.at[core], gath_att_out.at[core], a_send.at[4], a_recv.at[4], sibling
    )
    kept = [
        (out_stage.at[0, 3], quadrant(block_out, 0)),
        (out_stage.at[1, 3], quadrant(dtok_out, 0)),
        (dtab_ref, dtab_out),
        (gath_att.at[core], gath_att_out.at[core]),
    ] + [(gath_fc.at[core, third(n)], gath_fc_out.at[core, third(n)]) for n in range(3)]
    keep = [
        pltpu.make_async_copy(src, dst, out_sem.at[n]) for n, (src, dst) in enumerate(kept)
    ]

    def early1(n):
        for side, first, slot in ((core, 1, -1), (other, 0, 3)):
            for d in range(first, 4):
                at = lax.rem(places[n][0] + d, 4)
                remote(
                    parts_fc.at[side, block(n, at)], fold1.at[n, slot + d],
                    f_send.at[1, n], f_recv.at[1, n], on_axis(n, at, side),
                ).start()

    def early2(n):
        wait_bytes(fold1.at[n], f_recv.at[1, n])
        own_block = parts_fc[core, block(n, places[n][0])]
        sum1[n] = add(own_block, *[fold1[n, i] for i in range(7)])
        part_to_line(
            n, 2, 1, lambda n, at: sum1.at[n, at], lambda n, d: fold2.at[n, d - 1]
        )

    def early3(n):
        wait_bytes(fold2.at[n], f_recv.at[2, n])
        own_unit = sum1[n, places[n][1]]
        sum2[n] = add(own_unit, fold2[n, 0], fold2[n, 1], fold2[n, 2])
        fold3[n, places[n][2]] = sum2[n]
        part_to_line(
            n, 3, 2, lambda n, at: sum2.at[n], lambda n, d: fold3.at[n, places[n][2]]
        )

    def early4(n):
        wait_bytes(fold2.at[n], f_recv.at[3, n])
        gath_fc[core, unit(n)] = add(*[fold3[n, i] for i in range(4)])
        part_to_line(
            n, 4, 1, lambda n, at: gath_fc.at[core, unit(n)],
            lambda n, d: gath_fc.at[core, unit(n)],
        )

    def early5(n):
        wait_bytes(fold2.at[n], f_recv.at[4, n])
        part_to_line(
            n, 5, 0, lambda n, at: gath_fc.at[core, block(n, places[n][0])],
            lambda n, d: gath_fc.at[core, block(n, places[n][0])],
        )

    def early6(n):
        wait_bytes(fold1.at[n, pl.ds(0, 3)], f_recv.at[5, n])
        swap_fc[n].start()
        keep[4 + n].start()

    own_rows = pl.ds(pair_row * TALL, TALL)

    eighth = fold_att.at[pl.ds(0, ROWS - 1)]

    def late1():
        for side, first, slot in ((core, 1, -1), (other, 0, 7)):
            for d in range(first, ROWS):
                row = row_of(d)
                remote(
                    parts_att.at[side, pl.ds(row * TALL, TALL)], fold_att.at[slot + d],
                    a_send.at[1], a_recv.at[1], (lon, row * 2 + side),
                ).start()

    def late2():
        wait_bytes(fold_att, a_recv.at[1])
        sum_att[...] = add(parts_att[core, own_rows], *[fold_att[i] for i in range(BANDS - 1)])
        mid_att[lon] = sum_att[...]
        for d in range(1, STRIPS):
            remote(
                sum_att, mid_att.at[lon], a_send.at[2], a_recv.at[2], (strip(d), lat)
            ).start()

    def late3():
        wait_bytes(eighth, a_recv.at[2])
        gath_att[core, own_rows] = add(*[mid_att[i] for i in range(STRIPS)])
        for d in range(1, ROWS):
            remote(
                gath_att.at[core, own_rows], gath_att.at[core, own_rows],
                a_send.at[3], a_recv.at[3], (lon, row_of(d) * 2 + core),
            ).start()

    def late4():
        wait_bytes(eighth, a_recv.at[3])
        swap_att.start()
        keep[3].start()

    normed, hat2, inv2 = normalize(inner, gain2)
    second = normed.astype(BF16)
    second_t = second.T
    total = inner
    grad_second = jnp.zeros((T, C), F32)
    bfc1 = bfc1_ref[...].reshape(1, HID)
    vec[...] = jnp.zeros_like(vec)
    for n in range(3):
        cols = slice(256 * n, 256 * (n + 1))
        pre = dot(second, wfc1_ref[:, cols]) + bfc1[:, cols]
        cdf = 0.5 * (1.0 + lax.erf(pre * 0.7071067811865476))
        density = jnp.exp(-0.5 * pre * pre) * 0.3989422804014327
        act = (pre * cdf).astype(BF16)
        total = total + dot_nt(act, wfc2_ref[:, cols])
        grad_pre = (dot(cot_low, wfc2_ref[:, cols]) * (cdf + pre * density)).astype(BF16)
        grad_second = grad_second + dot_nt(grad_pre, wfc1_ref[:, cols])
        parts_fc[0, 12 * n : 12 * (n + 1)] = dot(second_t, grad_pre).astype(BF16).reshape(12, 16, 256)
        parts_fc[1, 12 * n : 12 * (n + 1)] = dot(cot_t, act).astype(BF16).reshape(12, 16, 256)
        vec[n : n + 1, :] = jnp.sum(grad_pre.astype(F32), 0, keepdims=True)
        if n:
            early1(n - 1)

    def give_back(a, i):
        return pltpu.make_async_remote_copy(
            src_ref=out_stage.at[a, 2 - i],
            dst_ref=quadrant((block_out, dtok_out)[a], i + 1),
            send_sem=rt_send.at[a, i],
            recv_sem=rt_recv.at[a, i],
            device_id=behind[i],
            device_id_type=MESH,
        )

    def hand_out(a):
        for slot, row, col, rows in pieces():
            out_stage[a, slot, row, col] = stage[a, rows, :].astype(BF16)
        for i in range(3):
            give_back(a, i).start()
        keep[a].start()

    grad_inner = cot + norm_back(hat2, inv2, gain2, grad_second)
    grad_att = grad_inner.astype(BF16)
    stage[0] = total
    grad_mixed = dot_nt(grad_att, wproj_ref[...]).astype(BF16)
    grad_mixed_t = grad_mixed.T
    grad_v_t = [
        dot(
            grad_mixed_t[HEAD * head : HEAD * (head + 1)],
            wide_rows[:, 256 * head : 256 * head + T],
        )
        for head in range(HEADS)
    ]
    grad_v = jnp.concatenate(grad_v_t, 0).T.astype(BF16)
    first_t = first.T
    value_grad = dot(first_t, grad_v).astype(BF16)
    proj_grad = dot_tn(mixed, grad_att).astype(BF16)
    last = value_grad[176:C]
    last = jnp.concatenate(
        [last[:, 0:64], last[:, 64:128], last[:, 128:C], jnp.zeros((144, 64), BF16)], 0
    )
    proj_grad = jnp.concatenate([proj_grad, last], -1).reshape(12, 16, 256)
    value_grad = jnp.concatenate([value_grad, jnp.zeros((C, 64), BF16)], -1).reshape(12, 16, 256)
    parts_fc[0, 36:42] = proj_grad[:6]
    parts_fc[1, 36:42] = proj_grad[6:]
    parts_fc[0, 43:48] = value_grad[0:5]
    parts_fc[1, 42:48] = value_grad[5:11]
    vec[3:4, 0:C] = jnp.sum(grad_second * hat2, 0, keepdims=True)
    vec[4:5, 0:C] = jnp.sum(grad_v.astype(F32), 0, keepdims=True)
    parts_fc[0, 42] = vec[...].astype(BF16)
    early1(2)

    for head in range(HEADS):
        wide_cols[256 * head : 256 * head + T, :] = keys * ones[head]
    grad_k_t = []
    for head in range(HEADS):
        rows = slice(HEAD * head, HEAD * (head + 1))
        gm = grad_mixed * ones[head]
        probs = prob[head]
        grad_probs = dot_nt(gm, values)
        inside = jnp.sum(probs * grad_probs, -1, keepdims=True)
        grad_scores = probs * (grad_probs - inside)
        dsc[head, 0:T, 0:T] = grad_scores
        scaled = (grad_scores * FACTOR).astype(BF16)
        wide_rows[:, 256 * head : 256 * head + T] = scaled
        grad_k_t.append(dot(queries_t[rows], scaled))
    grad_q = dot(wide_rows[...], wide_cols[...])
    grad_k = jnp.concatenate(grad_k_t, 0).T

    grad_qk = jnp.concatenate([grad_q, grad_k], -1).astype(BF16)
    wide = dot(first_t, grad_qk).astype(BF16)
    wide = [wide[:, 128 * n : 128 * (n + 1)].reshape(12, 16, 128) for n in range(3)]
    parts_att[0, 0:12] = wide[0]
    parts_att[0, 12:18] = wide[1][:6]
    parts_att[1, 0:6] = wide[1][6:]
    parts_att[1, 6:18] = wide[2]
    grad_first = dot_nt(grad_qk, wqkv_ref[:, 0 : 2 * C])
    grad_first = grad_first + dot_nt(grad_v, wqkv_ref[:, 2 * C : 3 * C])
    grad_first = grad_first.astype(BF16).astype(F32)
    vec[...] = jnp.zeros_like(vec)
    sums = jnp.sum(grad_qk.astype(F32), 0, keepdims=True)
    sums = [sums[:, C * n : C * (n + 1)] for n in range(2)]
    sums.append(jnp.sum(grad_first * hat1, 0, keepdims=True))
    for n in range(3):
        vec[2 * n : 2 * n + 1, 0:128] = sums[n][:, 0:128]
        vec[2 * n + 1 : 2 * n + 2, 0:64] = sums[n][:, 128:C]
    parts_att[0, 18] = vec[:, 0:128].astype(BF16)
    parts_att[1, 18] = jnp.zeros((16, 128), BF16)
    parts_att[:, 19:] = jnp.zeros((2, ATT - 19, 16, 128), BF16)
    late1()
    early2(0)
    early2(1)
    d_tokens = grad_inner + norm_back(hat1, inv1, gain1, grad_first)
    stage[1] = d_tokens
    hand_out(1)
    early2(2)

    for head in range(HEADS):
        if head == 3:
            early3(0)
            early3(1)
        acc = jnp.zeros((16, 384), F32)
        for w in range(WIN_W):
            acc = acc + pltpu.roll(
                dsc[head, w * GROUPS : w * GROUPS + 16, :], (WIN_W - 1 - w) * GROUPS, axis=1
            )
        for n in range(3):
            dmat[n, pl.ds(head, 16, stride=8), :] = acc[:, 128 * n : 128 * (n + 1)]

    def table_grad():
        return jnp.concatenate([dmat[n, 0:96, :] for n in range(3)], -1)

    def keep_table(field):
        for n in range(3):
            dmat[n, 0:96, :] = field[:, 128 * n : 128 * (n + 1)]

    def edge_copy():
        return pltpu.make_async_remote_copy(
            src_ref=bbs,
            dst_ref=bbr,
            send_sem=one_send.at[1],
            recv_sem=one_recv.at[1],
            device_id=(lon, north),
            device_id_type=MESH,
        )

    @pl.when(lat == 0)
    def _():
        upper = lax.broadcasted_iota(jnp.int32, (96, 384), 0) < 48
        full = table_grad()
        bbs[...] = jnp.where(upper, full, 0.0).astype(BF16)
        edge_copy().start()
        keep_table(jnp.where(upper, 0.0, full))

    early3(2)
    early4(0)
    early4(1)
    late2()

    @pl.when(lat == BANDS - 1)
    def _():
        edge_copy().wait_recv()
        keep_table(table_grad() + bbr[...].astype(F32))

    bsend[...] = table_grad().astype(BF16).reshape(PARTS, 16, 384)

    for owner in range(PARTS):
        @pl.when(lon != owner)
        def _():
            pltpu.make_async_remote_copy(
                src_ref=bsend.at[owner],
                dst_ref=brecv.at[lon],
                send_sem=b_send.at[0],
                recv_sem=b_recv.at[0],
                device_id=(owner, lat),
                device_id_type=MESH,
            ).start()

    hand_out(0)
    early4(2)
    early5(0)
    early5(1)
    late3()
    early5(2)
    seven = brecv.at[pl.ds(0, STRIPS - 1)]

    @pl.when(lon < PARTS)
    def _():
        brecv[lon] = bsend[lon]
        wait_bytes(seven, b_recv.at[0])
        bfin[lon] = jnp.sum(brecv[...].astype(F32), 0).astype(BF16)
        for d in range(1, STRIPS):
            pltpu.make_async_remote_copy(
                src_ref=bfin.at[lon],
                dst_ref=bfin.at[lon],
                send_sem=b_send.at[1],
                recv_sem=b_recv.at[1],
                device_id=(strip(d), lat),
                device_id_type=MESH,
            ).start()

    late4()
    for n in range(3):
        early6(n)

    @pl.when(lon < PARTS)
    def _():
        wait_bytes(bfin.at[pl.ds(0, PARTS - 1)], b_recv.at[1])

    @pl.when(lon >= PARTS)
    def _():
        wait_bytes(bfin, b_recv.at[1])

    tin[...] = dot_nt(bfin[...].reshape(96, 384), perm_ref[...])
    dtab_ref[...] = jnp.zeros_like(dtab_ref)
    for zp in range(WIN_Z):
        for zq in range(WIN_Z):
            for hp in range(WIN_H):
                j = (zp * WIN_Z + zq) * WIN_H + hp
                first_lane = j * WIN_H * SPAN
                base = first_lane // 128 * 128
                g = hp * WIN_Z + zp
                piece = tin[g * 8 : g * 8 + 8, zq * 256 : zq * 256 + 256]
                piece = jnp.concatenate([piece, jnp.zeros((8, 128), F32)], -1)
                moved = pltpu.roll(piece, first_lane - base, axis=1)
                dtab_ref[:, base : base + 384] = dtab_ref[:, base : base + 384] + moved

    keep[2].start()

    for a in range(2):
        for i in range(3):
            exchange(a, i).wait_send()
            give_back(a, i).wait()

    @pl.when(lat == BANDS - 1)
    def _():
        table_copy().wait_send()

    @pl.when(lat == 0)
    def _():
        edge_copy().wait_send()

    for n in range(3):
        wait_bytes(fold1.at[n], f_send.at[1, n])
        for stage_no in (2, 3, 4):
            wait_bytes(fold2.at[n], f_send.at[stage_no, n])
        wait_bytes(fold1.at[n, pl.ds(0, 3)], f_send.at[5, n])
    for stage_no, ref in ((1, fold_att), (2, eighth), (3, eighth)):
        wait_bytes(ref, a_send.at[stage_no])

    @pl.when(lon < PARTS)
    def _():
        wait_bytes(bsend.at[pl.ds(0, PARTS - 1)], b_send.at[0])
        wait_bytes(seven, b_send.at[1])

    @pl.when(lon >= PARTS)
    def _():
        wait_bytes(bsend, b_send.at[0])

    for copy in keep:
        copy.wait()
    for copy in swap_fc:
        copy.wait()
    swap_att.wait()


def output_kernel(*refs):
    ins, outs = refs[:5], refs[5:16]
    in_bufs, out_bufs = refs[16:21], refs[21:30]
    in_sem, out_sem = refs[30:]
    loads = [
        pltpu.make_async_copy(src, dst, in_sem.at[n])
        for n, (src, dst) in enumerate(zip(ins, in_bufs))
    ]
    stores = [
        pltpu.make_async_copy(src, dst, out_sem.at[n])
        for n, (src, dst) in enumerate(zip(in_bufs[:2] + out_bufs, outs))
    ]
    gath_ref, gath_att, dtab_ref = in_bufs[2:]
    (
        dln1_ref, dwqkv_ref, dbqkv_ref, dbias_ref, dwproj_ref, dln2_ref,
        dwfc1_ref, dbfc1_ref, dwfc2_ref,
    ) = out_bufs
    for n in (2, 0, 1, 3, 4):
        loads[n].start()
    loads[2].wait()
    for n in range(3):
        cols = slice(256 * n, 256 * (n + 1))
        rows = slice(12 * n, 12 * (n + 1))
        dwfc1_ref[:, cols] = gath_ref[0, rows].reshape(C, 256).astype(F32)
    stores[8].start()
    for n in range(3):
        cols = slice(256 * n, 256 * (n + 1))
        rows = slice(12 * n, 12 * (n + 1))
        dwfc2_ref[:, cols] = gath_ref[1, rows].reshape(C, 256).astype(F32)
    stores[10].start()
    for k in range(2):
        dwproj_ref[96 * k : 96 * (k + 1), :] = (
            gath_ref[k, 36:42].reshape(96, 256)[:, 0:C].astype(F32)
        )
    vec = gath_ref[0, 42].astype(F32)
    dbfc1_ref[...] = jnp.concatenate([vec[n : n + 1] for n in range(3)], -1).reshape(HID)
    dln2_ref[...] = vec[3:4, :C].reshape(C)
    for n in (6, 9, 7):
        stores[n].start()
    for n in range(2):
        loads[n].wait()
        stores[n].start()
    loads[3].wait()
    dwqkv_ref[:, 0:128] = gath_att[0, 0:12].reshape(C, 128).astype(F32)
    dwqkv_ref[0:96, 128:256] = gath_att[0, 12:18].reshape(96, 128).astype(F32)
    dwqkv_ref[96:C, 128:256] = gath_att[1, 0:6].reshape(96, 128).astype(F32)
    dwqkv_ref[:, 256:384] = gath_att[1, 6:18].reshape(C, 128).astype(F32)
    dwqkv_ref[0:80, 384:576] = gath_ref[0, 43:48].reshape(80, 256)[:, 0:C].astype(F32)
    dwqkv_ref[80:176, 384:576] = gath_ref[1, 42:48].reshape(96, 256)[:, 0:C].astype(F32)
    last = [gath_ref[0, 36 + n][:, C:256].astype(F32) for n in range(3)]
    dwqkv_ref[176:C, 384:576] = jnp.concatenate(last, -1)
    value_bias = vec[4:5, :C]
    vec = gath_att[0, 18].astype(F32)
    sums = [
        jnp.concatenate([vec[2 * n : 2 * n + 1], vec[2 * n + 1 : 2 * n + 2, :64]], -1)
        for n in range(3)
    ]
    dbqkv_ref[...] = jnp.concatenate(sums[:2] + [value_bias], -1).reshape(3 * C)
    dln1_ref[...] = sums[2].reshape(C)
    for n in (3, 4, 2):
        stores[n].start()
    loads[4].wait()
    for head in range(HEADS):
        dbias_ref[0, head] = dtab_ref[head : head + 1, 0:NREL]
    stores[5].start()
    for store in stores:
        store.wait()


def per_device(
    tokens, cotangent, ln1_gain, w_qkv, b_qkv, bias_table, w_proj, ln2_gain, w_fc1, b_fc1, w_fc2
):
    hbm = pl.BlockSpec(memory_space=pl.ANY)
    perm = table_order()
    dma = pltpu.SemaphoreType.DMA
    args = (
        tokens.transpose(1, 2, 0, 3), cotangent.transpose(1, 2, 0, 3), ln1_gain, w_qkv, b_qkv,
        bias_table.transpose(0, 2, 1, 3), w_proj, ln2_gain, w_fc1, b_fc1, w_fc2.T,
        jnp.asarray(perm, BF16), jnp.asarray(cross_pairs()),
    )
    gathered, gathered_att, block, d_tok, table = pl.pallas_call(
        block_kernel,
        out_shape=(
            jax.ShapeDtypeStruct((2, FC, 16, 256), BF16),
            jax.ShapeDtypeStruct((2, ATT, 16, 128), BF16),
            jax.ShapeDtypeStruct((WIN_H, WIN_W, WIN_Z, C), BF16),
            jax.ShapeDtypeStruct((WIN_H, WIN_W, WIN_Z, C), BF16),
            jax.ShapeDtypeStruct((8, 3456), F32),
        ),
        in_specs=[hbm] * len(args),
        out_specs=(hbm,) * 5,
        scratch_shapes=[pltpu.VMEM(a.shape, a.dtype) for a in args[2:]]
        + [
            pltpu.VMEM((2, T, C), F32),
            pltpu.VMEM((2, 4, 3, 6, WIN_Z, C), BF16),
            pltpu.VMEM((2, 4, 3, 6, WIN_Z, C), BF16),
            pltpu.VMEM((8, 3456), F32),
            pltpu.VMEM((1, HEADS, 1, NREL), F32),
            pltpu.VMEM((96, 512), F32),
            pltpu.VMEM((3, 128, 128), F32),
            pltpu.VMEM((HEADS, T, T), F32),
            pltpu.VMEM((HEADS, T, T), F32),
            pltpu.VMEM((T, HEADS * 256), BF16),
            pltpu.VMEM((HEADS * 256, C), BF16),
            pltpu.VMEM((HEADS, 160, 384), F32),
            pltpu.VMEM((3, 128, 128), F32),
            pltpu.VMEM((16, 256), F32),
            pltpu.VMEM((PARTS, 16, 384), BF16),
            pltpu.VMEM((STRIPS, 16, 384), BF16),
            pltpu.VMEM((PARTS, 16, 384), BF16),
            pltpu.VMEM((96, 384), BF16),
            pltpu.VMEM((96, 384), BF16),
            pltpu.VMEM((2, FC, 16, 256), BF16),
            pltpu.VMEM((2, ATT, 16, 128), BF16),
            pltpu.VMEM((3, 7, 4, 16, 256), BF16),
            pltpu.VMEM((3, 4, 16, 256), BF16),
            pltpu.VMEM((3, 3, 16, 256), BF16),
            pltpu.VMEM((3, 16, 256), BF16),
            pltpu.VMEM((3, 4, 16, 256), BF16),
            pltpu.VMEM((BANDS - 1, TALL, 16, 128), BF16),
            pltpu.VMEM((TALL, 16, 128), BF16),
            pltpu.VMEM((STRIPS, TALL, 16, 128), BF16),
            pltpu.VMEM((2, FC, 16, 256), BF16),
            pltpu.VMEM((2, ATT, 16, 128), BF16),
            pltpu.VMEM((8, 3456), F32),
            dma((len(args) - 2,)), dma((2,)), dma((7,)),
            dma((2, 3)), dma((2, 3)), dma((2, 3)), dma((2, 3)),
            dma((2,)), dma((2,)), dma((7, 3)), dma((7, 3)),
            dma((5,)), dma((5,)), dma((2,)), dma((2,)),
        ],
        compiler_params=pltpu.CompilerParams(
            collective_id=0, has_side_effects=True, vmem_limit_bytes=VMEM_LIMIT
        ),
    )(*args)
    shape = jax.ShapeDtypeStruct
    grid_shape = (WIN_H, WIN_W, WIN_Z, C)
    results_out = (
        shape(grid_shape, BF16), shape(grid_shape, BF16),
        shape((C,), F32), shape((C, 3 * C), F32), shape((3 * C,), F32),
        shape((1, HEADS, 1, NREL), F32), shape((C, C), F32), shape((C,), F32),
        shape((C, HID), F32), shape((HID,), F32), shape((C, HID), F32),
    )
    outs = pl.pallas_call(
        output_kernel,
        out_shape=results_out,
        in_specs=[hbm] * 5,
        out_specs=(hbm,) * 11,
        scratch_shapes=[
            pltpu.VMEM(a.shape, a.dtype)
            for a in (block, d_tok, gathered, gathered_att, table) + results_out[2:]
        ]
        + [dma((5,)), dma((11,))],
        compiler_params=pltpu.CompilerParams(vmem_limit_bytes=VMEM_LIMIT),
    )(block, d_tok, gathered, gathered_att, table)
    out, d_tok, d_ln1, d_wqkv, d_bqkv, d_bias, d_wproj, d_ln2, d_wfc1, d_bfc1, d_wfc2 = outs
    return (
        out.transpose(2, 0, 1, 3), d_tok.transpose(2, 0, 1, 3), d_ln1, d_wqkv, d_bqkv,
        d_bias.transpose(0, 2, 1, 3), d_wproj, d_ln2, d_wfc1, d_bfc1, d_wfc2.T,
    )


def solution(mesh):
    grid = P(None, "lat", "lon", None)
    rows = P(None, "lat", None, None)
    return jax.shard_map(
        per_device,
        mesh=mesh,
        in_specs=(grid, grid, P(), P(), P(), rows, P(), P(), P(), P(), P()),
        out_specs=(grid, grid, P(), P(), P(), rows, P(), P(), P(), P(), P()),
        check_vma=False,
    )
```

```python
import jax
import jax.numpy as jnp
import numpy as np
from jax import lax
from jax.experimental import pallas as pl
from jax.experimental.pallas import tpu as pltpu
from jax.sharding import PartitionSpec as P

HEADS = 6
WIN_Z = 2
WIN_H = 6
WIN_W = 12
SPAN = 2 * WIN_W - 1
GROUPS = WIN_Z * WIN_H
T = GROUPS * WIN_W
C = 192
HID = 768
HEAD = C // HEADS
NREL = GROUPS * GROUPS * SPAN
FC = 48
ATT = 24
TALL = 3
ROWS = 8
BANDS = 16
STRIPS = 8
PARTS = 6
EPSILON = 1e-05
VMEM_LIMIT = 56 * 1024 * 1024
FACTOR = HEAD ** (-0.5)
LOG2E = 1.4426950408889634
F32 = jnp.float32
BF16 = jnp.bfloat16
MESH = pl.DeviceIdType.MESH


def table_order():
    grid = np.zeros((512, 384), np.float32)
    for z in range(WIN_Z):
        for h in range(WIN_H):
            for i in range(SPAN):
                grid[z * 256 + h * SPAN + i, (SPAN - 1 - i) * GROUPS + h * WIN_Z + z] = 1
    return grid


def cross_pairs():
    g = np.arange(96)[:, None] // 8 // WIN_Z
    q = np.arange(384)[None, :] % GROUPS // WIN_Z
    return np.where((g < 3) != (q < 3), -1e30, 0.0).astype(np.float32)


def dot(a, b):
    return jnp.dot(a, b, preferred_element_type=F32)


def dot_nt(a, b):
    return lax.dot_general(a, b, (((1,), (1,)), ((), ())), preferred_element_type=F32)


def dot_tn(a, b):
    return lax.dot_general(a, b, (((0,), (0,)), ((), ())), preferred_element_type=F32)


def normalize(values, gain):
    average = jnp.mean(values, -1, keepdims=True)
    centered = values - average
    inv = lax.rsqrt(jnp.mean(centered * centered, -1, keepdims=True) + EPSILON)
    hat = centered * inv
    return hat * gain, hat, inv


def norm_back(hat, inv, gain, grad):
    scaled = grad * gain
    return inv * (
        scaled
        - jnp.mean(scaled, -1, keepdims=True)
        - hat * jnp.mean(scaled * hat, -1, keepdims=True)
    )


def pieces():
    for h in range(WIN_H):
        for w in range(WIN_W):
            at = w * GROUPS + h * WIN_Z
            yield (h // 3) * 2 + w // 6, h % 3, w % 6, slice(at, at + WIN_Z)


def quadrant(ref, q):
    return ref.at[pl.ds(q // 2 * 3, 3), pl.ds(q % 2 * 6, 6)]


def block_kernel(
    tok_any, cot_any, g1_any, wqkv_any, bqkv_any, table_any, wproj_any, g2_any, wfc1_any,
    bfc1_any, wfc2_any, perm_any, cross_any,
    gath_fc_out, gath_att_out, block_out, dtok_out, dtab_out,
    g1_ref, wqkv_ref, bqkv_ref, table_ref, wproj_ref, g2_ref, wfc1_ref,
    bfc1_ref, wfc2_ref, perm_ref, cross_ref,
    stage, arrive, out_stage,
    tabw, tab15, tin, ymat, bias, prob, wide_rows, wide_cols, dsc, dmat, vec,
    bsend, brecv, bfin, bbs, bbr,
    parts_fc, parts_att, core_att, fold1, sum1, fold2, sum2, fold3, fold_att, sum_att,
    mid_att, gath_fc, gath_att, dtab_ref,
    in_sem, own_sem, out_sem,
    ex_send, ex_recv, rt_send, rt_recv, one_send, one_recv, f_send, f_recv,
    a_send, a_recv, b_send, b_recv,
):
    sources = (
        (table_any, table_ref), (perm_any, perm_ref), (cross_any, cross_ref), (g1_any, g1_ref),
        (wqkv_any, wqkv_ref), (bqkv_any, bqkv_ref), (wproj_any, wproj_ref), (g2_any, g2_ref),
        (wfc1_any, wfc1_ref), (bfc1_any, bfc1_ref), (wfc2_any, wfc2_ref),
    )
    loads = [pltpu.make_async_copy(src, dst, in_sem.at[n]) for n, (src, dst) in enumerate(sources)]
    lon = lax.axis_index("lon")
    lat = lax.axis_index("lat")
    core = lax.rem(lat, 2)
    other = 1 - core
    pair_row = lat // 2
    east = lax.rem(lon + 1, STRIPS)
    west = lax.rem(lon + STRIPS - 1, STRIPS)
    south = lax.rem(lat + 1, BANDS)
    north = lax.rem(lat + BANDS - 1, BANDS)
    sibling = (lon, lat - core + other)

    spot = (lax.rem(pair_row, 4), lon // 2, lax.rem(lon, 2) * 2 + lat // 8)

    def on_axis(axis, at, side=core):
        if axis == 0:
            return (lon, lat // 8 * 8 + at * 2 + side)
        if axis == 1:
            return (at * 2 + lax.rem(lon, 2), lat - core + side)
        return (spot[1] * 2 + at // 2, lax.rem(at, 2) * 8 + spot[0] * 2 + side)

    def strip(d):
        return lax.rem(lon + d, STRIPS)

    def row_of(d):
        return lax.rem(pair_row + d, ROWS)

    barrier = pltpu.get_barrier_semaphore()

    def greet(target):
        pl.semaphore_signal(barrier, inc=1, device_id=target, device_id_type=MESH)

    for target in ((east, south), (west, north)):
        greet(target)
    for d in range(1, STRIPS):
        greet((strip(d), lat))
    for d in range(1, BANDS):
        greet((lon, lax.rem(lat + d, BANDS)))
    for d in range(1, 4):
        greet(on_axis(1, lax.rem(spot[1] + d, 4), other))
    across = lax.rem(spot[2] + 2, 4)
    greet(on_axis(2, across, other))
    greet(on_axis(2, 3 - spot[2]))
    greet(on_axis(2, 3 - spot[2], other))
    loads[0].start()
    own = [
        pltpu.make_async_copy(quadrant(src, 0), arrive.at[a, 3], own_sem.at[a])
        for a, src in enumerate((tok_any, cot_any))
    ]
    own[0].start()
    pl.semaphore_wait(barrier, 30)

    ahead = ((east, lat), (lon, south), (east, south))
    behind = ((west, lat), (lon, north), (west, north))

    def exchange(a, i):
        return pltpu.make_async_remote_copy(
            src_ref=quadrant((tok_any, cot_any)[a], i + 1),
            dst_ref=arrive.at[a, 2 - i],
            send_sem=ex_send.at[a, i],
            recv_sem=ex_recv.at[a, i],
            device_id=ahead[i],
            device_id_type=MESH,
        )

    def table_copy():
        return pltpu.make_async_remote_copy(
            src_ref=table_any,
            dst_ref=tab15,
            send_sem=one_send.at[0],
            recv_sem=one_recv.at[0],
            device_id=(lon, south),
            device_id_type=MESH,
        )

    @pl.when(lat == BANDS - 1)
    def _():
        table_copy().start()

    for a in range(2):
        for i in range(3):
            exchange(a, i).start()
    for load in loads[1:]:
        load.start()
    own[1].start()

    tabw[...] = jnp.zeros_like(tabw)
    loads[0].wait()
    for head in range(HEADS):
        tabw[head : head + 1, 0:NREL] = table_ref[0, head]

    tin[...] = jnp.zeros_like(tin)

    def spread(src, zp, zq, hp, width):
        j = (zp * WIN_Z + zq) * WIN_H + hp
        first = j * WIN_H * SPAN
        base = first // 128 * 128
        wide = src[:, base : base + 384]
        moved = pltpu.roll(wide, (384 - (first - base)) % 384, axis=1)
        g = hp * WIN_Z + zp
        tin[g * 8 : g * 8 + 8, zq * 256 : zq * 256 + width] = moved[:, :width]

    for zp in range(WIN_Z):
        for zq in range(WIN_Z):
            for hp in range(WIN_H):
                spread(tabw, zp, zq, hp, WIN_H * SPAN)

    def permuted(whole):
        high = whole.astype(BF16)
        rest = whole - high.astype(F32)
        middle = rest.astype(BF16)
        low = (rest - middle.astype(F32)).astype(BF16)
        perm = perm_ref[...]
        return (dot(high, perm) + dot(middle, perm) + dot(low, perm)) * LOG2E

    loads[1].wait()
    spread_rows = permuted(tin[...])
    for n in range(3):
        ymat[n, 0:96, :] = spread_rows[:, 128 * n : 128 * (n + 1)]
        ymat[n, 96:128, :] = jnp.zeros((32, 128), F32)
    loads[2].wait()

    @pl.when(lat == 0)
    def _():
        for n in range(3):
            ymat[n, 0:96, :] = ymat[n, 0:96, :] + cross_ref[:, 128 * n : 128 * (n + 1)]

    def place_bias(tall, count):
        for head in range(HEADS):
            rows = jnp.concatenate(
                [ymat[n, pl.ds(head, tall, stride=8), :] for n in range(3)], -1
            )
            for w in range(WIN_W):
                moved = pltpu.roll(rows, (384 - (WIN_W - 1 - w) * GROUPS) % 384, axis=1)
                bias[head, w * GROUPS : w * GROUPS + count, :] = moved[:count, :T]

    place_bias(16, GROUPS)
    for n in range(3, 11):
        loads[n].wait()
    lane = lax.broadcasted_iota(jnp.int32, (16, C), 1)
    ones = [
        jnp.where((lane >= HEAD * i) & (lane < HEAD * (i + 1)), 1.0, 0.0).astype(BF16)[0:1]
        for i in range(HEADS)
    ]
    gain1 = g1_ref[...].reshape(1, C)
    gain2 = g2_ref[...].reshape(1, C)

    def arrived(a):
        for i in range(3):
            exchange(a, i).wait_recv()
        own[a].wait()
        for slot, row, col, rows in pieces():
            stage[a, rows, :] = arrive[a, slot, row, col].astype(F32)
        return stage[a]

    tokens = arrived(0)
    normed, hat1, inv1 = normalize(tokens, gain1)
    first = normed.astype(BF16)
    qkv = (dot(first, wqkv_ref[...]) + bqkv_ref[...].reshape(1, 3 * C)).astype(BF16)
    queries = qkv[:, 0:C]
    keys = qkv[:, C : 2 * C]
    values = qkv[:, 2 * C : 3 * C]
    queries_t = queries.T

    @pl.when(lat == 0)
    def _():
        table_copy().wait_recv()
        for head in range(HEADS):
            tabw[head : head + 1, 0:NREL] = tab15[0, head]
        tin[0:48, :] = jnp.zeros((48, 512), F32)
        for zp in range(WIN_Z):
            for zq in range(WIN_Z):
                for hp in range(3):
                    spread(tabw, zp, zq, hp, 3 * SPAN)
        upper_rows = permuted(tin[0:48, :]) + cross_ref[0:48, :]
        for n in range(3):
            ymat[n, 0:48, :] = upper_rows[:, 128 * n : 128 * (n + 1)]
        place_bias(8, 6)

    wide_rows[...] = jnp.zeros_like(wide_rows)
    wide_cols[...] = jnp.zeros_like(wide_cols)
    for head in range(HEADS):
        wide_cols[256 * head : 256 * head + T, :] = values * ones[head]
    for head in range(HEADS):
        q = queries * ones[head]
        scores = dot_nt(q, keys) * (FACTOR * LOG2E) + bias[head]
        top = jnp.max(scores, -1, keepdims=True)
        raised = jnp.exp2(scores - top)
        probs = raised * (1.0 / jnp.sum(raised, -1, keepdims=True))
        prob[head] = probs
        probs_low = probs.astype(BF16)
        wide_rows[:, 256 * head : 256 * head + T] = probs_low
    mixed = dot(wide_rows[...], wide_cols[...]).astype(BF16)
    inner = tokens + dot(mixed, wproj_ref[...]).astype(BF16).astype(F32)

    def remote(src, dst, send_sem, recv_sem, target):
        return pltpu.make_async_remote_copy(
            src_ref=src, dst_ref=dst, send_sem=send_sem, recv_sem=recv_sem,
            device_id=target, device_id_type=MESH,
        )

    def wait_bytes(ref, sem):
        pltpu.make_async_copy(ref, ref, sem).wait()

    def add(*terms):
        total = terms[0].astype(F32)
        for term in terms[1:]:
            total = total + term.astype(F32)
        return total.astype(BF16)

    axes = [(n, (n + 1) % 3, (n + 2) % 3) for n in range(3)]
    places = [tuple(spot[axis] for axis in order) for order in axes]

    def block(n, i):
        return pl.ds(n * 16 + i * 4, 4)

    def unit(n):
        return n * 16 + places[n][0] * 4 + places[n][1]

    def part_to_line(n, stage_no, which, src, dst):
        for d in range(1, 4):
            at = lax.rem(places[n][which] + d, 4)
            remote(
                src(n, at), dst(n, d), f_send.at[stage_no, n], f_recv.at[stage_no, n],
                on_axis(axes[n][which], at),
            ).start()

    def third(n):
        return pl.ds(16 * n, 16)

    swap_fc = [
        remote(
            gath_fc.at[core, third(n)], gath_fc_out.at[core, third(n)],
            f_send.at[6, n], f_recv.at[6, n], sibling,
        )
        for n in range(3)
    ]
    pair_att = remote(parts_att.at[other], core_att, a_send.at[0], a_recv.at[0], sibling)
    swap_att = remote(
        gath_att.at[core], gath_att_out.at[core], a_send.at[4], a_recv.at[4], sibling
    )
    kept = [
        (out_stage.at[0, 3], quadrant(block_out, 0)),
        (out_stage.at[1, 3], quadrant(dtok_out, 0)),
        (dtab_ref, dtab_out),
        (gath_att.at[core], gath_att_out.at[core]),
    ] + [(gath_fc.at[core, third(n)], gath_fc_out.at[core, third(n)]) for n in range(3)]
    keep = [
        pltpu.make_async_copy(src, dst, out_sem.at[n]) for n, (src, dst) in enumerate(kept)
    ]

    def early1(n):
        for side, first, slot in ((core, 1, -1), (other, 0, 3)):
            for d in range(first, 4):
                at = lax.rem(places[n][0] + d, 4)
                remote(
                    parts_fc.at[side, block(n, at)], fold1.at[n, slot + d],
                    f_send.at[1, n], f_recv.at[1, n], on_axis(n, at, side),
                ).start()

    def early2():
        for n in range(3):
            wait_bytes(fold1.at[n], f_recv.at[1, n])
            own_block = parts_fc[core, block(n, places[n][0])]
            sum1[n] = add(own_block, *[fold1[n, i] for i in range(7)])
            part_to_line(
                n, 2, 1, lambda n, at: sum1.at[n, at], lambda n, d: fold2.at[n, d - 1]
            )

    def early3():
        for n in range(3):
            wait_bytes(fold2.at[n], f_recv.at[2, n])
            own_unit = sum1[n, places[n][1]]
            sum2[n] = add(own_unit, fold2[n, 0], fold2[n, 1], fold2[n, 2])
            fold3[n, places[n][2]] = sum2[n]
            part_to_line(
                n, 3, 2, lambda n, at: sum2.at[n], lambda n, d: fold3.at[n, places[n][2]]
            )

    def early4():
        for n in range(3):
            wait_bytes(fold2.at[n], f_recv.at[3, n])
            gath_fc[core, unit(n)] = add(*[fold3[n, i] for i in range(4)])
            part_to_line(
                n, 4, 1, lambda n, at: gath_fc.at[core, unit(n)],
                lambda n, d: gath_fc.at[core, unit(n)],
            )

    def early5():
        for n in range(3):
            wait_bytes(fold2.at[n], f_recv.at[4, n])
            part_to_line(
                n, 5, 0, lambda n, at: gath_fc.at[core, block(n, places[n][0])],
                lambda n, d: gath_fc.at[core, block(n, places[n][0])],
            )

    def early6():
        for n in range(3):
            wait_bytes(fold1.at[n, pl.ds(0, 3)], f_recv.at[5, n])
            swap_fc[n].start()
            keep[4 + n].start()

    own_rows = pl.ds(pair_row * TALL, TALL)

    def late1():
        pair_att.wait_recv()
        parts_att[core] = add(parts_att[core], core_att[...])
        for d in range(1, ROWS):
            remote(
                parts_att.at[core, pl.ds(row_of(d) * TALL, TALL)], fold_att.at[d - 1],
                a_send.at[1], a_recv.at[1], (lon, row_of(d) * 2 + core),
            ).start()

    def late2():
        wait_bytes(fold_att, a_recv.at[1])
        sum_att[...] = add(parts_att[core, own_rows], *[fold_att[d] for d in range(ROWS - 1)])
        mid_att[lon] = sum_att[...]
        for d in range(1, STRIPS):
            remote(
                sum_att, mid_att.at[lon], a_send.at[2], a_recv.at[2], (strip(d), lat)
            ).start()

    def late3():
        wait_bytes(fold_att, a_recv.at[2])
        gath_att[core, own_rows] = add(*[mid_att[i] for i in range(STRIPS)])
        for d in range(1, ROWS):
            remote(
                gath_att.at[core, own_rows], gath_att.at[core, own_rows],
                a_send.at[3], a_recv.at[3], (lon, row_of(d) * 2 + core),
            ).start()

    def late4():
        wait_bytes(fold_att, a_recv.at[3])
        swap_att.start()
        keep[3].start()

    cot = arrived(1)
    cot_low = cot.astype(BF16)
    normed, hat2, inv2 = normalize(inner, gain2)
    second = normed.astype(BF16)
    second_t = second.T
    cot_t = cot_low.T
    total = inner
    grad_second = jnp.zeros((T, C), F32)
    bfc1 = bfc1_ref[...].reshape(1, HID)
    vec[...] = jnp.zeros_like(vec)
    for n in range(3):
        cols = slice(256 * n, 256 * (n + 1))
        pre = dot(second, wfc1_ref[:, cols]) + bfc1[:, cols]
        cdf = 0.5 * (1.0 + lax.erf(pre * 0.7071067811865476))
        density = jnp.exp(-0.5 * pre * pre) * 0.3989422804014327
        act = (pre * cdf).astype(BF16)
        total = total + dot_nt(act, wfc2_ref[:, cols])
        grad_pre = (dot(cot_low, wfc2_ref[:, cols]) * (cdf + pre * density)).astype(BF16)
        grad_second = grad_second + dot_nt(grad_pre, wfc1_ref[:, cols])
        parts_fc[0, 12 * n : 12 * (n + 1)] = dot(second_t, grad_pre).astype(BF16).reshape(12, 16, 256)
        parts_fc[1, 12 * n : 12 * (n + 1)] = dot(cot_t, act).astype(BF16).reshape(12, 16, 256)
        vec[n : n + 1, :] = jnp.sum(grad_pre.astype(F32), 0, keepdims=True)
        if n:
            early1(n - 1)

    def give_back(a, i):
        return pltpu.make_async_remote_copy(
            src_ref=out_stage.at[a, 2 - i],
            dst_ref=quadrant((block_out, dtok_out)[a], i + 1),
            send_sem=rt_send.at[a, i],
            recv_sem=rt_recv.at[a, i],
            device_id=behind[i],
            device_id_type=MESH,
        )

    def hand_out(a, field):
        stage[a] = field
        for slot, row, col, rows in pieces():
            out_stage[a, slot, row, col] = stage[a, rows, :].astype(BF16)
        for i in range(3):
            give_back(a, i).start()
        keep[a].start()

    grad_inner = cot + norm_back(hat2, inv2, gain2, grad_second)
    grad_att = grad_inner.astype(BF16)
    hand_out(0, total)
    grad_mixed = dot_nt(grad_att, wproj_ref[...]).astype(BF16)
    grad_mixed_t = grad_mixed.T
    grad_v_t = [
        dot(
            grad_mixed_t[HEAD * head : HEAD * (head + 1)],
            wide_rows[:, 256 * head : 256 * head + T],
        )
        for head in range(HEADS)
    ]
    grad_v = jnp.concatenate(grad_v_t, 0).T.astype(BF16)
    first_t = first.T
    value_grad = dot(first_t, grad_v).astype(BF16)
    proj_grad = dot_tn(mixed, grad_att).astype(BF16)
    last = value_grad[176:C]
    last = jnp.concatenate(
        [last[:, 0:64], last[:, 64:128], last[:, 128:C], jnp.zeros((144, 64), BF16)], 0
    )
    proj_grad = jnp.concatenate([proj_grad, last], -1).reshape(12, 16, 256)
    value_grad = jnp.concatenate([value_grad, jnp.zeros((C, 64), BF16)], -1).reshape(12, 16, 256)
    parts_fc[0, 36:42] = proj_grad[:6]
    parts_fc[1, 36:42] = proj_grad[6:]
    parts_fc[0, 43:48] = value_grad[0:5]
    parts_fc[1, 42:48] = value_grad[5:11]
    vec[3:4, 0:C] = jnp.sum(grad_second * hat2, 0, keepdims=True)
    vec[4:5, 0:C] = jnp.sum(grad_v.astype(F32), 0, keepdims=True)
    parts_fc[0, 42] = vec[...].astype(BF16)
    early1(2)

    dsc[...] = jnp.zeros_like(dsc)
    for head in range(HEADS):
        wide_cols[256 * head : 256 * head + T, :] = keys * ones[head]
    grad_k_t = []
    for head in range(HEADS):
        rows = slice(HEAD * head, HEAD * (head + 1))
        gm = grad_mixed * ones[head]
        probs = prob[head]
        grad_probs = dot_nt(gm, values)
        inside = jnp.sum(probs * grad_probs, -1, keepdims=True)
        grad_scores = probs * (grad_probs - inside)
        dsc[head, 0:T, 0:T] = grad_scores
        scaled = (grad_scores * FACTOR).astype(BF16)
        wide_rows[:, 256 * head : 256 * head + T] = scaled
        grad_k_t.append(dot(queries_t[rows], scaled))
    grad_q = dot(wide_rows[...], wide_cols[...])
    grad_k = jnp.concatenate(grad_k_t, 0).T

    grad_qk = jnp.concatenate([grad_q, grad_k], -1).astype(BF16)
    wide = dot(first_t, grad_qk).astype(BF16)
    wide = [wide[:, 128 * n : 128 * (n + 1)].reshape(12, 16, 128) for n in range(3)]
    parts_att[0, 0:12] = wide[0]
    parts_att[0, 12:18] = wide[1][:6]
    parts_att[1, 0:6] = wide[1][6:]
    parts_att[1, 6:18] = wide[2]
    grad_first = dot_nt(grad_qk, wqkv_ref[:, 0 : 2 * C])
    grad_first = grad_first + dot_nt(grad_v, wqkv_ref[:, 2 * C : 3 * C])
    grad_first = grad_first.astype(BF16).astype(F32)
    vec[...] = jnp.zeros_like(vec)
    sums = jnp.sum(grad_qk.astype(F32), 0, keepdims=True)
    sums = [sums[:, C * n : C * (n + 1)] for n in range(2)]
    sums.append(jnp.sum(grad_first * hat1, 0, keepdims=True))
    for n in range(3):
        vec[2 * n : 2 * n + 1, 0:128] = sums[n][:, 0:128]
        vec[2 * n + 1 : 2 * n + 2, 0:64] = sums[n][:, 128:C]
    parts_att[0, 18] = vec[:, 0:128].astype(BF16)
    parts_att[1, 18] = jnp.zeros((16, 128), BF16)
    parts_att[:, 19:] = jnp.zeros((2, ATT - 19, 16, 128), BF16)
    pair_att.start()
    d_tokens = grad_inner + norm_back(hat1, inv1, gain1, grad_first)
    hand_out(1, d_tokens)

    dmat[...] = jnp.zeros_like(dmat)
    for head in range(HEADS):
        if head == 2:
            late1()
            early2()
        acc = jnp.zeros((16, 384), F32)
        for w in range(WIN_W):
            acc = acc + pltpu.roll(
                dsc[head, w * GROUPS : w * GROUPS + 16, :], (WIN_W - 1 - w) * GROUPS, axis=1
            )
        for n in range(3):
            dmat[n, pl.ds(head, 16, stride=8), :] = acc[:, 128 * n : 128 * (n + 1)]

    def table_grad():
        return jnp.concatenate([dmat[n, 0:96, :] for n in range(3)], -1)

    def keep_table(field):
        for n in range(3):
            dmat[n, 0:96, :] = field[:, 128 * n : 128 * (n + 1)]

    def edge_copy():
        return pltpu.make_async_remote_copy(
            src_ref=bbs,
            dst_ref=bbr,
            send_sem=one_send.at[1],
            recv_sem=one_recv.at[1],
            device_id=(lon, north),
            device_id_type=MESH,
        )

    @pl.when(lat == 0)
    def _():
        upper = lax.broadcasted_iota(jnp.int32, (96, 384), 0) < 48
        full = table_grad()
        bbs[...] = jnp.where(upper, full, 0.0).astype(BF16)
        edge_copy().start()
        keep_table(jnp.where(upper, 0.0, full))

    late2()
    early3()

    @pl.when(lat == BANDS - 1)
    def _():
        edge_copy().wait_recv()
        keep_table(table_grad() + bbr[...].astype(F32))

    bsend[...] = table_grad().astype(BF16).reshape(PARTS, 16, 384)

    for owner in range(PARTS):
        @pl.when(lon != owner)
        def _():
            pltpu.make_async_remote_copy(
                src_ref=bsend.at[owner],
                dst_ref=brecv.at[lon],
                send_sem=b_send.at[0],
                recv_sem=b_recv.at[0],
                device_id=(owner, lat),
                device_id_type=MESH,
            ).start()

    early4()
    late3()
    early5()
    seven = brecv.at[pl.ds(0, STRIPS - 1)]

    @pl.when(lon < PARTS)
    def _():
        brecv[lon] = bsend[lon]
        wait_bytes(seven, b_recv.at[0])
        bfin[lon] = jnp.sum(brecv[...].astype(F32), 0).astype(BF16)
        for d in range(1, STRIPS):
            pltpu.make_async_remote_copy(
                src_ref=bfin.at[lon],
                dst_ref=bfin.at[lon],
                send_sem=b_send.at[1],
                recv_sem=b_recv.at[1],
                device_id=(strip(d), lat),
                device_id_type=MESH,
            ).start()

    late4()
    early6()

    @pl.when(lon < PARTS)
    def _():
        wait_bytes(bfin.at[pl.ds(0, PARTS - 1)], b_recv.at[1])

    @pl.when(lon >= PARTS)
    def _():
        wait_bytes(bfin, b_recv.at[1])

    tin[...] = dot_nt(bfin[...].reshape(96, 384), perm_ref[...])
    dtab_ref[...] = jnp.zeros_like(dtab_ref)
    for zp in range(WIN_Z):
        for zq in range(WIN_Z):
            for hp in range(WIN_H):
                j = (zp * WIN_Z + zq) * WIN_H + hp
                first_lane = j * WIN_H * SPAN
                base = first_lane // 128 * 128
                g = hp * WIN_Z + zp
                piece = tin[g * 8 : g * 8 + 8, zq * 256 : zq * 256 + 256]
                piece = jnp.concatenate([piece, jnp.zeros((8, 128), F32)], -1)
                moved = pltpu.roll(piece, first_lane - base, axis=1)
                dtab_ref[:, base : base + 384] = dtab_ref[:, base : base + 384] + moved

    keep[2].start()

    for a in range(2):
        for i in range(3):
            exchange(a, i).wait_send()
            give_back(a, i).wait()

    @pl.when(lat == BANDS - 1)
    def _():
        table_copy().wait_send()

    @pl.when(lat == 0)
    def _():
        edge_copy().wait_send()

    for n in range(3):
        wait_bytes(fold1.at[n], f_send.at[1, n])
        for stage_no in (2, 3, 4):
            wait_bytes(fold2.at[n], f_send.at[stage_no, n])
        wait_bytes(fold1.at[n, pl.ds(0, 3)], f_send.at[5, n])
    pair_att.wait_send()
    for stage_no in (1, 2, 3):
        wait_bytes(fold_att, a_send.at[stage_no])

    @pl.when(lon < PARTS)
    def _():
        wait_bytes(bsend.at[pl.ds(0, PARTS - 1)], b_send.at[0])
        wait_bytes(seven, b_send.at[1])

    @pl.when(lon >= PARTS)
    def _():
        wait_bytes(bsend, b_send.at[0])

    for copy in keep:
        copy.wait()
    for copy in swap_fc:
        copy.wait()
    swap_att.wait()


def output_kernel(*refs):
    ins, outs = refs[:5], refs[5:16]
    in_bufs, out_bufs = refs[16:21], refs[21:30]
    in_sem, out_sem = refs[30:]
    loads = [
        pltpu.make_async_copy(src, dst, in_sem.at[n])
        for n, (src, dst) in enumerate(
            [(ins[2].at[k], in_bufs[2].at[k]) for k in range(2)]
            + [(ins[n], in_bufs[n]) for n in (4, 0, 1, 3)]
        )
    ]
    stores = [
        pltpu.make_async_copy(src, dst, out_sem.at[n])
        for n, (src, dst) in enumerate(zip(in_bufs[:2] + out_bufs, outs))
    ]
    gath_ref, gath_att, dtab_ref = in_bufs[2:]
    (
        dln1_ref, dwqkv_ref, dbqkv_ref, dbias_ref, dwproj_ref, dln2_ref,
        dwfc1_ref, dbfc1_ref, dwfc2_ref,
    ) = out_bufs
    for load in loads:
        load.start()
    loads[2].wait()
    for head in range(HEADS):
        dbias_ref[0, head] = dtab_ref[head : head + 1, 0:NREL]
    stores[5].start()
    for n in range(2):
        loads[3 + n].wait()
        stores[n].start()
    loads[0].wait()
    for n in range(3):
        cols = slice(256 * n, 256 * (n + 1))
        rows = slice(12 * n, 12 * (n + 1))
        dwfc1_ref[:, cols] = gath_ref[0, rows].reshape(C, 256).astype(F32)
    stores[8].start()
    loads[1].wait()
    for n in range(3):
        cols = slice(256 * n, 256 * (n + 1))
        rows = slice(12 * n, 12 * (n + 1))
        dwfc2_ref[:, cols] = gath_ref[1, rows].reshape(C, 256).astype(F32)
    stores[10].start()
    for k in range(2):
        dwproj_ref[96 * k : 96 * (k + 1), :] = (
            gath_ref[k, 36:42].reshape(96, 256)[:, 0:C].astype(F32)
        )
    vec = gath_ref[0, 42].astype(F32)
    dbfc1_ref[...] = jnp.concatenate([vec[n : n + 1] for n in range(3)], -1).reshape(HID)
    dln2_ref[...] = vec[3:4, :C].reshape(C)
    for n in (6, 9, 7):
        stores[n].start()
    loads[5].wait()
    dwqkv_ref[:, 0:128] = gath_att[0, 0:12].reshape(C, 128).astype(F32)
    dwqkv_ref[0:96, 128:256] = gath_att[0, 12:18].reshape(96, 128).astype(F32)
    dwqkv_ref[96:C, 128:256] = gath_att[1, 0:6].reshape(96, 128).astype(F32)
    dwqkv_ref[:, 256:384] = gath_att[1, 6:18].reshape(C, 128).astype(F32)
    dwqkv_ref[0:80, 384:576] = gath_ref[0, 43:48].reshape(80, 256)[:, 0:C].astype(F32)
    dwqkv_ref[80:176, 384:576] = gath_ref[1, 42:48].reshape(96, 256)[:, 0:C].astype(F32)
    last = [gath_ref[0, 36 + n][:, C:256].astype(F32) for n in range(3)]
    dwqkv_ref[176:C, 384:576] = jnp.concatenate(last, -1)
    value_bias = vec[4:5, :C]
    vec = gath_att[0, 18].astype(F32)
    sums = [
        jnp.concatenate([vec[2 * n : 2 * n + 1], vec[2 * n + 1 : 2 * n + 2, :64]], -1)
        for n in range(3)
    ]
    dbqkv_ref[...] = jnp.concatenate(sums[:2] + [value_bias], -1).reshape(3 * C)
    dln1_ref[...] = sums[2].reshape(C)
    for n in (3, 4, 2):
        stores[n].start()
    for store in stores:
        store.wait()


def per_device(
    tokens, cotangent, ln1_gain, w_qkv, b_qkv, bias_table, w_proj, ln2_gain, w_fc1, b_fc1, w_fc2
):
    hbm = pl.BlockSpec(memory_space=pl.ANY)
    perm = table_order()
    dma = pltpu.SemaphoreType.DMA
    args = (
        tokens.transpose(1, 2, 0, 3), cotangent.transpose(1, 2, 0, 3), ln1_gain, w_qkv, b_qkv,
        bias_table.transpose(0, 2, 1, 3), w_proj, ln2_gain, w_fc1, b_fc1, w_fc2.T,
        jnp.asarray(perm, BF16), jnp.asarray(cross_pairs()),
    )
    gathered, gathered_att, block, d_tok, table = pl.pallas_call(
        block_kernel,
        out_shape=(
            jax.ShapeDtypeStruct((2, FC, 16, 256), BF16),
            jax.ShapeDtypeStruct((2, ATT, 16, 128), BF16),
            jax.ShapeDtypeStruct((WIN_H, WIN_W, WIN_Z, C), BF16),
            jax.ShapeDtypeStruct((WIN_H, WIN_W, WIN_Z, C), BF16),
            jax.ShapeDtypeStruct((8, 3456), F32),
        ),
        in_specs=[hbm] * len(args),
        out_specs=(hbm,) * 5,
        scratch_shapes=[pltpu.VMEM(a.shape, a.dtype) for a in args[2:]]
        + [
            pltpu.VMEM((2, T, C), F32),
            pltpu.VMEM((2, 4, 3, 6, WIN_Z, C), BF16),
            pltpu.VMEM((2, 4, 3, 6, WIN_Z, C), BF16),
            pltpu.VMEM((8, 3456), F32),
            pltpu.VMEM((1, HEADS, 1, NREL), F32),
            pltpu.VMEM((96, 512), F32),
            pltpu.VMEM((3, 128, 128), F32),
            pltpu.VMEM((HEADS, T, T), F32),
            pltpu.VMEM((HEADS, T, T), F32),
            pltpu.VMEM((T, HEADS * 256), BF16),
            pltpu.VMEM((HEADS * 256, C), BF16),
            pltpu.VMEM((HEADS, 160, 384), F32),
            pltpu.VMEM((3, 128, 128), F32),
            pltpu.VMEM((16, 256), F32),
            pltpu.VMEM((PARTS, 16, 384), BF16),
            pltpu.VMEM((STRIPS, 16, 384), BF16),
            pltpu.VMEM((PARTS, 16, 384), BF16),
            pltpu.VMEM((96, 384), BF16),
            pltpu.VMEM((96, 384), BF16),
            pltpu.VMEM((2, FC, 16, 256), BF16),
            pltpu.VMEM((2, ATT, 16, 128), BF16),
            pltpu.VMEM((ATT, 16, 128), BF16),
            pltpu.VMEM((3, 7, 4, 16, 256), BF16),
            pltpu.VMEM((3, 4, 16, 256), BF16),
            pltpu.VMEM((3, 3, 16, 256), BF16),
            pltpu.VMEM((3, 16, 256), BF16),
            pltpu.VMEM((3, 4, 16, 256), BF16),
            pltpu.VMEM((ROWS - 1, TALL, 16, 128), BF16),
            pltpu.VMEM((TALL, 16, 128), BF16),
            pltpu.VMEM((STRIPS, TALL, 16, 128), BF16),
            pltpu.VMEM((2, FC, 16, 256), BF16),
            pltpu.VMEM((2, ATT, 16, 128), BF16),
            pltpu.VMEM((8, 3456), F32),
            dma((len(args) - 2,)), dma((2,)), dma((7,)),
            dma((2, 3)), dma((2, 3)), dma((2, 3)), dma((2, 3)),
            dma((2,)), dma((2,)), dma((7, 3)), dma((7, 3)),
            dma((5,)), dma((5,)), dma((2,)), dma((2,)),
        ],
        compiler_params=pltpu.CompilerParams(
            collective_id=0, has_side_effects=True, vmem_limit_bytes=VMEM_LIMIT
        ),
    )(*args)
    shape = jax.ShapeDtypeStruct
    grid_shape = (WIN_H, WIN_W, WIN_Z, C)
    results_out = (
        shape(grid_shape, BF16), shape(grid_shape, BF16),
        shape((C,), F32), shape((C, 3 * C), F32), shape((3 * C,), F32),
        shape((1, HEADS, 1, NREL), F32), shape((C, C), F32), shape((C,), F32),
        shape((C, HID), F32), shape((HID,), F32), shape((C, HID), F32),
    )
    outs = pl.pallas_call(
        output_kernel,
        out_shape=results_out,
        in_specs=[hbm] * 5,
        out_specs=(hbm,) * 11,
        scratch_shapes=[
            pltpu.VMEM(a.shape, a.dtype)
            for a in (block, d_tok, gathered, gathered_att, table) + results_out[2:]
        ]
        + [dma((6,)), dma((11,))],
        compiler_params=pltpu.CompilerParams(vmem_limit_bytes=VMEM_LIMIT),
    )(block, d_tok, gathered, gathered_att, table)
    out, d_tok, d_ln1, d_wqkv, d_bqkv, d_bias, d_wproj, d_ln2, d_wfc1, d_bfc1, d_wfc2 = outs
    return (
        out.transpose(2, 0, 1, 3), d_tok.transpose(2, 0, 1, 3), d_ln1, d_wqkv, d_bqkv,
        d_bias.transpose(0, 2, 1, 3), d_wproj, d_ln2, d_wfc1, d_bfc1, d_wfc2.T,
    )


def solution(mesh):
    grid = P(None, "lat", "lon", None)
    rows = P(None, "lat", None, None)
    return jax.shard_map(
        per_device,
        mesh=mesh,
        in_specs=(grid, grid, P(), P(), P(), rows, P(), P(), P(), P(), P()),
        out_specs=(grid, grid, P(), P(), P(), rows, P(), P(), P(), P(), P()),
        check_vma=False,
    )
```
